32 devices in a mesh: dp: 4 (over y, x), fsdp: 8 (over z, core).
Axes of the slice: x: 2, y: 2, z: 4, core: 2. Of those that a mesh axis runs over, the one named last changes fastest.
Arguments:
- features: bfloat16 [128, 2, 10, 10, 768], P(('dp', 'fsdp')), may hold values from -6 to 6
- cotangent: bfloat16 [128, 2, 10, 10, 768], P(('dp', 'fsdp')), may hold values from -6 to 6
- image_sizes: int32 [128], P(('dp', 'fsdp')), may hold values from 0 to 10, as said below
- warp_index: int32 [128, 100, 4], P(('dp', 'fsdp')), may hold values from 0 to 99, as said below
- warp_weight: float32 [128, 100, 4], P(('dp', 'fsdp')), may hold values from 0 to 1, as said below
- offsets: int32 [81, 2], replicated, may hold values from -4 to 4, as said below
- conv_kernel: bfloat16 [49, 768], P(None, 'fsdp'), may hold values from -0.875 to 0.875
- conv_bias: bfloat16 [768], P('fsdp'), may hold values from -3 to 3
- norm_gain: bfloat16 [768], P('fsdp'), may hold values from 0.5 to 1.5
- norm_bias: bfloat16 [768], P('fsdp'), may hold values from -2 to 2
- w_in: bfloat16 [768, 3072], P('fsdp'), may hold values from -0.21875 to 0.21875
- bias_in: bfloat16 [3072], P('fsdp'), may hold values from -2 to 2
- w_out: bfloat16 [3072, 768], P('fsdp'), may hold values from -0.109375 to 0.109375
- bias_out: bfloat16 [768], P('fsdp'), may hold values from -2 to 2
- layer_scale: bfloat16 [768], P('fsdp'), may hold values from 0.5 to 1.5
- w_estimate: bfloat16 [81, 768], P(None, 'fsdp'), may hold values from -0.625 to 0.625
Outputs:
- mixed_out: bfloat16 [128, 2, 10, 10, 768], P(('dp', 'fsdp'))
- grad_features: float32 [128, 2, 10, 10, 768], P(('dp', 'fsdp'))
- grad_conv_kernel: float32 [49, 768], P(None, 'fsdp')
- grad_conv_bias: float32 [768], P('fsdp')
- grad_norm_gain: float32 [768], P('fsdp')
- grad_norm_bias: float32 [768], P('fsdp')
- grad_w_in: float32 [768, 3072], P('fsdp')
- grad_bias_in: float32 [3072], P('fsdp')
- grad_w_out: float32 [3072, 768], P('fsdp')
- grad_bias_out: float32 [768], P('fsdp')
- grad_layer_scale: float32 [768], P('fsdp')
- grad_w_estimate: float32 [81, 768], P(None, 'fsdp')
The draws below stay inside these ranges and needn't reach their ends.
Inputs may be any that keep to these rules, and one draw needn't show every extreme that they name: `image_sizes`: each value is 0, 7, 8 or 10; in each device's 4 slots the live images come first and empty slots (0) last, and some device has no empty slot. `warp_index`: cells of the same slot; inside the image, the four corners of a unit square that lies in the image; outside it, the cell itself four times. `warp_weight`: nonnegative bilinear weights, four to a cell, summing to one. `offsets`: the rows are the 81 cells of a 9 x 9 window centred at zero, each once, in some order.
All inputs are finite; a program needn't handle non-finite values.
Results may differ from the reference program's by a relative error of at most 0.0072.
Values may be sent and summed in bfloat16 or wider, within the bound.
No kernel may reach another device: no remote copies, remote signals or barrier semaphores. Data moves between devices by JAX's collectives and lax.ppermute only.
A program may use at most 320 MiB of HBM per device.

```python
import jax
import jax.numpy as jnp
from jax import lax

D = 768
FF = 3072
IMG_DEV = 4
CANVAS = 10
KERNEL = 7
WINDOW = 9
PIX = 100
TAPS = 49
OFFSETS = 81
IMAGES = 128


def sizes_helper(key):
    live_key, size_key, full_key = jax.random.split(key, 3)
    device_count = IMAGES // IMG_DEV
    live_count = jax.random.randint(live_key, (device_count,), 1, IMG_DEV + 1)
    busiest = jax.random.randint(full_key, (), 0, device_count)
    live_count = jnp.where(jnp.arange(device_count) == busiest, IMG_DEV, live_count)
    picked = jax.random.randint(size_key, (IMAGES,), 0, 3)
    sides_all = jnp.where(picked == 0, 7, jnp.where(picked == 1, 8, CANVAS))
    slot_of = jnp.arange(IMAGES) % IMG_DEV
    device_of = jnp.arange(IMAGES) // IMG_DEV
    return jnp.where(slot_of < live_count[device_of], sides_all, 0).astype(jnp.int32)


def draw_image_sizes(key, part):
    return sizes_helper(key)


def draw_warp_index(key, part):
    sides_all = sizes_helper(key)
    key = jax.random.fold_in(key, 11)
    row_key, col_key = jax.random.split(key)
    cells = jnp.arange(PIX, dtype=jnp.int32)
    row_of = cells // CANVAS
    col_of = cells % CANVAS
    move_row = jax.random.randint(row_key, (IMAGES, PIX), -2, 3)
    move_col = jax.random.randint(col_key, (IMAGES, PIX), -2, 3)
    side_col = sides_all[:, None]
    inside = (row_of[None, :] < side_col) & (col_of[None, :] < side_col)
    upper = jnp.maximum(side_col - 2, 0)
    base_row = jnp.clip(row_of[None, :] + move_row, 0, upper)
    base_col = jnp.clip(col_of[None, :] + move_col, 0, upper)
    corner = base_row * CANVAS + base_col
    stacked = jnp.stack([corner, corner + 1, corner + CANVAS, corner + CANVAS + 1], axis=-1)
    own_cell = jnp.broadcast_to(cells[None, :, None], (IMAGES, PIX, 4))
    return jnp.where(inside[..., None], stacked, own_cell).astype(jnp.int32)


def draw_warp_weight(key, part):
    key = jax.random.fold_in(key, 13)
    row_key, col_key = jax.random.split(key)
    frac_row = jax.random.uniform(row_key, (IMAGES, PIX), jnp.float32)
    frac_col = jax.random.uniform(col_key, (IMAGES, PIX), jnp.float32)
    return jnp.stack([(1.0 - frac_row) * (1.0 - frac_col), (1.0 - frac_row) * frac_col, frac_row * (1.0 - frac_col), frac_row * frac_col], axis=-1)


def draw_offsets(key, part):
    key = jax.random.fold_in(key, 17)
    ordering = jax.random.permutation(key, OFFSETS)
    return jnp.stack([ordering // WINDOW - WINDOW // 2, ordering % WINDOW - WINDOW // 2], axis=-1).astype(jnp.int32)


def steps_of(key, extent, shards, least, high):
    factor_of, own = 1.0, jax.random.fold_in(key, 6)
    for position, shards_of in shards:
        heights = jnp.exp(jax.random.uniform(jax.random.fold_in(own, position), (shards_of,), jnp.float32, least / len(shards), high / len(shards)))
        factor_of = factor_of * jnp.repeat(heights, extent[position] // shards_of).reshape([-1 if axis == position else 1 for axis in range(len(extent))])
    return factor_of


def scatter_about(stream_key, extent, deviation, bound, shards=(), kind=jnp.bfloat16):
    entries = jax.random.normal(stream_key, extent, jnp.float32) * deviation
    if len(shards) > 0:
        entries = steps_of(stream_key, extent, shards, -0.22, 0.18) * entries
    return jnp.clip(entries, min=-bound, max=bound).astype(kind)


def setup_inputs(seed: int = 0) -> dict:
    arg_keys = jax.random.split(jax.random.key(seed), 17)
    return {
        "features": scatter_about(arg_keys[0], (IMAGES, 2, CANVAS, CANVAS, D), 1.0, 6.0, ((0, 32),)),
        "cotangent": scatter_about(arg_keys[1], (IMAGES, 2, CANVAS, CANVAS, D), 1.0, 6.0, ((0, 32),)),
        "image_sizes": draw_image_sizes(jax.random.fold_in(arg_keys[16], 71), 0),
        "warp_index": draw_warp_index(jax.random.fold_in(arg_keys[16], 71), 0),
        "warp_weight": draw_warp_weight(jax.random.fold_in(arg_keys[16], 71), 0),
        "offsets": draw_offsets(jax.random.fold_in(arg_keys[16], 71), 0),
        "conv_kernel": scatter_about(arg_keys[6], (TAPS, D), TAPS ** -0.5, 0.875, ((1, 8),)),
        "conv_bias": scatter_about(arg_keys[7], (D,), 0.5, 3.0, ((0, 8),)),
        "norm_gain": jnp.clip(1.0 + 0.1 * jax.random.normal(arg_keys[8], (D,), jnp.float32), 0.5, 1.5).astype(jnp.bfloat16),
        "norm_bias": scatter_about(arg_keys[9], (D,), 0.3, 2.0, ((0, 8),)),
        "w_in": scatter_about(arg_keys[10], (D, FF), D ** -0.5, 0.21875, ((0, 8),)),
        "bias_in": scatter_about(arg_keys[11], (FF,), 0.3, 2.0, ((0, 8),)),
        "w_out": scatter_about(arg_keys[12], (FF, D), FF ** -0.5, 0.109375, ((0, 8),)),
        "bias_out": scatter_about(arg_keys[13], (D,), 0.3, 2.0, ((0, 8),)),
        "layer_scale": jnp.clip(1.0 + 0.1 * jax.random.normal(arg_keys[14], (D,), jnp.float32), 0.5, 1.5).astype(jnp.bfloat16),
        "w_estimate": scatter_about(arg_keys[15], (OFFSETS, D), OFFSETS ** -0.5, 0.625, ((1, 8),)),
    }


EPSILON = 1e-06
HIGHEST = lax.Precision.HIGHEST

@jax.custom_vjp
def low(v):
    return lax.optimization_barrier(v.astype(jnp.bfloat16)).astype(jnp.float32)

@jax.custom_vjp
def low_back(v):
    return v

def low_keep(v):
    return (low(v), None)

def low_pass(kept, grad):
    return (grad,)

def back_keep(v):
    return (v, None)

def back_low(kept, grad):
    return (low(grad),)
low.defvjp(low_keep, low_pass)
low_back.defvjp(back_keep, back_low)

def gelu_exact(values):
    return jax.nn.gelu(values, approximate=False)

def pixel_mask(image_sizes):
    places = jnp.arange(CANVAS, dtype=jnp.int32)
    inside = places[None, :] < image_sizes[:, None]
    return (inside[:, :, None] & inside[:, None, :]).astype(jnp.float32)

def warp_matrix(warp_index, warp_weight):
    cells = jnp.arange(PIX, dtype=jnp.int32)
    onehot = (warp_index[..., None] == cells).astype(jnp.float32)
    return lax.optimization_barrier(jnp.sum(warp_weight[..., None] * onehot, axis=2))

def select_table(offsets):
    cells = jnp.arange(PIX, dtype=jnp.int32)
    row_of = cells // CANVAS
    col_of = cells % CANVAS
    target_row = row_of[:, None] + offsets[None, :, 0]
    target_col = col_of[:, None] + offsets[None, :, 1]
    valid = (target_row >= 0) & (target_row < CANVAS) & (target_col >= 0) & (target_col < CANVAS)
    target = target_row * CANVAS + target_col
    return (valid[..., None] & (target[..., None] == cells)).astype(jnp.float32)

def depthwise(images_flat, kernel):
    reach = KERNEL // 2
    padded = jnp.pad(images_flat, ((0, 0), (reach, reach), (reach, reach), (0, 0)))
    total = jnp.zeros(images_flat.shape, images_flat.dtype)
    for row_tap in range(KERNEL):
        for col_tap in range(KERNEL):
            total = total + padded[:, row_tap:row_tap + CANVAS, col_tap:col_tap + CANVAS, :] * kernel[row_tap * KERNEL + col_tap]
    return total

def mix_norm(images_flat, kernel, conv_bias, norm_gain, norm_bias):
    conv_out = depthwise(images_flat, kernel) + conv_bias
    rows_in = conv_out.reshape(-1, conv_out.shape[-1])
    centred = rows_in - lax.optimization_barrier(jnp.mean(rows_in, axis=-1, keepdims=True))
    variance = lax.optimization_barrier(jnp.mean(centred * centred, axis=-1, keepdims=True))
    return centred * lax.rsqrt(variance + EPSILON) * norm_gain + norm_bias

def forward(inputs, side_mask, mats, table, params):
    conv_kernel, conv_bias, norm_gain, norm_bias, w_in, bias_in, w_out, bias_out, layer_scale, w_estimate = params
    images_here = inputs.shape[0]
    masked = inputs * side_mask[:, None, :, :, None]
    normed = low(mix_norm(masked.reshape(-1, CANVAS, CANVAS, D), conv_kernel, conv_bias, norm_gain, norm_bias))
    hidden = low_back(jnp.dot(normed, w_in, precision=HIGHEST) + bias_in)
    active = low(gelu_exact(hidden))
    branch = low_back(jnp.dot(active, w_out, precision=HIGHEST) + bias_out)
    frame_mask = jnp.broadcast_to(side_mask[:, None], (images_here, 2, CANVAS, CANVAS)).reshape(-1, 1)
    mixed = ((masked.reshape(-1, D) + layer_scale * branch) * frame_mask).reshape(images_here, 2, PIX, D)
    first = mixed[:, 0]
    second = mixed[:, 1]
    warped = low(low_back(jnp.einsum('npq,nqd->npd', mats, low(second), precision=HIGHEST)))
    scores = low_back(jnp.einsum('npd,nqd->npq', low(first), warped, precision=HIGHEST))
    cost = jnp.einsum('npq,pkq->npk', scores, table, precision=HIGHEST) * D ** (-0.5)
    gated = low(gelu_exact(cost))
    head = low_back(jnp.einsum('npk,kd->npd', gated, w_estimate, precision=HIGHEST))
    first_out = (first + head) * side_mask.reshape(images_here, PIX, 1)
    return jnp.stack([first_out, second], axis=1).reshape(inputs.shape)

def reference(features, cotangent, image_sizes, warp_index, warp_weight, offsets, conv_kernel, conv_bias, norm_gain, norm_bias, w_in, bias_in, w_out, bias_out, layer_scale, w_estimate):
    weights = tuple((value.astype(jnp.float32) for value in (conv_kernel, conv_bias, norm_gain, norm_bias, w_in, bias_in, w_out, bias_out, layer_scale, w_estimate)))
    table = select_table(offsets)

    def one_block(totals, block_index):
        first_image = block_index * IMG_DEV

        def take_block(array):
            return lax.dynamic_slice_in_dim(array, first_image, IMG_DEV, 0)
        inputs = take_block(features).astype(jnp.float32)
        upstream = take_block(cotangent).astype(jnp.float32)
        side_mask = pixel_mask(take_block(image_sizes))
        mats = warp_matrix(take_block(warp_index), take_block(warp_weight).astype(jnp.float32))

        def local_forward(values, params):
            return forward(values, side_mask, mats, table, params)
        output, pull_back = jax.vjp(local_forward, inputs, weights)
        d_inputs, d_weights = pull_back(upstream)
        totals = jax.tree.map(lambda left, right: left + right, totals, d_weights)
        return (totals, (output.astype(jnp.bfloat16), d_inputs))
    zeros_init = jax.tree.map(jnp.zeros_like, weights)
    totals, (outputs, d_all) = lax.scan(one_block, zeros_init, jnp.arange(IMAGES // IMG_DEV, dtype=jnp.int32))
    outputs = outputs.reshape(features.shape)
    d_all = d_all.reshape(features.shape)
    return (outputs, d_all, totals[0], totals[1], totals[2], totals[3], totals[4], totals[5], totals[6], totals[7], totals[8], totals[9])
```

```python
import functools

import jax
import jax.numpy as jnp
import numpy as np
from jax import lax
from jax.experimental import pallas as pl
from jax.experimental.pallas import tpu as pltpu
from jax.sharding import PartitionSpec as P

CANVAS = 10
KERNEL = 7
REACH = KERNEL // 2
TAPS = KERNEL * KERNEL
WINDOW = 9
PIX = CANVAS * CANVAS
PADDED = 104
LANES = 128
EPSILON = 1e-06
f32 = jnp.float32
bf16 = jnp.bfloat16
VMEM_LIMIT = 56 * 1024 * 1024


def params(limit=VMEM_LIMIT):
    return pltpu.CompilerParams(vmem_limit_bytes=limit)


def cost(flops, nbytes, trans=0):
    return pl.CostEstimate(flops=int(flops), bytes_accessed=int(nbytes), transcendentals=int(trans))


def whole(shape):
    return pl.BlockSpec(shape, lambda *_: (0,) * len(shape))


def conv_rows(src, kernel_ref, cols, flip, finish):
    for row in range(CANVAS):
        sums = [None] * CANVAS
        for ky in range(KERNEL):
            source_row = row + ky - REACH
            if not 0 <= source_row < CANVAS:
                continue
            cells = [src[source_row * CANVAS + col, :, cols] for col in range(CANVAS)]
            for kx in range(KERNEL):
                tap = ky * KERNEL + kx
                tap = TAPS - 1 - tap if flip else tap
                weight = jnp.broadcast_to(kernel_ref[pl.ds(tap, 1), cols], cells[0].shape)
                for col in range(CANVAS):
                    source = col + kx - REACH
                    if 0 <= source < CANVAS:
                        term = cells[source] * weight
                        sums[col] = term if sums[col] is None else sums[col] + term
        for col in range(CANVAS):
            finish(row * CANVAS + col, sums[col])


def conv_norm_kernel(x_ref, kernel_ref, cbias_ref, gain_ref, shift_ref, normed_ref, xhat_ref, rstd_ref, xf, cf):
    frames = xf.shape[1]
    channels = xf.shape[2]
    xf[...] = x_ref[...].astype(f32).reshape(xf.shape)

    @pl.loop(0, channels // LANES)
    def _(tile):
        cols = pl.ds(pl.multiple_of(tile * LANES, LANES), LANES)

        def finish(cell, total):
            cf[cell, :, cols] = total + jnp.broadcast_to(cbias_ref[:, cols], total.shape)

        conv_rows(xf, kernel_ref, cols, False, finish)

    step = 10

    @pl.loop(0, PIX // step)
    def _(block):
        values = cf[pl.ds(block * step, step)].reshape(step * frames, channels)
        mean = jnp.sum(values, axis=-1, keepdims=True) * (1.0 / channels)
        centred = values - mean
        variance = jnp.sum(centred * centred, axis=-1, keepdims=True) * (1.0 / channels)
        scale = lax.rsqrt(variance + EPSILON)
        xhat = centred * scale
        rows = pl.ds(pl.multiple_of(block * step * frames, step * frames), step * frames)
        xhat_ref[rows, :] = xhat
        rstd_ref[rows, :] = scale
        normed_ref[rows, :] = (xhat * gain_ref[...] + shift_ref[...]).astype(bf16)


def conv_norm(x_rows, kernel, cbias, gain, shift, frames):
    rows, channels = x_rows.shape
    shape = (PIX, frames, channels)
    return pl.pallas_call(
        conv_norm_kernel,
        name="conv_norm",
        out_shape=(
            jax.ShapeDtypeStruct((rows, channels), bf16),
            jax.ShapeDtypeStruct((rows, channels), f32),
            jax.ShapeDtypeStruct((rows, 1), f32),
        ),
        scratch_shapes=[pltpu.VMEM(shape, f32), pltpu.VMEM(shape, f32)],
        compiler_params=params(),
        cost_estimate=cost(2 * TAPS * rows * channels * 20, rows * channels * 8),
    )(x_rows, kernel, cbias, gain, shift)


def gelu_pair(hidden):
    cdf = 0.5 * lax.erf(hidden * 0.7071067811865476) + 0.5
    density = jnp.exp(hidden * hidden * -0.5) * 0.3989422804014327
    return hidden * cdf, cdf + hidden * density


def widen_kernel(chunks, normed_ref, weight_ref, bias_ref, active_ref, slope_ref):
    size = normed_ref.shape[0] // chunks
    for chunk in range(chunks):
        rows = pl.ds(chunk * size, size)
        hidden = jnp.dot(normed_ref[rows, :], weight_ref[...], preferred_element_type=f32) + bias_ref[...]
        active, slope = gelu_pair(hidden)
        active_ref[rows, :] = active.astype(bf16)
        slope_ref[rows, :] = slope.astype(bf16)


def widen(normed, weight, bias, tile=384, chunks=5):
    rows, channels = normed.shape
    units = weight.shape[1]
    block = pl.BlockSpec((rows, tile), lambda i: (0, i))
    return pl.pallas_call(
        functools.partial(widen_kernel, chunks),
        name="widen",
        grid=(units // tile,),
        in_specs=[
            whole((rows, channels)),
            pl.BlockSpec((channels, tile), lambda i: (0, i)),
            pl.BlockSpec((1, tile), lambda i: (0, i)),
        ],
        out_specs=(block, block),
        out_shape=(jax.ShapeDtypeStruct((rows, units), bf16),) * 2,
        compiler_params=params(),
        cost_estimate=cost(2 * rows * channels * units * 2, 2 * (rows * channels + channels * units + 2 * rows * units)),
    )(normed, weight, bias)


def narrow_kernel(active_ref, weight_ref, bias_ref, branch_ref):
    part = jnp.dot(active_ref[...], weight_ref[...], preferred_element_type=f32)

    @pl.when(pl.program_id(0) == 0)
    def _():
        branch_ref[...] = part + bias_ref[...]

    @pl.when(pl.program_id(0) > 0)
    def _():
        branch_ref[...] += part


def narrow(active, weight, bias, tile=512):
    rows, units = active.shape
    channels = weight.shape[1]
    return pl.pallas_call(
        narrow_kernel,
        name="narrow",
        grid=(units // tile,),
        in_specs=[
            pl.BlockSpec((rows, tile), lambda i: (0, i)),
            pl.BlockSpec((tile, channels), lambda i: (i, 0)),
            whole((1, channels)),
        ],
        out_specs=whole((rows, channels)),
        out_shape=jax.ShapeDtypeStruct((rows, channels), f32),
        compiler_params=params(),
        cost_estimate=cost(2 * rows * channels * units, 2 * (rows * units + channels * units + 2 * rows * channels)),
    )(active, weight, bias)


def skew(values, inverse):
    rows = lax.broadcasted_iota(jnp.int32, values.shape, 0)
    centre = (WINDOW // 2) * (CANVAS + 1)
    amount = centre - rows if not inverse else rows - centre
    amount = jnp.bitwise_and(amount, LANES - 1)
    for bit in range(7):
        moved = pltpu.roll(values, 1 << bit, 1)
        values = jnp.where(jnp.bitwise_and(amount, 1 << bit) != 0, moved, values)
    return values


def split(values):
    high = values.astype(bf16)
    return high, (values - high.astype(f32)).astype(bf16)


def nt(left, right):
    return lax.dot_general(left, right, (((1,), (1,)), ((), ())), preferred_element_type=f32)


def tn(left, right):
    return lax.dot_general(left, right, (((0,), (0,)), ((), ())), preferred_element_type=f32)


def flow_kernel(
    images,
    x_ref,
    branch_ref,
    scale_ref,
    mask_ref,
    cell_mask_ref,
    upstream_ref,
    index_ref,
    weight_ref,
    place_ref,
    west_ref,
    window_ref,
    out_ref,
    dmixed_ref,
    dbranch_ref,
    gscale_ref,
    gbout_ref,
    gwest_ref,
    mixed,
    back,
):
    rows, channels = branch_ref.shape
    frames = 2 * images
    factor = channels ** (-0.5)
    tiles = channels // LANES
    for tile in range(tiles):
        cols = pl.ds(tile * LANES, LANES)
        total = x_ref[:, cols].astype(f32) + scale_ref[:, cols] * branch_ref[:, cols]
        mixed[tile, pl.ds(0, rows), :] = total * mask_ref[...]
        mixed[tile, pl.ds(rows, PADDED * frames - rows), :] = jnp.zeros((PADDED * frames - rows, LANES), f32)

    def take(frame):
        rows_of = pl.ds(frame, PADDED, stride=frames)
        return jnp.concatenate([mixed[tile, rows_of, :] for tile in range(tiles)], axis=1)

    def put(frame, values):
        rows_of = pl.ds(frame, PADDED, stride=frames)
        for tile in range(tiles):
            back[tile, rows_of, :] = values[:, tile * LANES : (tile + 1) * LANES]

    lanes = lax.broadcasted_iota(jnp.int32, (LANES, LANES), 0)
    chosen = (lanes == place_ref[...]).astype(bf16)
    west = jnp.dot(chosen, west_ref[...], preferred_element_type=f32).astype(bf16)
    window = window_ref[...]
    cells = lax.broadcasted_iota(jnp.int32, (PADDED, LANES), 1)
    gwest = jnp.zeros((LANES, channels), f32)
    for image in range(images):
        first = take(image)
        second = take(images + image)
        inside = cell_mask_ref[image]
        first_low = first.astype(bf16)
        second_low = second.astype(bf16)
        warp = jnp.zeros((PADDED, LANES), f32)
        for corner in range(4):
            place = index_ref[image, :, pl.ds(corner, 1)]
            amount = weight_ref[image, :, pl.ds(corner, 1)]
            warp = warp + jnp.where(cells == place, amount, 0.0)
        warp_high, warp_low = split(warp[:, :PADDED])
        warped = (
            jnp.dot(warp_high, second_low, preferred_element_type=f32)
            + jnp.dot(warp_low, second_low, preferred_element_type=f32)
        ).astype(bf16)
        warped_wide = jnp.concatenate([warped, jnp.zeros((LANES - PADDED, channels), bf16)], axis=0)
        scores = nt(first_low, warped_wide)
        costs = skew(scores, False) * window * factor
        gated, slope = gelu_pair(costs)
        gated_low = gated.astype(bf16)
        head = jnp.dot(gated_low, west, preferred_element_type=f32)
        out_ref[image, 0] = ((first + head) * inside)[:PIX].astype(bf16)
        out_ref[image, 1] = second_low[:PIX]
        d_first = upstream_ref[image, 0].astype(f32) * inside
        d_head = d_first.astype(bf16)
        gwest = gwest + tn(gated_low, d_head)
        d_costs = slope * nt(d_head, west) * window * factor
        d_scores = skew(d_costs, True).astype(bf16)
        d_first = d_first + jnp.dot(d_scores, warped_wide, preferred_element_type=f32)
        d_warped = tn(d_scores, first_low)[:PADDED].astype(bf16)
        d_second = upstream_ref[image, 1].astype(f32) + tn(warp_high, d_warped) + tn(warp_low, d_warped)
        put(image, d_first)
        put(images + image, d_second)
    gwest_ref[...] = gwest
    for tile in range(tiles):
        cols = pl.ds(tile * LANES, LANES)
        d_mixed = back[tile, pl.ds(0, rows), :] * mask_ref[...]
        dmixed_ref[:, cols] = d_mixed
        gscale_ref[:, cols] = jnp.sum(d_mixed * branch_ref[:, cols], axis=0, keepdims=True)
        d_branch = (d_mixed * scale_ref[:, cols]).astype(bf16)
        dbranch_ref[:, cols] = d_branch
        gbout_ref[:, cols] = jnp.sum(d_branch.astype(f32), axis=0, keepdims=True)


def window_table():
    cells = np.arange(PADDED)[:, None]
    lane = np.arange(LANES)[None, :]
    reach = WINDOW // 2
    row = cells // CANVAS + lane // CANVAS - reach
    col = cells % CANVAS + lane % CANVAS - reach
    good = (lane % CANVAS < WINDOW) & (lane // CANVAS < WINDOW) & (cells < PIX)
    good &= (row >= 0) & (row < CANVAS) & (col >= 0) & (col < CANVAS)
    return good.astype(np.float32)


def flow(x_rows, branch, scale, mask, cell_mask, upstream, index, weight, place, west):
    rows, channels = branch.shape
    images = upstream.shape[0]
    frames = 2 * images
    window = jnp.asarray(window_table())
    return pl.pallas_call(
        functools.partial(flow_kernel, images),
        name="flow",
        out_shape=(
            jax.ShapeDtypeStruct((images, 2, PIX, channels), bf16),
            jax.ShapeDtypeStruct((rows, channels), f32),
            jax.ShapeDtypeStruct((rows, channels), bf16),
            jax.ShapeDtypeStruct((1, channels), f32),
            jax.ShapeDtypeStruct((1, channels), f32),
            jax.ShapeDtypeStruct((LANES, channels), f32),
        ),
        scratch_shapes=[
            pltpu.VMEM((channels // LANES, PADDED * frames, LANES), f32),
            pltpu.VMEM((channels // LANES, PADDED * frames, LANES), f32),
        ],
        compiler_params=params(),
        cost_estimate=cost(4e9, rows * channels * 16),
    )(x_rows, branch, scale, mask, cell_mask, upstream, index, weight, place, west, window)


def grad_narrow_kernel(dbranch_t_ref, active_ref, out_ref):
    out_ref[0] = jnp.dot(dbranch_t_ref[...], active_ref[...], preferred_element_type=f32).astype(bf16)


def grad_narrow(dbranch_t, active, blocks=8):
    channels, rows = dbranch_t.shape
    units = active.shape[1]
    tile = units // blocks
    return pl.pallas_call(
        grad_narrow_kernel,
        name="grad_narrow",
        grid=(blocks,),
        in_specs=[whole((channels, rows)), pl.BlockSpec((rows, tile), lambda i: (0, i))],
        out_specs=pl.BlockSpec((1, channels, tile), lambda i: (i, 0, 0)),
        out_shape=jax.ShapeDtypeStruct((blocks, channels, tile), bf16),
        compiler_params=params(),
        cost_estimate=cost(2 * rows * channels * units, 2 * (rows * units + channels * units + rows * channels)),
    )(dbranch_t, active)


def hidden_back_kernel(dbranch_ref, weight_ref, slope_ref, normed_t_ref, dhidden_ref, gbin_ref, gwin_ref):
    d_active = nt(dbranch_ref[...], weight_ref[...])
    d_hidden = (d_active * slope_ref[...].astype(f32)).astype(bf16)
    dhidden_ref[...] = d_hidden
    gbin_ref[...] = jnp.sum(d_hidden.astype(f32), axis=0, keepdims=True)
    gwin_ref[0] = jnp.dot(normed_t_ref[...], d_hidden, preferred_element_type=f32).astype(bf16)


def hidden_back(dbranch, weight, slope, normed_t, blocks=8):
    rows, channels = dbranch.shape
    units = weight.shape[0]
    tile = units // blocks
    return pl.pallas_call(
        hidden_back_kernel,
        name="hidden_back",
        grid=(blocks,),
        in_specs=[
            whole((rows, channels)),
            pl.BlockSpec((tile, channels), lambda i: (i, 0)),
            pl.BlockSpec((rows, tile), lambda i: (0, i)),
            whole((channels, rows)),
        ],
        out_specs=(
            pl.BlockSpec((rows, tile), lambda i: (0, i)),
            pl.BlockSpec((1, tile), lambda i: (0, i)),
            pl.BlockSpec((1, channels, tile), lambda i: (i, 0, 0)),
        ),
        out_shape=(
            jax.ShapeDtypeStruct((rows, units), bf16),
            jax.ShapeDtypeStruct((1, units), f32),
            jax.ShapeDtypeStruct((blocks, channels, tile), bf16),
        ),
        compiler_params=params(),
        cost_estimate=cost(4 * rows * channels * units, 2 * (3 * rows * units + 2 * channels * units)),
    )(dbranch, weight, slope, normed_t)


def norm_back_kernel(dhidden_ref, weight_ref, xhat_ref, rstd_ref, gain_ref, dconv_ref, ggain_ref, gshift_ref, gcbias_ref):
    step = pl.program_id(0)
    part = nt(dhidden_ref[...], weight_ref[...])

    @pl.when(step == 0)
    def _():
        dconv_ref[...] = part

    @pl.when(step > 0)
    def _():
        dconv_ref[...] += part

    @pl.when(step == pl.num_programs(0) - 1)
    def _():
        rows, channels = dconv_ref.shape
        size = 80
        ggain_ref[...] = jnp.zeros_like(ggain_ref)
        gshift_ref[...] = jnp.zeros_like(gshift_ref)
        gcbias_ref[...] = jnp.zeros_like(gcbias_ref)

        @pl.loop(0, rows // size)
        def _(block):
            span = pl.ds(pl.multiple_of(block * size, size), size)
            d_normed = dconv_ref[span, :]
            xhat = xhat_ref[span, :]
            product = d_normed * xhat
            ggain_ref[...] += jnp.sum(product, axis=0, keepdims=True)
            gshift_ref[...] += jnp.sum(d_normed, axis=0, keepdims=True)
            d_xhat = d_normed * gain_ref[...]
            mean = jnp.sum(d_xhat, axis=-1, keepdims=True) * (1.0 / channels)
            along = jnp.sum(product * gain_ref[...], axis=-1, keepdims=True) * (1.0 / channels)
            d_conv = (d_xhat - mean - xhat * along) * rstd_ref[span, :]
            dconv_ref[span, :] = d_conv
            gcbias_ref[...] += jnp.sum(d_conv, axis=0, keepdims=True)


def norm_back(dhidden, weight, xhat, rstd, gain, tile=768):
    rows, units = dhidden.shape
    channels = weight.shape[0]
    vector = jax.ShapeDtypeStruct((1, channels), f32)
    return pl.pallas_call(
        norm_back_kernel,
        name="norm_back",
        grid=(units // tile,),
        in_specs=[
            pl.BlockSpec((rows, tile), lambda i: (0, i)),
            pl.BlockSpec((channels, tile), lambda i: (0, i)),
            whole((rows, channels)),
            whole((rows, 1)),
            whole((1, channels)),
        ],
        out_specs=(whole((rows, channels)),) + (whole((1, channels)),) * 3,
        out_shape=(jax.ShapeDtypeStruct((rows, channels), f32), vector, vector, vector),
        compiler_params=params(),
        cost_estimate=cost(2 * rows * channels * units, 2 * (rows * units + channels * units + 4 * rows * channels)),
    )(dhidden, weight, xhat, rstd, gain)


def grad_taps_kernel(x_ref, dconv_ref, out_ref, xf):
    xf[...] = x_ref[...].astype(f32).reshape(xf.shape)
    channels = xf.shape[2]

    @pl.loop(0, channels // LANES)
    def _(tile):
        cols = pl.ds(pl.multiple_of(tile * LANES, LANES), LANES)
        for ky in range(KERNEL):
            totals = [None] * KERNEL
            for row in range(CANVAS):
                source_row = row + ky - REACH
                if not 0 <= source_row < CANVAS:
                    continue
                cells = [xf[source_row * CANVAS + col, :, cols] for col in range(CANVAS)]
                grads = [dconv_ref[row * CANVAS + col, :, cols] for col in range(CANVAS)]
                for kx in range(KERNEL):
                    for col in range(CANVAS):
                        source = col + kx - REACH
                        if 0 <= source < CANVAS:
                            term = cells[source] * grads[col]
                            totals[kx] = term if totals[kx] is None else totals[kx] + term
            for kx in range(KERNEL):
                out_ref[pl.ds(ky * KERNEL + kx, 1), cols] = jnp.sum(totals[kx], axis=0, keepdims=True)


def grad_taps(x_rows, dconv, frames):
    rows, channels = x_rows.shape
    return pl.pallas_call(
        grad_taps_kernel,
        name="grad_taps",
        out_shape=jax.ShapeDtypeStruct((TAPS, channels), f32),
        scratch_shapes=[pltpu.VMEM((PIX, frames, channels), f32)],
        compiler_params=params(),
        cost_estimate=cost(2 * TAPS * rows * channels * 20, rows * channels * 6),
    )(x_rows, dconv.reshape(PIX, frames, channels))


def conv_back_kernel(dconv_ref, kernel_ref, dmixed_ref, mask_ref, out_ref):
    channels = dconv_ref.shape[2]

    @pl.loop(0, channels // LANES)
    def _(tile):
        cols = pl.ds(pl.multiple_of(tile * LANES, LANES), LANES)

        def finish(cell, total):
            out_ref[cell, :, cols] = (total + dmixed_ref[cell, :, cols]) * mask_ref[cell]

        conv_rows(dconv_ref, kernel_ref, cols, True, finish)


def conv_back(dconv, kernel, dmixed, mask, frames):
    rows, channels = dconv.shape
    shape = (PIX, frames, channels)
    return pl.pallas_call(
        conv_back_kernel,
        name="conv_back",
        out_shape=jax.ShapeDtypeStruct(shape, f32),
        compiler_params=params(),
        cost_estimate=cost(2 * TAPS * rows * channels * 20, rows * channels * 12),
    )(dconv.reshape(shape), kernel, dmixed.reshape(shape), mask.reshape(PIX, frames, 1))


def shards(
    features,
    cotangent,
    image_sizes,
    warp_index,
    warp_weight,
    offsets,
    conv_kernel,
    conv_bias,
    norm_gain,
    norm_bias,
    w_in,
    bias_in,
    w_out,
    bias_out,
    layer_scale,
    w_estimate,
):
    images = features.shape[0]
    frames = 2 * images
    channels = features.shape[-1]
    units = w_in.shape[1]

    def gather(value, axis=0):
        return lax.all_gather(value, "fsdp", axis=axis, tiled=True)

    vectors = jnp.concatenate(
        [conv_kernel, w_estimate, conv_bias[None], norm_gain[None], norm_bias[None], bias_out[None], layer_scale[None]]
    )
    vectors = gather(vectors, 1)
    kernel_all = vectors[:TAPS].astype(f32)
    west_all = vectors[TAPS : TAPS + offsets.shape[0]]
    rest = vectors[TAPS + offsets.shape[0] :].astype(f32)
    cbias_all, gain_all, shift_all, bout_all, scale_all = (rest[i : i + 1] for i in range(5))
    bin_all = gather(bias_in).astype(f32)[None]
    win_all = gather(w_in)
    wout_all = gather(w_out)

    places = jnp.arange(CANVAS, dtype=jnp.int32)
    inside = places[None, :] < image_sizes[:, None]
    side_mask = (inside[:, :, None] & inside[:, None, :]).astype(f32)
    cell_mask = jnp.pad(side_mask.reshape(images, PIX, 1), ((0, 0), (0, PADDED - PIX), (0, 0)))
    mask_rows = jnp.broadcast_to(side_mask.reshape(images, PIX).T[:, None, :], (PIX, 2, images)).reshape(-1, 1)
    masked = jnp.where(side_mask[:, None, :, :, None] != 0, features, jnp.zeros((), bf16))
    x_rows = masked.transpose(2, 3, 1, 0, 4).reshape(-1, channels)
    upstream = jnp.pad(cotangent.reshape(images, 2, PIX, channels), ((0, 0), (0, 0), (0, PADDED - PIX), (0, 0)))
    index = jnp.pad(warp_index, ((0, 0), (0, PADDED - PIX), (0, 0)))
    weight = jnp.pad(warp_weight, ((0, 0), (0, PADDED - PIX), (0, 0)))
    reach = WINDOW // 2
    lane_of = (offsets[:, 0] + reach) * CANVAS + offsets[:, 1] + reach
    count = offsets.shape[0]
    place = jnp.pad(lane_of, (0, LANES - count), constant_values=-1)[None]
    west_wide = jnp.pad(west_all, ((0, LANES - count), (0, 0)))

    normed, xhat, rstd = conv_norm(x_rows, kernel_all, cbias_all, gain_all, shift_all, frames)
    normed_t = normed.T
    active, slope = widen(normed, win_all, bin_all)
    branch = narrow(active, wout_all, bout_all)
    mixed_out, d_mixed, d_branch, g_scale, g_bout, g_west = flow(
        x_rows, branch, scale_all, mask_rows, cell_mask, upstream, index, weight, place, west_wide
    )
    g_wout = grad_narrow(d_branch.T, active)
    d_hidden, g_bin, g_win = hidden_back(d_branch, wout_all, slope, normed_t)
    d_conv, g_gain, g_shift, g_cbias = norm_back(d_hidden, win_all, xhat, rstd, gain_all)
    g_taps = grad_taps(x_rows, d_conv, frames)
    grad_rows = conv_back(d_conv, kernel_all, d_mixed, mask_rows, frames)
    grad_features = grad_rows.reshape(CANVAS, CANVAS, 2, images, channels).transpose(3, 2, 0, 1, 4)

    def reduce(value, axis):
        return lax.psum(lax.psum_scatter(value, "fsdp", scatter_dimension=axis, tiled=True).astype(f32), "dp")

    g_wout = reduce(g_wout.transpose(0, 2, 1).reshape(units, channels), 0)
    g_win = reduce(g_win.transpose(1, 0, 2).reshape(channels, units), 0)
    small = reduce(jnp.concatenate([g_taps, g_cbias, g_gain, g_shift, g_bout, g_scale, g_west]), 1)
    g_bin = reduce(g_bin[0], 0)
    return (
        mixed_out.reshape(features.shape),
        grad_features,
        small[:TAPS],
        small[TAPS],
        small[TAPS + 1],
        small[TAPS + 2],
        g_win,
        g_bin,
        g_wout,
        small[TAPS + 3],
        small[TAPS + 4],
        jnp.take(small[TAPS + 5 :], lane_of, axis=0),
    )


def solution(mesh):
    in_specs = (
        P(("dp", "fsdp"), None, None, None, None),
        P(("dp", "fsdp"), None, None, None, None),
        P(("dp", "fsdp")),
        P(("dp", "fsdp"), None, None),
        P(("dp", "fsdp"), None, None),
        P(),
        P(None, "fsdp"),
        P("fsdp"),
        P("fsdp"),
        P("fsdp"),
        P("fsdp", None),
        P("fsdp"),
        P("fsdp", None),
        P("fsdp"),
        P("fsdp"),
        P(None, "fsdp"),
    )
    out_specs = (
        P(("dp", "fsdp"), None, None, None, None),
        P(("dp", "fsdp"), None, None, None, None),
        P(None, "fsdp"),
        P("fsdp"),
        P("fsdp"),
        P("fsdp"),
        P("fsdp", None),
        P("fsdp"),
        P("fsdp", None),
        P("fsdp"),
        P("fsdp"),
        P(None, "fsdp"),
    )
    return jax.shard_map(shards, mesh=mesh, in_specs=in_specs, out_specs=out_specs, check_vma=False)
```

```python
import functools

import jax
import jax.numpy as jnp
import numpy as np
from jax import lax
from jax.experimental import pallas as pl
from jax.experimental.pallas import tpu as pltpu
from jax.sharding import PartitionSpec as P

CANVAS = 10
KERNEL = 7
REACH = KERNEL // 2
TAPS = KERNEL * KERNEL
WINDOW = 9
OFFSETS = WINDOW * WINDOW
PIX = CANVAS * CANVAS
PADDED = 104
LANES = 128
EPSILON = 1e-06
f32 = jnp.float32
bf16 = jnp.bfloat16
WEST = TAPS
CBIAS, GAIN, SHIFT, BOUT, SCALE = range(TAPS + OFFSETS, TAPS + OFFSETS + 5)
SMALL = TAPS + OFFSETS + 5


def call(kernel, name, out_shape, flops, scratch=(), limit=16, smem=0, **more):
    sizes = [np.prod(s.shape) * s.dtype.itemsize for s in jax.tree.leaves(out_shape)]
    specs = None

    def run(*args):
        nbytes = sum(sizes) + sum(np.prod(a.shape) * a.dtype.itemsize for a in args)
        specs = [pl.BlockSpec(memory_space=pltpu.SMEM)] * smem
        specs += [pl.BlockSpec(memory_space=pltpu.VMEM)] * (len(args) - smem)
        return pl.pallas_call(
            kernel,
            name=name,
            in_specs=specs,
            out_shape=out_shape,
            scratch_shapes=list(scratch),
            compiler_params=pltpu.CompilerParams(vmem_limit_bytes=limit * 1024 * 1024, **more),
            cost_estimate=pl.CostEstimate(flops=int(flops), bytes_accessed=int(nbytes), transcendentals=0),
        )(*args)

    return run


def array(shape, dtype=f32):
    return jax.ShapeDtypeStruct(shape, dtype)


def nt(left, right):
    return lax.dot_general(left, right, (((1,), (1,)), ((), ())), preferred_element_type=f32)


def tn(left, right):
    return lax.dot_general(left, right, (((0,), (0,)), ((), ())), preferred_element_type=f32)


def dot(left, right):
    return jnp.dot(left, right, preferred_element_type=f32)


def split(values):
    high = values.astype(bf16)
    return high, (values - high.astype(f32)).astype(bf16)


def lane_tile(tile):
    return pl.ds(tile * LANES, LANES)


def conv_rows(source, tile, kernel_ref, flip, finish):
    cols = pl.ds(pl.multiple_of(tile * LANES, LANES), LANES)
    for row in range(CANVAS):
        sums = [None] * CANVAS
        for ky in range(KERNEL):
            source_row = row + ky - REACH
            if not 0 <= source_row < CANVAS:
                continue
            cells = [source[tile, pl.ds((source_row * CANVAS + col) * 8, 8), :] for col in range(CANVAS)]
            for kx in range(KERNEL):
                tap = ky * KERNEL + kx
                tap = TAPS - 1 - tap if flip else tap
                weight = jnp.broadcast_to(kernel_ref[pl.ds(tap, 1), cols], (8, LANES))
                for col in range(CANVAS):
                    other = col + kx - REACH
                    if 0 <= other < CANVAS:
                        term = cells[other] * weight
                        sums[col] = term if sums[col] is None else sums[col] + term
        for col in range(CANVAS):
            finish(row * CANVAS + col, sums[col])


def side_of(sizes_ref, images):
    lines = lax.broadcasted_iota(jnp.int32, (2 * images, LANES), 0)
    side = jnp.zeros(lines.shape, jnp.int32)
    for image in range(images):
        side = jnp.where((lines == image) | (lines == images + image), sizes_ref[image], side)
    return side


def conv_norm_kernel(
    sizes_ref, where_ref, features_ref, upstream_ref, small_ref,
    x_ref, up_ref, normed_ref, pair_ref, xhat_ref, rstd_ref, conv, order,
):
    images = features_ref.shape[0]
    frames = 2 * images
    tiles, rows, _ = x_ref.shape
    channels = tiles * LANES
    side = side_of(sizes_ref, images)
    for tile in range(tiles):
        up_ref[tile, pl.ds(rows, PADDED * frames - rows), :] = jnp.zeros((PADDED * frames - rows, LANES), f32)
    for image in range(images):
        for which in range(2):
            for row in range(CANVAS):
                lines = pl.ds(row * CANVAS * frames + which * images + image, CANVAS, stride=frames)
                for tile in range(tiles):
                    x_ref[tile, lines, :] = features_ref[image, which, row, :, lane_tile(tile)].astype(f32)
                    up_ref[tile, lines, :] = upstream_ref[image, which, row, :, lane_tile(tile)].astype(f32)

    @pl.loop(0, tiles)
    def _(tile):
        for cell in range(PIX):
            inside = side > max(cell // CANVAS, cell % CANVAS)
            lines = pl.ds(cell * 8, 8)
            x_ref[tile, lines, :] = jnp.where(inside, x_ref[tile, lines, :], 0.0)
        cols = pl.ds(pl.multiple_of(tile * LANES, LANES), LANES)
        bias = jnp.broadcast_to(small_ref[pl.ds(CBIAS, 1), cols], (8, LANES))

        def finish(cell, total):
            conv[tile, pl.ds(cell * 8, 8), :] = total + bias

        conv_rows(x_ref, tile, small_ref, False, finish)

    share = channels // 8
    core = where_ref[1]
    for tile in range(tiles):
        source = lax.broadcasted_iota(jnp.int32, (channels, LANES), 0)
        target = lax.broadcasted_iota(jnp.int32, (channels, LANES), 1) + tile * LANES
        shard = target // share
        wanted = jnp.where(shard < 4, 2 * shard + 1 - core, 2 * (shard - 4) + core) * share + target % share
        order[:, lane_tile(tile)] = (source == wanted).astype(bf16)
    size = 160

    @pl.loop(0, rows // size)
    def _(block):
        lines = pl.ds(pl.multiple_of(block * size, size), size)
        values = jnp.concatenate([conv[tile, lines, :] for tile in range(tiles)], axis=1)
        mean = jnp.sum(values, axis=-1, keepdims=True) * (1.0 / channels)
        centred = values - mean
        variance = jnp.sum(centred * centred, axis=-1, keepdims=True) * (1.0 / channels)
        scale = lax.rsqrt(variance + EPSILON)
        xhat = centred * scale
        xhat_ref[lines, :] = xhat
        rstd_ref[lines, :] = scale
        normed = (xhat * small_ref[pl.ds(GAIN, 1), :] + small_ref[pl.ds(SHIFT, 1), :]).astype(bf16)
        normed_ref[lines, :] = normed
        pair_ref[lines, :] = dot(normed, order[...]).astype(bf16)


def conv_norm(sizes, where, features, upstream, small):
    images, channels = features.shape[0], features.shape[-1]
    rows, tiles = PIX * 2 * images, channels // LANES
    tiled = array((tiles, rows, LANES))
    padded = array((tiles, PADDED * 2 * images, LANES))
    return call(
        conv_norm_kernel,
        "conv_norm",
        (tiled, padded, array((rows, channels), bf16), array((rows, channels), bf16), array((rows, channels)), array((rows, 1))),
        4e9,
        [pltpu.VMEM(tiled.shape, f32), pltpu.VMEM((channels, channels), bf16)],
        smem=2,
    )(sizes, where, features, upstream, small)


def gelu_pair(hidden):
    cdf = 0.5 * lax.erf(hidden * 0.7071067811865476) + 0.5
    density = jnp.exp(hidden * hidden * -0.5) * 0.3989422804014327
    return hidden * cdf, cdf + hidden * density


def widen_kernel(normed_ref, weight_ref, bias_ref, active_ref, slope_ref):
    tile = 256
    for part in range(weight_ref.shape[1] // tile):
        cols = pl.ds(part * tile, tile)
        hidden = dot(normed_ref[...], weight_ref[:, cols]) + bias_ref[:, cols]
        active, slope = gelu_pair(hidden)
        active_ref[:, cols] = active.astype(bf16)
        slope_ref[:, cols] = slope.astype(bf16)


def widen(normed, weight, bias):
    rows, units = normed.shape[0], weight.shape[1]
    return call(widen_kernel, "widen", (array((rows, units), bf16),) * 2, 6e9)(normed, weight, bias)


def narrow_kernel(active_ref, weight_ref, small_ref, branch_ref):
    size = 160
    for part in range(active_ref.shape[0] // size):
        lines = pl.ds(part * size, size)
        branch = dot(active_ref[lines, :], weight_ref[...]) + small_ref[pl.ds(BOUT, 1), :]
        for tile in range(branch_ref.shape[0]):
            branch_ref[tile, lines, :] = branch[:, tile * LANES : (tile + 1) * LANES]


def narrow(active, weight, small):
    rows, channels = active.shape[0], weight.shape[1]
    return call(narrow_kernel, "narrow", array((channels // LANES, rows, LANES)), 4e9)(active, weight, small)


def skew(values, inverse):
    rows = lax.broadcasted_iota(jnp.int32, values.shape, 0)
    centre = (WINDOW // 2) * (CANVAS + 1)
    amount = jnp.bitwise_and(rows - centre if inverse else centre - rows, LANES - 1)
    for bit in range(7):
        moved = pltpu.roll(values, 1 << bit, 1)
        values = jnp.where(jnp.bitwise_and(amount, 1 << bit) != 0, moved, values)
    return values


def flow_kernel(
    sizes_ref, x_ref, branch_ref, up_ref, index_ref, weight_ref, place_ref, small_ref, window_ref,
    out_ref, dmixed_ref, dbranch_ref, gscale_ref, gbout_ref, gwest_ref, mixed, back, west_in, warp_in,
):
    tiles, rows, _ = x_ref.shape
    images = index_ref.shape[0]
    frames = 2 * images
    channels = tiles * LANES
    factor = channels ** (-0.5)
    every = range(images)
    for tile in range(tiles):
        scale = small_ref[pl.ds(SCALE, 1), lane_tile(tile)]
        mixed[tile, pl.ds(0, rows), :] = x_ref[tile] + scale * branch_ref[tile]
        mixed[tile, pl.ds(rows, PADDED * frames - rows), :] = jnp.zeros((PADDED * frames - rows, LANES), f32)

    def take(ref, frame):
        lines = pl.ds(frame, PADDED, stride=frames)
        return jnp.concatenate([ref[tile, lines, :] for tile in range(tiles)], axis=1)

    def put(ref, frame, values):
        lines = pl.ds(frame, PADDED, stride=frames)
        for tile in range(tiles):
            ref[tile, lines, :] = values[:, tile * LANES : (tile + 1) * LANES]

    west_in[...] = jnp.zeros_like(west_in)
    west_in[pl.ds(0, OFFSETS), :] = small_ref[pl.ds(WEST, OFFSETS), :]
    lanes = lax.broadcasted_iota(jnp.int32, (LANES, LANES), 0)
    west = dot((lanes == place_ref[...]).astype(bf16), west_in[...].astype(bf16)).astype(bf16)
    window = window_ref[0]
    reach = window_ref[1]
    cells = lax.broadcasted_iota(jnp.int32, (PIX, LANES), 1)
    warp_in[...] = jnp.zeros_like(warp_in)
    for image in every:
        warp = jnp.zeros((PIX, LANES), f32)
        for corner in range(4):
            place = index_ref[image, :, pl.ds(corner, 1)]
            amount = weight_ref[image, :, pl.ds(corner, 1)]
            warp = warp + jnp.where(cells == place, amount, 0.0)
        warp_in[image, pl.ds(0, PIX), :] = warp
    warps = [split(warp_in[image][:, :PADDED]) for image in every]
    inside = [(reach < sizes_ref[image].astype(f32)).astype(f32)[:, :1] for image in every]
    first = [take(mixed, image) * inside[image] for image in every]
    second = [take(mixed, images + image) * inside[image] for image in every]
    first_low = [value.astype(bf16) for value in first]
    second_low = [value.astype(bf16) for value in second]
    empty = jnp.zeros((LANES - PADDED, channels), bf16)
    warped = [
        jnp.concatenate([(dot(high, value) + dot(low, value)).astype(bf16), empty], axis=0)
        for (high, low), value in zip(warps, second_low)
    ]
    scores = [nt(left, right) for left, right in zip(first_low, warped)]
    costs = [skew(value, False) * window * factor for value in scores]
    pairs = [gelu_pair(value) for value in costs]
    gated = [value.astype(bf16) for value, _ in pairs]
    d_firsts = [take(up_ref, image) * inside[image] for image in every]
    d_heads = [value.astype(bf16) for value in d_firsts]
    d_costs = [slope * nt(d_head, west) * window * factor for (_, slope), d_head in zip(pairs, d_heads)]
    d_scores = [skew(value, True).astype(bf16) for value in d_costs]
    for image in every:
        put(back, image, d_firsts[image] + dot(d_scores[image], warped[image]))
    d_warped = [tn(value, low)[:PADDED].astype(bf16) for value, low in zip(d_scores, first_low)]
    for image in every:
        high, low = warps[image]
        d_second = take(up_ref, images + image) + tn(high, d_warped[image]) + tn(low, d_warped[image])
        put(back, images + image, d_second * inside[image])
    for tile in range(tiles):
        cols = lane_tile(tile)
        d_mixed = back[tile, pl.ds(0, rows), :]
        dmixed_ref[tile] = d_mixed
        gscale_ref[:, cols] = jnp.sum(d_mixed * branch_ref[tile], axis=0, keepdims=True)
        d_branch = (d_mixed * small_ref[pl.ds(SCALE, 1), cols]).astype(bf16)
        dbranch_ref[:, cols] = d_branch
        gbout_ref[:, cols] = jnp.sum(d_branch.astype(f32), axis=0, keepdims=True)
    gwest = tn(gated[0], d_heads[0])
    for image in every[1:]:
        gwest = gwest + tn(gated[image], d_heads[image])
    gwest_ref[...] = gwest
    for image in every:
        put(mixed, image, (first[image] + dot(gated[image], west)) * inside[image])
        put(mixed, images + image, second[image])
    for image in every:
        for which in range(2):
            for row in range(CANVAS):
                lines = pl.ds(row * CANVAS * frames + which * images + image, CANVAS, stride=frames)
                for tile in range(tiles):
                    out_ref[image, which, row, :, lane_tile(tile)] = mixed[tile, lines, :].astype(bf16)


def tables():
    cells = np.arange(PADDED)[:, None]
    lane = np.arange(LANES)[None, :]
    reach = WINDOW // 2
    row = cells // CANVAS + lane // CANVAS - reach
    col = cells % CANVAS + lane % CANVAS - reach
    good = (lane % CANVAS < WINDOW) & (lane // CANVAS < WINDOW) & (cells < PIX)
    good &= (row >= 0) & (row < CANVAS) & (col >= 0) & (col < CANVAS)
    far = np.maximum(cells // CANVAS, cells % CANVAS) + 0 * lane
    return np.stack([good, far]).astype(np.float32)


def flow(sizes, x, branch, up, index, weight, place, small):
    tiles, rows, _ = x.shape
    images, channels = index.shape[0], tiles * LANES
    padded = pltpu.VMEM((tiles, PADDED * 2 * images, LANES), f32)
    vector = array((1, channels))
    return call(
        flow_kernel,
        "flow",
        (
            array((images, 2, CANVAS, CANVAS, channels), bf16),
            array(x.shape),
            array((rows, channels), bf16),
            vector,
            vector,
            array((LANES, channels)),
        ),
        4e9,
        [padded, padded, pltpu.VMEM((LANES, channels), f32), pltpu.VMEM((images, PADDED, LANES), f32)],
        smem=1,
    )(sizes, x, branch, up, index, weight, place, small, jnp.asarray(tables()))


def grad_narrow_kernel(first_ref, active_ref, dbranch_ref, *refs):
    count, tile, _ = refs[-1].shape
    for part in range(count):
        block = 2 * part + first_ref[0] if count < 8 else part
        cols = pl.ds(pl.multiple_of(block * tile, LANES), tile)
        total = tn(active_ref[:, cols], dbranch_ref[...])
        if len(refs) > 1:
            total = total + refs[0][part].astype(f32)
        refs[-1][part] = total.astype(bf16)


def grad_narrow(first, active, dbranch, count, *received):
    units, channels = active.shape[1], dbranch.shape[1]
    shape = array((count, units // 8, channels), bf16)
    return call(grad_narrow_kernel, "grad_narrow", shape, 5e8 * count, smem=1)(first, active, dbranch, *received)


def hidden_back_kernel(dbranch_ref, weight_ref, slope_ref, pair_ref, dhidden_ref, gbin_ref, gwin_ref):
    blocks, lines, width = gwin_ref.shape
    tile = 2 * width
    for part in range(blocks // 2):
        cols = pl.ds(part * tile, tile)
        d_active = nt(dbranch_ref[...], weight_ref[cols, :])
        d_hidden = (d_active * slope_ref[:, cols].astype(f32)).astype(bf16)
        dhidden_ref[:, cols] = d_hidden
        gbin_ref[:, cols] = jnp.sum(d_hidden.astype(f32), axis=0, keepdims=True)
        total = tn(pair_ref[:, pl.ds(0, lines)], d_hidden).astype(bf16)
        gwin_ref[2 * part] = total[:, :width]
        gwin_ref[2 * part + 1] = total[:, width:]


def hidden_back(dbranch, weight, slope, pair, lines):
    rows, units = slope.shape
    return call(
        hidden_back_kernel,
        "hidden_back",
        (array((rows, units), bf16), array((1, units)), array((8, lines, units // 8), bf16)),
        6e9,
    )(dbranch, weight, slope, pair)


def grad_widen_kernel(pair_ref, dhidden_ref, received_ref, out_ref):
    blocks, lines, width = out_ref.shape
    for part in range(blocks // 2):
        cols = pl.ds(2 * part * width, 2 * width)
        total = tn(pair_ref[:, pl.ds(lines, lines)], dhidden_ref[:, cols])
        out_ref[2 * part] = (total[:, :width] + received_ref[2 * part].astype(f32)).astype(bf16)
        out_ref[2 * part + 1] = (total[:, width:] + received_ref[2 * part + 1].astype(f32)).astype(bf16)


def grad_widen(pair, dhidden, received):
    return call(grad_widen_kernel, "grad_widen", array(received.shape, bf16), 3e9)(pair, dhidden, received)


def norm_back_kernel(dhidden_ref, weight_ref, xhat_ref, rstd_ref, small_ref, dconv_ref, sums_ref):
    rows, channels = xhat_ref.shape
    size = 160
    gain = small_ref[pl.ds(GAIN, 1), :]
    sums = [jnp.zeros((1, channels), f32)] * 3
    for part in range(rows // size):
        lines = pl.ds(part * size, size)
        d_normed = nt(dhidden_ref[lines, :], weight_ref[...])
        xhat = xhat_ref[lines, :]
        product = d_normed * xhat
        d_xhat = d_normed * gain
        mean = jnp.sum(d_xhat, axis=-1, keepdims=True) * (1.0 / channels)
        along = jnp.sum(product * gain, axis=-1, keepdims=True) * (1.0 / channels)
        d_conv = (d_xhat - mean - xhat * along) * rstd_ref[lines, :]
        for tile in range(dconv_ref.shape[0]):
            dconv_ref[tile, lines, :] = d_conv[:, tile * LANES : (tile + 1) * LANES]
        for number, value in enumerate((d_conv, product, d_normed)):
            sums[number] = sums[number] + jnp.sum(value, axis=0, keepdims=True)
    sums_ref[...] = jnp.concatenate(sums, axis=0)


def norm_back(dhidden, weight, xhat, rstd, small):
    rows, channels = xhat.shape
    return call(
        norm_back_kernel, "norm_back", (array((channels // LANES, rows, LANES)), array((3, channels))), 5e9
    )(dhidden, weight, xhat, rstd, small)


def grad_taps_kernel(x_ref, dconv_ref, out_ref):
    @pl.loop(0, x_ref.shape[0])
    def _(tile):
        cols = pl.ds(pl.multiple_of(tile * LANES, LANES), LANES)
        for ky in range(KERNEL):
            totals = [None] * KERNEL
            for row in range(CANVAS):
                source_row = row + ky - REACH
                if not 0 <= source_row < CANVAS:
                    continue
                cells = [x_ref[tile, pl.ds((source_row * CANVAS + col) * 8, 8), :] for col in range(CANVAS)]
                grads = [dconv_ref[tile, pl.ds((row * CANVAS + col) * 8, 8), :] for col in range(CANVAS)]
                for kx in range(KERNEL):
                    for col in range(CANVAS):
                        source = col + kx - REACH
                        if 0 <= source < CANVAS:
                            term = cells[source] * grads[col]
                            totals[kx] = term if totals[kx] is None else totals[kx] + term
            for kx in range(KERNEL):
                out_ref[pl.ds(ky * KERNEL + kx, 1), cols] = jnp.sum(totals[kx], axis=0, keepdims=True)


def grad_taps(x, dconv):
    return call(grad_taps_kernel, "grad_taps", array((TAPS, x.shape[0] * LANES)), 4e9)(x, dconv)


def conv_back_kernel(sizes_ref, dconv_ref, small_ref, dmixed_ref, out_ref, total):
    tiles = dconv_ref.shape[0]
    images = out_ref.shape[0]
    frames = 2 * images
    side = side_of(sizes_ref, images)

    @pl.loop(0, tiles)
    def _(tile):
        def finish(cell, value):
            lines = pl.ds(cell * 8, 8)
            inside = side > max(cell // CANVAS, cell % CANVAS)
            total[tile, lines, :] = jnp.where(inside, value + dmixed_ref[tile, lines, :], 0.0)

        conv_rows(dconv_ref, tile, small_ref, True, finish)

    for image in range(images):
        for which in range(2):
            for row in range(CANVAS):
                lines = pl.ds(row * CANVAS * frames + which * images + image, CANVAS, stride=frames)
                for tile in range(tiles):
                    out_ref[image, which, row, :, lane_tile(tile)] = total[tile, lines, :]


def conv_back(sizes, dconv, small, dmixed):
    tiles, rows, _ = dconv.shape
    images = sizes.shape[0]
    return call(
        conv_back_kernel,
        "conv_back",
        array((images, 2, CANVAS, CANVAS, tiles * LANES)),
        4e9,
        [pltpu.VMEM(dconv.shape, f32)],
        smem=1,
    )(sizes, dconv, small, dmixed)


def assemble_kernel(place, where_ref, *refs):
    out_ref = refs[-1]
    z, core, group, slabs = (where_ref[number] for number in range(4))
    for side in range(2):
        own_ref, column_ref, *others = refs[5 * side : 5 * side + 5]
        parity = core if side == 0 else 1 - core
        for quarter in range(4):
            out_ref[place(2 * z + parity, quarter)] = own_ref[quarter]
        for step in range(1, 4):
            shard = 2 * lax.rem(z - step + slabs, slabs) + parity
            out_ref[place(shard, group)] = column_ref[step - 1]
            for flip in range(1, 4):
                out_ref[place(shard, jnp.bitwise_xor(group, flip))] = others[flip - 1][step - 1]


def assemble(name, place, shape, where, mine, theirs):
    kernel = functools.partial(assemble_kernel, place)
    return call(kernel, name, array(shape, bf16), 0, smem=1)(where, *mine, *theirs)


AXES = ("dp", "fsdp")


class Routes:
    def __init__(self, groups, members):
        self.groups, self.members, self.slabs = groups, members, members // 2
        self.group = lax.axis_index("dp")
        member = lax.axis_index("fsdp")
        self.slab, self.core = member // 2, member % 2

    def send(self, value, target):
        pairs = [
            (group * self.members + 2 * slab + core, self.index(*target(group, slab, core)))
            for group in range(self.groups)
            for slab in range(self.slabs)
            for core in range(2)
        ]
        return lax.ppermute(value, AXES, pairs)

    def index(self, group, slab, core):
        return group * self.members + 2 * slab + core

    def to_core(self, value):
        return self.send(value, lambda group, slab, core: (group, slab, 1 - core))

    def to_slab(self, value, step):
        return self.send(value, lambda group, slab, core: (group, (slab + step) % self.slabs, core))

    def to_group(self, value, flip):
        return self.send(value, lambda group, slab, core: (group ^ flip, slab, core))


def pick(value, index, axis=0):
    return lax.dynamic_index_in_dim(value, index, axis, keepdims=False)


def gather_pieces(routes, pieces):
    quarter = pick(pieces, routes.group)
    column = jnp.stack([routes.to_slab(quarter, step) for step in range(1, routes.slabs)])
    others = [routes.to_group(column, flip) for flip in range(1, 4)]
    mine = [pieces, column, *others]
    return mine, [routes.to_core(value) for value in mine]


def gather_small(routes, value):
    both = jnp.stack([value, routes.to_core(value)])
    both = jnp.where(routes.core == 0, both, both[::-1])
    parts = [both] + [routes.to_slab(both, step) for step in range(1, routes.slabs)]
    stacked = jnp.stack(parts)
    order = (routes.slab - jnp.arange(routes.slabs)) % routes.slabs
    return jnp.take(stacked, order, axis=0).reshape(routes.members, *value.shape)


def add(*values):
    return functools.reduce(lambda left, right: left + right, [value.astype(f32) for value in values])


def reduce_wout(routes, blocks):
    slab, slabs = routes.slab, routes.slabs
    running = pick(blocks, (slab - 1) % slabs)
    for step in range(1, slabs):
        received = routes.to_slab(running, 1)
        running = add(received, pick(blocks, (slab - 1 - step) % slabs)).astype(bf16)
    half = running.shape[0] // 2
    left, right = running[:half], running[half:]
    left_in, right_in = routes.to_group(left, 1), routes.to_group(right, 2)
    left, right = add(left, left_in).astype(bf16), add(right, right_in).astype(bf16)
    left_in, right_in = routes.to_group(left, 2), routes.to_group(right, 1)
    return jnp.concatenate([add(left, left_in), add(right, right_in)], axis=0)


def reduce_win(routes, blocks):
    x, y = routes.group % 2, routes.group // 2
    _, rows, columns = blocks.shape
    left, right = blocks[:4].reshape(2, 2, rows, columns), blocks[4:].reshape(2, 2, rows, columns)
    left_in = routes.to_group(pick(left, 1 - x), 1)
    right_in = routes.to_group(pick(right, 1 - y), 2)
    left = add(pick(left, x), left_in).astype(bf16)
    right = add(pick(right, y), right_in).astype(bf16)
    left_in = routes.to_group(pick(left, 1 - y), 2)
    right_in = routes.to_group(pick(right, 1 - x), 1)
    both = jnp.stack([add(pick(left, y), left_in), add(pick(right, x), right_in)]).astype(bf16)
    both = both.reshape(2, routes.slabs, rows // routes.slabs, columns)
    arrived = [
        routes.to_slab(pick(both, (routes.slab + step) % routes.slabs, 1), step) for step in range(1, routes.slabs)
    ]
    total = add(pick(both, routes.slab, 1), *arrived).astype(bf16)
    every = jnp.stack([total] + [routes.to_group(total, flip) for flip in range(1, 4)])
    every = jnp.take(every, jnp.arange(4) ^ routes.group, axis=0).astype(f32)
    every = every.reshape(2, 2, 2, rows // routes.slabs, columns)
    left = every[:, :, 0].transpose(1, 0, 2, 3)
    right = every[:, :, 1]
    joined = jnp.concatenate([left.reshape(4, -1, columns), right.reshape(4, -1, columns)])
    return joined.transpose(1, 0, 2).reshape(rows // routes.slabs, 8 * columns)


def reduce_small(routes, blocks):
    halves = blocks.reshape(routes.slabs, 2, *blocks.shape[1:])
    chip = pick(halves, routes.core, 1) + routes.to_core(pick(halves, 1 - routes.core, 1))
    arrived = [
        routes.to_slab(pick(chip, (routes.slab + step) % routes.slabs), step) for step in range(1, routes.slabs)
    ]
    total = add(pick(chip, routes.slab), *arrived)
    total = total + routes.to_group(total, 1)
    return total + routes.to_group(total, 2)


def shards(
    features,
    cotangent,
    image_sizes,
    warp_index,
    warp_weight,
    offsets,
    conv_kernel,
    conv_bias,
    norm_gain,
    norm_bias,
    w_in,
    bias_in,
    w_out,
    bias_out,
    layer_scale,
    w_estimate,
):
    share, units = w_in.shape
    channels = features.shape[-1]
    members = channels // share
    groups = lax.axis_size("dp")
    paired = groups == 4 and members == 8

    small = jnp.concatenate(
        [
            conv_kernel,
            w_estimate,
            jnp.stack([conv_bias, norm_gain, norm_bias, bias_out, layer_scale]),
            bias_in.reshape(-1, share),
        ]
    )
    if paired:
        routes = Routes(groups, members)
        where = jnp.stack([routes.slab, routes.core, routes.group, jnp.int32(routes.slabs)])
        pieces = w_in.reshape(share, 4, units // 4).transpose(1, 0, 2)
        mine, theirs = gather_pieces(routes, pieces)
        small = gather_small(routes, small)
        wide = units // 4

        def in_place(shard, quarter):
            return (
                pl.ds(pl.multiple_of(shard * share, 16), share),
                pl.ds(pl.multiple_of(quarter * wide, LANES), wide),
            )

        win_all = assemble("place_in", in_place, (channels, units), where, mine, theirs)
        tall = units // members // 4
        mine, theirs = gather_pieces(routes, w_out.reshape(4, tall, channels))

        def out_place(shard, quarter):
            return (pl.ds(pl.multiple_of(shard * 4 * tall + quarter * tall, 16), tall), slice(None))

        wout_all = assemble("place_out", out_place, (units, channels), where, mine, theirs)
    else:
        where = jnp.zeros((4,), jnp.int32)
        small = lax.all_gather(small, "fsdp")
        win_all = lax.all_gather(w_in, "fsdp", axis=0, tiled=True)
        wout_all = lax.all_gather(w_out, "fsdp", axis=0, tiled=True)
    bin_all = small[:, SMALL:].reshape(1, units).astype(f32)
    small = small[:, :SMALL].transpose(1, 0, 2).reshape(SMALL, channels).astype(f32)
    reach = WINDOW // 2
    lane_of = (offsets[:, 0] + reach) * CANVAS + offsets[:, 1] + reach
    place = jnp.pad(lane_of, (0, LANES - OFFSETS), constant_values=-1)[None]

    x, up, normed, pair, xhat, rstd = conv_norm(image_sizes, where, features, cotangent, small)
    active, slope = widen(normed, win_all, bin_all)
    branch = narrow(active, wout_all, small)
    mixed_out, d_mixed, d_branch, g_scale, g_bout, g_west = flow(
        image_sizes, x, branch, up, warp_index, warp_weight, place, small
    )
    if paired:
        core = where[1:2]
        away = routes.to_core(grad_narrow(1 - core, active, d_branch, 4))
        g_wout = reduce_wout(routes, grad_narrow(core, active, d_branch, 4, away))
        d_hidden, g_bin, away = hidden_back(d_branch, wout_all, slope, pair, channels // 2)
        g_win = reduce_win(routes, grad_widen(pair, d_hidden, routes.to_core(away)))
    else:
        g_wout = grad_narrow(where[:1], active, d_branch, 8).reshape(units, channels)
        d_hidden, g_bin, g_win = hidden_back(d_branch, wout_all, slope, normed, channels)
        g_win = g_win.transpose(1, 0, 2).reshape(channels, units)
    d_conv, g_norm = norm_back(d_hidden, win_all, xhat, rstd, small)
    g_taps = grad_taps(x, d_conv)
    g_small = jnp.concatenate([g_taps, g_norm, g_bout, g_scale, g_west])
    g_small = g_small.reshape(-1, members, share).transpose(1, 0, 2)
    g_small = jnp.concatenate([g_small, g_bin.reshape(members, -1, share)], axis=1)
    if paired:
        g_small = reduce_small(routes, g_small)
    else:

        def reduce(value):
            return lax.psum(lax.psum_scatter(value, "fsdp", scatter_dimension=0, tiled=True).astype(f32), "dp")

        g_wout, g_win, g_small = reduce(g_wout), reduce(g_win), reduce(g_small)[0]
    grad_features = conv_back(image_sizes, d_conv, small, d_mixed)
    tail = TAPS + 5 + LANES
    return (
        mixed_out,
        grad_features,
        g_small[:TAPS],
        g_small[TAPS],
        g_small[TAPS + 1],
        g_small[TAPS + 2],
        g_win,
        g_small[tail:].reshape(-1),
        g_wout,
        g_small[TAPS + 3],
        g_small[TAPS + 4],
        jnp.take(g_small[TAPS + 5 : tail], lane_of, axis=0),
    )


def solution(mesh):
    in_specs = (
        P(("dp", "fsdp"), None, None, None, None),
        P(("dp", "fsdp"), None, None, None, None),
        P(("dp", "fsdp")),
        P(("dp", "fsdp"), None, None),
        P(("dp", "fsdp"), None, None),
        P(),
        P(None, "fsdp"),
        P("fsdp"),
        P("fsdp"),
        P("fsdp"),
        P("fsdp", None),
        P("fsdp"),
        P("fsdp", None),
        P("fsdp"),
        P("fsdp"),
        P(None, "fsdp"),
    )
    out_specs = (
        P(("dp", "fsdp"), None, None, None, None),
        P(("dp", "fsdp"), None, None, None, None),
        P(None, "fsdp"),
        P("fsdp"),
        P("fsdp"),
        P("fsdp"),
        P("fsdp", None),
        P("fsdp"),
        P("fsdp", None),
        P("fsdp"),
        P("fsdp"),
        P(None, "fsdp"),
    )
    return jax.shard_map(shards, mesh=mesh, in_specs=in_specs, out_specs=out_specs, check_vma=False)
```

```python
import functools

import jax
import jax.numpy as jnp
import numpy as np
from jax import lax
from jax.experimental import pallas as pl
from jax.experimental.pallas import tpu as pltpu
from jax.sharding import PartitionSpec as P

CANVAS = 10
KERNEL = 7
REACH = KERNEL // 2
TAPS = KERNEL * KERNEL
WINDOW = 9
OFFSETS = WINDOW * WINDOW
PIX = CANVAS * CANVAS
PADDED = 104
LANES = 128
EPSILON = 1e-06
f32 = jnp.float32
bf16 = jnp.bfloat16
WEST = TAPS
CBIAS, GAIN, SHIFT, BOUT, SCALE = range(TAPS + OFFSETS, TAPS + OFFSETS + 5)
SMALL = TAPS + OFFSETS + 5


def call(kernel, name, out_shape, micros, scratch=(), limit=8, smem=0, left=0, after=()):
    def body(*refs):
        kernel(*refs[len(after) :])

    def run(*args):
        specs = [pl.BlockSpec(memory_space=pl.ANY)] * len(after)
        specs += [pl.BlockSpec(memory_space=pltpu.SMEM)] * smem
        specs += [pl.BlockSpec(memory_space=pl.ANY)] * left
        specs += [pl.BlockSpec(memory_space=pltpu.VMEM)] * (len(args) - smem - left)
        return pl.pallas_call(
            body,
            name=name,
            in_specs=specs,
            out_shape=out_shape,
            scratch_shapes=list(scratch),
            compiler_params=pltpu.CompilerParams(vmem_limit_bytes=limit * 1024 * 1024),
            cost_estimate=pl.CostEstimate(flops=int(micros * 1.15e9), bytes_accessed=0, transcendentals=0),
        )(*after, *args)

    return run


def array(shape, dtype=f32):
    return jax.ShapeDtypeStruct(shape, dtype)


def nt(left, right):
    return lax.dot_general(left, right, (((1,), (1,)), ((), ())), preferred_element_type=f32)


def tn(left, right):
    return lax.dot_general(left, right, (((0,), (0,)), ((), ())), preferred_element_type=f32)


def dot(left, right):
    return jnp.dot(left, right, preferred_element_type=f32)


def split(values):
    high = values.astype(bf16)
    return high, (values - high.astype(f32)).astype(bf16)


def lane_tile(tile):
    return pl.ds(tile * LANES, LANES)


def conv_rows(source, tile, kernel_ref, flip, finish):
    cols = pl.ds(pl.multiple_of(tile * LANES, LANES), LANES)
    for row in range(CANVAS):
        sums = [None] * CANVAS
        for ky in range(KERNEL):
            source_row = row + ky - REACH
            if not 0 <= source_row < CANVAS:
                continue
            cells = [source[tile, pl.ds((source_row * CANVAS + col) * 8, 8), :] for col in range(CANVAS)]
            for kx in range(KERNEL):
                tap = ky * KERNEL + kx
                tap = TAPS - 1 - tap if flip else tap
                weight = jnp.broadcast_to(kernel_ref[pl.ds(tap, 1), cols], (8, LANES))
                for col in range(CANVAS):
                    other = col + kx - REACH
                    if 0 <= other < CANVAS:
                        term = cells[other] * weight
                        sums[col] = term if sums[col] is None else sums[col] + term
        for col in range(CANVAS):
            finish(row * CANVAS + col, sums[col])


def side_of(sizes_ref, images):
    lines = lax.broadcasted_iota(jnp.int32, (2 * images, LANES), 0)
    side = jnp.zeros(lines.shape, jnp.int32)
    for image in range(images):
        side = jnp.where((lines == image) | (lines == images + image), sizes_ref[image], side)
    return side


def conv_tile(x_ref, tile, small_ref, conv_ref, target):
    cols = pl.ds(pl.multiple_of(tile * LANES, LANES), LANES)
    bias = jnp.broadcast_to(small_ref[pl.ds(CBIAS, 1), cols], (8, LANES))

    def finish(cell, total):
        conv_ref[target, pl.ds(cell * 8, 8), :] = total + bias

    conv_rows(x_ref, tile, small_ref, False, finish)


def conv_begin_kernel(
    sizes_ref, features_ref, upstream_ref, small_ref, x_ref, up_ref, conv_ref, features, upstream, sems,
):
    images = features_ref.shape[0]
    frames = 2 * images
    tiles, rows, _ = x_ref.shape
    side = side_of(sizes_ref, images)
    copies = [
        pltpu.make_async_copy(source.at[image], target.at[image], sems.at[number, image])
        for number, (source, target) in enumerate(((features_ref, features), (upstream_ref, upstream)))
        for image in range(images)
    ]
    for copy in copies:
        copy.start()

    def lay(source, image, target):
        for which in range(2):
            for row in range(CANVAS):
                lines = pl.ds(row * CANVAS * frames + which * images + image, CANVAS, stride=frames)
                for tile in range(tiles):
                    target[tile, lines, :] = source[image, which, row, :, lane_tile(tile)].astype(f32)

    for image in range(images):
        copies[image].wait()
        lay(features, image, x_ref)

    @pl.loop(0, tiles)
    def _(tile):
        for cell in range(PIX):
            inside = side > max(cell // CANVAS, cell % CANVAS)
            lines = pl.ds(cell * 8, 8)
            x_ref[tile, lines, :] = jnp.where(inside, x_ref[tile, lines, :], 0.0)

    @pl.loop(0, tiles // 2)
    def _(tile):
        conv_tile(x_ref, tile, small_ref, conv_ref, tile)

    for tile in range(tiles):
        up_ref[tile, pl.ds(rows, PADDED * frames - rows), :] = jnp.zeros((PADDED * frames - rows, LANES), f32)
    for image in range(images):
        copies[images + image].wait()
        lay(upstream, image, up_ref)


def conv_begin(sizes, features, upstream, small, after=()):
    images, channels = features.shape[0], features.shape[-1]
    rows, tiles = PIX * 2 * images, channels // LANES
    shapes = (
        array((tiles, rows, LANES)),
        array((tiles, PADDED * 2 * images, LANES)),
        array((tiles // 2, rows, LANES)),
    )
    scratch = [pltpu.VMEM(features.shape, bf16), pltpu.VMEM(features.shape, bf16), pltpu.SemaphoreType.DMA((2, images))]
    return call(conv_begin_kernel, "conv_begin", shapes, 6, scratch, smem=1, left=2, after=after)(
        sizes, features, upstream, small
    )


def conv_norm_kernel(where_ref, x_ref, begun_ref, small_ref, normed_ref, pair_ref, xhat_ref, rstd_ref, conv, order):
    tiles, rows, _ = x_ref.shape
    channels = tiles * LANES

    @pl.loop(0, tiles // 2)
    def _(tile):
        conv_tile(x_ref, tile + tiles // 2, small_ref, conv, tile)

    share = channels // 8
    core = where_ref[1]
    for tile in range(tiles):
        source = lax.broadcasted_iota(jnp.int32, (channels, LANES), 0)
        target = lax.broadcasted_iota(jnp.int32, (1, LANES), 1) + tile * LANES
        shard = target // share
        wanted = jnp.where(shard < 4, 2 * shard + 1 - core, 2 * (shard - 4) + core) * share + target % share
        order[:, lane_tile(tile)] = (source == wanted).astype(bf16)
    size = 160

    @pl.loop(0, rows // size)
    def _(block):
        lines = pl.ds(pl.multiple_of(block * size, size), size)
        values = [begun_ref[tile, lines, :] for tile in range(tiles // 2)]
        values = jnp.concatenate(values + [conv[tile, lines, :] for tile in range(tiles // 2)], axis=1)
        mean = jnp.sum(values, axis=-1, keepdims=True) * (1.0 / channels)
        centred = values - mean
        variance = jnp.sum(centred * centred, axis=-1, keepdims=True) * (1.0 / channels)
        scale = lax.rsqrt(variance + EPSILON)
        xhat = centred * scale
        xhat_ref[lines, :] = xhat.astype(bf16)
        rstd_ref[lines, :] = scale
        normed = (xhat * small_ref[pl.ds(GAIN, 1), :] + small_ref[pl.ds(SHIFT, 1), :]).astype(bf16)
        normed_ref[lines, :] = normed
        pair_ref[lines, :] = dot(normed, order[...]).astype(bf16)


def conv_norm(where, x, begun, small, after=()):
    tiles, rows, _ = x.shape
    channels = tiles * LANES
    low = array((rows, channels), bf16)
    return call(
        conv_norm_kernel,
        "conv_norm",
        (low, low, low, array((rows, 1))),
        6.6,
        [pltpu.VMEM(begun.shape, f32), pltpu.VMEM((channels, channels), bf16)],
        smem=1,
        after=after,
    )(where, x, begun, small)


def gelu_pair(hidden):
    cdf = 0.5 * lax.erf(hidden * 0.7071067811865476) + 0.5
    density = jnp.exp(hidden * hidden * -0.5) * 0.3989422804014327
    return hidden * cdf, cdf + hidden * density


def widen_part(normed_ref, weight_ref, bias_ref, active_ref, slope_ref, part, tile=256):
    cols = pl.ds(part * tile, tile)
    hidden = dot(normed_ref[...], weight_ref[:, cols]) + bias_ref[:, cols]
    active, slope = gelu_pair(hidden)
    active_ref[:, cols] = active.astype(bf16)
    slope_ref[:, cols] = slope.astype(bf16)


def widen_kernel(normed_ref, weight_ref, bias_ref, active_ref, slope_ref):
    for part in range(weight_ref.shape[1] // 256):
        widen_part(normed_ref, weight_ref, bias_ref, active_ref, slope_ref, part)


def widen(normed, weight, bias):
    rows, units = normed.shape[0], weight.shape[1]
    return call(widen_kernel, "widen", (array((rows, units), bf16),) * 2, 6.5)(normed, weight, bias)


def start_all(copies, sems):
    running = [pltpu.make_async_copy(source, target, sems.at[number]) for number, (source, target) in enumerate(copies)]
    for copy in running:
        copy.start()
    return running


def place_widen_kernel(where_ref, *refs):
    pieces, (normed_ref, bias_ref, weight_ref, active_ref, slope_ref, sems) = refs[:10], refs[10:]
    z, core, group, slabs = (where_ref[number] for number in range(4))
    share = pieces[0].shape[0]
    copies = []
    for side in range(2):
        own_ref, to_x, to_y, from_x, from_y = pieces[5 * side : 5 * side + 5]
        width = to_x.shape[3]
        parity = core if side == 0 else 1 - core
        start = pl.multiple_of((2 * z + parity) * share, 16)
        copies.append((own_ref, weight_ref.at[pl.ds(start, share)]))
        lefts = (to_y.at[0], to_y.at[1], from_y.at[0], from_y.at[1])
        rights = (to_x.at[0], from_x.at[0], to_x.at[1], from_x.at[1])
        for step in range(1, 4):
            shard = 2 * lax.rem(z - step + slabs, slabs) + parity
            lines = pl.ds(pl.multiple_of(shard * share, 16), share)
            for flip in range(4):
                first = jnp.bitwise_xor(group, flip) * 2 * width
                for turn, halves in enumerate((lefts, rights)):
                    cols = pl.ds(pl.multiple_of(first + turn * width, LANES), width)
                    copies.append((halves[flip].at[step - 1], weight_ref.at[lines, cols]))
    for copy in start_all(copies, sems):
        copy.wait()
    for part in range(weight_ref.shape[1] // 256):
        widen_part(normed_ref, weight_ref, bias_ref, active_ref, slope_ref, part)


def place_widen(where, mine, theirs, normed, bias, after=()):
    share, units = mine[0].shape
    rows, channels = normed.shape
    wide = array((rows, units), bf16)
    return call(
        place_widen_kernel,
        "place_widen",
        (array((channels, units), bf16), wide, wide),
        8,
        [pltpu.SemaphoreType.DMA((50,))],
        smem=1,
        left=10,
        after=after,
    )(where, *mine, *theirs, normed, bias)


def narrow_rows(active_ref, weight_ref, small_ref, branch_ref):
    size = 160
    for part in range(active_ref.shape[0] // size):
        lines = pl.ds(part * size, size)
        branch = dot(active_ref[lines, :], weight_ref[...]) + small_ref[pl.ds(BOUT, 1), :]
        for tile in range(branch_ref.shape[0]):
            branch_ref[tile, lines, :] = branch[:, tile * LANES : (tile + 1) * LANES]


def narrow(active, weight, small):
    rows, channels = active.shape[0], weight.shape[1]
    return call(narrow_rows, "narrow", array((channels // LANES, rows, LANES)), 4)(active, weight, small)


def place_narrow_kernel(where_ref, *refs):
    pieces, (active_ref, small_ref, weight_ref, branch_ref, sems) = refs[:10], refs[10:]
    z, core, group, slabs = (where_ref[number] for number in range(4))
    half = lax.rem(group + group // 2, 2)
    tall = pieces[0].shape[0]
    quarter = tall // 4
    copies = []
    for side in range(2):
        own_ref, *others = pieces[5 * side : 5 * side + 5]
        parity = core if side == 0 else 1 - core
        start = pl.multiple_of((2 * z + parity) * tall, 16)
        copies.append((own_ref, weight_ref.at[pl.ds(start, tall)]))
        for step in range(1, 4):
            base = (2 * lax.rem(z - step + slabs, slabs) + parity) * tall
            for number, other in enumerate(others):
                start = 2 * quarter * (half if number < 2 else 1 - half) + number % 2 * quarter
                lines = pl.ds(pl.multiple_of(base + start, 16), quarter)
                copies.append((other.at[step - 1], weight_ref.at[lines]))
    for copy in start_all(copies, sems):
        copy.wait()
    narrow_rows(active_ref, weight_ref, small_ref, branch_ref)


def place_narrow(where, mine, theirs, active, small, after=()):
    tall, channels = mine[0].shape
    rows, units = active.shape
    return call(
        place_narrow_kernel,
        "place_narrow",
        (array((units, channels), bf16), array((channels // LANES, rows, LANES))),
        6,
        [pltpu.SemaphoreType.DMA((26,))],
        smem=1,
        left=10,
        after=after,
    )(where, *mine, *theirs, active, small)


def skew(values, inverse):
    rows = lax.broadcasted_iota(jnp.int32, values.shape, 0)
    centre = (WINDOW // 2) * (CANVAS + 1)
    amount = jnp.bitwise_and(rows - centre if inverse else centre - rows, LANES - 1)
    for bit in range(7):
        moved = pltpu.roll(values, 1 << bit, 1)
        values = jnp.where(jnp.bitwise_and(amount, 1 << bit) != 0, moved, values)
    return values


def flow_kernel(
    sizes_ref, x_ref, branch_ref, up_ref, index_ref, weight_ref, place_ref, small_ref, window_ref,
    out_ref, dmixed_ref, dbranch_ref, gscale_ref, gbout_ref, gwest_ref, mixed, back, west_in, warp_in,
):
    tiles, rows, _ = x_ref.shape
    images = index_ref.shape[0]
    frames = 2 * images
    channels = tiles * LANES
    factor = channels ** (-0.5)
    every = range(images)
    for tile in range(tiles):
        scale = small_ref[pl.ds(SCALE, 1), lane_tile(tile)]
        mixed[tile, pl.ds(0, rows), :] = x_ref[tile] + scale * branch_ref[tile]
        mixed[tile, pl.ds(rows, PADDED * frames - rows), :] = jnp.zeros((PADDED * frames - rows, LANES), f32)

    def take(ref, frame):
        lines = pl.ds(frame, PADDED, stride=frames)
        return jnp.concatenate([ref[tile, lines, :] for tile in range(tiles)], axis=1)

    def put(ref, frame, values):
        lines = pl.ds(frame, PADDED, stride=frames)
        for tile in range(tiles):
            ref[tile, lines, :] = values[:, tile * LANES : (tile + 1) * LANES]

    west_in[...] = jnp.zeros_like(west_in)
    west_in[pl.ds(0, OFFSETS), :] = small_ref[pl.ds(WEST, OFFSETS), :]
    lanes = lax.broadcasted_iota(jnp.int32, (LANES, LANES), 0)
    west = dot((lanes == place_ref[...]).astype(bf16), west_in[...].astype(bf16)).astype(bf16)
    window = window_ref[0]
    reach = window_ref[1]
    cells = lax.broadcasted_iota(jnp.int32, (PIX, LANES), 1)
    warp_in[...] = jnp.zeros_like(warp_in)
    for image in every:
        warp = jnp.zeros((PIX, LANES), f32)
        for corner in range(4):
            place = index_ref[image, :, pl.ds(corner, 1)]
            amount = weight_ref[image, :, pl.ds(corner, 1)]
            warp = warp + jnp.where(cells == place, amount, 0.0)
        warp_in[image, pl.ds(0, PIX), :] = warp
    warps = [split(warp_in[image][:, :PADDED]) for image in every]
    inside = [(reach < sizes_ref[image].astype(f32)).astype(f32)[:, :1] for image in every]
    first = [take(mixed, image) * inside[image] for image in every]
    second = [take(mixed, images + image) * inside[image] for image in every]
    first_low = [value.astype(bf16) for value in first]
    second_low = [value.astype(bf16) for value in second]
    empty = jnp.zeros((LANES - PADDED, channels), bf16)
    warped = [
        jnp.concatenate([(dot(high, value) + dot(low, value)).astype(bf16), empty], axis=0)
        for (high, low), value in zip(warps, second_low)
    ]
    scores = [nt(left, right) for left, right in zip(first_low, warped)]
    costs = [skew(value, False) * window * factor for value in scores]
    pairs = [gelu_pair(value) for value in costs]
    gated = [value.astype(bf16) for value, _ in pairs]
    d_firsts = [take(up_ref, image) * inside[image] for image in every]
    d_heads = [value.astype(bf16) for value in d_firsts]
    d_costs = [slope * nt(d_head, west) * window * factor for (_, slope), d_head in zip(pairs, d_heads)]
    d_scores = [skew(value, True).astype(bf16) for value in d_costs]
    for image in every:
        put(back, image, d_firsts[image] + dot(d_scores[image], warped[image]))
    d_warped = [tn(value, low)[:PADDED].astype(bf16) for value, low in zip(d_scores, first_low)]
    for image in every:
        high, low = warps[image]
        d_second = take(up_ref, images + image) + tn(high, d_warped[image]) + tn(low, d_warped[image])
        put(back, images + image, d_second * inside[image])
    for tile in range(tiles):
        cols = lane_tile(tile)
        d_mixed = back[tile, pl.ds(0, rows), :]
        dmixed_ref[tile] = d_mixed
        gscale_ref[:, cols] = jnp.sum(d_mixed * branch_ref[tile], axis=0, keepdims=True)
        d_branch = (d_mixed * small_ref[pl.ds(SCALE, 1), cols]).astype(bf16)
        dbranch_ref[:, cols] = d_branch
        gbout_ref[:, cols] = jnp.sum(d_branch.astype(f32), axis=0, keepdims=True)
    gwest = tn(gated[0], d_heads[0])
    for image in every[1:]:
        gwest = gwest + tn(gated[image], d_heads[image])
    gwest_ref[...] = gwest
    for image in every:
        put(mixed, image, (first[image] + dot(gated[image], west)) * inside[image])
        put(mixed, images + image, second[image])
    for image in every:
        for which in range(2):
            for row in range(CANVAS):
                lines = pl.ds(row * CANVAS * frames + which * images + image, CANVAS, stride=frames)
                for tile in range(tiles):
                    out_ref[image, which, row, :, lane_tile(tile)] = mixed[tile, lines, :].astype(bf16)


def tables():
    cells = np.arange(PADDED)[:, None]
    lane = np.arange(LANES)[None, :]
    reach = WINDOW // 2
    row = cells // CANVAS + lane // CANVAS - reach
    col = cells % CANVAS + lane % CANVAS - reach
    good = (lane % CANVAS < WINDOW) & (lane // CANVAS < WINDOW) & (cells < PIX)
    good &= (row >= 0) & (row < CANVAS) & (col >= 0) & (col < CANVAS)
    far = np.maximum(cells // CANVAS, cells % CANVAS) + 0 * lane
    return np.stack([good, far]).astype(np.float32)


def flow(sizes, x, branch, up, index, weight, place, small, after=()):
    tiles, rows, _ = x.shape
    images, channels = index.shape[0], tiles * LANES
    padded = pltpu.VMEM((tiles, PADDED * 2 * images, LANES), f32)
    vector = array((1, channels))
    return call(
        flow_kernel,
        "flow",
        (
            array((images, 2, CANVAS, CANVAS, channels), bf16),
            array(x.shape),
            array((rows, channels), bf16),
            vector,
            vector,
            array((LANES, channels)),
        ),
        6.5,
        [padded, padded, pltpu.VMEM((LANES, channels), f32), pltpu.VMEM((images, PADDED, LANES), f32)],
        limit=14,
        smem=1,
        after=after,
    )(sizes, x, branch, up, index, weight, place, small, jnp.asarray(tables()))


def grad_narrow_kernel(where_ref, active_ref, dbranch_ref, out_ref):
    count, tile, _ = out_ref.shape
    for part in range(count):
        block = 2 * part + 1 - where_ref[1] if count < 8 else part
        cols = pl.ds(pl.multiple_of(block * tile, LANES), tile)
        out_ref[part] = tn(active_ref[:, cols], dbranch_ref[...]).astype(bf16)


def grad_narrow(where, active, dbranch, count, after=()):
    units, channels = active.shape[1], dbranch.shape[1]
    shape = array((count, units // 8, channels), bf16)
    return call(grad_narrow_kernel, "grad_narrow", shape, 0.8 * count, smem=1, after=after)(where, active, dbranch)


def send_halves(where_ref, blocks, keep_ref, left_ref, right_ref):
    x, y = lax.rem(where_ref[2], 2), where_ref[2] // 2
    for turn in range(2):
        keep_ref[0, turn] = blocks[2 * x + turn]
        keep_ref[1, turn] = blocks[4 + 2 * y + turn]
        left_ref[turn] = blocks[2 * (1 - x) + turn]
        right_ref[turn] = blocks[4 + 2 * (1 - y) + turn]


def halves_of(lines, width):
    half = array((2, lines, width), bf16)
    return (array((2, 2, lines, width), bf16), half, half), [pltpu.VMEM((8, lines, width), bf16)]


def grad_narrow_here_kernel(where_ref, active_ref, dbranch_ref, received_ref, keep_ref, left_ref, right_ref, blocks):
    count, tile, _ = received_ref.shape
    lines = tile // 8
    for part in range(count):
        cols = pl.ds(pl.multiple_of((2 * part + where_ref[1]) * tile, LANES), tile)
        total = tn(active_ref[:, cols], dbranch_ref[...]) + received_ref[part].astype(f32)
        for block in range(8):
            blocks[block, pl.ds(part * lines, lines), :] = total[block * lines : (block + 1) * lines].astype(bf16)
    send_halves(where_ref, blocks, keep_ref, left_ref, right_ref)


def grad_narrow_here(where, active, dbranch, received, after=()):
    count, tile, channels = received.shape
    shapes, scratch = halves_of(count * tile // 8, channels)
    return call(grad_narrow_here_kernel, "grad_narrow_here", shapes, 3.6, scratch, smem=1, after=after)(
        where, active, dbranch, received
    )


def hidden_back_kernel(dbranch_ref, weight_ref, slope_ref, dhidden_ref, gbin_ref):
    tile = 768
    for part in range(slope_ref.shape[1] // tile):
        cols = pl.ds(part * tile, tile)
        d_active = nt(dbranch_ref[...], weight_ref[cols, :])
        d_hidden = (d_active * slope_ref[:, cols].astype(f32)).astype(bf16)
        dhidden_ref[:, cols] = d_hidden
        gbin_ref[:, cols] = jnp.sum(d_hidden.astype(f32), axis=0, keepdims=True)


def hidden_back(dbranch, weight, slope, after=()):
    rows, units = slope.shape
    shapes = (array((rows, units), bf16), array((1, units)))
    return call(hidden_back_kernel, "hidden_back", shapes, 4.2, after=after)(dbranch, weight, slope)


def grad_widen_full_kernel(normed_ref, dhidden_ref, out_ref):
    tile = 768
    for part in range(out_ref.shape[1] // tile):
        cols = pl.ds(part * tile, tile)
        out_ref[:, cols] = tn(normed_ref[...], dhidden_ref[:, cols]).astype(bf16)


def grad_widen_full(normed, dhidden):
    shape = array((normed.shape[1], dhidden.shape[1]), bf16)
    return call(grad_widen_full_kernel, "grad_widen_full", shape, 5)(normed, dhidden)


def grad_widen_away_kernel(pair_ref, dhidden_ref, out_ref):
    blocks, lines, width = out_ref.shape
    for part in range(blocks // 2):
        total = tn(pair_ref[:, pl.ds(0, lines)], dhidden_ref[:, pl.ds(2 * part * width, 2 * width)]).astype(bf16)
        out_ref[2 * part] = total[:, :width]
        out_ref[2 * part + 1] = total[:, width:]


def grad_widen_away(pair, dhidden, after=()):
    shape = array((8, pair.shape[1] // 2, dhidden.shape[1] // 8), bf16)
    return call(grad_widen_away_kernel, "grad_widen_away", shape, 2.6, after=after)(pair, dhidden)


def grad_widen_here_kernel(where_ref, pair_ref, dhidden_ref, received_ref, keep_ref, left_ref, right_ref, blocks):
    _, lines, width = blocks.shape
    for part in range(4):
        both = tn(pair_ref[:, pl.ds(lines, lines)], dhidden_ref[:, pl.ds(2 * part * width, 2 * width)])
        for turn in range(2):
            block = 2 * part + turn
            value = both[:, turn * width : (turn + 1) * width] + received_ref[block].astype(f32)
            blocks[block] = value.astype(bf16)
    send_halves(where_ref, blocks, keep_ref, left_ref, right_ref)


def grad_widen_here(where, pair, dhidden, received, after=()):
    shapes, scratch = halves_of(*received.shape[1:])
    return call(grad_widen_here_kernel, "grad_widen_here", shapes, 3.8, scratch, smem=1, after=after)(
        where, pair, dhidden, received
    )


def norm_back_kernel(dhidden_ref, weight_ref, xhat_ref, rstd_ref, small_ref, dconv_ref, sums_ref):
    rows, channels = xhat_ref.shape
    size = 160
    gain = small_ref[pl.ds(GAIN, 1), :]
    sums = [jnp.zeros((1, channels), f32)] * 3
    for part in range(rows // size):
        lines = pl.ds(part * size, size)
        d_normed = nt(dhidden_ref[lines, :], weight_ref[...])
        xhat = xhat_ref[lines, :].astype(f32)
        product = d_normed * xhat
        d_xhat = d_normed * gain
        mean = jnp.sum(d_xhat, axis=-1, keepdims=True) * (1.0 / channels)
        along = jnp.sum(product * gain, axis=-1, keepdims=True) * (1.0 / channels)
        d_conv = (d_xhat - mean - xhat * along) * rstd_ref[lines, :]
        for tile in range(dconv_ref.shape[0]):
            dconv_ref[tile, lines, :] = d_conv[:, tile * LANES : (tile + 1) * LANES]
        for number, value in enumerate((d_conv, product, d_normed)):
            sums[number] = sums[number] + jnp.sum(value, axis=0, keepdims=True)
    sums_ref[...] = jnp.concatenate(sums, axis=0)


def norm_back(dhidden, weight, xhat, rstd, small, after=()):
    rows, channels = xhat.shape
    return call(
        norm_back_kernel, "norm_back", (array((channels // LANES, rows, LANES)), array((3, channels))), 8.4, after=after
    )(dhidden, weight, xhat, rstd, small)


def grad_taps_kernel(x_ref, dconv_ref, out_ref):
    @pl.loop(0, x_ref.shape[0])
    def _(tile):
        cols = pl.ds(pl.multiple_of(tile * LANES, LANES), LANES)
        for ky in range(KERNEL):
            totals = [None] * KERNEL
            for row in range(CANVAS):
                source_row = row + ky - REACH
                if not 0 <= source_row < CANVAS:
                    continue
                cells = [x_ref[tile, pl.ds((source_row * CANVAS + col) * 8, 8), :] for col in range(CANVAS)]
                grads = [dconv_ref[tile, pl.ds((row * CANVAS + col) * 8, 8), :] for col in range(CANVAS)]
                for kx in range(KERNEL):
                    for col in range(CANVAS):
                        source = col + kx - REACH
                        if 0 <= source < CANVAS:
                            term = cells[source] * grads[col]
                            totals[kx] = term if totals[kx] is None else totals[kx] + term
            for kx in range(KERNEL):
                out_ref[pl.ds(ky * KERNEL + kx, 1), cols] = jnp.sum(totals[kx], axis=0, keepdims=True)


def grad_taps(x, dconv, after=()):
    return call(grad_taps_kernel, "grad_taps", array((TAPS, x.shape[0] * LANES)), 7.5, after=after)(x, dconv)


def conv_back_kernel(sizes_ref, dconv_ref, small_ref, dmixed_ref, out_ref, total):
    tiles = dconv_ref.shape[0]
    images = out_ref.shape[0]
    frames = 2 * images
    side = side_of(sizes_ref, images)

    @pl.loop(0, tiles)
    def _(tile):
        def finish(cell, value):
            lines = pl.ds(cell * 8, 8)
            inside = side > max(cell // CANVAS, cell % CANVAS)
            total[tile, lines, :] = jnp.where(inside, value + dmixed_ref[tile, lines, :], 0.0)

        conv_rows(dconv_ref, tile, small_ref, True, finish)

    for image in range(images):
        for which in range(2):
            for row in range(CANVAS):
                lines = pl.ds(row * CANVAS * frames + which * images + image, CANVAS, stride=frames)
                for tile in range(tiles):
                    out_ref[image, which, row, :, lane_tile(tile)] = total[tile, lines, :]


def conv_back(sizes, dconv, small, dmixed, after=()):
    tiles, rows, _ = dconv.shape
    images = sizes.shape[0]
    return call(
        conv_back_kernel,
        "conv_back",
        array((images, 2, CANVAS, CANVAS, tiles * LANES)),
        8,
        [pltpu.VMEM(dconv.shape, f32)],
        smem=1,
        after=after,
    )(sizes, dconv, small, dmixed)


GROUPS = 6
LINES = 24
BIAS = SMALL


def pack_kernel(where_ref, weight_ref, taps_ref, west_ref, *refs):
    vectors, (bias_ref, out_ref, small, taps, west, vector, bias, sems) = refs[:5], refs[5:]
    share = weight_ref.shape[0]
    wide = out_ref.shape[1]
    cols = pl.ds(pl.multiple_of(where_ref[2] * wide, LANES), wide)
    copies = [(taps_ref, taps), (west_ref, west), (bias_ref, bias)]
    copies += [(ref, vector.at[number]) for number, ref in enumerate(vectors)]
    copies += [(weight_ref.at[:, cols], out_ref.at[pl.ds(0, share)])]
    running = start_all(copies, sems)
    small[...] = jnp.zeros_like(small)
    lane = pl.ds(0, share)
    for copy in running[:-1]:
        copy.wait()
    small[pl.ds(0, TAPS), lane] = taps[...].astype(f32)
    small[pl.ds(WEST, OFFSETS), lane] = west[...].astype(f32)
    for number in range(len(vectors)):
        small[pl.ds(CBIAS + number, 1), lane] = vector[number].astype(f32)
    for part in range(bias.shape[1] // LANES):
        small[pl.ds(BIAS + part, 1), :] = bias[:, lane_tile(part)].astype(f32)
    for group in range(GROUPS):
        out_ref[pl.ds(share, LINES), lane_tile(group)] = small[pl.ds(group * LINES, LINES), :].astype(bf16)
    running[-1].wait()


def pack(where, weight, taps, west, vectors, bias, after=()):
    share, units = weight.shape
    args = (weight, taps, west, *[v[None] for v in vectors], bias[None])
    return call(
        pack_kernel,
        "pack",
        array((share + LINES, units // 4), bf16),
        2,
        [
            pltpu.VMEM((GROUPS * LINES, LANES), f32),
            pltpu.VMEM(taps.shape, bf16),
            pltpu.VMEM(west.shape, bf16),
            pltpu.VMEM((len(vectors), 1, share), bf16),
            pltpu.VMEM((1, bias.shape[0]), bf16),
            pltpu.SemaphoreType.DMA((len(args),)),
        ],
        smem=1,
        left=len(args),
        after=after,
    )(where, *args)


def column_in_kernel(*refs):
    own_ref, *parts, left_ref, right_ref, small_ref = refs
    share, width = left_ref.shape[1:]
    for number, part in enumerate(parts):
        left_ref[number] = part[pl.ds(0, share), pl.ds(0, width)]
        right_ref[number] = part[pl.ds(0, share), pl.ds(width, width)]
    for number, part in enumerate((own_ref, *parts)):
        small_ref[number] = part[pl.ds(share, LINES), :]


def column_in(own, parts, after=()):
    rows, wide = own.shape
    half = array((len(parts), rows - LINES, wide // 2), bf16)
    small = array((len(parts) + 1, LINES, wide), bf16)
    return call(column_in_kernel, "column_in", (half, half, small), 1, after=after)(own, *parts)


def unpack_kernel(where_ref, mine_ref, theirs_ref, small_ref, bias_ref):
    z, core, slabs = where_ref[0], where_ref[1], where_ref[3]
    channels = small_ref.shape[1]
    share = channels // 8
    everything = None
    for number in range(8):
        ref = mine_ref if number < 4 else theirs_ref
        shard = 2 * lax.rem(z - number % 4 + slabs, slabs) + (core if number < 4 else 1 - core)
        rows = jnp.concatenate([ref[number % 4, :, lane_tile(group)].astype(f32) for group in range(GROUPS)], axis=0)
        source = lax.broadcasted_iota(jnp.int32, (LANES, channels), 0)
        target = lax.broadcasted_iota(jnp.int32, (LANES, channels), 1)
        spread = ((target - shard * share == source) & (source < share)).astype(bf16)
        value = dot(rows.astype(bf16), spread)
        everything = value if everything is None else everything + value
        width = bias_ref.shape[1] // 8
        for part in range(width // LANES):
            cols = pl.ds(pl.multiple_of(shard * width + part * LANES, LANES), LANES)
            bias_ref[:, cols] = rows[BIAS + part : BIAS + part + 1, :]
    small_ref[...] = everything[: small_ref.shape[0]]


def unpack(where, mine, theirs, units, channels):
    return call(unpack_kernel, "unpack", (array((SMALL, channels)), array((1, units))), 1.2, smem=1)(where, mine, theirs)


def column_out_kernel(*refs):
    parts, outs = refs[:3], refs[3:]
    rows = outs[0].shape[1]
    for turn, out in enumerate(outs):
        for number, part in enumerate(parts):
            out[number] = part[pl.ds(turn * rows, rows), :]


def column_out(parts, after=()):
    rows, channels = parts[0].shape
    half = array((len(parts), rows // 2, channels), bf16)
    return call(column_out_kernel, "column_out", (half, half), 1, after=after)(*parts)


def cut_kernel(where_ref, weight_ref, out_ref, sem):
    tall = out_ref.shape[0]
    half = lax.rem(where_ref[2] + where_ref[2] // 2, 2)
    lines = pl.ds(pl.multiple_of(half * tall, 16), tall)
    copy = pltpu.make_async_copy(weight_ref.at[lines], out_ref, sem)
    copy.start()
    copy.wait()


def cut(where, weight, after=()):
    tall, channels = weight.shape
    shape = array((tall // 2, channels), bf16)
    return call(cut_kernel, "cut", shape, 1, [pltpu.SemaphoreType.DMA], smem=1, left=1, after=after)(where, weight)


def onward_kernel(left_ref, right_ref, left_in_ref, right_in_ref, to_x_ref, to_y_ref):
    to_y_ref[0] = left_ref[...]
    to_y_ref[1] = left_in_ref[...]
    to_x_ref[0] = right_ref[...]
    to_x_ref[1] = right_in_ref[...]


def onward(left, right, left_in, right_in, after=()):
    shape = array((2, *left.shape), bf16)
    return call(onward_kernel, "onward", (shape, shape), 1, after=after)(left, right, left_in, right_in)


def halve_kernel(where_ref, keep_ref, left_in_ref, right_in_ref, keep_out_ref, left_ref, right_ref):
    x, y = lax.rem(where_ref[2], 2), where_ref[2] // 2

    def total(side, which):
        received = left_in_ref if side == 0 else right_in_ref
        return keep_ref[side, which].astype(f32) + received[which].astype(f32)

    keep_out_ref[0] = total(0, y).astype(bf16)
    keep_out_ref[1] = total(1, x).astype(bf16)
    left_ref[...] = total(0, 1 - y).astype(bf16)
    right_ref[...] = total(1, 1 - x).astype(bf16)


def halve(where, keep, left_in, right_in, after=()):
    _, _, lines, width = keep.shape
    half = array((lines, width), bf16)
    shapes = (array((2, lines, width), bf16), half, half)
    return call(halve_kernel, "halve", shapes, 1, smem=1, after=after)(where, keep, left_in, right_in)


def deal_total(where_ref, keep_ref, left_in_ref, right_in_ref, total):
    total[0] = (keep_ref[0].astype(f32) + left_in_ref[...].astype(f32)).astype(bf16)
    total[1] = (keep_ref[1].astype(f32) + right_in_ref[...].astype(f32)).astype(bf16)


def deal_kernel(where_ref, keep_ref, left_in_ref, right_in_ref, *refs):
    outs, total = refs[:-1], refs[-1]
    share = outs[0].shape[1]
    deal_total(where_ref, keep_ref, left_in_ref, right_in_ref, total)
    for step, out in enumerate(outs):
        slab = lax.rem(where_ref[0] + step, len(outs))
        for side in range(2):
            out[side] = total[side, pl.ds(pl.multiple_of(slab * share, 16), share), :]


def deal(where, keep, left_in, right_in, slabs, after=()):
    _, lines, width = keep.shape
    shapes = (array((2, lines // slabs, width), bf16),) * slabs
    scratch = [pltpu.VMEM(keep.shape, bf16)]
    return call(deal_kernel, "deal", shapes, 1, scratch, smem=1, after=after)(where, keep, left_in, right_in)


SMALL_ROWS = 192


def deal_small_kernel(where_ref, keep_ref, left_in_ref, right_in_ref, here_ref, received_ref, *refs):
    outs, total = refs[:-1], refs[-1]
    deal_total(where_ref, keep_ref, left_in_ref, right_in_ref, total)
    share = total.shape[1] // len(outs)
    extra = outs[0].shape[1] - share
    for step, out in enumerate(outs):
        slab = lax.rem(where_ref[0] + step, len(outs))
        small = here_ref[slab] + received_ref[slab]
        lines = SMALL_ROWS // 4
        small = jnp.concatenate([small[part * lines : (part + 1) * lines] for part in range(4)], axis=1)
        for side in range(2):
            out[side, pl.ds(0, share), :] = total[side, pl.ds(pl.multiple_of(slab * share, 16), share), :]
            out[side, pl.ds(share, extra), :] = small[side * extra : (side + 1) * extra].astype(bf16)


def deal_small(where, keep, left_in, right_in, here, received, after=()):
    slabs = here.shape[0]
    _, lines, width = keep.shape
    extra = SMALL_ROWS * here.shape[2] // width // 2
    shapes = (array((2, lines // slabs + extra, width), bf16),) * slabs
    scratch = [pltpu.VMEM(keep.shape, bf16)]
    return call(deal_small_kernel, "deal_small", shapes, 1, scratch, smem=1, after=after)(
        where, keep, left_in, right_in, here, received
    )


def total_kernel(*refs):
    total = refs[0][...].astype(f32)
    for ref in refs[1:-1]:
        total = total + ref[...].astype(f32)
    refs[-1][...] = total.astype(refs[-1].dtype)


def total(values, after=()):
    return call(total_kernel, "total", array(values[0].shape, values[0].dtype), 1, after=after)(*values)


def blocks_of(where_ref, flip):
    group = jnp.bitwise_xor(where_ref[2], flip)
    x, y = lax.rem(group, 2), group // 2
    return 2 * x + y, 4 + 2 * y + x


def spread_wout_kernel(where_ref, *refs):
    *values, out_ref = refs
    lines = values[0].shape[1]
    for flip, ref in enumerate(values):
        for side, block in enumerate(blocks_of(where_ref, flip)):
            out_ref[pl.ds(pl.multiple_of(block * lines, 16), lines), :] = ref[side].astype(f32)


def spread_wout(where, values, after=()):
    _, lines, channels = values[0].shape
    return call(spread_wout_kernel, "spread_wout", array((8 * lines, channels)), 1, smem=1, after=after)(where, *values)


def spread_win_kernel(where_ref, *refs):
    *values, out_ref, small_ref = refs
    share = out_ref.shape[0]
    _, lines, width = values[0].shape
    extra = lines - share
    for flip, ref in enumerate(values):
        for side, block in enumerate(blocks_of(where_ref, flip)):
            out_ref[:, pl.ds(pl.multiple_of(block * width, LANES), width)] = ref[side, pl.ds(0, share), :].astype(f32)
    for side in range(2):
        part = [ref[side, pl.ds(share, extra), :].astype(f32) for ref in values]
        both = (part[0] + part[1]) + (part[2] + part[3])
        for group in range(4):
            lines = pl.ds(group * 2 * extra + side * extra, extra)
            small_ref[lines, :] = both[:, group * share : (group + 1) * share]


def spread_win(where, values, share, after=()):
    width = values[0].shape[2]
    shapes = (array((share, 8 * width)), array((SMALL_ROWS, share)))
    return call(spread_win_kernel, "spread_win", shapes, 1, smem=1, after=after)(where, *values)


def pack_small_kernel(where_ref, gtaps_ref, gnorm_ref, gbout_ref, gscale_ref, gwest_ref, gbin_ref, here_ref, away_ref):
    slabs, _, share = here_ref.shape

    def fill(even_ref, odd_ref):
        for shard in range(2 * slabs):
            out = odd_ref if shard % 2 else even_ref
            cols = pl.ds(shard * share, share)
            line = 0
            for ref in (gtaps_ref, gnorm_ref, gbout_ref, gscale_ref, gwest_ref):
                out[shard // 2, pl.ds(line, ref.shape[0]), :] = ref[:, cols]
                line += ref.shape[0]
            lines = gbin_ref.shape[1] // gtaps_ref.shape[1]
            for extra in range(lines):
                span = pl.ds((shard * lines + extra) * share, share)
                out[shard // 2, pl.ds(line + extra, 1), :] = gbin_ref[:, span]
            rest = SMALL_ROWS - line - lines
            out[shard // 2, pl.ds(line + lines, rest), :] = jnp.zeros((rest, share), f32)

    @pl.when(where_ref[1] == 0)
    def _():
        fill(here_ref, away_ref)

    @pl.when(where_ref[1] == 1)
    def _():
        fill(away_ref, here_ref)


def pack_small(where, parts, slabs, share, after=()):
    shape = array((slabs, SMALL_ROWS, share))
    return call(pack_small_kernel, "pack_small", (shape, shape), 1, smem=1, after=after)(where, *parts)


AXES = ("dp", "fsdp")


class Routes:
    def __init__(self, groups, members):
        self.groups, self.members, self.slabs = groups, members, members // 2
        self.group = lax.axis_index("dp")
        member = lax.axis_index("fsdp")
        self.slab, self.core = member // 2, member % 2

    def send(self, value, target):
        pairs = [
            (group * self.members + 2 * slab + core, self.index(*target(group, slab, core)))
            for group in range(self.groups)
            for slab in range(self.slabs)
            for core in range(2)
        ]
        return lax.ppermute(value, AXES, pairs)

    def index(self, group, slab, core):
        return group * self.members + 2 * slab + core

    def to_core(self, value):
        return self.send(value, lambda group, slab, core: (group, slab, 1 - core))

    def to_slab(self, value, step):
        return self.send(value, lambda group, slab, core: (group, (slab + step) % self.slabs, core))

    def to_near(self, value, flip):
        return self.send(value, lambda group, slab, core: (group, slab ^ flip, core))

    def to_group(self, value, flip):
        return self.send(value, lambda group, slab, core: (group ^ flip, slab, core))


def shards(
    features,
    cotangent,
    image_sizes,
    warp_index,
    warp_weight,
    offsets,
    conv_kernel,
    conv_bias,
    norm_gain,
    norm_bias,
    w_in,
    bias_in,
    w_out,
    bias_out,
    layer_scale,
    w_estimate,
):
    share, units = w_in.shape
    channels = features.shape[-1]
    members = channels // share
    groups = lax.axis_size("dp")
    paired = groups == 4 and members == 8

    if paired:
        routes = Routes(groups, members)
        slabs = routes.slabs
        where = jnp.stack([routes.slab, routes.core, routes.group, jnp.int32(slabs)])
        vectors = (conv_bias, norm_gain, norm_bias, bias_out, layer_scale)
        packed = pack(where, w_in, conv_kernel, w_estimate, vectors, bias_in)
        win_parts = [routes.to_slab(packed, step) for step in range(1, slabs)]
        win_own = routes.to_core(w_in)
        left, right, small = column_in(packed, win_parts)
        left_in, right_in = routes.to_group(left, 1), routes.to_group(right, 2)
        half = cut(where, w_out, after=(left,))
        wout_parts = [routes.to_slab(half, step) for step in range(1, slabs)]
        wout_own = routes.to_core(w_out)
        small, bin_all = unpack(where, small, routes.to_core(small), units, channels)
    else:
        where = jnp.zeros((4,), jnp.int32)
        small = jnp.concatenate(
            [
                conv_kernel,
                w_estimate,
                jnp.stack([conv_bias, norm_gain, norm_bias, bias_out, layer_scale]),
                bias_in.reshape(-1, share),
            ]
        )
        small = lax.all_gather(small, "fsdp")
        win_all = lax.all_gather(w_in, "fsdp", axis=0, tiled=True)
        wout_all = lax.all_gather(w_out, "fsdp", axis=0, tiled=True)
        bin_all = small[:, SMALL:].reshape(1, units).astype(f32)
        small = small[:, :SMALL].transpose(1, 0, 2).reshape(SMALL, channels).astype(f32)
    reach = WINDOW // 2
    lane_of = (offsets[:, 0] + reach) * CANVAS + offsets[:, 1] + reach
    place = jnp.pad(lane_of, (0, LANES - OFFSETS), constant_values=-1)[None]

    x, up, begun = conv_begin(image_sizes, features, cotangent, small)
    if paired:
        to_x, to_y = onward(left, right, left_in, right_in, after=(begun,))
        halves = [to_x, to_y, routes.to_group(to_x, 1), routes.to_group(to_y, 2)]
        win_theirs = [win_own] + [routes.to_core(value) for value in halves]
        normed, pair, xhat, rstd = conv_norm(where, x, begun, small, after=(to_x,))
        left, right = column_out(wout_parts, after=(normed,))
        quarters = [left, right, routes.to_group(left, 1), routes.to_group(right, 2)]
        wout_theirs = [wout_own] + [routes.to_core(value) for value in quarters]
        win_all, active, slope = place_widen(where, [w_in, *halves], win_theirs, normed, bin_all, after=(left,))
        wout_all, branch = place_narrow(where, [w_out, *quarters], wout_theirs, active, small)
    else:
        normed, pair, xhat, rstd = conv_norm(where, x, begun, small)
        active, slope = widen(normed, win_all, bin_all)
        branch = narrow(active, wout_all, small)
    mixed_out, d_mixed, d_branch, g_scale, g_bout, g_west = flow(
        image_sizes, x, branch, up, warp_index, warp_weight, place, small
    )
    if paired:
        wout_away = grad_narrow(where, active, d_branch, slabs)
        wout_in = routes.to_core(wout_away)
        d_hidden, g_bin = hidden_back(d_branch, wout_all, slope, after=(wout_away,))
        win_away = grad_widen_away(pair, d_hidden)
        win_in = routes.to_core(win_away)
        keep_out, left, right = grad_narrow_here(where, active, d_branch, wout_in, after=(win_away,))
        left_out, right_out = routes.to_group(left, 1), routes.to_group(right, 2)
        keep_in, left, right = grad_widen_here(where, pair, d_hidden, win_in, after=(keep_out,))
        left_in, right_in = routes.to_group(left, 1), routes.to_group(right, 2)
        d_conv, g_norm = norm_back(d_hidden, win_all, xhat, rstd, small, after=(keep_in,))
        g_taps = grad_taps(x, d_conv)
        keep_out, left, right = halve(where, keep_out, left_out, right_out, after=(g_taps,))
        left_out, right_out = routes.to_group(left, 2), routes.to_group(right, 1)
        parts = (g_taps, g_norm, g_bout, g_scale, g_west, g_bin)
        small_here, small_away = pack_small(where, parts, slabs, share, after=(keep_out,))
        small_in = routes.to_core(small_away)
        grad_features = conv_back(image_sizes, d_conv, small, d_mixed, after=(small_away,))
        keep_in, left, right = halve(where, keep_in, left_in, right_in, after=(grad_features,))
        left_in, right_in = routes.to_group(left, 2), routes.to_group(right, 1)
        wout_parts = deal(where, keep_out, left_out, right_out, slabs, after=(keep_in,))
        wout_parts = wout_parts[:1] + tuple(routes.to_slab(v, n + 1) for n, v in enumerate(wout_parts[1:]))
        win_parts = deal_small(where, keep_in, left_in, right_in, small_here, small_in, after=wout_parts[:1])
        win_parts = win_parts[:1] + tuple(routes.to_slab(v, n + 1) for n, v in enumerate(win_parts[1:]))
        g_wout = total(wout_parts, after=win_parts[:1])
        wout_parts = [g_wout] + [routes.to_group(g_wout, flip) for flip in range(1, 4)]
        g_win = total(win_parts, after=(g_wout,))
        win_parts = [g_win] + [routes.to_group(g_win, flip) for flip in range(1, 4)]
        g_wout = spread_wout(where, wout_parts, after=(g_win,))
        g_win, g_small = spread_win(where, win_parts, share, after=(g_wout,))
    else:
        g_wout = grad_narrow(where, active, d_branch, 8).reshape(units, channels)
        d_hidden, g_bin = hidden_back(d_branch, wout_all, slope)
        g_win = grad_widen_full(normed, d_hidden)
        d_conv, g_norm = norm_back(d_hidden, win_all, xhat, rstd, small)
        g_taps = grad_taps(x, d_conv)
        grad_features = conv_back(image_sizes, d_conv, small, d_mixed)
        g_small = jnp.concatenate([g_taps, g_norm, g_bout, g_scale, g_west])
        g_small = g_small.reshape(-1, members, share).transpose(1, 0, 2)
        g_small = jnp.concatenate([g_small, g_bin.reshape(members, -1, share)], axis=1)

        def reduce(value):
            return lax.psum(lax.psum_scatter(value, "fsdp", scatter_dimension=0, tiled=True).astype(f32), "dp")

        g_wout, g_win, g_small = reduce(g_wout), reduce(g_win), reduce(g_small)[0]
    tail = TAPS + 5 + LANES
    return (
        mixed_out,
        grad_features,
        g_small[:TAPS],
        g_small[TAPS],
        g_small[TAPS + 1],
        g_small[TAPS + 2],
        g_win,
        g_small[tail : tail + units // channels].reshape(-1),
        g_wout,
        g_small[TAPS + 3],
        g_small[TAPS + 4],
        jnp.take(g_small[TAPS + 5 : tail], lane_of, axis=0),
    )


def solution(mesh):
    in_specs = (
        P(("dp", "fsdp"), None, None, None, None),
        P(("dp", "fsdp"), None, None, None, None),
        P(("dp", "fsdp")),
        P(("dp", "fsdp"), None, None),
        P(("dp", "fsdp"), None, None),
        P(),
        P(None, "fsdp"),
        P("fsdp"),
        P("fsdp"),
        P("fsdp"),
        P("fsdp", None),
        P("fsdp"),
        P("fsdp", None),
        P("fsdp"),
        P("fsdp"),
        P(None, "fsdp"),
    )
    out_specs = (
        P(("dp", "fsdp"), None, None, None, None),
        P(("dp", "fsdp"), None, None, None, None),
        P(None, "fsdp"),
        P("fsdp"),
        P("fsdp"),
        P("fsdp"),
        P("fsdp", None),
        P("fsdp"),
        P("fsdp", None),
        P("fsdp"),
        P("fsdp"),
        P(None, "fsdp"),
    )
    return jax.shard_map(shards, mesh=mesh, in_specs=in_specs, out_specs=out_specs, check_vma=False)
```

```python
import functools

import jax
import jax.numpy as jnp
import numpy as np
from jax import lax
from jax.experimental import pallas as pl
from jax.experimental.pallas import tpu as pltpu
from jax.sharding import PartitionSpec as P

CANVAS = 10
KERNEL = 7
REACH = KERNEL // 2
TAPS = KERNEL * KERNEL
WINDOW = 9
OFFSETS = WINDOW * WINDOW
PIX = CANVAS * CANVAS
PADDED = 104
LANES = 128
EPSILON = 1e-06
f32 = jnp.float32
bf16 = jnp.bfloat16
WEST = TAPS
CBIAS, GAIN, SHIFT, BOUT, SCALE = range(TAPS + OFFSETS, TAPS + OFFSETS + 5)
SMALL = TAPS + OFFSETS + 5


def call(kernel, name, out_shape, micros, scratch=(), limit=4, smem=0, left=0, after=(), aliases=None):
    def body(*refs):
        kernel(*refs[len(after) :])

    def run(*args):
        specs = [pl.BlockSpec(memory_space=pl.ANY)] * len(after)
        specs += [pl.BlockSpec(memory_space=pltpu.SMEM)] * smem
        specs += [pl.BlockSpec(memory_space=pl.ANY)] * left
        specs += [pl.BlockSpec(memory_space=pltpu.VMEM)] * (len(args) - smem - left)
        return pl.pallas_call(
            body,
            name=name,
            in_specs=specs,
            out_shape=out_shape,
            input_output_aliases={len(after) + source: target for source, target in (aliases or {}).items()},
            scratch_shapes=list(scratch),
            compiler_params=pltpu.CompilerParams(vmem_limit_bytes=limit * 1024 * 1024),
            cost_estimate=pl.CostEstimate(flops=int(micros * 1.15e9), bytes_accessed=0, transcendentals=0),
        )(*after, *args[:smem], *[in_hbm(value) for value in args[smem : smem + left]], *args[smem + left :])

    return run


def in_hbm(value):
    return pltpu.with_memory_space_constraint(value, pltpu.HBM)


def gate(values, after):
    space = pl.BlockSpec(memory_space=pl.ANY)
    return pl.pallas_call(
        lambda *refs: None,
        name="gate",
        in_specs=[space] * (len(values) + len(after)),
        out_specs=[space] * len(values),
        out_shape=[array(value.shape, value.dtype) for value in values],
        input_output_aliases={number: number for number in range(len(values))},
        compiler_params=pltpu.CompilerParams(vmem_limit_bytes=1024 * 1024),
        cost_estimate=pl.CostEstimate(flops=0, bytes_accessed=0, transcendentals=0),
    )(*values, *after)


def array(shape, dtype=f32):
    return jax.ShapeDtypeStruct(shape, dtype)


def nt(left, right):
    return lax.dot_general(left, right, (((1,), (1,)), ((), ())), preferred_element_type=f32)


def tn(left, right):
    return lax.dot_general(left, right, (((0,), (0,)), ((), ())), preferred_element_type=f32)


def dot(left, right):
    return jnp.dot(left, right, preferred_element_type=f32)


def split(values):
    high = values.astype(bf16)
    return high, (values - high.astype(f32)).astype(bf16)


def lane_tile(tile):
    return pl.ds(tile * LANES, LANES)


def conv_rows(source, tile, kernel_ref, flip, finish):
    cols = pl.ds(pl.multiple_of(tile * LANES, LANES), LANES)
    for row in range(CANVAS):
        sums = [None] * CANVAS
        for ky in range(KERNEL):
            source_row = row + ky - REACH
            if not 0 <= source_row < CANVAS:
                continue
            cells = [source[tile, pl.ds((source_row * CANVAS + col) * 8, 8), :] for col in range(CANVAS)]
            for kx in range(KERNEL):
                tap = ky * KERNEL + kx
                tap = TAPS - 1 - tap if flip else tap
                weight = jnp.broadcast_to(kernel_ref[pl.ds(tap, 1), cols], (8, LANES))
                for col in range(CANVAS):
                    other = col + kx - REACH
                    if 0 <= other < CANVAS:
                        term = cells[other] * weight
                        sums[col] = term if sums[col] is None else sums[col] + term
        for col in range(CANVAS):
            finish(row * CANVAS + col, sums[col])


def side_of(sizes_ref, images):
    lines = lax.broadcasted_iota(jnp.int32, (2 * images, LANES), 0)
    side = jnp.zeros(lines.shape, jnp.int32)
    for image in range(images):
        side = jnp.where((lines == image) | (lines == images + image), sizes_ref[image], side)
    return side


def conv_tile(x_ref, tile, small_ref, conv_ref, target):
    cols = pl.ds(pl.multiple_of(tile * LANES, LANES), LANES)
    bias = jnp.broadcast_to(small_ref[pl.ds(CBIAS, 1), cols], (8, LANES))

    def finish(cell, total):
        conv_ref[target, pl.ds(cell * 8, 8), :] = total + bias

    conv_rows(x_ref, tile, small_ref, False, finish)


def conv_begin_kernel(
    sizes_ref, features_ref, upstream_ref, small_ref, x_ref, up_ref, conv_ref, features, upstream, sems,
):
    images = features_ref.shape[0]
    frames = 2 * images
    tiles, rows, _ = x_ref.shape
    side = side_of(sizes_ref, images)
    copies = [
        pltpu.make_async_copy(source.at[image], target.at[image], sems.at[number, image])
        for number, (source, target) in enumerate(((features_ref, features), (upstream_ref, upstream)))
        for image in range(images)
    ]
    for copy in copies:
        copy.start()

    def lay(source, image, target):
        for which in range(2):
            for row in range(CANVAS):
                lines = pl.ds(row * CANVAS * frames + which * images + image, CANVAS, stride=frames)
                for tile in range(tiles):
                    target[tile, lines, :] = source[image, which, row, :, lane_tile(tile)].astype(f32)

    for image in range(images):
        copies[image].wait()
        lay(features, image, x_ref)

    @pl.loop(0, tiles)
    def _(tile):
        for cell in range(PIX):
            inside = side > max(cell // CANVAS, cell % CANVAS)
            lines = pl.ds(cell * 8, 8)
            x_ref[tile, lines, :] = jnp.where(inside, x_ref[tile, lines, :], 0.0)

    @pl.loop(0, tiles // 2)
    def _(tile):
        conv_tile(x_ref, tile, small_ref, conv_ref, tile)

    for tile in range(tiles):
        up_ref[tile, pl.ds(rows, PADDED * frames - rows), :] = jnp.zeros((PADDED * frames - rows, LANES), f32)
    for image in range(images):
        copies[images + image].wait()
        lay(upstream, image, up_ref)


def conv_begin(sizes, features, upstream, small, after=()):
    images, channels = features.shape[0], features.shape[-1]
    rows, tiles = PIX * 2 * images, channels // LANES
    shapes = (
        array((tiles, rows, LANES)),
        array((tiles, PADDED * 2 * images, LANES)),
        array((tiles // 2, rows, LANES)),
    )
    scratch = [pltpu.VMEM(features.shape, bf16), pltpu.VMEM(features.shape, bf16), pltpu.SemaphoreType.DMA((2, images))]
    return call(conv_begin_kernel, "conv_begin", shapes, 6, scratch, limit=8, smem=1, left=2, after=after)(
        sizes, features, upstream, small
    )


def conv_norm_kernel(where_ref, x_ref, begun_ref, small_ref, normed_ref, pair_ref, xhat_ref, rstd_ref, conv, order):
    tiles, rows, _ = x_ref.shape
    channels = tiles * LANES

    @pl.loop(0, tiles // 2)
    def _(tile):
        conv_tile(x_ref, tile + tiles // 2, small_ref, conv, tile)

    share = channels // 8
    core = where_ref[1]
    for tile in range(tiles):
        source = lax.broadcasted_iota(jnp.int32, (channels, LANES), 0)
        target = lax.broadcasted_iota(jnp.int32, (1, LANES), 1) + tile * LANES
        shard = target // share
        wanted = jnp.where(shard < 4, 2 * shard + 1 - core, 2 * (shard - 4) + core) * share + target % share
        order[:, lane_tile(tile)] = (source == wanted).astype(bf16)
    size = 160

    @pl.loop(0, rows // size)
    def _(block):
        lines = pl.ds(pl.multiple_of(block * size, size), size)
        values = [begun_ref[tile, lines, :] for tile in range(tiles // 2)]
        values = jnp.concatenate(values + [conv[tile, lines, :] for tile in range(tiles // 2)], axis=1)
        mean = jnp.sum(values, axis=-1, keepdims=True) * (1.0 / channels)
        centred = values - mean
        variance = jnp.sum(centred * centred, axis=-1, keepdims=True) * (1.0 / channels)
        scale = lax.rsqrt(variance + EPSILON)
        xhat = centred * scale
        xhat_ref[lines, :] = xhat.astype(bf16)
        rstd_ref[lines, :] = scale
        normed = (xhat * small_ref[pl.ds(GAIN, 1), :] + small_ref[pl.ds(SHIFT, 1), :]).astype(bf16)
        normed_ref[lines, :] = normed
        pair_ref[lines, :] = dot(normed, order[...]).astype(bf16)


def conv_norm(where, x, begun, small, after=()):
    tiles, rows, _ = x.shape
    channels = tiles * LANES
    low = array((rows, channels), bf16)
    return call(
        conv_norm_kernel,
        "conv_norm",
        (low, low, low, array((rows, 1))),
        6.6,
        [pltpu.VMEM(begun.shape, f32), pltpu.VMEM((channels, channels), bf16)],
        limit=8,
        smem=1,
        after=after,
    )(where, x, begun, small)


def gelu_pair(hidden):
    cdf = 0.5 * lax.erf(hidden * 0.7071067811865476) + 0.5
    density = jnp.exp(hidden * hidden * -0.5) * 0.3989422804014327
    return hidden * cdf, cdf + hidden * density


def widen_part(group, normed_ref, weight_ref, bias_ref, active_ref, slope_ref, part):
    cols = pl.ds(part * 256, 256)
    quarter = weight_ref.shape[1] // 4
    start = jnp.bitwise_xor(group, part * 256 // quarter) * quarter + part * 256 % quarter
    hidden = dot(normed_ref[...], weight_ref[:, cols]) + bias_ref[:, pl.ds(pl.multiple_of(start, 256), 256)]
    active, slope = gelu_pair(hidden)
    active_ref[:, cols] = active.astype(bf16)
    slope_ref[:, cols] = slope.astype(bf16)


def widen_kernel(normed_ref, weight_ref, bias_ref, active_ref, slope_ref):
    for part in range(weight_ref.shape[1] // 256):
        widen_part(0, normed_ref, weight_ref, bias_ref, active_ref, slope_ref, part)


def widen(normed, weight, bias):
    rows, units = normed.shape[0], weight.shape[1]
    return call(widen_kernel, "widen", (array((rows, units), bf16),) * 2, 6.5, limit=24)(normed, weight, bias)


def start_all(copies, sems):
    running = [pltpu.make_async_copy(source, target, sems.at[number]) for number, (source, target) in enumerate(copies)]
    for copy in running:
        copy.start()
    return running


def place_widen_kernel(where_ref, *refs):
    pieces, (normed_ref, bias_ref, weight_ref, active_ref, slope_ref, sems) = refs[:10], refs[10:]
    z, core, group, slabs = (where_ref[number] for number in range(4))
    share = pieces[0].shape[0]
    width = pieces[1].shape[3]
    copies = []
    for flip in range(4):
        for side in range(2):
            own_ref, to_x, to_y, from_x, from_y = pieces[5 * side : 5 * side + 5]
            left = (to_y.at[0], to_y.at[1], from_y.at[0], from_y.at[1])[flip]
            right = (to_x.at[0], from_x.at[0], to_x.at[1], from_x.at[1])[flip]
            parity = core if side == 0 else 1 - core
            for step in range(4):
                shard = 2 * lax.rem(z - step + slabs, slabs) + parity
                lines = pl.ds(pl.multiple_of(shard * share, 16), share)
                if step == 0:
                    source = pl.ds(pl.multiple_of(jnp.bitwise_xor(group, flip) * 2 * width, LANES), 2 * width)
                    copies.append((own_ref.at[:, source], weight_ref.at[lines, pl.ds(flip * 2 * width, 2 * width)]))
                    continue
                for turn, part in enumerate((left, right)):
                    cols = pl.ds((2 * flip + turn) * width, width)
                    copies.append((part.at[step - 1], weight_ref.at[lines, cols]))
    running = start_all(copies, sems)
    for flip in range(4):
        for copy in running[14 * flip : 14 * flip + 14]:
            copy.wait()
        parts = 2 * width // 256
        for part in range(flip * parts, flip * parts + parts):
            widen_part(group, normed_ref, weight_ref, bias_ref, active_ref, slope_ref, part)


def place_widen(where, mine, theirs, normed, bias, after=()):
    share, units = mine[0].shape
    rows, channels = normed.shape
    wide = array((rows, units), bf16)
    return call(
        place_widen_kernel,
        "place_widen",
        (array((channels, units), bf16), wide, wide),
        8,
        [pltpu.SemaphoreType.DMA((56,))],
        smem=1,
        left=10,
        after=after,
    )(where, *mine, *theirs, normed, bias)


def narrow_rows(active_ref, weight_ref, small_ref, branch_ref):
    size = 160
    for part in range(active_ref.shape[0] // size):
        lines = pl.ds(part * size, size)
        branch = dot(active_ref[lines, :], weight_ref[...]) + small_ref[pl.ds(BOUT, 1), :]
        for tile in range(branch_ref.shape[0]):
            branch_ref[tile, lines, :] = branch[:, tile * LANES : (tile + 1) * LANES]


def narrow(active, weight, small):
    rows, channels = active.shape[0], weight.shape[1]
    return call(narrow_rows, "narrow", array((channels // LANES, rows, LANES)), 4, limit=24)(active, weight, small)


def place_narrow_kernel(side, where_ref, *refs):
    own_ref, *others = refs[:5]
    if side == 0:
        active_ref, small_ref, weight_ref, branch_ref, sems = refs[5:]
    else:
        active_ref, _, begun_ref, weight_ref, branch_ref, sems = refs[5:]
    z, core, group, slabs = (where_ref[number] for number in range(4))
    parity = core if side == 0 else 1 - core
    half = lax.rem(group + group // 2, 2)
    tall = own_ref.shape[0]
    quarter = tall // 4

    def base(slab):
        return jnp.bitwise_xor(slab, group) * 2 * tall + parity * tall

    copies = [(own_ref, weight_ref.at[pl.ds(pl.multiple_of(base(z), 16), tall)])]
    for step in range(1, 4):
        for number, other in enumerate(others):
            start = base(lax.rem(z - step + slabs, slabs))
            start = start + 2 * quarter * (half if number < 2 else 1 - half) + number % 2 * quarter
            copies.append((other.at[step - 1], weight_ref.at[pl.ds(pl.multiple_of(start, 16), quarter)]))
    for copy in start_all(copies, sems):
        copy.wait()
    spans = [pl.ds(pl.multiple_of(part * 2 * tall + parity * tall, LANES), tall) for part in range(4)]
    weight = jnp.concatenate([weight_ref[span, :] for span in spans], axis=0)
    size = 160
    for part in range(active_ref.shape[0] // size):
        rows = pl.ds(part * size, size)
        branch = dot(jnp.concatenate([active_ref[rows, span] for span in spans], axis=1), weight)
        if side == 0:
            branch = branch + small_ref[pl.ds(BOUT, 1), :]
        for tile in range(branch_ref.shape[0]):
            value = branch[:, tile * LANES : (tile + 1) * LANES]
            branch_ref[tile, rows, :] = value if side == 0 else begun_ref[tile, rows, :] + value


def place_narrow(side, where, pieces, active, *more, after=()):
    tall, channels = pieces[0].shape
    rows, units = active.shape
    return call(
        functools.partial(place_narrow_kernel, side),
        "place_narrow",
        (array((units, channels), bf16), array((channels // LANES, rows, LANES))),
        4,
        [pltpu.SemaphoreType.DMA((13,))],
        smem=1,
        left=5,
        after=after,
        aliases={} if side == 0 else {7: 0},
    )(where, *pieces, active, *more)


def skew(values, inverse):
    rows = lax.broadcasted_iota(jnp.int32, values.shape, 0)
    centre = (WINDOW // 2) * (CANVAS + 1)
    amount = jnp.bitwise_and(rows - centre if inverse else centre - rows, LANES - 1)
    for bit in range(7):
        moved = pltpu.roll(values, 1 << bit, 1)
        values = jnp.where(jnp.bitwise_and(amount, 1 << bit) != 0, moved, values)
    return values


def flow_kernel(
    sizes_ref, x_ref, branch_ref, up_ref, index_ref, weight_ref, place_ref, small_ref, window_ref,
    out_ref, dmixed_ref, dbranch_ref, gscale_ref, gbout_ref, gwest_ref, mixed, back, west_in, warp_in,
):
    tiles, rows, _ = x_ref.shape
    images = index_ref.shape[0]
    frames = 2 * images
    channels = tiles * LANES
    factor = channels ** (-0.5)
    every = range(images)
    for tile in range(tiles):
        scale = small_ref[pl.ds(SCALE, 1), lane_tile(tile)]
        mixed[tile, pl.ds(0, rows), :] = x_ref[tile] + scale * branch_ref[tile]
        mixed[tile, pl.ds(rows, PADDED * frames - rows), :] = jnp.zeros((PADDED * frames - rows, LANES), f32)

    def take(ref, frame):
        lines = pl.ds(frame, PADDED, stride=frames)
        return jnp.concatenate([ref[tile, lines, :] for tile in range(tiles)], axis=1)

    def put(ref, frame, values):
        lines = pl.ds(frame, PADDED, stride=frames)
        for tile in range(tiles):
            ref[tile, lines, :] = values[:, tile * LANES : (tile + 1) * LANES]

    west_in[...] = jnp.zeros_like(west_in)
    west_in[pl.ds(0, OFFSETS), :] = small_ref[pl.ds(WEST, OFFSETS), :]
    lanes = lax.broadcasted_iota(jnp.int32, (LANES, LANES), 0)
    west = dot((lanes == place_ref[...]).astype(bf16), west_in[...].astype(bf16)).astype(bf16)
    window = window_ref[0]
    reach = window_ref[1]
    cells = lax.broadcasted_iota(jnp.int32, (PIX, LANES), 1)
    warp_in[...] = jnp.zeros_like(warp_in)
    for image in every:
        warp = jnp.zeros((PIX, LANES), f32)
        for corner in range(4):
            place = index_ref[image, :, pl.ds(corner, 1)]
            amount = weight_ref[image, :, pl.ds(corner, 1)]
            warp = warp + jnp.where(cells == place, amount, 0.0)
        warp_in[image, pl.ds(0, PIX), :] = warp
    warps = [split(warp_in[image][:, :PADDED]) for image in every]
    inside = [(reach < sizes_ref[image].astype(f32)).astype(f32)[:, :1] for image in every]
    first = [take(mixed, image) * inside[image] for image in every]
    second = [take(mixed, images + image) * inside[image] for image in every]
    first_low = [value.astype(bf16) for value in first]
    second_low = [value.astype(bf16) for value in second]
    empty = jnp.zeros((LANES - PADDED, channels), bf16)
    warped = [
        jnp.concatenate([(dot(high, value) + dot(low, value)).astype(bf16), empty], axis=0)
        for (high, low), value in zip(warps, second_low)
    ]
    scores = [nt(left, right) for left, right in zip(first_low, warped)]
    costs = [skew(value, False) * window * factor for value in scores]
    pairs = [gelu_pair(value) for value in costs]
    gated = [value.astype(bf16) for value, _ in pairs]
    d_firsts = [take(up_ref, image) * inside[image] for image in every]
    d_heads = [value.astype(bf16) for value in d_firsts]
    d_costs = [slope * nt(d_head, west) * window * factor for (_, slope), d_head in zip(pairs, d_heads)]
    d_scores = [skew(value, True).astype(bf16) for value in d_costs]
    for image in every:
        put(back, image, d_firsts[image] + dot(d_scores[image], warped[image]))
    d_warped = [tn(value, low)[:PADDED].astype(bf16) for value, low in zip(d_scores, first_low)]
    for image in every:
        high, low = warps[image]
        d_second = take(up_ref, images + image) + tn(high, d_warped[image]) + tn(low, d_warped[image])
        put(back, images + image, d_second * inside[image])
    for tile in range(tiles):
        cols = lane_tile(tile)
        d_mixed = back[tile, pl.ds(0, rows), :]
        dmixed_ref[tile] = d_mixed
        gscale_ref[:, cols] = jnp.sum(d_mixed * branch_ref[tile], axis=0, keepdims=True)
        d_branch = (d_mixed * small_ref[pl.ds(SCALE, 1), cols]).astype(bf16)
        dbranch_ref[:, cols] = d_branch
        gbout_ref[:, cols] = jnp.sum(d_branch.astype(f32), axis=0, keepdims=True)
    gwest = tn(gated[0], d_heads[0])
    for image in every[1:]:
        gwest = gwest + tn(gated[image], d_heads[image])
    gwest_ref[...] = gwest
    for image in every:
        put(mixed, image, (first[image] + dot(gated[image], west)) * inside[image])
        put(mixed, images + image, second[image])
    for image in every:
        for which in range(2):
            for row in range(CANVAS):
                lines = pl.ds(row * CANVAS * frames + which * images + image, CANVAS, stride=frames)
                for tile in range(tiles):
                    out_ref[image, which, row, :, lane_tile(tile)] = mixed[tile, lines, :].astype(bf16)


def tables():
    cells = np.arange(PADDED)[:, None]
    lane = np.arange(LANES)[None, :]
    reach = WINDOW // 2
    row = cells // CANVAS + lane // CANVAS - reach
    col = cells % CANVAS + lane % CANVAS - reach
    good = (lane % CANVAS < WINDOW) & (lane // CANVAS < WINDOW) & (cells < PIX)
    good &= (row >= 0) & (row < CANVAS) & (col >= 0) & (col < CANVAS)
    far = np.maximum(cells // CANVAS, cells % CANVAS) + 0 * lane
    return np.stack([good, far]).astype(np.float32)


def flow(sizes, x, branch, up, index, weight, place, small, after=()):
    tiles, rows, _ = x.shape
    images, channels = index.shape[0], tiles * LANES
    padded = pltpu.VMEM((tiles, PADDED * 2 * images, LANES), f32)
    vector = array((1, channels))
    return call(
        flow_kernel,
        "flow",
        (
            array((images, 2, CANVAS, CANVAS, channels), bf16),
            array(x.shape),
            array((rows, channels), bf16),
            vector,
            vector,
            array((LANES, channels)),
        ),
        6.5,
        [padded, padded, pltpu.VMEM((LANES, channels), f32), pltpu.VMEM((images, PADDED, LANES), f32)],
        limit=14,
        smem=1,
        after=after,
    )(sizes, x, branch, up, index, weight, place, small, jnp.asarray(tables()))


def grad_narrow_kernel(where_ref, active_ref, dbranch_ref, out_ref):
    count, tile, _ = out_ref.shape
    for part in range(count):
        block = 2 * jnp.bitwise_xor(part, where_ref[2]) + 1 - where_ref[1] if count < 8 else part
        cols = pl.ds(pl.multiple_of(block * tile, LANES), tile)
        out_ref[part] = tn(active_ref[:, cols], dbranch_ref[...]).astype(bf16)


def grad_narrow(where, active, dbranch, count, after=()):
    units, channels = active.shape[1], dbranch.shape[1]
    shape = array((count, units // 8, channels), bf16)
    return call(grad_narrow_kernel, "grad_narrow", shape, 0.8 * count, limit=2 * count, smem=1, after=after)(where, active, dbranch)


def send_halves(where_ref, blocks, keep_ref, left_ref, right_ref):
    x, y = lax.rem(where_ref[2], 2), where_ref[2] // 2
    for turn in range(2):
        keep_ref[0, turn] = blocks[2 * x + turn]
        keep_ref[1, turn] = blocks[4 + 2 * y + turn]
        left_ref[turn] = blocks[2 * (1 - x) + turn]
        right_ref[turn] = blocks[4 + 2 * (1 - y) + turn]


def halves_of(lines, width):
    half = array((2, lines, width), bf16)
    return (array((2, 2, lines, width), bf16), half, half), [pltpu.VMEM((8, lines, width), bf16)]


def grad_narrow_here_kernel(where_ref, active_ref, dbranch_ref, received_ref, keep_ref, left_ref, right_ref, blocks):
    count, tile, _ = received_ref.shape
    lines = tile // 8
    for part in range(count):
        block = 2 * jnp.bitwise_xor(part, where_ref[2]) + where_ref[1]
        cols = pl.ds(pl.multiple_of(block * tile, LANES), tile)
        total = tn(active_ref[:, cols], dbranch_ref[...]) + received_ref[part].astype(f32)
        for block in range(8):
            blocks[block, pl.ds(part * lines, lines), :] = total[block * lines : (block + 1) * lines].astype(bf16)
    send_halves(where_ref, blocks, keep_ref, left_ref, right_ref)


def grad_narrow_here(where, active, dbranch, received, after=()):
    count, tile, channels = received.shape
    shapes, scratch = halves_of(count * tile // 8, channels)
    return call(grad_narrow_here_kernel, "grad_narrow_here", shapes, 3.6, scratch, limit=6, smem=1, after=after)(
        where, active, dbranch, received
    )


def hidden_back_kernel(where_ref, dbranch_ref, weight_ref, slope_ref, dhidden_ref, gbin_ref):
    tile = slope_ref.shape[1] // 4
    for part in range(4):
        cols = pl.ds(part * tile, tile)
        d_active = nt(dbranch_ref[...], weight_ref[cols, :])
        d_hidden = (d_active * slope_ref[:, cols].astype(f32)).astype(bf16)
        dhidden_ref[:, cols] = d_hidden
        start = jnp.bitwise_xor(part, where_ref[2]) * tile
        gbin_ref[:, pl.ds(pl.multiple_of(start, LANES), tile)] = jnp.sum(d_hidden.astype(f32), axis=0, keepdims=True)


def hidden_back(where, dbranch, weight, slope, after=()):
    rows, units = slope.shape
    shapes = (array((rows, units), bf16), array((1, units)))
    return call(hidden_back_kernel, "hidden_back", shapes, 4.2, smem=1, after=after)(
        where, dbranch, weight, slope
    )


def grad_widen_full_kernel(normed_ref, dhidden_ref, out_ref):
    tile = 768
    for part in range(out_ref.shape[1] // tile):
        cols = pl.ds(part * tile, tile)
        out_ref[:, cols] = tn(normed_ref[...], dhidden_ref[:, cols]).astype(bf16)


def grad_widen_full(normed, dhidden):
    shape = array((normed.shape[1], dhidden.shape[1]), bf16)
    return call(grad_widen_full_kernel, "grad_widen_full", shape, 5, limit=24)(normed, dhidden)


def grad_widen_away_kernel(where_ref, pair_ref, dhidden_ref, out_ref):
    blocks, lines, width = out_ref.shape
    for part in range(blocks // 2):
        total = tn(pair_ref[:, pl.ds(0, lines)], dhidden_ref[:, pl.ds(2 * part * width, 2 * width)]).astype(bf16)
        block = 2 * jnp.bitwise_xor(part, where_ref[2])
        out_ref[block] = total[:, :width]
        out_ref[block + 1] = total[:, width:]


def grad_widen_away(where, pair, dhidden, after=()):
    shape = array((8, pair.shape[1] // 2, dhidden.shape[1] // 8), bf16)
    return call(grad_widen_away_kernel, "grad_widen_away", shape, 2.6, smem=1, after=after)(where, pair, dhidden)


def grad_widen_here_kernel(where_ref, pair_ref, dhidden_ref, received_ref, keep_ref, left_ref, right_ref, blocks):
    _, lines, width = blocks.shape
    for part in range(4):
        both = tn(pair_ref[:, pl.ds(lines, lines)], dhidden_ref[:, pl.ds(2 * part * width, 2 * width)])
        for turn in range(2):
            block = 2 * jnp.bitwise_xor(part, where_ref[2]) + turn
            value = both[:, turn * width : (turn + 1) * width] + received_ref[block].astype(f32)
            blocks[block] = value.astype(bf16)
    send_halves(where_ref, blocks, keep_ref, left_ref, right_ref)


def grad_widen_here(where, pair, dhidden, received, after=()):
    shapes, scratch = halves_of(*received.shape[1:])
    return call(grad_widen_here_kernel, "grad_widen_here", shapes, 3.8, scratch, limit=6, smem=1, after=after)(
        where, pair, dhidden, received
    )


def norm_back_kernel(dhidden_ref, weight_ref, xhat_ref, rstd_ref, small_ref, dconv_ref, sums_ref):
    rows, channels = xhat_ref.shape
    size = 160
    gain = small_ref[pl.ds(GAIN, 1), :]
    sums = [jnp.zeros((1, channels), f32)] * 3
    for part in range(rows // size):
        lines = pl.ds(part * size, size)
        d_normed = nt(dhidden_ref[lines, :], weight_ref[...])
        xhat = xhat_ref[lines, :].astype(f32)
        product = d_normed * xhat
        d_xhat = d_normed * gain
        mean = jnp.sum(d_xhat, axis=-1, keepdims=True) * (1.0 / channels)
        along = jnp.sum(product * gain, axis=-1, keepdims=True) * (1.0 / channels)
        d_conv = (d_xhat - mean - xhat * along) * rstd_ref[lines, :]
        for tile in range(dconv_ref.shape[0]):
            dconv_ref[tile, lines, :] = d_conv[:, tile * LANES : (tile + 1) * LANES]
        for number, value in enumerate((d_conv, product, d_normed)):
            sums[number] = sums[number] + jnp.sum(value, axis=0, keepdims=True)
    sums_ref[...] = jnp.concatenate(sums, axis=0)


def norm_back(dhidden, weight, xhat, rstd, small, after=()):
    rows, channels = xhat.shape
    return call(
        norm_back_kernel, "norm_back", (array((channels // LANES, rows, LANES)), array((3, channels))), 8.4, after=after
    )(dhidden, weight, xhat, rstd, small)


def grad_taps_kernel(x_ref, dconv_ref, out_ref):
    @pl.loop(0, x_ref.shape[0])
    def _(tile):
        cols = pl.ds(pl.multiple_of(tile * LANES, LANES), LANES)
        for ky in range(KERNEL):
            totals = [None] * KERNEL
            for row in range(CANVAS):
                source_row = row + ky - REACH
                if not 0 <= source_row < CANVAS:
                    continue
                cells = [x_ref[tile, pl.ds((source_row * CANVAS + col) * 8, 8), :] for col in range(CANVAS)]
                grads = [dconv_ref[tile, pl.ds((row * CANVAS + col) * 8, 8), :] for col in range(CANVAS)]
                for kx in range(KERNEL):
                    for col in range(CANVAS):
                        source = col + kx - REACH
                        if 0 <= source < CANVAS:
                            term = cells[source] * grads[col]
                            totals[kx] = term if totals[kx] is None else totals[kx] + term
            for kx in range(KERNEL):
                out_ref[pl.ds(ky * KERNEL + kx, 1), cols] = jnp.sum(totals[kx], axis=0, keepdims=True)


def grad_taps(x, dconv, after=()):
    return call(grad_taps_kernel, "grad_taps", array((TAPS, x.shape[0] * LANES)), 7.5, after=after)(x, dconv)


def conv_back_kernel(sizes_ref, dconv_ref, small_ref, dmixed_ref, out_ref, total):
    tiles = dconv_ref.shape[0]
    images = out_ref.shape[0]
    frames = 2 * images
    side = side_of(sizes_ref, images)

    @pl.loop(0, tiles)
    def _(tile):
        def finish(cell, value):
            lines = pl.ds(cell * 8, 8)
            inside = side > max(cell // CANVAS, cell % CANVAS)
            total[tile, lines, :] = jnp.where(inside, value + dmixed_ref[tile, lines, :], 0.0)

        conv_rows(dconv_ref, tile, small_ref, True, finish)

    for image in range(images):
        for which in range(2):
            for row in range(CANVAS):
                lines = pl.ds(row * CANVAS * frames + which * images + image, CANVAS, stride=frames)
                for tile in range(tiles):
                    out_ref[image, which, row, :, lane_tile(tile)] = total[tile, lines, :]


def conv_back(sizes, dconv, small, dmixed, after=()):
    tiles, rows, _ = dconv.shape
    images = sizes.shape[0]
    return call(
        conv_back_kernel,
        "conv_back",
        array((images, 2, CANVAS, CANVAS, tiles * LANES)),
        8,
        [pltpu.VMEM(dconv.shape, f32)],
        limit=6,
        smem=1,
        after=after,
    )(sizes, dconv, small, dmixed)


GROUPS = 6
LINES = 24
BIAS = SMALL


def pack_kernel(where_ref, weight_ref, taps_ref, west_ref, *refs):
    vectors, (bias_ref, out_ref, small, taps, west, vector, bias, sems) = refs[:5], refs[5:]
    share = weight_ref.shape[0]
    wide = out_ref.shape[1]
    cols = pl.ds(pl.multiple_of(where_ref[2] * wide, LANES), wide)
    copies = [(taps_ref, taps), (west_ref, west), (bias_ref, bias)]
    copies += [(ref, vector.at[number]) for number, ref in enumerate(vectors)]
    copies += [(weight_ref.at[:, cols], out_ref.at[pl.ds(0, share)])]
    running = start_all(copies, sems)
    small[...] = jnp.zeros_like(small)
    lane = pl.ds(0, share)
    for copy in running[:-1]:
        copy.wait()
    small[pl.ds(0, TAPS), lane] = taps[...].astype(f32)
    small[pl.ds(WEST, OFFSETS), lane] = west[...].astype(f32)
    for number in range(len(vectors)):
        small[pl.ds(CBIAS + number, 1), lane] = vector[number].astype(f32)
    for part in range(bias.shape[1] // LANES):
        small[pl.ds(BIAS + part, 1), :] = bias[:, lane_tile(part)].astype(f32)
    for group in range(GROUPS):
        out_ref[pl.ds(share, LINES), lane_tile(group)] = small[pl.ds(group * LINES, LINES), :].astype(bf16)
    running[-1].wait()


def pack(where, weight, taps, west, vectors, bias, after=()):
    share, units = weight.shape
    args = (weight, taps, west, *[v[None] for v in vectors], bias[None])
    return call(
        pack_kernel,
        "pack",
        array((share + LINES, units // 4), bf16),
        2,
        [
            pltpu.VMEM((GROUPS * LINES, LANES), f32),
            pltpu.VMEM(taps.shape, bf16),
            pltpu.VMEM(west.shape, bf16),
            pltpu.VMEM((len(vectors), 1, share), bf16),
            pltpu.VMEM((1, bias.shape[0]), bf16),
            pltpu.SemaphoreType.DMA((len(args),)),
        ],
        smem=1,
        left=len(args),
        after=after,
    )(where, *args)


def column_in_kernel(*refs):
    own_ref, *parts, left_ref, right_ref, small_ref = refs
    share, width = left_ref.shape[1:]
    for number, part in enumerate(parts):
        left_ref[number] = part[pl.ds(0, share), pl.ds(0, width)]
        right_ref[number] = part[pl.ds(0, share), pl.ds(width, width)]
    for number, part in enumerate((own_ref, *parts)):
        small_ref[number] = part[pl.ds(share, LINES), :]


def column_in(own, parts, after=()):
    rows, wide = own.shape
    half = array((len(parts), rows - LINES, wide // 2), bf16)
    small = array((len(parts) + 1, LINES, wide), bf16)
    return call(column_in_kernel, "column_in", (half, half, small), 1, after=after)(own, *parts)


def unpack_kernel(where_ref, mine_ref, theirs_ref, small_ref, bias_ref):
    z, core, slabs = where_ref[0], where_ref[1], where_ref[3]
    channels = small_ref.shape[1]
    share = channels // 8
    everything = None
    for number in range(8):
        ref = mine_ref if number < 4 else theirs_ref
        shard = 2 * lax.rem(z - number % 4 + slabs, slabs) + (core if number < 4 else 1 - core)
        rows = jnp.concatenate([ref[number % 4, :, lane_tile(group)].astype(f32) for group in range(GROUPS)], axis=0)
        source = lax.broadcasted_iota(jnp.int32, (LANES, channels), 0)
        target = lax.broadcasted_iota(jnp.int32, (LANES, channels), 1)
        spread = ((target - shard * share == source) & (source < share)).astype(bf16)
        value = dot(rows.astype(bf16), spread)
        everything = value if everything is None else everything + value
        width = bias_ref.shape[1] // 8
        for part in range(width // LANES):
            cols = pl.ds(pl.multiple_of(shard * width + part * LANES, LANES), LANES)
            bias_ref[:, cols] = rows[BIAS + part : BIAS + part + 1, :]
    small_ref[...] = everything[: small_ref.shape[0]]


def unpack(where, mine, theirs, units, channels):
    return call(unpack_kernel, "unpack", (array((SMALL, channels)), array((1, units))), 1.2, smem=1)(where, mine, theirs)


def column_out_kernel(*refs):
    parts, outs = refs[:3], refs[3:]
    rows = outs[0].shape[1]
    for turn, out in enumerate(outs):
        for number, part in enumerate(parts):
            out[number] = part[pl.ds(turn * rows, rows), :]


def column_out(parts, after=()):
    rows, channels = parts[0].shape
    half = array((len(parts), rows // 2, channels), bf16)
    return call(column_out_kernel, "column_out", (half, half), 1, after=after)(*parts)


def cut_kernel(where_ref, weight_ref, out_ref, sem):
    tall = out_ref.shape[0]
    half = lax.rem(where_ref[2] + where_ref[2] // 2, 2)
    lines = pl.ds(pl.multiple_of(half * tall, 16), tall)
    copy = pltpu.make_async_copy(weight_ref.at[lines], out_ref, sem)
    copy.start()
    copy.wait()


def cut(where, weight, after=()):
    tall, channels = weight.shape
    shape = array((tall // 2, channels), bf16)
    return call(cut_kernel, "cut", shape, 1, [pltpu.SemaphoreType.DMA], smem=1, left=1, after=after)(where, weight)


def onward_kernel(left_ref, right_ref, left_in_ref, right_in_ref, to_x_ref, to_y_ref):
    to_y_ref[0] = left_ref[...]
    to_y_ref[1] = left_in_ref[...]
    to_x_ref[0] = right_ref[...]
    to_x_ref[1] = right_in_ref[...]


def onward(left, right, left_in, right_in, after=()):
    shape = array((2, *left.shape), bf16)
    return call(onward_kernel, "onward", (shape, shape), 1, after=after)(left, right, left_in, right_in)


def halve_kernel(where_ref, keep_ref, left_in_ref, right_in_ref, keep_out_ref, left_ref, right_ref):
    x, y = lax.rem(where_ref[2], 2), where_ref[2] // 2

    def total(side, which):
        received = left_in_ref if side == 0 else right_in_ref
        return keep_ref[side, which].astype(f32) + received[which].astype(f32)

    keep_out_ref[0] = total(0, y).astype(bf16)
    keep_out_ref[1] = total(1, x).astype(bf16)
    left_ref[...] = total(0, 1 - y).astype(bf16)
    right_ref[...] = total(1, 1 - x).astype(bf16)


def halve(where, keep, left_in, right_in, after=()):
    _, _, lines, width = keep.shape
    half = array((lines, width), bf16)
    shapes = (array((2, lines, width), bf16), half, half)
    return call(halve_kernel, "halve", shapes, 1, smem=1, after=after)(where, keep, left_in, right_in)


def deal_total(where_ref, keep_ref, left_in_ref, right_in_ref, total):
    total[0] = (keep_ref[0].astype(f32) + left_in_ref[...].astype(f32)).astype(bf16)
    total[1] = (keep_ref[1].astype(f32) + right_in_ref[...].astype(f32)).astype(bf16)


def deal_kernel(where_ref, keep_ref, left_in_ref, right_in_ref, *refs):
    outs, total = refs[:-1], refs[-1]
    share = outs[0].shape[1]
    deal_total(where_ref, keep_ref, left_in_ref, right_in_ref, total)
    for step, out in enumerate(outs):
        slab = lax.rem(where_ref[0] + step, len(outs))
        for side in range(2):
            out[side] = total[side, pl.ds(pl.multiple_of(slab * share, 16), share), :]


def deal(where, keep, left_in, right_in, slabs, after=()):
    _, lines, width = keep.shape
    shapes = (array((2, lines // slabs, width), bf16),) * slabs
    scratch = [pltpu.VMEM(keep.shape, bf16)]
    return call(deal_kernel, "deal", shapes, 1, scratch, smem=1, after=after)(where, keep, left_in, right_in)


SMALL_ROWS = 192


def deal_small_kernel(where_ref, keep_ref, left_in_ref, right_in_ref, here_ref, received_ref, *refs):
    outs, total = refs[:-1], refs[-1]
    deal_total(where_ref, keep_ref, left_in_ref, right_in_ref, total)
    share = total.shape[1] // len(outs)
    extra = outs[0].shape[1] - share
    for step, out in enumerate(outs):
        slab = lax.rem(where_ref[0] + step, len(outs))
        small = here_ref[slab] + received_ref[slab]
        lines = SMALL_ROWS // 4
        small = jnp.concatenate([small[part * lines : (part + 1) * lines] for part in range(4)], axis=1)
        for side in range(2):
            out[side, pl.ds(0, share), :] = total[side, pl.ds(pl.multiple_of(slab * share, 16), share), :]
            out[side, pl.ds(share, extra), :] = small[side * extra : (side + 1) * extra].astype(bf16)


def deal_small(where, keep, left_in, right_in, here, received, after=()):
    slabs = here.shape[0]
    _, lines, width = keep.shape
    extra = SMALL_ROWS * here.shape[2] // width // 2
    shapes = (array((2, lines // slabs + extra, width), bf16),) * slabs
    scratch = [pltpu.VMEM(keep.shape, bf16)]
    return call(deal_small_kernel, "deal_small", shapes, 1, scratch, smem=1, after=after)(
        where, keep, left_in, right_in, here, received
    )


def total_kernel(*refs):
    total = refs[0][...].astype(f32)
    for ref in refs[1:-1]:
        total = total + ref[...].astype(f32)
    refs[-1][...] = total.astype(refs[-1].dtype)


def total(values, after=()):
    return call(total_kernel, "total", array(values[0].shape, values[0].dtype), 1, after=after)(*values)


def blocks_of(where_ref, flip):
    group = jnp.bitwise_xor(where_ref[2], flip)
    x, y = lax.rem(group, 2), group // 2
    return 2 * x + y, 4 + 2 * y + x


def spread_wout_kernel(where_ref, *refs):
    *values, out_ref = refs
    lines = values[0].shape[1]
    for flip, ref in enumerate(values):
        for side, block in enumerate(blocks_of(where_ref, flip)):
            out_ref[pl.ds(pl.multiple_of(block * lines, 16), lines), :] = ref[side].astype(f32)


def spread_wout(where, values, after=()):
    _, lines, channels = values[0].shape
    return call(spread_wout_kernel, "spread_wout", array((8 * lines, channels)), 1, smem=1, after=after)(where, *values)


def spread_win_kernel(where_ref, lane_ref, *refs):
    values, (out_ref, taps_ref, sums_ref, west_ref, bias_ref, small) = refs[:4], refs[4:]
    share = out_ref.shape[0]
    _, lines, width = values[0].shape
    extra = lines - share
    for flip, ref in enumerate(values):
        for side, block in enumerate(blocks_of(where_ref, flip)):
            out_ref[:, pl.ds(pl.multiple_of(block * width, LANES), width)] = ref[side, pl.ds(0, share), :].astype(f32)
    for side in range(2):
        part = [ref[side, pl.ds(share, extra), :].astype(f32) for ref in values]
        both = (part[0] + part[1]) + (part[2] + part[3])
        for group in range(4):
            span = pl.ds(group * 2 * extra + side * extra, extra)
            small[span, :] = both[:, group * share : (group + 1) * share]
    taps_ref[...] = small[pl.ds(0, TAPS), :]
    sums_ref[...] = small[pl.ds(TAPS, 5), :]
    for offset in range(OFFSETS):
        west_ref[pl.ds(offset, 1), :] = small[pl.ds(TAPS + 5 + lane_ref[offset], 1), :]
    bias_ref[...] = small[pl.ds(TAPS + 5 + LANES, bias_ref.shape[0]), :]


def spread_win(where, lane_of, values, share, after=()):
    width = values[0].shape[2]
    shapes = (
        array((share, 8 * width)),
        array((TAPS, share)),
        array((5, share)),
        array((OFFSETS, share)),
        array((width // share, share)),
    )
    scratch = [pltpu.VMEM((SMALL_ROWS, share), f32)]
    return call(spread_win_kernel, "spread_win", shapes, 1, scratch, smem=2, after=after)(where, lane_of, *values)


def pack_small_kernel(where_ref, gtaps_ref, gnorm_ref, gbout_ref, gscale_ref, gwest_ref, gbin_ref, here_ref, away_ref):
    slabs, _, share = here_ref.shape

    def fill(even_ref, odd_ref):
        for shard in range(2 * slabs):
            out = odd_ref if shard % 2 else even_ref
            cols = pl.ds(shard * share, share)
            line = 0
            for ref in (gtaps_ref, gnorm_ref, gbout_ref, gscale_ref, gwest_ref):
                out[shard // 2, pl.ds(line, ref.shape[0]), :] = ref[:, cols]
                line += ref.shape[0]
            lines = gbin_ref.shape[1] // gtaps_ref.shape[1]
            for extra in range(lines):
                span = pl.ds((shard * lines + extra) * share, share)
                out[shard // 2, pl.ds(line + extra, 1), :] = gbin_ref[:, span]
            rest = SMALL_ROWS - line - lines
            out[shard // 2, pl.ds(line + lines, rest), :] = jnp.zeros((rest, share), f32)

    @pl.when(where_ref[1] == 0)
    def _():
        fill(here_ref, away_ref)

    @pl.when(where_ref[1] == 1)
    def _():
        fill(away_ref, here_ref)


def pack_small(where, parts, slabs, share, after=()):
    shape = array((slabs, SMALL_ROWS, share))
    return call(pack_small_kernel, "pack_small", (shape, shape), 1, smem=1, after=after)(where, *parts)


AXES = ("dp", "fsdp")


class Routes:
    def __init__(self, groups, members):
        self.groups, self.members, self.slabs = groups, members, members // 2
        self.group = lax.axis_index("dp")
        member = lax.axis_index("fsdp")
        self.slab, self.core = member // 2, member % 2

    def send(self, value, target):
        pairs = [
            (group * self.members + 2 * slab + core, self.index(*target(group, slab, core)))
            for group in range(self.groups)
            for slab in range(self.slabs)
            for core in range(2)
        ]
        return lax.ppermute(value, AXES, pairs)

    def index(self, group, slab, core):
        return group * self.members + 2 * slab + core

    def to_core(self, value):
        return self.send(value, lambda group, slab, core: (group, slab, 1 - core))

    def to_slab(self, value, step):
        return self.send(value, lambda group, slab, core: (group, (slab + step) % self.slabs, core))

    def to_near(self, value, flip):
        return self.send(value, lambda group, slab, core: (group, slab ^ flip, core))

    def to_group(self, value, flip):
        return self.send(value, lambda group, slab, core: (group ^ flip, slab, core))


def shards(
    features,
    cotangent,
    image_sizes,
    warp_index,
    warp_weight,
    offsets,
    conv_kernel,
    conv_bias,
    norm_gain,
    norm_bias,
    w_in,
    bias_in,
    w_out,
    bias_out,
    layer_scale,
    w_estimate,
):
    share, units = w_in.shape
    channels = features.shape[-1]
    members = channels // share
    groups = lax.axis_size("dp")
    paired = groups == 4 and members == 8

    reach = WINDOW // 2
    lane_of = (offsets[:, 0] + reach) * CANVAS + offsets[:, 1] + reach
    place = jnp.pad(lane_of, (0, LANES - OFFSETS), constant_values=-1)[None]

    early = (features, cotangent, warp_index, warp_weight, place, lane_of)
    if paired:
        routes = Routes(groups, members)
        slabs = routes.slabs
        where = jnp.stack([routes.slab, routes.core, routes.group, jnp.int32(slabs)])
        vectors = (conv_bias, norm_gain, norm_bias, bias_out, layer_scale)
        packed = pack(where, w_in, conv_kernel, w_estimate, vectors, bias_in)
        win_parts = [routes.to_slab(packed, step) for step in range(1, slabs)]
        win_own = routes.to_core(w_in)
        half = cut(where, w_out, after=(packed,))
        wout_parts = [routes.to_slab(half, step) for step in range(1, slabs)]
        wout_own = routes.to_core(w_out)
        left, right, small = column_in(packed, win_parts, after=(wout_parts[0], *early))
        left_in, right_in = routes.to_group(left, 1), routes.to_group(right, 2)
        small, bin_all = unpack(where, small, routes.to_core(small), units, channels)
    else:
        where = jnp.zeros((4,), jnp.int32)
        small = jnp.concatenate(
            [
                conv_kernel,
                w_estimate,
                jnp.stack([conv_bias, norm_gain, norm_bias, bias_out, layer_scale]),
                bias_in.reshape(-1, share),
            ]
        )
        small = lax.all_gather(small, "fsdp")
        win_all = lax.all_gather(w_in, "fsdp", axis=0, tiled=True)
        wout_all = lax.all_gather(w_out, "fsdp", axis=0, tiled=True)
        bin_all = small[:, SMALL:].reshape(1, units).astype(f32)
        small = small[:, :SMALL].transpose(1, 0, 2).reshape(SMALL, channels).astype(f32)
    x, up, begun = conv_begin(image_sizes, features, cotangent, small)
    if paired:
        to_x, to_y = onward(left, right, left_in, right_in, after=(begun,))
        halves = [to_x, to_y, routes.to_group(to_x, 1), routes.to_group(to_y, 2)]
        normed, pair, xhat, rstd = conv_norm(where, x, begun, small, after=(to_x,))
        halves = gate(halves, (normed,))
        win_theirs = [win_own] + [routes.to_core(value) for value in halves]
        left, right = column_out(wout_parts, after=(normed,))
        left_in, right_in = routes.to_group(left, 1), routes.to_group(right, 2)
        win_all, active, slope = place_widen(where, [w_in, *halves], win_theirs, normed, bin_all, after=(left,))
        quarters = [left, right, *gate((left_in, right_in), (active,))]
        wout_theirs = [wout_own] + [routes.to_core(value) for value in quarters]
        begun = place_narrow(0, where, [w_out, *quarters], active, small)
        wout_all, branch = place_narrow(1, where, wout_theirs, active, *begun)
    else:
        normed, pair, xhat, rstd = conv_norm(where, x, begun, small)
        active, slope = widen(normed, win_all, bin_all)
        branch = narrow(active, wout_all, small)
    mixed_out, d_mixed, d_branch, g_scale, g_bout, g_west = flow(
        image_sizes, x, branch, up, warp_index, warp_weight, place, small
    )
    if paired:
        wout_away = grad_narrow(where, active, d_branch, slabs)
        wout_in = routes.to_core(wout_away)
        d_hidden, g_bin = hidden_back(where, d_branch, wout_all, slope, after=(wout_away,))
        keep_out, left, right = grad_narrow_here(where, active, d_branch, wout_in, after=(d_hidden,))
        left_out, right_out = routes.to_group(left, 1), routes.to_group(right, 2)
        win_away = grad_widen_away(where, pair, d_hidden, after=(keep_out,))
        win_in = routes.to_core(win_away)
        d_conv, g_norm = norm_back(d_hidden, win_all, xhat, rstd, small, after=(win_away,))
        keep_in, left, right = grad_widen_here(where, pair, d_hidden, win_in, after=(d_conv,))
        left_in, right_in = routes.to_group(left, 1), routes.to_group(right, 2)
        keep_out, left, right = halve(where, keep_out, left_out, right_out, after=(keep_in,))
        left_out, right_out = routes.to_group(left, 2), routes.to_group(right, 1)
        g_taps = grad_taps(x, d_conv, after=(keep_out,))
        parts = (g_taps, g_norm, g_bout, g_scale, g_west, g_bin)
        small_here, small_away = pack_small(where, parts, slabs, share)
        small_in = routes.to_core(small_away)
        wout_parts = deal(where, keep_out, left_out, right_out, slabs, after=(small_away,))
        wout_parts = wout_parts[:1] + tuple(routes.to_slab(v, n + 1) for n, v in enumerate(wout_parts[1:]))
        keep_in, left, right = halve(where, keep_in, left_in, right_in, after=wout_parts[:1])
        left_in, right_in = routes.to_group(left, 2), routes.to_group(right, 1)
        grad_features = conv_back(image_sizes, d_conv, small, d_mixed, after=(keep_in,))
        win_parts = deal_small(where, keep_in, left_in, right_in, small_here, small_in, after=(grad_features,))
        win_parts = win_parts[:1] + tuple(routes.to_slab(v, n + 1) for n, v in enumerate(win_parts[1:]))
        g_wout = total(wout_parts, after=win_parts[:1])
        wout_parts = [g_wout] + [routes.to_group(g_wout, flip) for flip in range(1, 4)]
        g_win = total(win_parts, after=(g_wout,))
        win_parts = [g_win] + [routes.to_group(g_win, flip) for flip in range(1, 4)]
        g_wout = spread_wout(where, wout_parts, after=(g_win,))
        g_win, g_taps, g_small, g_west, g_bin = spread_win(where, lane_of, win_parts, share, after=(g_wout,))
    else:
        g_wout = grad_narrow(where, active, d_branch, 8).reshape(units, channels)
        d_hidden, g_bin = hidden_back(where, d_branch, wout_all, slope)
        g_win = grad_widen_full(normed, d_hidden)
        d_conv, g_norm = norm_back(d_hidden, win_all, xhat, rstd, small)
        g_taps = grad_taps(x, d_conv)
        grad_features = conv_back(image_sizes, d_conv, small, d_mixed)
        g_small = jnp.concatenate([g_taps, g_norm, g_bout, g_scale, g_west])
        g_small = g_small.reshape(-1, members, share).transpose(1, 0, 2)
        g_small = jnp.concatenate([g_small, g_bin.reshape(members, -1, share)], axis=1)

        def reduce(value):
            return lax.psum(lax.psum_scatter(value, "fsdp", scatter_dimension=0, tiled=True).astype(f32), "dp")

        g_wout, g_win, g_small = reduce(g_wout), reduce(g_win), reduce(g_small)[0]
        tail = TAPS + 5 + LANES
        g_taps, g_west, g_bin = g_small[:TAPS], jnp.take(g_small[TAPS + 5 : tail], lane_of, axis=0), g_small[tail:]
        g_small = g_small[TAPS : TAPS + 5]
    return (
        mixed_out,
        grad_features,
        g_taps,
        g_small[0],
        g_small[1],
        g_small[2],
        g_win,
        g_bin.reshape(-1),
        g_wout,
        g_small[3],
        g_small[4],
        g_west,
    )


def solution(mesh):
    in_specs = (
        P(("dp", "fsdp"), None, None, None, None),
        P(("dp", "fsdp"), None, None, None, None),
        P(("dp", "fsdp")),
        P(("dp", "fsdp"), None, None),
        P(("dp", "fsdp"), None, None),
        P(),
        P(None, "fsdp"),
        P("fsdp"),
        P("fsdp"),
        P("fsdp"),
        P("fsdp", None),
        P("fsdp"),
        P("fsdp", None),
        P("fsdp"),
        P("fsdp"),
        P(None, "fsdp"),
    )
    out_specs = (
        P(("dp", "fsdp"), None, None, None, None),
        P(("dp", "fsdp"), None, None, None, None),
        P(None, "fsdp"),
        P("fsdp"),
        P("fsdp"),
        P("fsdp"),
        P("fsdp", None),
        P("fsdp"),
        P("fsdp", None),
        P("fsdp"),
        P("fsdp"),
        P(None, "fsdp"),
    )
    return jax.shard_map(shards, mesh=mesh, in_specs=in_specs, out_specs=out_specs, check_vma=False)
```

```python
import functools

import jax
import jax.numpy as jnp
import numpy as np
from jax import lax
from jax.experimental import pallas as pl
from jax.experimental.pallas import tpu as pltpu
from jax.sharding import PartitionSpec as P

CANVAS = 10
KERNEL = 7
REACH = KERNEL // 2
TAPS = KERNEL * KERNEL
WINDOW = 9
OFFSETS = WINDOW * WINDOW
PIX = CANVAS * CANVAS
PADDED = 104
LANES = 128
EPSILON = 1e-06
f32 = jnp.float32
bf16 = jnp.bfloat16
WEST = TAPS
CBIAS, GAIN, SHIFT, BOUT, SCALE = range(TAPS + OFFSETS, TAPS + OFFSETS + 5)
SMALL = TAPS + OFFSETS + 5


def call(kernel, name, out_shape, micros, scratch=(), limit=4, smem=0, left=0, after=(), aliases=None):
    def body(*refs):
        kernel(*refs[len(after) :])

    def run(*args):
        specs = [pl.BlockSpec(memory_space=pl.ANY)] * len(after)
        specs += [pl.BlockSpec(memory_space=pltpu.SMEM)] * smem
        specs += [pl.BlockSpec(memory_space=pl.ANY)] * left
        specs += [pl.BlockSpec(memory_space=pltpu.VMEM)] * (len(args) - smem - left)
        return pl.pallas_call(
            body,
            name=name,
            in_specs=specs,
            out_specs=jax.tree.map(out_space, out_shape),
            out_shape=out_shape,
            input_output_aliases={len(after) + source: target for source, target in (aliases or {}).items()},
            scratch_shapes=list(scratch),
            compiler_params=pltpu.CompilerParams(vmem_limit_bytes=limit * 1024 * 1024),
            cost_estimate=pl.CostEstimate(flops=int(micros * 1.15e9), bytes_accessed=0, transcendentals=0),
        )(*after, *args[:smem], *[in_hbm(value) for value in args[smem : smem + left]], *args[smem + left :])

    return run


def out_space(shape):
    return pl.BlockSpec(memory_space=pltpu.VMEM if isinstance(shape, jax.ShapeDtypeStruct) else pltpu.HBM)


def in_hbm(value):
    return pltpu.with_memory_space_constraint(value, pltpu.HBM)


def gate(values, after):
    space = pl.BlockSpec(memory_space=pl.ANY)
    return pl.pallas_call(
        lambda *refs: None,
        name="gate",
        in_specs=[space] * (len(values) + len(after)),
        out_specs=[space] * len(values),
        out_shape=[array(value.shape, value.dtype) for value in values],
        input_output_aliases={number: number for number in range(len(values))},
        compiler_params=pltpu.CompilerParams(vmem_limit_bytes=1024 * 1024),
        cost_estimate=pl.CostEstimate(flops=0, bytes_accessed=0, transcendentals=0),
    )(*values, *after)


def array(shape, dtype=f32):
    return jax.ShapeDtypeStruct(shape, dtype)


def nt(left, right):
    return lax.dot_general(left, right, (((1,), (1,)), ((), ())), preferred_element_type=f32)


def tn(left, right):
    return lax.dot_general(left, right, (((0,), (0,)), ((), ())), preferred_element_type=f32)


def dot(left, right):
    return jnp.dot(left, right, preferred_element_type=f32)


def split(values):
    high = values.astype(bf16)
    return high, (values - high.astype(f32)).astype(bf16)


def lane_tile(tile):
    return pl.ds(tile * LANES, LANES)


def conv_rows(source, tile, kernel_ref, flip, finish):
    cols = pl.ds(pl.multiple_of(tile * LANES, LANES), LANES)
    for row in range(CANVAS):
        sums = [None] * CANVAS
        for ky in range(KERNEL):
            source_row = row + ky - REACH
            if not 0 <= source_row < CANVAS:
                continue
            cells = [source[tile, pl.ds((source_row * CANVAS + col) * 8, 8), :] for col in range(CANVAS)]
            for kx in range(KERNEL):
                tap = ky * KERNEL + kx
                tap = TAPS - 1 - tap if flip else tap
                weight = jnp.broadcast_to(kernel_ref[pl.ds(tap, 1), cols], (8, LANES))
                for col in range(CANVAS):
                    other = col + kx - REACH
                    if 0 <= other < CANVAS:
                        term = cells[other] * weight
                        sums[col] = term if sums[col] is None else sums[col] + term
        for col in range(CANVAS):
            finish(row * CANVAS + col, sums[col])


def side_of(sizes_ref, images):
    lines = lax.broadcasted_iota(jnp.int32, (2 * images, LANES), 0)
    side = jnp.zeros(lines.shape, jnp.int32)
    for image in range(images):
        side = jnp.where((lines == image) | (lines == images + image), sizes_ref[image], side)
    return side


def conv_tile(x_ref, tile, small_ref, conv_ref, target):
    cols = pl.ds(pl.multiple_of(tile * LANES, LANES), LANES)
    bias = jnp.broadcast_to(small_ref[pl.ds(CBIAS, 1), cols], (8, LANES))

    def finish(cell, total):
        conv_ref[target, pl.ds(cell * 8, 8), :] = total + bias

    conv_rows(x_ref, tile, small_ref, False, finish)


def conv_begin_kernel(
    sizes_ref, features_ref, upstream_ref, small_ref, x_ref, up_ref, conv_ref, features, upstream, sems,
):
    images = features_ref.shape[0]
    frames = 2 * images
    tiles, rows, _ = x_ref.shape
    side = side_of(sizes_ref, images)
    copies = [
        pltpu.make_async_copy(source.at[image], target.at[image], sems.at[number, image])
        for number, (source, target) in enumerate(((features_ref, features), (upstream_ref, upstream)))
        for image in range(images)
    ]
    for copy in copies:
        copy.start()

    def lay(source, image, target):
        for which in range(2):
            for row in range(CANVAS):
                lines = pl.ds(row * CANVAS * frames + which * images + image, CANVAS, stride=frames)
                for tile in range(tiles):
                    target[tile, lines, :] = source[image, which, row, :, lane_tile(tile)].astype(f32)

    for image in range(images):
        copies[image].wait()
        lay(features, image, x_ref)

    @pl.loop(0, tiles)
    def _(tile):
        for cell in range(PIX):
            inside = side > max(cell // CANVAS, cell % CANVAS)
            lines = pl.ds(cell * 8, 8)
            x_ref[tile, lines, :] = jnp.where(inside, x_ref[tile, lines, :], 0.0)

    @pl.loop(0, tiles // 2)
    def _(tile):
        conv_tile(x_ref, tile, small_ref, conv_ref, tile)

    for tile in range(tiles):
        up_ref[tile, pl.ds(rows, PADDED * frames - rows), :] = jnp.zeros((PADDED * frames - rows, LANES), f32)
    for image in range(images):
        copies[images + image].wait()
        lay(upstream, image, up_ref)


def conv_begin(sizes, features, upstream, small, after=()):
    images, channels = features.shape[0], features.shape[-1]
    rows, tiles = PIX * 2 * images, channels // LANES
    shapes = (
        array((tiles, rows, LANES)),
        array((tiles, PADDED * 2 * images, LANES)),
        array((tiles // 2, rows, LANES)),
    )
    scratch = [pltpu.VMEM(features.shape, bf16), pltpu.VMEM(features.shape, bf16), pltpu.SemaphoreType.DMA((2, images))]
    return call(conv_begin_kernel, "conv_begin", shapes, 1, scratch, limit=8, smem=1, left=2, after=after)(
        sizes, features, upstream, small
    )


def conv_norm_kernel(where_ref, x_ref, begun_ref, small_ref, normed_ref, pair_ref, xhat_ref, rstd_ref, conv, order):
    tiles, rows, _ = x_ref.shape
    channels = tiles * LANES

    @pl.loop(0, tiles // 2)
    def _(tile):
        conv_tile(x_ref, tile + tiles // 2, small_ref, conv, tile)

    share = channels // 8
    core = where_ref[1]
    for tile in range(tiles):
        source = lax.broadcasted_iota(jnp.int32, (channels, LANES), 0)
        target = lax.broadcasted_iota(jnp.int32, (1, LANES), 1) + tile * LANES
        shard = target // share
        wanted = jnp.where(shard < 4, 2 * shard + 1 - core, 2 * (shard - 4) + core) * share + target % share
        order[:, lane_tile(tile)] = (source == wanted).astype(bf16)
    size = 160

    @pl.loop(0, rows // size)
    def _(block):
        lines = pl.ds(pl.multiple_of(block * size, size), size)
        values = [begun_ref[tile, lines, :] for tile in range(tiles // 2)]
        values = jnp.concatenate(values + [conv[tile, lines, :] for tile in range(tiles // 2)], axis=1)
        mean = jnp.sum(values, axis=-1, keepdims=True) * (1.0 / channels)
        centred = values - mean
        variance = jnp.sum(centred * centred, axis=-1, keepdims=True) * (1.0 / channels)
        scale = lax.rsqrt(variance + EPSILON)
        xhat = centred * scale
        xhat_ref[lines, :] = xhat.astype(bf16)
        rstd_ref[lines, :] = scale
        normed = (xhat * small_ref[pl.ds(GAIN, 1), :] + small_ref[pl.ds(SHIFT, 1), :]).astype(bf16)
        normed_ref[lines, :] = normed
        pair_ref[lines, :] = dot(normed, order[...]).astype(bf16)


def conv_norm(where, x, begun, small, after=()):
    tiles, rows, _ = x.shape
    channels = tiles * LANES
    low = array((rows, channels), bf16)
    return call(
        conv_norm_kernel,
        "conv_norm",
        (low, low, low, array((rows, 1))),
        1,
        [pltpu.VMEM(begun.shape, f32), pltpu.VMEM((channels, channels), bf16)],
        limit=8,
        smem=1,
        after=after,
    )(where, x, begun, small)


def gelu_pair(hidden):
    cdf = 0.5 * lax.erf(hidden * 0.7071067811865476) + 0.5
    density = jnp.exp(hidden * hidden * -0.5) * 0.3989422804014327
    return hidden * cdf, cdf + hidden * density


def widen_part(group, normed_ref, weight_ref, bias_ref, active_ref, slope_ref, part):
    cols = pl.ds(part * 256, 256)
    quarter = weight_ref.shape[1] // 4
    start = jnp.bitwise_xor(group, part * 256 // quarter) * quarter + part * 256 % quarter
    hidden = dot(normed_ref[...], weight_ref[:, cols]) + bias_ref[:, pl.ds(pl.multiple_of(start, 256), 256)]
    active, slope = gelu_pair(hidden)
    active_ref[:, cols] = active.astype(bf16)
    slope_ref[:, cols] = slope.astype(bf16)


def widen_kernel(normed_ref, weight_ref, bias_ref, active_ref, slope_ref):
    for part in range(weight_ref.shape[1] // 256):
        widen_part(0, normed_ref, weight_ref, bias_ref, active_ref, slope_ref, part)


def widen(normed, weight, bias):
    rows, units = normed.shape[0], weight.shape[1]
    return call(widen_kernel, "widen", (array((rows, units), bf16),) * 2, 6.5, limit=24)(normed, weight, bias)


def crossed(pieces, flip):
    _, to_x, to_y, from_x, from_y = pieces
    left = (to_y.at[0], to_y.at[1], from_y.at[0], from_y.at[1])[flip]
    right = (to_x.at[0], from_x.at[0], to_x.at[1], from_x.at[1])[flip]
    return left, right


def place_widen_kernel(where_ref, *refs):
    pieces, (normed_ref, bias_ref, weight_ref, active_ref, slope_ref) = refs[:10], refs[10:]
    z, core, group, slabs = (where_ref[number] for number in range(4))
    share = pieces[0].shape[0]
    width = pieces[1].shape[3]
    for flip in range(4):
        for side in range(2):
            parity = core if side == 0 else 1 - core
            own_ref = pieces[5 * side]
            for step in range(4):
                shard = 2 * lax.rem(z - step + slabs, slabs) + parity
                lines = pl.ds(pl.multiple_of(shard * share, 16), share)
                if step == 0:
                    source = pl.ds(pl.multiple_of(jnp.bitwise_xor(group, flip) * 2 * width, LANES), 2 * width)
                    weight_ref[lines, pl.ds(flip * 2 * width, 2 * width)] = own_ref[:, source]
                    continue
                for turn, part in enumerate(crossed(pieces[5 * side : 5 * side + 5], flip)):
                    weight_ref[lines, pl.ds((2 * flip + turn) * width, width)] = part[step - 1]
    for part in range(weight_ref.shape[1] // 256):
        widen_part(group, normed_ref, weight_ref, bias_ref, active_ref, slope_ref, part)


def place_widen(where, mine, theirs, normed, bias, after=()):
    share, units = mine[0].shape
    rows, channels = normed.shape
    wide = array((rows, units), bf16)
    shapes = (array((channels, units), bf16), wide, wide)
    return call(place_widen_kernel, "place_widen", shapes, 8, smem=1, after=after)(where, *mine, *theirs, normed, bias)


def narrow_rows(active_ref, weight_ref, small_ref, branch_ref):
    size = 160
    for part in range(active_ref.shape[0] // size):
        lines = pl.ds(part * size, size)
        branch = dot(active_ref[lines, :], weight_ref[...]) + small_ref[pl.ds(BOUT, 1), :]
        for tile in range(branch_ref.shape[0]):
            branch_ref[tile, lines, :] = branch[:, tile * LANES : (tile + 1) * LANES]


def narrow(active, weight, small):
    rows, channels = active.shape[0], weight.shape[1]
    return call(narrow_rows, "narrow", array((channels // LANES, rows, LANES)), 4, limit=24)(active, weight, small)


def place_narrow_kernel(side, where_ref, *refs):
    pieces = refs[:5]
    if side == 0:
        active_ref, small_ref, weight_ref, branch_ref = refs[5:]
    else:
        active_ref, _, begun_ref, weight_ref, branch_ref = refs[5:]
    z, core, group, slabs = (where_ref[number] for number in range(4))
    parity = core if side == 0 else 1 - core
    tall = pieces[0].shape[0]
    _, _, lines, width = pieces[1].shape

    def base(slab):
        return pl.multiple_of(jnp.bitwise_xor(slab, group) * 2 * tall + parity * tall, 16)

    weight_ref[pl.ds(base(z), tall), :] = pieces[0][...]
    for step in range(1, 4):
        for flip in range(4):
            start = base(lax.rem(z - step + slabs, slabs)) + jnp.bitwise_xor(group, flip) * lines
            for turn, part in enumerate(crossed(pieces, flip)):
                weight_ref[pl.ds(pl.multiple_of(start, 16), lines), pl.ds(turn * width, width)] = part[step - 1]
    spans = [pl.ds(pl.multiple_of(part * 2 * tall + parity * tall, LANES), tall) for part in range(4)]
    weight = jnp.concatenate([weight_ref[span, :] for span in spans], axis=0)
    size = 160
    for part in range(active_ref.shape[0] // size):
        rows = pl.ds(part * size, size)
        branch = dot(jnp.concatenate([active_ref[rows, span] for span in spans], axis=1), weight)
        if side == 0:
            branch = branch + small_ref[pl.ds(BOUT, 1), :]
        for tile in range(branch_ref.shape[0]):
            value = branch[:, tile * LANES : (tile + 1) * LANES]
            branch_ref[tile, rows, :] = value if side == 0 else begun_ref[tile, rows, :] + value


def place_narrow(side, where, pieces, active, *more, after=()):
    tall, channels = pieces[0].shape
    rows, units = active.shape
    shapes = (array((units, channels), bf16), array((channels // LANES, rows, LANES)))
    return call(
        functools.partial(place_narrow_kernel, side),
        "place_narrow",
        shapes,
        3,
        smem=1,
        after=after,
        aliases={} if side == 0 else {7: 0},
    )(where, *pieces, active, *more)


def skew(values, inverse):
    rows = lax.broadcasted_iota(jnp.int32, values.shape, 0)
    centre = (WINDOW // 2) * (CANVAS + 1)
    amount = jnp.bitwise_and(rows - centre if inverse else centre - rows, LANES - 1)
    for bit in range(7):
        moved = pltpu.roll(values, 1 << bit, 1)
        values = jnp.where(jnp.bitwise_and(amount, 1 << bit) != 0, moved, values)
    return values


def movers(tiles, frames):
    def take(ref, frame):
        lines = pl.ds(frame, PADDED, stride=frames)
        return jnp.concatenate([ref[tile, lines, :] for tile in range(tiles)], axis=1)

    def put(ref, frame, values):
        lines = pl.ds(frame, PADDED, stride=frames)
        for tile in range(tiles):
            ref[tile, lines, :] = values[:, tile * LANES : (tile + 1) * LANES]

    return take, put


def mix(x_ref, branch_ref, small_ref, mixed):
    tiles, rows, _ = x_ref.shape
    rest = mixed.shape[1] - rows
    for tile in range(tiles):
        scale = small_ref[pl.ds(SCALE, 1), lane_tile(tile)]
        mixed[tile, pl.ds(0, rows), :] = x_ref[tile] + scale * branch_ref[tile]
        mixed[tile, pl.ds(rows, rest), :] = jnp.zeros((rest, LANES), f32)


def estimator(place_ref, small_ref, west_in):
    west_in[...] = jnp.zeros_like(west_in)
    west_in[pl.ds(0, OFFSETS), :] = small_ref[pl.ds(WEST, OFFSETS), :]
    lanes = lax.broadcasted_iota(jnp.int32, (LANES, LANES), 0)
    return dot((lanes == place_ref[...]).astype(bf16), west_in[...].astype(bf16)).astype(bf16)


def flow_kernel(
    sizes_ref, x_ref, branch_ref, up_ref, index_ref, weight_ref, place_ref, small_ref, window_ref,
    gated_ref, dmixed_ref, dbranch_ref, gscale_ref, gbout_ref, mixed, back, west_in, warp_in, sem,
):
    tiles, rows, _ = x_ref.shape
    images = index_ref.shape[0]
    frames = 2 * images
    channels = tiles * LANES
    factor = channels ** (-0.5)
    every = range(images)
    mix(x_ref, branch_ref, small_ref, mixed)
    take, put = movers(tiles, frames)
    west = estimator(place_ref, small_ref, west_in)
    window = window_ref[0]
    reach = window_ref[1]
    cells = lax.broadcasted_iota(jnp.int32, (PIX, LANES), 1)
    warp_in[...] = jnp.zeros_like(warp_in)
    for image in every:
        warp = jnp.zeros((PIX, LANES), f32)
        for corner in range(4):
            place = index_ref[image, :, pl.ds(corner, 1)]
            amount = weight_ref[image, :, pl.ds(corner, 1)]
            warp = warp + jnp.where(cells == place, amount, 0.0)
        warp_in[image, pl.ds(0, PIX), :] = warp
    warps = [split(warp_in[image][:, :PADDED]) for image in every]
    inside = [(reach < sizes_ref[image].astype(f32)).astype(f32)[:, :1] for image in every]
    first = [take(mixed, image) * inside[image] for image in every]
    second = [take(mixed, images + image) * inside[image] for image in every]
    first_low = [value.astype(bf16) for value in first]
    second_low = [value.astype(bf16) for value in second]
    empty = jnp.zeros((LANES - PADDED, channels), bf16)
    warped = [
        jnp.concatenate([(dot(high, value) + dot(low, value)).astype(bf16), empty], axis=0)
        for (high, low), value in zip(warps, second_low)
    ]
    scores = [nt(left, right) for left, right in zip(first_low, warped)]
    costs = [skew(value, False) * window * factor for value in scores]
    pairs = [gelu_pair(value) for value in costs]
    for image, (value, _) in enumerate(pairs):
        gated_ref[image] = value.astype(bf16)
    d_firsts = [take(up_ref, image) * inside[image] for image in every]
    d_heads = [value.astype(bf16) for value in d_firsts]
    d_costs = [slope * nt(d_head, west) * window * factor for (_, slope), d_head in zip(pairs, d_heads)]
    d_scores = [skew(value, True).astype(bf16) for value in d_costs]
    for image in every:
        put(back, image, d_firsts[image] + dot(d_scores[image], warped[image]))
    d_warped = [tn(value, low)[:PADDED].astype(bf16) for value, low in zip(d_scores, first_low)]
    for image in every:
        high, low = warps[image]
        d_second = take(up_ref, images + image) + tn(high, d_warped[image]) + tn(low, d_warped[image])
        put(back, images + image, d_second * inside[image])
    save = pltpu.make_async_copy(back.at[:, pl.ds(0, rows)], dmixed_ref, sem)
    save.start()
    for tile in range(tiles):
        cols = lane_tile(tile)
        d_mixed = back[tile, pl.ds(0, rows), :]
        gscale_ref[:, cols] = jnp.sum(d_mixed * branch_ref[tile], axis=0, keepdims=True)
        d_branch = (d_mixed * small_ref[pl.ds(SCALE, 1), cols]).astype(bf16)
        dbranch_ref[:, cols] = d_branch
        gbout_ref[:, cols] = jnp.sum(d_branch.astype(f32), axis=0, keepdims=True)
    save.wait()


def finish_kernel(
    sizes_ref, x_ref, branch_ref, up_ref, gated_ref, place_ref, small_ref, window_ref,
    out_ref, gwest_ref, mixed, west_in,
):
    tiles, _, _ = x_ref.shape
    images = gated_ref.shape[0]
    frames = 2 * images
    take, put = movers(tiles, frames)
    mix(x_ref, branch_ref, small_ref, mixed)
    west = estimator(place_ref, small_ref, west_in)
    reach = window_ref[1]
    for image in range(images):
        inside = (reach < sizes_ref[image].astype(f32)).astype(f32)[:, :1]
        gated = gated_ref[image]
        part = tn(gated, (take(up_ref, image) * inside).astype(bf16))
        gwest_ref[...] = part if image == 0 else gwest_ref[...] + part
        put(mixed, image, (take(mixed, image) * inside + dot(gated, west)) * inside)
        put(mixed, images + image, take(mixed, images + image) * inside)
    for image in range(images):
        for which in range(2):
            for row in range(CANVAS):
                lines = pl.ds(row * CANVAS * frames + which * images + image, CANVAS, stride=frames)
                for tile in range(tiles):
                    out_ref[image, which, row, :, lane_tile(tile)] = mixed[tile, lines, :].astype(bf16)


def finish(sizes, x, branch, up, gated, place, small, after=()):
    tiles, rows, _ = x.shape
    images, channels = gated.shape[0], tiles * LANES
    return call(
        finish_kernel,
        "finish",
        (array((images, 2, CANVAS, CANVAS, channels), bf16), array((LANES, channels))),
        0.1,
        [pltpu.VMEM((tiles, PADDED * 2 * images, LANES), f32), pltpu.VMEM((LANES, channels), f32)],
        limit=10,
        smem=1,
        after=after,
    )(sizes, x, branch, up, gated, place, small, jnp.asarray(tables()))


def tables():
    cells = np.arange(PADDED)[:, None]
    lane = np.arange(LANES)[None, :]
    reach = WINDOW // 2
    row = cells // CANVAS + lane // CANVAS - reach
    col = cells % CANVAS + lane % CANVAS - reach
    good = (lane % CANVAS < WINDOW) & (lane // CANVAS < WINDOW) & (cells < PIX)
    good &= (row >= 0) & (row < CANVAS) & (col >= 0) & (col < CANVAS)
    far = np.maximum(cells // CANVAS, cells % CANVAS) + 0 * lane
    return np.stack([good, far]).astype(np.float32)


def flow(sizes, x, branch, up, index, weight, place, small, after=()):
    tiles, rows, _ = x.shape
    images, channels = index.shape[0], tiles * LANES
    padded = pltpu.VMEM((tiles, PADDED * 2 * images, LANES), f32)
    vector = array((1, channels))
    return call(
        flow_kernel,
        "flow",
        (
            array((images, PADDED, LANES), bf16),
            pltpu.HBM(x.shape, f32),
            array((rows, channels), bf16),
            vector,
            vector,
        ),
        6.5,
        [padded, padded, pltpu.VMEM((LANES, channels), f32), pltpu.VMEM((images, PADDED, LANES), f32), pltpu.SemaphoreType.DMA],
        limit=14,
        smem=1,
        after=after,
    )(sizes, x, branch, up, index, weight, place, small, jnp.asarray(tables()))


def grad_narrow_kernel(where_ref, active_ref, dbranch_ref, out_ref):
    count, tile, _ = out_ref.shape
    for part in range(count):
        block = 2 * jnp.bitwise_xor(part, where_ref[2]) + 1 - where_ref[1] if count < 8 else part
        cols = pl.ds(pl.multiple_of(block * tile, LANES), tile)
        out_ref[part] = tn(active_ref[:, cols], dbranch_ref[...]).astype(bf16)


def grad_narrow(where, active, dbranch, count, after=()):
    units, channels = active.shape[1], dbranch.shape[1]
    shape = array((count, units // 8, channels), bf16)
    return call(grad_narrow_kernel, "grad_narrow", shape, 0.3 * count, limit=2 * count, smem=1, after=after)(where, active, dbranch)


def send_halves(where_ref, blocks, keep_ref, left_ref, right_ref):
    x, y = lax.rem(where_ref[2], 2), where_ref[2] // 2
    for turn in range(2):
        keep_ref[0, turn] = blocks[2 * x + turn]
        keep_ref[1, turn] = blocks[4 + 2 * y + turn]
        left_ref[turn] = blocks[2 * (1 - x) + turn]
        right_ref[turn] = blocks[4 + 2 * (1 - y) + turn]


def halves_of(lines, width):
    half = array((2, lines, width), bf16)
    return (array((2, 2, lines, width), bf16), half, half), [pltpu.VMEM((8, lines, width), bf16)]


def grad_narrow_here_kernel(where_ref, active_ref, dbranch_ref, received_ref, keep_ref, left_ref, right_ref, blocks):
    count, tile, _ = received_ref.shape
    lines = tile // 8
    for part in range(count):
        block = 2 * jnp.bitwise_xor(part, where_ref[2]) + where_ref[1]
        cols = pl.ds(pl.multiple_of(block * tile, LANES), tile)
        total = tn(active_ref[:, cols], dbranch_ref[...]) + received_ref[part].astype(f32)
        for block in range(8):
            blocks[block, pl.ds(part * lines, lines), :] = total[block * lines : (block + 1) * lines].astype(bf16)
    send_halves(where_ref, blocks, keep_ref, left_ref, right_ref)


def grad_narrow_here(where, active, dbranch, received, after=()):
    count, tile, channels = received.shape
    shapes, scratch = halves_of(count * tile // 8, channels)
    return call(grad_narrow_here_kernel, "grad_narrow_here", shapes, 1, scratch, limit=6, smem=1, after=after)(
        where, active, dbranch, received
    )


def hidden_back_kernel(where_ref, dbranch_ref, weight_ref, slope_ref, dhidden_ref, gbin_ref):
    tile = slope_ref.shape[1] // 4
    for part in range(4):
        cols = pl.ds(part * tile, tile)
        d_active = nt(dbranch_ref[...], weight_ref[cols, :])
        d_hidden = (d_active * slope_ref[:, cols].astype(f32)).astype(bf16)
        dhidden_ref[:, cols] = d_hidden
        start = jnp.bitwise_xor(part, where_ref[2]) * tile
        gbin_ref[:, pl.ds(pl.multiple_of(start, LANES), tile)] = jnp.sum(d_hidden.astype(f32), axis=0, keepdims=True)


def hidden_back(where, dbranch, weight, slope, after=()):
    rows, units = slope.shape
    shapes = (array((rows, units), bf16), array((1, units)))
    return call(hidden_back_kernel, "hidden_back", shapes, 2, smem=1, after=after)(
        where, dbranch, weight, slope
    )


def grad_widen_full_kernel(normed_ref, dhidden_ref, out_ref):
    tile = 768
    for part in range(out_ref.shape[1] // tile):
        cols = pl.ds(part * tile, tile)
        out_ref[:, cols] = tn(normed_ref[...], dhidden_ref[:, cols]).astype(bf16)


def grad_widen_full(normed, dhidden):
    shape = array((normed.shape[1], dhidden.shape[1]), bf16)
    return call(grad_widen_full_kernel, "grad_widen_full", shape, 5, limit=24)(normed, dhidden)


def grad_widen_away_kernel(where_ref, pair_ref, dhidden_ref, out_ref):
    blocks, lines, width = out_ref.shape
    for part in range(blocks // 2):
        total = tn(pair_ref[:, pl.ds(0, lines)], dhidden_ref[:, pl.ds(2 * part * width, 2 * width)]).astype(bf16)
        block = 2 * jnp.bitwise_xor(part, where_ref[2])
        out_ref[block] = total[:, :width]
        out_ref[block + 1] = total[:, width:]


def grad_widen_away(where, pair, dhidden, after=()):
    shape = array((8, pair.shape[1] // 2, dhidden.shape[1] // 8), bf16)
    return call(grad_widen_away_kernel, "grad_widen_away", shape, 1, smem=1, after=after)(where, pair, dhidden)


def grad_widen_here_kernel(where_ref, pair_ref, dhidden_ref, received_ref, keep_ref, left_ref, right_ref, blocks):
    _, lines, width = blocks.shape
    for part in range(4):
        both = tn(pair_ref[:, pl.ds(lines, lines)], dhidden_ref[:, pl.ds(2 * part * width, 2 * width)])
        for turn in range(2):
            block = 2 * jnp.bitwise_xor(part, where_ref[2]) + turn
            value = both[:, turn * width : (turn + 1) * width] + received_ref[block].astype(f32)
            blocks[block] = value.astype(bf16)
    send_halves(where_ref, blocks, keep_ref, left_ref, right_ref)


def grad_widen_here(where, pair, dhidden, received, after=()):
    shapes, scratch = halves_of(*received.shape[1:])
    return call(grad_widen_here_kernel, "grad_widen_here", shapes, 1, scratch, limit=6, smem=1, after=after)(
        where, pair, dhidden, received
    )


def norm_back_kernel(dhidden_ref, weight_ref, xhat_ref, rstd_ref, small_ref, dconv_ref, sums_ref):
    rows, channels = xhat_ref.shape
    size = 160
    gain = small_ref[pl.ds(GAIN, 1), :]
    sums = [jnp.zeros((1, channels), f32)] * 3
    for part in range(rows // size):
        lines = pl.ds(part * size, size)
        d_normed = nt(dhidden_ref[lines, :], weight_ref[...])
        xhat = xhat_ref[lines, :].astype(f32)
        product = d_normed * xhat
        d_xhat = d_normed * gain
        mean = jnp.sum(d_xhat, axis=-1, keepdims=True) * (1.0 / channels)
        along = jnp.sum(product * gain, axis=-1, keepdims=True) * (1.0 / channels)
        d_conv = (d_xhat - mean - xhat * along) * rstd_ref[lines, :]
        for tile in range(dconv_ref.shape[0]):
            dconv_ref[tile, lines, :] = d_conv[:, tile * LANES : (tile + 1) * LANES]
        for number, value in enumerate((d_conv, product, d_normed)):
            sums[number] = sums[number] + jnp.sum(value, axis=0, keepdims=True)
    sums_ref[...] = jnp.concatenate(sums, axis=0)


def norm_back(dhidden, weight, xhat, rstd, small, after=()):
    rows, channels = xhat.shape
    return call(
        norm_back_kernel, "norm_back", (array((channels // LANES, rows, LANES)), array((3, channels))), 1, after=after
    )(dhidden, weight, xhat, rstd, small)


def grad_taps_kernel(x_ref, dconv_ref, out_ref):
    @pl.loop(0, x_ref.shape[0])
    def _(tile):
        cols = pl.ds(pl.multiple_of(tile * LANES, LANES), LANES)
        for ky in range(KERNEL):
            totals = [None] * KERNEL
            for row in range(CANVAS):
                source_row = row + ky - REACH
                if not 0 <= source_row < CANVAS:
                    continue
                cells = [x_ref[tile, pl.ds((source_row * CANVAS + col) * 8, 8), :] for col in range(CANVAS)]
                grads = [dconv_ref[tile, pl.ds((row * CANVAS + col) * 8, 8), :] for col in range(CANVAS)]
                for kx in range(KERNEL):
                    for col in range(CANVAS):
                        source = col + kx - REACH
                        if 0 <= source < CANVAS:
                            term = cells[source] * grads[col]
                            totals[kx] = term if totals[kx] is None else totals[kx] + term
            for kx in range(KERNEL):
                out_ref[pl.ds(ky * KERNEL + kx, 1), cols] = jnp.sum(totals[kx], axis=0, keepdims=True)


def grad_taps(x, dconv, after=()):
    return call(grad_taps_kernel, "grad_taps", array((TAPS, x.shape[0] * LANES)), 0.2, after=after)(x, dconv)


def conv_back_kernel(sizes_ref, dconv_ref, small_ref, dmixed_ref, out_ref, total):
    tiles = dconv_ref.shape[0]
    images = out_ref.shape[0]
    frames = 2 * images
    side = side_of(sizes_ref, images)

    @pl.loop(0, tiles)
    def _(tile):
        def finish(cell, value):
            lines = pl.ds(cell * 8, 8)
            inside = side > max(cell // CANVAS, cell % CANVAS)
            total[tile, lines, :] = jnp.where(inside, value + dmixed_ref[tile, lines, :], 0.0)

        conv_rows(dconv_ref, tile, small_ref, True, finish)

    for image in range(images):
        for which in range(2):
            for row in range(CANVAS):
                lines = pl.ds(row * CANVAS * frames + which * images + image, CANVAS, stride=frames)
                for tile in range(tiles):
                    out_ref[image, which, row, :, lane_tile(tile)] = total[tile, lines, :]


def conv_back(sizes, dconv, small, dmixed, after=()):
    tiles, rows, _ = dconv.shape
    images = sizes.shape[0]
    return call(
        conv_back_kernel,
        "conv_back",
        array((images, 2, CANVAS, CANVAS, tiles * LANES)),
        0.2,
        [pltpu.VMEM(dconv.shape, f32)],
        limit=6,
        smem=1,
        after=after,
    )(sizes, dconv, small, dmixed)


def start_all(copies, sems):
    running = [pltpu.make_async_copy(source, target, sems.at[number]) for number, (source, target) in enumerate(copies)]
    for copy in running:
        copy.start()
    return running

GROUPS = 6
LINES = 24
LEAD = 32
BIAS = SMALL


def pack_kernel(where_ref, weight_ref, taps_ref, west_ref, *refs):
    vectors, (bias_ref, out_ref, small_ref, small, taps, west, *held, bias, sems) = refs[:5], refs[5:]
    share = weight_ref.shape[0]
    wide = out_ref.shape[1]
    cols = pl.ds(pl.multiple_of(where_ref[2] * wide, LANES), wide)
    copies = [(taps_ref, taps), (west_ref, west), (bias_ref, bias)]
    copies += list(zip(vectors, held))
    lead = small_ref.shape[0] - LINES
    copies += [(weight_ref.at[pl.ds(0, lead), cols], small_ref.at[pl.ds(0, lead)])]
    copies += [(weight_ref.at[pl.ds(lead, share - lead), cols], out_ref)]
    running = start_all(copies, sems)
    small[...] = jnp.zeros_like(small)
    lane = pl.ds(0, share)
    for copy in running[:-2]:
        copy.wait()
    small[pl.ds(0, TAPS), lane] = taps[...].astype(f32)
    small[pl.ds(WEST, OFFSETS), lane] = west[...].astype(f32)
    for number, vector in enumerate(held):
        small[pl.ds(CBIAS + number, 1), lane] = vector[...].astype(f32).reshape(1, share)
    for part in range(bias.shape[0] // LANES):
        small[pl.ds(BIAS + part, 1), :] = bias[lane_tile(part)].astype(f32).reshape(1, LANES)
    for group in range(GROUPS):
        small_ref[pl.ds(lead, LINES), lane_tile(group)] = small[pl.ds(group * LINES, LINES), :].astype(bf16)
    for copy in running[-2:]:
        copy.wait()


def pack(where, weight, taps, west, vectors, bias, after=()):
    share, units = weight.shape
    args = (weight, taps, west, *vectors, bias)
    return call(
        pack_kernel,
        "pack",
        (array((share - LEAD, units // 4), bf16), array((LEAD + LINES, GROUPS * LANES), bf16)),
        2,
        [
            pltpu.VMEM((GROUPS * LINES, LANES), f32),
            pltpu.VMEM(taps.shape, bf16),
            pltpu.VMEM(west.shape, bf16),
            *[pltpu.VMEM((share,), bf16)] * len(vectors),
            pltpu.VMEM(bias.shape, bf16),
            pltpu.SemaphoreType.DMA((len(args) + 1,)),
        ],
        smem=1,
        left=len(args),
        after=after,
    )(where, *args)


def stack_kernel(*refs):
    lead = refs[0].shape[0] - LINES
    for number, ref in enumerate(refs[:-1]):
        refs[-1][number] = ref[pl.ds(lead, LINES), :]


def stack(parts, after=()):
    shape = array((len(parts), LINES, parts[0].shape[1]), bf16)
    return call(stack_kernel, "stack", shape, 1, after=after)(*parts)


def unpack_kernel(where_ref, mine_ref, theirs_ref, small_ref, bias_ref):
    z, core, slabs = where_ref[0], where_ref[1], where_ref[3]
    channels = small_ref.shape[1]
    share = channels // 8
    everything = None
    for number in range(8):
        ref = mine_ref if number < 4 else theirs_ref
        shard = 2 * lax.rem(z - number % 4 + slabs, slabs) + (core if number < 4 else 1 - core)
        rows = jnp.concatenate([ref[number % 4, :, lane_tile(group)].astype(f32) for group in range(GROUPS)], axis=0)
        source = lax.broadcasted_iota(jnp.int32, (LANES, channels), 0)
        target = lax.broadcasted_iota(jnp.int32, (LANES, channels), 1)
        spread = ((target - shard * share == source) & (source < share)).astype(bf16)
        value = dot(rows.astype(bf16), spread)
        everything = value if everything is None else everything + value
        width = bias_ref.shape[1] // 8
        for part in range(width // LANES):
            cols = pl.ds(pl.multiple_of(shard * width + part * LANES, LANES), LANES)
            bias_ref[:, cols] = rows[BIAS + part : BIAS + part + 1, :]
    small_ref[...] = everything[: small_ref.shape[0]]


def unpack(where, mine, theirs, units, channels):
    return call(unpack_kernel, "unpack", (array((SMALL, channels)), array((1, units))), 1.2, smem=1)(where, mine, theirs)


def column_kernel(*refs):
    parts, outs = refs[:-2], refs[-2:]
    count, rows, width = outs[0].shape
    leads = parts[: len(parts) - count]
    lead = rows - parts[-1].shape[0]
    for turn, out in enumerate(outs):
        for number in range(count):
            cols = pl.ds(turn * width, width)
            if leads:
                out[number, pl.ds(0, lead), :] = leads[number][pl.ds(0, lead), cols]
            out[number, pl.ds(lead, rows - lead), :] = parts[len(leads) + number][:, cols]


def column(parts, leads=(), after=()):
    rows, channels = parts[0].shape
    rows += LEAD if leads else 0
    half = array((len(parts), rows, channels // 2), bf16)
    return call(column_kernel, "column", (half, half), 1, after=after)(*leads, *parts)


def cut_kernel(where_ref, weight_ref, out_ref, sem):
    tall = out_ref.shape[0]
    lines = pl.ds(pl.multiple_of(where_ref[2] * tall, 16), tall)
    copy = pltpu.make_async_copy(weight_ref.at[lines], out_ref, sem)
    copy.start()
    copy.wait()


def cut(where, weight, after=()):
    tall, channels = weight.shape
    shape = array((tall // 4, channels), bf16)
    return call(cut_kernel, "cut", shape, 1, [pltpu.SemaphoreType.DMA], smem=1, left=1, after=after)(where, weight)


def onward_kernel(left_ref, right_ref, left_in_ref, right_in_ref, to_x_ref, to_y_ref):
    to_y_ref[0] = left_ref[...]
    to_y_ref[1] = left_in_ref[...]
    to_x_ref[0] = right_ref[...]
    to_x_ref[1] = right_in_ref[...]


def onward(left, right, left_in, right_in, after=()):
    shape = array((2, *left.shape), bf16)
    return call(onward_kernel, "onward", (shape, shape), 1, after=after)(left, right, left_in, right_in)


def halve_kernel(where_ref, keep_ref, left_in_ref, right_in_ref, keep_out_ref, left_ref, right_ref):
    x, y = lax.rem(where_ref[2], 2), where_ref[2] // 2

    def total(side, which):
        received = left_in_ref if side == 0 else right_in_ref
        return keep_ref[side, which].astype(f32) + received[which].astype(f32)

    keep_out_ref[0] = total(0, y).astype(bf16)
    keep_out_ref[1] = total(1, x).astype(bf16)
    left_ref[...] = total(0, 1 - y).astype(bf16)
    right_ref[...] = total(1, 1 - x).astype(bf16)


def halve(where, keep, left_in, right_in, after=()):
    _, _, lines, width = keep.shape
    half = array((lines, width), bf16)
    shapes = (array((2, lines, width), bf16), half, half)
    return call(halve_kernel, "halve", shapes, 1, smem=1, after=after)(where, keep, left_in, right_in)


def deal_total(where_ref, keep_ref, left_in_ref, right_in_ref, total):
    total[0] = (keep_ref[0].astype(f32) + left_in_ref[...].astype(f32)).astype(bf16)
    total[1] = (keep_ref[1].astype(f32) + right_in_ref[...].astype(f32)).astype(bf16)


def deal_kernel(where_ref, keep_ref, left_in_ref, right_in_ref, *refs):
    outs, total = refs[:-1], refs[-1]
    share = outs[0].shape[1]
    deal_total(where_ref, keep_ref, left_in_ref, right_in_ref, total)
    for step, out in enumerate(outs):
        slab = lax.rem(where_ref[0] + step, len(outs))
        for side in range(2):
            out[side] = total[side, pl.ds(pl.multiple_of(slab * share, 16), share), :]


def deal(where, keep, left_in, right_in, slabs, after=()):
    _, lines, width = keep.shape
    shapes = (array((2, lines // slabs, width), bf16),) * slabs
    scratch = [pltpu.VMEM(keep.shape, bf16)]
    return call(deal_kernel, "deal", shapes, 1, scratch, smem=1, after=after)(where, keep, left_in, right_in)


SMALL_ROWS = 192


def deal_small_kernel(where_ref, keep_ref, left_in_ref, right_in_ref, here_ref, received_ref, *refs):
    outs, total = refs[:-1], refs[-1]
    deal_total(where_ref, keep_ref, left_in_ref, right_in_ref, total)
    share = total.shape[1] // len(outs)
    extra = outs[0].shape[1] - share
    for step, out in enumerate(outs):
        slab = lax.rem(where_ref[0] + step, len(outs))
        small = here_ref[slab] + received_ref[slab]
        lines = SMALL_ROWS // 4
        small = jnp.concatenate([small[part * lines : (part + 1) * lines] for part in range(4)], axis=1)
        for side in range(2):
            out[side, pl.ds(0, share), :] = total[side, pl.ds(pl.multiple_of(slab * share, 16), share), :]
            out[side, pl.ds(share, extra), :] = small[side * extra : (side + 1) * extra].astype(bf16)


def deal_small(where, keep, left_in, right_in, here, received, after=()):
    slabs = here.shape[0]
    _, lines, width = keep.shape
    extra = SMALL_ROWS * here.shape[2] // width // 2
    shapes = (array((2, lines // slabs + extra, width), bf16),) * slabs
    scratch = [pltpu.VMEM(keep.shape, bf16)]
    return call(deal_small_kernel, "deal_small", shapes, 1, scratch, smem=1, after=after)(
        where, keep, left_in, right_in, here, received
    )


def total_kernel(*refs):
    total = refs[0][...].astype(f32)
    for ref in refs[1:-1]:
        total = total + ref[...].astype(f32)
    refs[-1][...] = total.astype(refs[-1].dtype)


def total(values, after=()):
    return call(total_kernel, "total", array(values[0].shape, values[0].dtype), 1, after=after)(*values)


def blocks_of(where_ref, flip):
    group = jnp.bitwise_xor(where_ref[2], flip)
    x, y = lax.rem(group, 2), group // 2
    return 2 * x + y, 4 + 2 * y + x


def spread_wout_kernel(where_ref, *refs):
    *values, out_ref = refs
    lines = values[0].shape[1]
    for flip, ref in enumerate(values):
        for side, block in enumerate(blocks_of(where_ref, flip)):
            out_ref[pl.ds(pl.multiple_of(block * lines, 16), lines), :] = ref[side].astype(f32)


def spread_wout(where, values, after=()):
    _, lines, channels = values[0].shape
    return call(spread_wout_kernel, "spread_wout", array((8 * lines, channels)), 1, smem=1, after=after)(where, *values)


def spread_win_kernel(where_ref, lane_ref, *refs):
    values, (out_ref, taps_ref, west_ref, bias_ref, *vectors, small) = refs[:4], refs[4:]
    share = out_ref.shape[0]
    _, lines, width = values[0].shape
    extra = lines - share
    for flip, ref in enumerate(values):
        for side, block in enumerate(blocks_of(where_ref, flip)):
            out_ref[:, pl.ds(pl.multiple_of(block * width, LANES), width)] = ref[side, pl.ds(0, share), :].astype(f32)
    for side in range(2):
        part = [ref[side, pl.ds(share, extra), :].astype(f32) for ref in values]
        both = (part[0] + part[1]) + (part[2] + part[3])
        for group in range(4):
            span = pl.ds(group * 2 * extra + side * extra, extra)
            small[span, :] = both[:, group * share : (group + 1) * share]
    taps_ref[...] = small[pl.ds(0, TAPS), :]
    for number, ref in enumerate(vectors):
        ref[...] = small[pl.ds(TAPS + number, 1), :]
    for offset in range(OFFSETS):
        west_ref[pl.ds(offset, 1), :] = small[pl.ds(TAPS + 5 + lane_ref[offset], 1), :]
    rows = bias_ref.shape[1] // share
    first = TAPS + 5 + LANES
    bias_ref[...] = jnp.concatenate([small[pl.ds(first + row, 1), :] for row in range(rows)], axis=1)


def spread_win(where, lane_of, values, share, after=()):
    width = values[0].shape[2]
    shapes = [array((share, 8 * width)), array((TAPS, share)), array((OFFSETS, share)), array((1, width))]
    shapes += [array((1, share))] * 5
    scratch = [pltpu.VMEM((SMALL_ROWS, share), f32)]
    return call(spread_win_kernel, "spread_win", shapes, 1, scratch, smem=2, after=after)(where, lane_of, *values)


def pack_small_kernel(where_ref, gtaps_ref, gnorm_ref, gbout_ref, gscale_ref, gwest_ref, gbin_ref, here_ref, away_ref):
    slabs, _, share = here_ref.shape

    def fill(even_ref, odd_ref):
        for shard in range(2 * slabs):
            out = odd_ref if shard % 2 else even_ref
            cols = pl.ds(shard * share, share)
            line = 0
            for ref in (gtaps_ref, gnorm_ref, gbout_ref, gscale_ref, gwest_ref):
                out[shard // 2, pl.ds(line, ref.shape[0]), :] = ref[:, cols]
                line += ref.shape[0]
            lines = gbin_ref.shape[1] // gtaps_ref.shape[1]
            for extra in range(lines):
                span = pl.ds((shard * lines + extra) * share, share)
                out[shard // 2, pl.ds(line + extra, 1), :] = gbin_ref[:, span]
            rest = SMALL_ROWS - line - lines
            out[shard // 2, pl.ds(line + lines, rest), :] = jnp.zeros((rest, share), f32)

    @pl.when(where_ref[1] == 0)
    def _():
        fill(here_ref, away_ref)

    @pl.when(where_ref[1] == 1)
    def _():
        fill(away_ref, here_ref)


def pack_small(where, parts, slabs, share, after=()):
    shape = array((slabs, SMALL_ROWS, share))
    return call(pack_small_kernel, "pack_small", (shape, shape), 0.1, smem=1, after=after)(where, *parts)


AXES = ("dp", "fsdp")


class Routes:
    def __init__(self, groups, members):
        self.groups, self.members, self.slabs = groups, members, members // 2
        self.group = lax.axis_index("dp")
        member = lax.axis_index("fsdp")
        self.slab, self.core = member // 2, member % 2

    def send(self, value, target):
        pairs = [
            (group * self.members + 2 * slab + core, self.index(*target(group, slab, core)))
            for group in range(self.groups)
            for slab in range(self.slabs)
            for core in range(2)
        ]
        return lax.ppermute(value, AXES, pairs)

    def index(self, group, slab, core):
        return group * self.members + 2 * slab + core

    def to_core(self, value):
        return self.send(value, lambda group, slab, core: (group, slab, 1 - core))

    def to_slab(self, value, step):
        return self.send(value, lambda group, slab, core: (group, (slab + step) % self.slabs, core))

    def to_near(self, value, flip):
        return self.send(value, lambda group, slab, core: (group, slab ^ flip, core))

    def to_group(self, value, flip):
        return self.send(value, lambda group, slab, core: (group ^ flip, slab, core))


def shards(
    features,
    cotangent,
    image_sizes,
    warp_index,
    warp_weight,
    offsets,
    conv_kernel,
    conv_bias,
    norm_gain,
    norm_bias,
    w_in,
    bias_in,
    w_out,
    bias_out,
    layer_scale,
    w_estimate,
):
    share, units = w_in.shape
    channels = features.shape[-1]
    members = channels // share
    groups = lax.axis_size("dp")
    paired = groups == 4 and members == 8

    reach = WINDOW // 2
    lane_of = (offsets[:, 0] + reach) * CANVAS + offsets[:, 1] + reach
    place = jnp.pad(lane_of, (0, LANES - OFFSETS), constant_values=-1)[None]

    early = (features, cotangent, warp_index, warp_weight, place, lane_of)
    if paired:
        routes = Routes(groups, members)
        slabs = routes.slabs
        where = jnp.stack([routes.slab, routes.core, routes.group, jnp.int32(slabs)])
        vectors = (conv_bias, norm_gain, norm_bias, bias_out, layer_scale)
        quarter, small = pack(where, w_in, conv_kernel, w_estimate, vectors, bias_in)
        leads = [routes.to_slab(small, step) for step in range(1, slabs)]
        small = stack([small] + leads, after=early)
        win_parts = [routes.to_slab(quarter, step) for step in range(1, slabs)]
        win_own = routes.to_core(w_in)
        quarter = cut(where, w_out, after=(quarter,))
        wout_parts = [routes.to_slab(quarter, step) for step in range(1, slabs)]
        wout_own = routes.to_core(w_out)
        small, bin_all = unpack(where, small, routes.to_core(small), units, channels)
    else:
        where = jnp.zeros((4,), jnp.int32)
        small = jnp.concatenate(
            [
                conv_kernel,
                w_estimate,
                jnp.stack([conv_bias, norm_gain, norm_bias, bias_out, layer_scale]),
                bias_in.reshape(-1, share),
            ]
        )
        small = lax.all_gather(small, "fsdp")
        win_all = lax.all_gather(w_in, "fsdp", axis=0, tiled=True)
        wout_all = lax.all_gather(w_out, "fsdp", axis=0, tiled=True)
        bin_all = small[:, SMALL:].reshape(1, units).astype(f32)
        small = small[:, :SMALL].transpose(1, 0, 2).reshape(SMALL, channels).astype(f32)
    x, up, begun = conv_begin(image_sizes, features, cotangent, small)
    after = ()
    if paired:
        left, right = column(win_parts, leads, after=(begun, wout_parts[0]))
        left_in, right_in = routes.to_group(left, 1), routes.to_group(right, 2)
        to_x, to_y = onward(left, right, left_in, right_in)
        win_halves = [to_x, to_y, routes.to_group(to_x, 1), routes.to_group(to_y, 2)]
        left, right = column(wout_parts, after=(to_x,))
        left_in, right_in = routes.to_group(left, 1), routes.to_group(right, 2)
        after = (left,)
    normed, pair, xhat, rstd = conv_norm(where, x, begun, small, after)
    if paired:
        to_x, to_y = onward(left, right, left_in, right_in, after=(normed,))
        wout_halves = [to_x, to_y, routes.to_group(to_x, 1), routes.to_group(to_y, 2)]
        win_halves = gate(win_halves, (to_x,))
        win_theirs = [win_own] + [routes.to_core(value) for value in win_halves]
        win_all, active, slope = place_widen(where, [w_in, *win_halves], win_theirs, normed, bin_all)
        wout_halves = gate(wout_halves, (active,))
        wout_theirs = [wout_own] + [routes.to_core(value) for value in wout_halves]
        begun = place_narrow(0, where, [w_out, *wout_halves], active, small)
        wout_all, branch = place_narrow(1, where, wout_theirs, active, *begun)
    else:
        active, slope = widen(normed, win_all, bin_all)
        branch = narrow(active, wout_all, small)
    gated, d_mixed, d_branch, g_scale, g_bout = flow(
        image_sizes, x, branch, up, warp_index, warp_weight, place, small
    )
    if paired:
        d_hidden, g_bin = hidden_back(where, d_branch, wout_all, slope)
        win_away = grad_widen_away(where, pair, d_hidden)
        win_in = routes.to_core(win_away)
        wout_away = grad_narrow(where, active, d_branch, slabs, after=(win_away,))
        wout_in = routes.to_core(wout_away)
        keep_in, left, right = grad_widen_here(where, pair, d_hidden, win_in, after=(wout_away,))
        left_in, right_in = routes.to_group(left, 1), routes.to_group(right, 2)
        d_conv, g_norm = norm_back(d_hidden, win_all, xhat, rstd, small, after=(keep_in,))
        keep_out, left, right = grad_narrow_here(where, active, d_branch, wout_in, after=(d_conv,))
        left_out, right_out = routes.to_group(left, 1), routes.to_group(right, 2)
        keep_in, left, right = halve(where, keep_in, left_in, right_in, after=(keep_out,))
        left_in, right_in = routes.to_group(left, 2), routes.to_group(right, 1)
        g_taps = grad_taps(x, d_conv, after=(keep_in,))
        mixed_out, g_west = finish(image_sizes, x, branch, up, gated, place, small, after=(g_taps,))
        parts = (g_taps, g_norm, g_bout, g_scale, g_west, g_bin)
        small_here, small_away = pack_small(where, parts, slabs, share)
        small_in = routes.to_core(small_away)
        win_parts = deal_small(where, keep_in, left_in, right_in, small_here, small_in)
        win_parts = win_parts[:1] + tuple(routes.to_slab(v, n + 1) for n, v in enumerate(win_parts[1:]))
        keep_out, left, right = halve(where, keep_out, left_out, right_out, after=win_parts[:1])
        left_out, right_out = routes.to_group(left, 2), routes.to_group(right, 1)
        grad_features = conv_back(image_sizes, d_conv, small, d_mixed, after=(keep_out,))
        wout_parts = deal(where, keep_out, left_out, right_out, slabs, after=(grad_features,))
        wout_parts = wout_parts[:1] + tuple(routes.to_slab(v, n + 1) for n, v in enumerate(wout_parts[1:]))
        g_win = total(win_parts, after=wout_parts[:1])
        win_parts = [g_win] + [routes.to_group(g_win, flip) for flip in range(1, 4)]
        g_wout = total(wout_parts, after=(g_win,))
        wout_parts = [g_wout] + [routes.to_group(g_wout, flip) for flip in range(1, 4)]
        g_win, g_taps, g_west, g_bin, *g_small = spread_win(where, lane_of, win_parts, share, after=(g_wout,))
        g_wout = spread_wout(where, wout_parts)
        g_small = [value.reshape(share) for value in g_small]
    else:
        g_wout = grad_narrow(where, active, d_branch, 8).reshape(units, channels)
        d_hidden, g_bin = hidden_back(where, d_branch, wout_all, slope)
        g_win = grad_widen_full(normed, d_hidden)
        d_conv, g_norm = norm_back(d_hidden, win_all, xhat, rstd, small)
        g_taps = grad_taps(x, d_conv)
        mixed_out, g_west = finish(image_sizes, x, branch, up, gated, place, small)
        grad_features = conv_back(image_sizes, d_conv, small, d_mixed)
        g_small = jnp.concatenate([g_taps, g_norm, g_bout, g_scale, g_west])
        g_small = g_small.reshape(-1, members, share).transpose(1, 0, 2)
        g_small = jnp.concatenate([g_small, g_bin.reshape(members, -1, share)], axis=1)

        def reduce(value):
            return lax.psum(lax.psum_scatter(value, "fsdp", scatter_dimension=0, tiled=True).astype(f32), "dp")

        g_wout, g_win, g_small = reduce(g_wout), reduce(g_win), reduce(g_small)[0]
        tail = TAPS + 5 + LANES
        g_taps, g_west, g_bin = g_small[:TAPS], jnp.take(g_small[TAPS + 5 : tail], lane_of, axis=0), g_small[tail:]
        g_small = g_small[TAPS : TAPS + 5]
    return (
        mixed_out,
        grad_features,
        g_taps,
        g_small[0],
        g_small[1],
        g_small[2],
        g_win,
        g_bin.reshape(-1),
        g_wout,
        g_small[3],
        g_small[4],
        g_west,
    )


def solution(mesh):
    in_specs = (
        P(("dp", "fsdp"), None, None, None, None),
        P(("dp", "fsdp"), None, None, None, None),
        P(("dp", "fsdp")),
        P(("dp", "fsdp"), None, None),
        P(("dp", "fsdp"), None, None),
        P(),
        P(None, "fsdp"),
        P("fsdp"),
        P("fsdp"),
        P("fsdp"),
        P("fsdp", None),
        P("fsdp"),
        P("fsdp", None),
        P("fsdp"),
        P("fsdp"),
        P(None, "fsdp"),
    )
    out_specs = (
        P(("dp", "fsdp"), None, None, None, None),
        P(("dp", "fsdp"), None, None, None, None),
        P(None, "fsdp"),
        P("fsdp"),
        P("fsdp"),
        P("fsdp"),
        P("fsdp", None),
        P("fsdp"),
        P("fsdp", None),
        P("fsdp"),
        P("fsdp"),
        P(None, "fsdp"),
    )
    return jax.shard_map(shards, mesh=mesh, in_specs=in_specs, out_specs=out_specs, check_vma=False)
```

```python
import functools

import jax
import jax.numpy as jnp
import numpy as np
from jax import lax
from jax.experimental import pallas as pl
from jax.experimental.pallas import tpu as pltpu
from jax.sharding import PartitionSpec as P

CANVAS = 10
KERNEL = 7
REACH = KERNEL // 2
TAPS = KERNEL * KERNEL
WINDOW = 9
OFFSETS = WINDOW * WINDOW
PIX = CANVAS * CANVAS
PADDED = 104
LANES = 128
EPSILON = 1e-06
f32 = jnp.float32
bf16 = jnp.bfloat16
WEST = TAPS
CBIAS, GAIN, SHIFT, BOUT, SCALE = range(TAPS + OFFSETS, TAPS + OFFSETS + 5)
SMALL = TAPS + OFFSETS + 5


def call(kernel, name, out_shape, micros, scratch=(), limit=4, smem=0, left=0, after=(), aliases=None):
    def body(*refs):
        kernel(*refs[len(after) :])

    def run(*args):
        specs = [pl.BlockSpec(memory_space=pl.ANY)] * len(after)
        specs += [pl.BlockSpec(memory_space=pltpu.SMEM)] * smem
        specs += [pl.BlockSpec(memory_space=pl.ANY)] * left
        specs += [pl.BlockSpec(memory_space=pltpu.VMEM)] * (len(args) - smem - left)
        return pl.pallas_call(
            body,
            name=name,
            in_specs=specs,
            out_specs=jax.tree.map(out_space, out_shape),
            out_shape=out_shape,
            input_output_aliases={len(after) + source: target for source, target in (aliases or {}).items()},
            scratch_shapes=list(scratch),
            compiler_params=pltpu.CompilerParams(vmem_limit_bytes=limit * 1024 * 1024),
            cost_estimate=pl.CostEstimate(flops=int(micros * 1.15e9), bytes_accessed=0, transcendentals=0),
        )(*after, *args[:smem], *[in_hbm(value) for value in args[smem : smem + left]], *args[smem + left :])

    return run


def out_space(shape):
    return pl.BlockSpec(memory_space=pltpu.VMEM if isinstance(shape, jax.ShapeDtypeStruct) else pltpu.HBM)


def in_hbm(value):
    return pltpu.with_memory_space_constraint(value, pltpu.HBM)


def gate(values, after):
    space = pl.BlockSpec(memory_space=pl.ANY)
    return pl.pallas_call(
        lambda *refs: None,
        name="gate",
        in_specs=[space] * (len(values) + len(after)),
        out_specs=[space] * len(values),
        out_shape=[array(value.shape, value.dtype) for value in values],
        input_output_aliases={number: number for number in range(len(values))},
        compiler_params=pltpu.CompilerParams(vmem_limit_bytes=1024 * 1024),
        cost_estimate=pl.CostEstimate(flops=0, bytes_accessed=0, transcendentals=0),
    )(*values, *after)


def array(shape, dtype=f32):
    return jax.ShapeDtypeStruct(shape, dtype)


def nt(left, right):
    return lax.dot_general(left, right, (((1,), (1,)), ((), ())), preferred_element_type=f32)


def tn(left, right):
    return lax.dot_general(left, right, (((0,), (0,)), ((), ())), preferred_element_type=f32)


def dot(left, right):
    return jnp.dot(left, right, preferred_element_type=f32)


def split(values):
    high = values.astype(bf16)
    return high, (values - high.astype(f32)).astype(bf16)


def lane_tile(tile):
    return pl.ds(tile * LANES, LANES)


def conv_rows(source, tile, kernel_ref, flip, finish):
    cols = pl.ds(pl.multiple_of(tile * LANES, LANES), LANES)
    for row in range(CANVAS):
        sums = [None] * CANVAS
        for ky in range(KERNEL):
            source_row = row + ky - REACH
            if not 0 <= source_row < CANVAS:
                continue
            cells = [source[tile, pl.ds((source_row * CANVAS + col) * 8, 8), :] for col in range(CANVAS)]
            for kx in range(KERNEL):
                tap = ky * KERNEL + kx
                tap = TAPS - 1 - tap if flip else tap
                weight = jnp.broadcast_to(kernel_ref[pl.ds(tap, 1), cols], (8, LANES))
                for col in range(CANVAS):
                    other = col + kx - REACH
                    if 0 <= other < CANVAS:
                        term = cells[other] * weight
                        sums[col] = term if sums[col] is None else sums[col] + term
        for col in range(CANVAS):
            finish(row * CANVAS + col, sums[col])


def side_of(sizes_ref, images):
    lines = lax.broadcasted_iota(jnp.int32, (2 * images, LANES), 0)
    side = jnp.zeros(lines.shape, jnp.int32)
    for image in range(images):
        side = jnp.where((lines == image) | (lines == images + image), sizes_ref[image], side)
    return side


def conv_tile(x_ref, tile, small_ref, conv_ref, target):
    cols = pl.ds(pl.multiple_of(tile * LANES, LANES), LANES)
    bias = jnp.broadcast_to(small_ref[pl.ds(CBIAS, 1), cols], (8, LANES))

    def finish(cell, total):
        conv_ref[target, pl.ds(cell * 8, 8), :] = total + bias

    conv_rows(x_ref, tile, small_ref, False, finish)


def conv_begin_kernel(
    sizes_ref, features_ref, upstream_ref, small_ref, x_ref, up_ref, conv_ref, features, upstream, sems,
):
    images = features_ref.shape[0]
    frames = 2 * images
    tiles, rows, _ = x_ref.shape
    side = side_of(sizes_ref, images)
    copies = [
        pltpu.make_async_copy(source.at[image], target.at[image], sems.at[number, image])
        for number, (source, target) in enumerate(((features_ref, features), (upstream_ref, upstream)))
        for image in range(images)
    ]
    for copy in copies:
        copy.start()

    def lay(source, image, target):
        for which in range(2):
            for row in range(CANVAS):
                lines = pl.ds(row * CANVAS * frames + which * images + image, CANVAS, stride=frames)
                for tile in range(tiles):
                    target[tile, lines, :] = source[image, which, row, :, lane_tile(tile)].astype(f32)

    for image in range(images):
        copies[image].wait()
        lay(features, image, x_ref)

    @pl.loop(0, tiles)
    def _(tile):
        for cell in range(PIX):
            inside = side > max(cell // CANVAS, cell % CANVAS)
            lines = pl.ds(cell * 8, 8)
            x_ref[tile, lines, :] = jnp.where(inside, x_ref[tile, lines, :], 0.0)

    @pl.loop(0, tiles // 2)
    def _(tile):
        conv_tile(x_ref, tile, small_ref, conv_ref, tile)

    for tile in range(tiles):
        up_ref[tile, pl.ds(rows, PADDED * frames - rows), :] = jnp.zeros((PADDED * frames - rows, LANES), f32)
    for image in range(images):
        copies[images + image].wait()
        lay(upstream, image, up_ref)


def conv_begin(sizes, features, upstream, small, after=()):
    images, channels = features.shape[0], features.shape[-1]
    rows, tiles = PIX * 2 * images, channels // LANES
    shapes = (
        array((tiles, rows, LANES)),
        array((tiles, PADDED * 2 * images, LANES)),
        array((tiles // 2, rows, LANES)),
    )
    scratch = [pltpu.VMEM(features.shape, bf16), pltpu.VMEM(features.shape, bf16), pltpu.SemaphoreType.DMA((2, images))]
    return call(conv_begin_kernel, "conv_begin", shapes, 1, scratch, limit=8, smem=1, left=2, after=after)(
        sizes, features, upstream, small
    )


def conv_norm_kernel(where_ref, x_ref, begun_ref, small_ref, normed_ref, pair_ref, xhat_ref, rstd_ref, conv, order):
    tiles, rows, _ = x_ref.shape
    channels = tiles * LANES

    @pl.loop(0, tiles // 2)
    def _(tile):
        conv_tile(x_ref, tile + tiles // 2, small_ref, conv, tile)

    share = channels // 8
    core = where_ref[1]
    for tile in range(tiles):
        source = lax.broadcasted_iota(jnp.int32, (channels, LANES), 0)
        target = lax.broadcasted_iota(jnp.int32, (1, LANES), 1) + tile * LANES
        shard = target // share
        wanted = jnp.where(shard < 4, 2 * shard + 1 - core, 2 * (shard - 4) + core) * share + target % share
        order[:, lane_tile(tile)] = (source == wanted).astype(bf16)
    size = 160

    @pl.loop(0, rows // size)
    def _(block):
        lines = pl.ds(pl.multiple_of(block * size, size), size)
        values = [begun_ref[tile, lines, :] for tile in range(tiles // 2)]
        values = jnp.concatenate(values + [conv[tile, lines, :] for tile in range(tiles // 2)], axis=1)
        mean = jnp.sum(values, axis=-1, keepdims=True) * (1.0 / channels)
        centred = values - mean
        variance = jnp.sum(centred * centred, axis=-1, keepdims=True) * (1.0 / channels)
        scale = lax.rsqrt(variance + EPSILON)
        xhat = centred * scale
        xhat_ref[lines, :] = xhat.astype(bf16)
        rstd_ref[lines, :] = scale
        normed = (xhat * small_ref[pl.ds(GAIN, 1), :] + small_ref[pl.ds(SHIFT, 1), :]).astype(bf16)
        normed_ref[lines, :] = normed
        pair_ref[lines, :] = dot(normed, order[...]).astype(bf16)


def conv_norm(where, x, begun, small, after=()):
    tiles, rows, _ = x.shape
    channels = tiles * LANES
    low = array((rows, channels), bf16)
    return call(
        conv_norm_kernel,
        "conv_norm",
        (low, low, low, array((rows, 1))),
        1,
        [pltpu.VMEM(begun.shape, f32), pltpu.VMEM((channels, channels), bf16)],
        limit=8,
        smem=1,
        after=after,
    )(where, x, begun, small)


def gelu_pair(hidden):
    cdf = 0.5 * lax.erf(hidden * 0.7071067811865476) + 0.5
    density = jnp.exp(hidden * hidden * -0.5) * 0.3989422804014327
    return hidden * cdf, cdf + hidden * density


def widen_part(group, normed_ref, weight_ref, bias_ref, active_ref, slope_ref, part):
    cols = pl.ds(part * 256, 256)
    quarter = weight_ref.shape[1] // 4
    start = jnp.bitwise_xor(group, part * 256 // quarter) * quarter + part * 256 % quarter
    hidden = dot(normed_ref[...], weight_ref[:, cols]) + bias_ref[:, pl.ds(pl.multiple_of(start, 256), 256)]
    active, slope = gelu_pair(hidden)
    active_ref[:, cols] = active.astype(bf16)
    slope_ref[:, cols] = slope.astype(bf16)


def widen_kernel(normed_ref, weight_ref, bias_ref, active_ref, slope_ref):
    for part in range(weight_ref.shape[1] // 256):
        widen_part(0, normed_ref, weight_ref, bias_ref, active_ref, slope_ref, part)


def widen(normed, weight, bias):
    rows, units = normed.shape[0], weight.shape[1]
    return call(widen_kernel, "widen", (array((rows, units), bf16),) * 2, 6.5, limit=24)(normed, weight, bias)


def crossed(pieces, flip):
    _, to_x, to_y, from_x, from_y = pieces
    left = (to_y.at[0], to_y.at[1], from_y.at[0], from_y.at[1])[flip]
    right = (to_x.at[0], from_x.at[0], to_x.at[1], from_x.at[1])[flip]
    return left, right


def place_widen_kernel(where_ref, *refs):
    pieces, (normed_ref, bias_ref, weight_ref, active_ref, slope_ref) = refs[:10], refs[10:]
    z, core, group, slabs = (where_ref[number] for number in range(4))
    share = pieces[0].shape[0]
    width = pieces[1].shape[3]
    for flip in range(4):
        for side in range(2):
            parity = core if side == 0 else 1 - core
            own_ref = pieces[5 * side]
            for step in range(4):
                shard = 2 * lax.rem(z - step + slabs, slabs) + parity
                lines = pl.ds(pl.multiple_of(shard * share, 16), share)
                if step == 0:
                    source = pl.ds(pl.multiple_of(jnp.bitwise_xor(group, flip) * 2 * width, LANES), 2 * width)
                    weight_ref[lines, pl.ds(flip * 2 * width, 2 * width)] = own_ref[:, source]
                    continue
                for turn, part in enumerate(crossed(pieces[5 * side : 5 * side + 5], flip)):
                    weight_ref[lines, pl.ds((2 * flip + turn) * width, width)] = part[step - 1]
    for part in range(weight_ref.shape[1] // 256):
        widen_part(group, normed_ref, weight_ref, bias_ref, active_ref, slope_ref, part)


def place_widen(where, mine, theirs, normed, bias, after=()):
    share, units = mine[0].shape
    rows, channels = normed.shape
    wide = array((rows, units), bf16)
    shapes = (array((channels, units), bf16), wide, wide)
    return call(place_widen_kernel, "place_widen", shapes, 8, smem=1, after=after)(where, *mine, *theirs, normed, bias)


def narrow_rows(active_ref, weight_ref, small_ref, branch_ref):
    size = 160
    for part in range(active_ref.shape[0] // size):
        lines = pl.ds(part * size, size)
        branch = dot(active_ref[lines, :], weight_ref[...]) + small_ref[pl.ds(BOUT, 1), :]
        for tile in range(branch_ref.shape[0]):
            branch_ref[tile, lines, :] = branch[:, tile * LANES : (tile + 1) * LANES]


def narrow(active, weight, small):
    rows, channels = active.shape[0], weight.shape[1]
    return call(narrow_rows, "narrow", array((channels // LANES, rows, LANES)), 4, limit=24)(active, weight, small)


def place_narrow_kernel(side, where_ref, *refs):
    pieces = refs[:5]
    if side == 0:
        active_ref, small_ref, weight_ref, branch_ref = refs[5:]
    else:
        active_ref, _, begun_ref, weight_ref, branch_ref = refs[5:]
    z, core, group, slabs = (where_ref[number] for number in range(4))
    parity = core if side == 0 else 1 - core
    tall = pieces[0].shape[0]
    _, _, lines, width = pieces[1].shape

    def base(slab):
        return pl.multiple_of(jnp.bitwise_xor(slab, group) * 2 * tall + parity * tall, 16)

    weight_ref[pl.ds(base(z), tall), :] = pieces[0][...]
    for step in range(1, 4):
        for flip in range(4):
            start = base(lax.rem(z - step + slabs, slabs)) + jnp.bitwise_xor(group, flip) * lines
            for turn, part in enumerate(crossed(pieces, flip)):
                weight_ref[pl.ds(pl.multiple_of(start, 16), lines), pl.ds(turn * width, width)] = part[step - 1]
    spans = [pl.ds(pl.multiple_of(part * 2 * tall + parity * tall, LANES), tall) for part in range(4)]
    weight = jnp.concatenate([weight_ref[span, :] for span in spans], axis=0)
    size = 160
    for part in range(active_ref.shape[0] // size):
        rows = pl.ds(part * size, size)
        branch = dot(jnp.concatenate([active_ref[rows, span] for span in spans], axis=1), weight)
        if side == 0:
            branch = branch + small_ref[pl.ds(BOUT, 1), :]
        for tile in range(branch_ref.shape[0]):
            value = branch[:, tile * LANES : (tile + 1) * LANES]
            branch_ref[tile, rows, :] = value if side == 0 else begun_ref[tile, rows, :] + value


def place_narrow(side, where, pieces, active, *more, after=()):
    tall, channels = pieces[0].shape
    rows, units = active.shape
    shapes = (array((units, channels), bf16), array((channels // LANES, rows, LANES)))
    return call(
        functools.partial(place_narrow_kernel, side),
        "place_narrow",
        shapes,
        3,
        smem=1,
        after=after,
        aliases={} if side == 0 else {7: 0},
    )(where, *pieces, active, *more)


def skew(values, inverse):
    rows = lax.broadcasted_iota(jnp.int32, values.shape, 0)
    centre = (WINDOW // 2) * (CANVAS + 1)
    amount = jnp.bitwise_and(rows - centre if inverse else centre - rows, LANES - 1)
    for bit in range(7):
        moved = pltpu.roll(values, 1 << bit, 1)
        values = jnp.where(jnp.bitwise_and(amount, 1 << bit) != 0, moved, values)
    return values


def movers(tiles, frames):
    def take(ref, frame):
        lines = pl.ds(frame, PADDED, stride=frames)
        return jnp.concatenate([ref[tile, lines, :] for tile in range(tiles)], axis=1)

    def put(ref, frame, values):
        lines = pl.ds(frame, PADDED, stride=frames)
        for tile in range(tiles):
            ref[tile, lines, :] = values[:, tile * LANES : (tile + 1) * LANES]

    return take, put


def mix(x_ref, branch_ref, small_ref, mixed):
    tiles, rows, _ = x_ref.shape
    rest = mixed.shape[1] - rows
    for tile in range(tiles):
        scale = small_ref[pl.ds(SCALE, 1), lane_tile(tile)]
        mixed[tile, pl.ds(0, rows), :] = x_ref[tile] + scale * branch_ref[tile]
        mixed[tile, pl.ds(rows, rest), :] = jnp.zeros((rest, LANES), f32)


def estimator(place_ref, small_ref, west_in):
    west_in[...] = jnp.zeros_like(west_in)
    west_in[pl.ds(0, OFFSETS), :] = small_ref[pl.ds(WEST, OFFSETS), :]
    lanes = lax.broadcasted_iota(jnp.int32, (LANES, LANES), 0)
    return dot((lanes == place_ref[...]).astype(bf16), west_in[...].astype(bf16)).astype(bf16)


def flow_kernel(
    sizes_ref, x_ref, branch_ref, up_ref, index_ref, weight_ref, place_ref, small_ref, window_ref,
    gated_ref, dmixed_ref, dbranch_ref, gscale_ref, gbout_ref, mixed, back, west_in, warp_in, sem,
):
    tiles, rows, _ = x_ref.shape
    images = index_ref.shape[0]
    frames = 2 * images
    channels = tiles * LANES
    factor = channels ** (-0.5)
    every = range(images)
    mix(x_ref, branch_ref, small_ref, mixed)
    take, put = movers(tiles, frames)
    west = estimator(place_ref, small_ref, west_in)
    window = window_ref[0]
    reach = window_ref[1]
    cells = lax.broadcasted_iota(jnp.int32, (PIX, LANES), 1)
    warp_in[...] = jnp.zeros_like(warp_in)
    for image in every:
        warp = jnp.zeros((PIX, LANES), f32)
        for corner in range(4):
            place = index_ref[image, :, pl.ds(corner, 1)]
            amount = weight_ref[image, :, pl.ds(corner, 1)]
            warp = warp + jnp.where(cells == place, amount, 0.0)
        warp_in[image, pl.ds(0, PIX), :] = warp
    halves = [split(warp_in[image]) for image in every]
    wide_warps = [jnp.concatenate(pair, axis=1)[:PADDED] for pair in halves]
    tall_warps = [jnp.concatenate(pair, axis=0) for pair in halves]
    rest = jnp.zeros((LANES - PADDED, channels), f32)

    def twice(values):
        value = jnp.concatenate([values, rest], axis=0).astype(bf16)
        return jnp.concatenate([value, value], axis=0)

    inside = [(reach < sizes_ref[image].astype(f32)).astype(f32)[:, :1] for image in every]
    first = [take(mixed, image) * inside[image] for image in every]
    second = [take(mixed, images + image) * inside[image] for image in every]
    first_low = [value.astype(bf16) for value in first]
    warped = [dot(warp, twice(value)) for warp, value in zip(wide_warps, second)]
    warped = [jnp.concatenate([value, rest], axis=0).astype(bf16) for value in warped]
    scores = [nt(left, right) for left, right in zip(first_low, warped)]
    costs = [skew(value, False) * window * factor for value in scores]
    pairs = [gelu_pair(value) for value in costs]
    for image, (value, _) in enumerate(pairs):
        gated_ref[image] = value.astype(bf16)
    d_firsts = [take(up_ref, image) * inside[image] for image in every]
    d_heads = [value.astype(bf16) for value in d_firsts]
    d_costs = [slope * nt(d_head, west) * window * factor for (_, slope), d_head in zip(pairs, d_heads)]
    d_scores = [skew(value, True).astype(bf16) for value in d_costs]
    for image in every:
        put(back, image, d_firsts[image] + dot(d_scores[image], warped[image]))
    d_warped = [tn(value, low)[:PADDED] for value, low in zip(d_scores, first_low)]
    for image in every:
        d_second = take(up_ref, images + image) + tn(tall_warps[image], twice(d_warped[image]))[:PADDED]
        put(back, images + image, d_second * inside[image])
    save = pltpu.make_async_copy(back.at[:, pl.ds(0, rows)], dmixed_ref, sem)
    save.start()
    for tile in range(tiles):
        cols = lane_tile(tile)
        d_mixed = back[tile, pl.ds(0, rows), :]
        gscale_ref[:, cols] = jnp.sum(d_mixed * branch_ref[tile], axis=0, keepdims=True)
        d_branch = (d_mixed * small_ref[pl.ds(SCALE, 1), cols]).astype(bf16)
        dbranch_ref[:, cols] = d_branch
        gbout_ref[:, cols] = jnp.sum(d_branch.astype(f32), axis=0, keepdims=True)
    save.wait()


def finish_kernel(
    sizes_ref, x_ref, branch_ref, up_ref, gated_ref, place_ref, small_ref, window_ref,
    out_ref, gwest_ref, mixed, west_in,
):
    tiles, _, _ = x_ref.shape
    images = gated_ref.shape[0]
    frames = 2 * images
    take, put = movers(tiles, frames)
    mix(x_ref, branch_ref, small_ref, mixed)
    west = estimator(place_ref, small_ref, west_in)
    reach = window_ref[1]
    for image in range(images):
        inside = (reach < sizes_ref[image].astype(f32)).astype(f32)[:, :1]
        gated = gated_ref[image]
        part = tn(gated, (take(up_ref, image) * inside).astype(bf16))
        gwest_ref[...] = part if image == 0 else gwest_ref[...] + part
        put(mixed, image, (take(mixed, image) * inside + dot(gated, west)) * inside)
        put(mixed, images + image, take(mixed, images + image) * inside)
    for image in range(images):
        for which in range(2):
            for row in range(CANVAS):
                lines = pl.ds(row * CANVAS * frames + which * images + image, CANVAS, stride=frames)
                for tile in range(tiles):
                    out_ref[image, which, row, :, lane_tile(tile)] = mixed[tile, lines, :].astype(bf16)


def finish(sizes, x, branch, up, gated, place, small, after=()):
    tiles, rows, _ = x.shape
    images, channels = gated.shape[0], tiles * LANES
    return call(
        finish_kernel,
        "finish",
        (array((images, 2, CANVAS, CANVAS, channels), bf16), array((LANES, channels))),
        0.01,
        [pltpu.VMEM((tiles, PADDED * 2 * images, LANES), f32), pltpu.VMEM((LANES, channels), f32)],
        limit=10,
        smem=1,
        after=after,
    )(sizes, x, branch, up, gated, place, small, jnp.asarray(tables()))


def tables():
    cells = np.arange(PADDED)[:, None]
    lane = np.arange(LANES)[None, :]
    reach = WINDOW // 2
    row = cells // CANVAS + lane // CANVAS - reach
    col = cells % CANVAS + lane % CANVAS - reach
    good = (lane % CANVAS < WINDOW) & (lane // CANVAS < WINDOW) & (cells < PIX)
    good &= (row >= 0) & (row < CANVAS) & (col >= 0) & (col < CANVAS)
    far = np.maximum(cells // CANVAS, cells % CANVAS) + 0 * lane
    return np.stack([good, far]).astype(np.float32)


def flow(sizes, x, branch, up, index, weight, place, small, after=()):
    tiles, rows, _ = x.shape
    images, channels = index.shape[0], tiles * LANES
    padded = pltpu.VMEM((tiles, PADDED * 2 * images, LANES), f32)
    vector = array((1, channels))
    return call(
        flow_kernel,
        "flow",
        (
            array((images, PADDED, LANES), bf16),
            pltpu.HBM(x.shape, f32),
            array((rows, channels), bf16),
            vector,
            vector,
        ),
        6.5,
        [padded, padded, pltpu.VMEM((LANES, channels), f32), pltpu.VMEM((images, LANES, LANES), f32), pltpu.SemaphoreType.DMA],
        limit=14,
        smem=1,
        after=after,
    )(sizes, x, branch, up, index, weight, place, small, jnp.asarray(tables()))


def grad_narrow_kernel(where_ref, active_ref, dbranch_ref, out_ref):
    count, tile, _ = out_ref.shape
    for part in range(count):
        block = 2 * jnp.bitwise_xor(part, where_ref[2]) + 1 - where_ref[1] if count < 8 else part
        cols = pl.ds(pl.multiple_of(block * tile, LANES), tile)
        out_ref[part] = tn(active_ref[:, cols], dbranch_ref[...]).astype(bf16)


def grad_narrow(where, active, dbranch, count, after=()):
    units, channels = active.shape[1], dbranch.shape[1]
    shape = array((count, units // 8, channels), bf16)
    return call(grad_narrow_kernel, "grad_narrow", shape, 0.3 * count, limit=2 * count, smem=1, after=after)(where, active, dbranch)


def send_halves(where_ref, blocks, keep_ref, left_ref, right_ref):
    x, y = lax.rem(where_ref[2], 2), where_ref[2] // 2
    for turn in range(2):
        keep_ref[0, turn] = blocks[2 * x + turn]
        keep_ref[1, turn] = blocks[4 + 2 * y + turn]
        left_ref[turn] = blocks[2 * (1 - x) + turn]
        right_ref[turn] = blocks[4 + 2 * (1 - y) + turn]


def halves_of(lines, width):
    half = array((2, lines, width), bf16)
    return (array((2, 2, lines, width), bf16), half, half), [pltpu.VMEM((8, lines, width), bf16)]


def grad_narrow_here_kernel(where_ref, active_ref, dbranch_ref, received_ref, keep_ref, left_ref, right_ref, blocks):
    count, tile, _ = received_ref.shape
    lines = tile // 8
    for part in range(count):
        block = 2 * jnp.bitwise_xor(part, where_ref[2]) + where_ref[1]
        cols = pl.ds(pl.multiple_of(block * tile, LANES), tile)
        total = tn(active_ref[:, cols], dbranch_ref[...]) + received_ref[part].astype(f32)
        for block in range(8):
            blocks[block, pl.ds(part * lines, lines), :] = total[block * lines : (block + 1) * lines].astype(bf16)
    send_halves(where_ref, blocks, keep_ref, left_ref, right_ref)


def grad_narrow_here(where, active, dbranch, received, after=()):
    count, tile, channels = received.shape
    shapes, scratch = halves_of(count * tile // 8, channels)
    return call(grad_narrow_here_kernel, "grad_narrow_here", shapes, 0.1, scratch, limit=6, smem=1, after=after)(
        where, active, dbranch, received
    )


def hidden_back_kernel(where_ref, dbranch_ref, weight_ref, slope_ref, dhidden_ref, gbin_ref):
    tile = slope_ref.shape[1] // 4
    for part in range(4):
        cols = pl.ds(part * tile, tile)
        d_active = nt(dbranch_ref[...], weight_ref[cols, :])
        d_hidden = (d_active * slope_ref[:, cols].astype(f32)).astype(bf16)
        dhidden_ref[:, cols] = d_hidden
        start = jnp.bitwise_xor(part, where_ref[2]) * tile
        gbin_ref[:, pl.ds(pl.multiple_of(start, LANES), tile)] = jnp.sum(d_hidden.astype(f32), axis=0, keepdims=True)


def hidden_back(where, dbranch, weight, slope, after=()):
    rows, units = slope.shape
    shapes = (array((rows, units), bf16), array((1, units)))
    return call(hidden_back_kernel, "hidden_back", shapes, 2, smem=1, after=after)(
        where, dbranch, weight, slope
    )


def grad_widen_full_kernel(normed_ref, dhidden_ref, out_ref):
    tile = 768
    for part in range(out_ref.shape[1] // tile):
        cols = pl.ds(part * tile, tile)
        out_ref[:, cols] = tn(normed_ref[...], dhidden_ref[:, cols]).astype(bf16)


def grad_widen_full(normed, dhidden):
    shape = array((normed.shape[1], dhidden.shape[1]), bf16)
    return call(grad_widen_full_kernel, "grad_widen_full", shape, 5, limit=24)(normed, dhidden)


def grad_widen_away_kernel(where_ref, pair_ref, dhidden_ref, out_ref):
    blocks, lines, width = out_ref.shape
    for part in range(blocks // 2):
        total = tn(pair_ref[:, pl.ds(0, lines)], dhidden_ref[:, pl.ds(2 * part * width, 2 * width)]).astype(bf16)
        block = 2 * jnp.bitwise_xor(part, where_ref[2])
        out_ref[block] = total[:, :width]
        out_ref[block + 1] = total[:, width:]


def grad_widen_away(where, pair, dhidden, after=()):
    shape = array((8, pair.shape[1] // 2, dhidden.shape[1] // 8), bf16)
    return call(grad_widen_away_kernel, "grad_widen_away", shape, 0.01, smem=1, after=after)(where, pair, dhidden)


def grad_widen_here_kernel(where_ref, pair_ref, dhidden_ref, received_ref, keep_ref, left_ref, right_ref, blocks):
    _, lines, width = blocks.shape
    for part in range(4):
        both = tn(pair_ref[:, pl.ds(lines, lines)], dhidden_ref[:, pl.ds(2 * part * width, 2 * width)])
        for turn in range(2):
            block = 2 * jnp.bitwise_xor(part, where_ref[2]) + turn
            value = both[:, turn * width : (turn + 1) * width] + received_ref[block].astype(f32)
            blocks[block] = value.astype(bf16)
    send_halves(where_ref, blocks, keep_ref, left_ref, right_ref)


def grad_widen_here(where, pair, dhidden, received, after=()):
    shapes, scratch = halves_of(*received.shape[1:])
    return call(grad_widen_here_kernel, "grad_widen_here", shapes, 0.01, scratch, limit=6, smem=1, after=after)(
        where, pair, dhidden, received
    )


def norm_back_kernel(dhidden_ref, weight_ref, xhat_ref, rstd_ref, small_ref, dconv_ref, sums_ref):
    rows, channels = xhat_ref.shape
    size = 160
    gain = small_ref[pl.ds(GAIN, 1), :]
    sums = [jnp.zeros((1, channels), f32)] * 3
    for part in range(rows // size):
        lines = pl.ds(part * size, size)
        d_normed = nt(dhidden_ref[lines, :], weight_ref[...])
        xhat = xhat_ref[lines, :].astype(f32)
        product = d_normed * xhat
        d_xhat = d_normed * gain
        mean = jnp.sum(d_xhat, axis=-1, keepdims=True) * (1.0 / channels)
        along = jnp.sum(product * gain, axis=-1, keepdims=True) * (1.0 / channels)
        d_conv = (d_xhat - mean - xhat * along) * rstd_ref[lines, :]
        for tile in range(dconv_ref.shape[0]):
            dconv_ref[tile, lines, :] = d_conv[:, tile * LANES : (tile + 1) * LANES]
        for number, value in enumerate((d_conv, product, d_normed)):
            sums[number] = sums[number] + jnp.sum(value, axis=0, keepdims=True)
    sums_ref[...] = jnp.concatenate(sums, axis=0)


def norm_back(dhidden, weight, xhat, rstd, small, after=()):
    rows, channels = xhat.shape
    return call(
        norm_back_kernel, "norm_back", (array((channels // LANES, rows, LANES)), array((3, channels))), 0.01, after=after
    )(dhidden, weight, xhat, rstd, small)


def grad_taps_kernel(x_ref, dconv_ref, out_ref):
    @pl.loop(0, x_ref.shape[0])
    def _(tile):
        cols = pl.ds(pl.multiple_of(tile * LANES, LANES), LANES)
        for ky in range(KERNEL):
            totals = [None] * KERNEL
            for row in range(CANVAS):
                source_row = row + ky - REACH
                if not 0 <= source_row < CANVAS:
                    continue
                cells = [x_ref[tile, pl.ds((source_row * CANVAS + col) * 8, 8), :] for col in range(CANVAS)]
                grads = [dconv_ref[tile, pl.ds((row * CANVAS + col) * 8, 8), :] for col in range(CANVAS)]
                for kx in range(KERNEL):
                    for col in range(CANVAS):
                        source = col + kx - REACH
                        if 0 <= source < CANVAS:
                            term = cells[source] * grads[col]
                            totals[kx] = term if totals[kx] is None else totals[kx] + term
            for kx in range(KERNEL):
                out_ref[pl.ds(ky * KERNEL + kx, 1), cols] = jnp.sum(totals[kx], axis=0, keepdims=True)


def grad_taps(x, dconv, after=()):
    return call(grad_taps_kernel, "grad_taps", array((TAPS, x.shape[0] * LANES)), 0.01, after=after)(x, dconv)


def conv_back_kernel(sizes_ref, dconv_ref, small_ref, dmixed_ref, out_ref, total):
    tiles = dconv_ref.shape[0]
    images = out_ref.shape[0]
    frames = 2 * images
    side = side_of(sizes_ref, images)

    @pl.loop(0, tiles)
    def _(tile):
        def finish(cell, value):
            lines = pl.ds(cell * 8, 8)
            inside = side > max(cell // CANVAS, cell % CANVAS)
            total[tile, lines, :] = jnp.where(inside, value + dmixed_ref[tile, lines, :], 0.0)

        conv_rows(dconv_ref, tile, small_ref, True, finish)

    for image in range(images):
        for which in range(2):
            for row in range(CANVAS):
                lines = pl.ds(row * CANVAS * frames + which * images + image, CANVAS, stride=frames)
                for tile in range(tiles):
                    out_ref[image, which, row, :, lane_tile(tile)] = total[tile, lines, :]


def conv_back(sizes, dconv, small, dmixed, after=()):
    tiles, rows, _ = dconv.shape
    images = sizes.shape[0]
    return call(
        conv_back_kernel,
        "conv_back",
        array((images, 2, CANVAS, CANVAS, tiles * LANES)),
        0.1,
        [pltpu.VMEM(dconv.shape, f32)],
        limit=6,
        smem=1,
        after=after,
    )(sizes, dconv, small, dmixed)


def start_all(copies, sems):
    running = [pltpu.make_async_copy(source, target, sems.at[number]) for number, (source, target) in enumerate(copies)]
    for copy in running:
        copy.start()
    return running

GROUPS = 6
LINES = 24
BIAS = SMALL


def pack_kernel(where_ref, weight_ref, taps_ref, west_ref, *refs):
    vectors, (bias_ref, out_ref, small, taps, west, *held, bias, sems) = refs[:5], refs[5:]
    share = weight_ref.shape[0]
    wide = out_ref.shape[1]
    cols = pl.ds(pl.multiple_of(where_ref[2] * wide, LANES), wide)
    copies = [(taps_ref, taps), (west_ref, west), (bias_ref, bias)]
    copies += list(zip(vectors, held))
    copies += [(weight_ref.at[:, cols], out_ref.at[pl.ds(0, share)])]
    running = start_all(copies, sems)
    small[...] = jnp.zeros_like(small)
    lane = pl.ds(0, share)
    for copy in running[:-1]:
        copy.wait()
    small[pl.ds(0, TAPS), lane] = taps[...].astype(f32)
    small[pl.ds(WEST, OFFSETS), lane] = west[...].astype(f32)
    for number, vector in enumerate(held):
        small[pl.ds(CBIAS + number, 1), lane] = vector[...].astype(f32).reshape(1, share)
    for part in range(bias.shape[0] // LANES):
        small[pl.ds(BIAS + part, 1), :] = bias[lane_tile(part)].astype(f32).reshape(1, LANES)
    for group in range(GROUPS):
        out_ref[pl.ds(share, LINES), lane_tile(group)] = small[pl.ds(group * LINES, LINES), :].astype(bf16)
    running[-1].wait()


def pack(where, weight, taps, west, vectors, bias, after=()):
    share, units = weight.shape
    args = (weight, taps, west, *vectors, bias)
    return call(
        pack_kernel,
        "pack",
        array((share + LINES, units // 4), bf16),
        2,
        [
            pltpu.VMEM((GROUPS * LINES, LANES), f32),
            pltpu.VMEM(taps.shape, bf16),
            pltpu.VMEM(west.shape, bf16),
            *[pltpu.VMEM((share,), bf16)] * len(vectors),
            pltpu.VMEM(bias.shape, bf16),
            pltpu.SemaphoreType.DMA((len(args),)),
        ],
        smem=1,
        left=len(args),
        after=after,
    )(where, *args)


def stack_kernel(*refs):
    first = refs[0].shape[0] - LINES
    for number, ref in enumerate(refs[:-1]):
        refs[-1][number] = ref[pl.ds(first, LINES), :]


def stack(parts, after=()):
    shape = array((len(parts), LINES, parts[0].shape[1]), bf16)
    return call(stack_kernel, "stack", shape, 0.05, after=after)(*parts)


def unpack_kernel(where_ref, mine_ref, theirs_ref, small_ref, bias_ref):
    z, core, slabs = where_ref[0], where_ref[1], where_ref[3]
    channels = small_ref.shape[1]
    share = channels // 8
    everything = None
    for number in range(8):
        ref = mine_ref if number < 4 else theirs_ref
        shard = 2 * lax.rem(z - number % 4 + slabs, slabs) + (core if number < 4 else 1 - core)
        rows = jnp.concatenate([ref[number % 4, :, lane_tile(group)].astype(f32) for group in range(GROUPS)], axis=0)
        source = lax.broadcasted_iota(jnp.int32, (LANES, channels), 0)
        target = lax.broadcasted_iota(jnp.int32, (LANES, channels), 1)
        spread = ((target - shard * share == source) & (source < share)).astype(bf16)
        value = dot(rows.astype(bf16), spread)
        everything = value if everything is None else everything + value
        width = bias_ref.shape[1] // 8
        for part in range(width // LANES):
            cols = pl.ds(pl.multiple_of(shard * width + part * LANES, LANES), LANES)
            bias_ref[:, cols] = rows[BIAS + part : BIAS + part + 1, :]
    small_ref[...] = everything[: small_ref.shape[0]]


def unpack(where, mine, theirs, units, channels):
    return call(unpack_kernel, "unpack", (array((SMALL, channels)), array((1, units))), 1.2, smem=1)(where, mine, theirs)


def column_kernel(*refs):
    parts, outs = refs[:-2], refs[-2:]
    rows, width = outs[0].shape[1:]
    for turn, out in enumerate(outs):
        for number, part in enumerate(parts):
            out[number] = part[pl.ds(0, rows), pl.ds(turn * width, width)]


def column(parts, rows, after=()):
    half = array((len(parts), rows, parts[0].shape[1] // 2), bf16)
    return call(column_kernel, "column", (half, half), 0.05, after=after)(*parts)


def cut_kernel(where_ref, weight_ref, out_ref, sem):
    tall = out_ref.shape[0]
    lines = pl.ds(pl.multiple_of(where_ref[2] * tall, 16), tall)
    copy = pltpu.make_async_copy(weight_ref.at[lines], out_ref, sem)
    copy.start()
    copy.wait()


def cut(where, weight, after=()):
    tall, channels = weight.shape
    shape = array((tall // 4, channels), bf16)
    return call(cut_kernel, "cut", shape, 1, [pltpu.SemaphoreType.DMA], smem=1, left=1, after=after)(where, weight)


def onward_kernel(left_ref, right_ref, left_in_ref, right_in_ref, to_x_ref, to_y_ref):
    to_y_ref[0] = left_ref[...]
    to_y_ref[1] = left_in_ref[...]
    to_x_ref[0] = right_ref[...]
    to_x_ref[1] = right_in_ref[...]


def onward(left, right, left_in, right_in, after=()):
    shape = array((2, *left.shape), bf16)
    return call(onward_kernel, "onward", (shape, shape), 1, after=after)(left, right, left_in, right_in)


def halve_kernel(where_ref, keep_ref, left_in_ref, right_in_ref, keep_out_ref, left_ref, right_ref):
    x, y = lax.rem(where_ref[2], 2), where_ref[2] // 2

    def total(side, which):
        received = left_in_ref if side == 0 else right_in_ref
        return keep_ref[side, which].astype(f32) + received[which].astype(f32)

    keep_out_ref[0] = total(0, y).astype(bf16)
    keep_out_ref[1] = total(1, x).astype(bf16)
    left_ref[...] = total(0, 1 - y).astype(bf16)
    right_ref[...] = total(1, 1 - x).astype(bf16)


def halve(where, keep, left_in, right_in, after=()):
    _, _, lines, width = keep.shape
    half = array((lines, width), bf16)
    shapes = (array((2, lines, width), bf16), half, half)
    return call(halve_kernel, "halve", shapes, 0.01, smem=1, after=after)(where, keep, left_in, right_in)


def deal_total(where_ref, keep_ref, left_in_ref, right_in_ref, total):
    total[0] = (keep_ref[0].astype(f32) + left_in_ref[...].astype(f32)).astype(bf16)
    total[1] = (keep_ref[1].astype(f32) + right_in_ref[...].astype(f32)).astype(bf16)


def deal_kernel(where_ref, keep_ref, left_in_ref, right_in_ref, *refs):
    outs, total = refs[:-1], refs[-1]
    share = outs[0].shape[1]
    deal_total(where_ref, keep_ref, left_in_ref, right_in_ref, total)
    for step, out in enumerate(outs):
        slab = lax.rem(where_ref[0] + step, len(outs))
        for side in range(2):
            out[side] = total[side, pl.ds(pl.multiple_of(slab * share, 16), share), :]


def deal(where, keep, left_in, right_in, slabs, after=()):
    _, lines, width = keep.shape
    shapes = (array((2, lines // slabs, width), bf16),) * slabs
    scratch = [pltpu.VMEM(keep.shape, bf16)]
    return call(deal_kernel, "deal", shapes, 0.01, scratch, smem=1, after=after)(where, keep, left_in, right_in)


SMALL_ROWS = 192


def deal_small_kernel(where_ref, keep_ref, left_in_ref, right_in_ref, here_ref, received_ref, *refs):
    outs, total = refs[:-1], refs[-1]
    deal_total(where_ref, keep_ref, left_in_ref, right_in_ref, total)
    share = total.shape[1] // len(outs)
    extra = outs[0].shape[1] - share
    for step, out in enumerate(outs):
        slab = lax.rem(where_ref[0] + step, len(outs))
        small = here_ref[slab] + received_ref[slab]
        lines = SMALL_ROWS // 4
        small = jnp.concatenate([small[part * lines : (part + 1) * lines] for part in range(4)], axis=1)
        for side in range(2):
            out[side, pl.ds(0, share), :] = total[side, pl.ds(pl.multiple_of(slab * share, 16), share), :]
            out[side, pl.ds(share, extra), :] = small[side * extra : (side + 1) * extra].astype(bf16)


def deal_small(where, keep, left_in, right_in, here, received, after=()):
    slabs = here.shape[0]
    _, lines, width = keep.shape
    extra = SMALL_ROWS * here.shape[2] // width // 2
    shapes = (array((2, lines // slabs + extra, width), bf16),) * slabs
    scratch = [pltpu.VMEM(keep.shape, bf16)]
    return call(deal_small_kernel, "deal_small", shapes, 0.01, scratch, smem=1, after=after)(
        where, keep, left_in, right_in, here, received
    )


def total_kernel(*refs):
    total = refs[0][...].astype(f32)
    for ref in refs[1:-1]:
        total = total + ref[...].astype(f32)
    refs[-1][...] = total.astype(refs[-1].dtype)


def total(values, after=()):
    return call(total_kernel, "total", array(values[0].shape, values[0].dtype), 1, after=after)(*values)


def blocks_of(where_ref, flip):
    group = jnp.bitwise_xor(where_ref[2], flip)
    x, y = lax.rem(group, 2), group // 2
    return 2 * x + y, 4 + 2 * y + x


def spread_wout_kernel(where_ref, *refs):
    *values, out_ref = refs
    lines = values[0].shape[1]
    for flip, ref in enumerate(values):
        for side, block in enumerate(blocks_of(where_ref, flip)):
            out_ref[pl.ds(pl.multiple_of(block * lines, 16), lines), :] = ref[side].astype(f32)


def spread_wout(where, values, after=()):
    _, lines, channels = values[0].shape
    return call(spread_wout_kernel, "spread_wout", array((8 * lines, channels)), 1, smem=1, after=after)(where, *values)


def spread_win_kernel(where_ref, lane_ref, *refs):
    values, (out_ref, taps_ref, west_ref, bias_ref, *vectors, small) = refs[:4], refs[4:]
    share = out_ref.shape[0]
    _, lines, width = values[0].shape
    extra = lines - share
    for flip, ref in enumerate(values):
        for side, block in enumerate(blocks_of(where_ref, flip)):
            out_ref[:, pl.ds(pl.multiple_of(block * width, LANES), width)] = ref[side, pl.ds(0, share), :].astype(f32)
    for side in range(2):
        part = [ref[side, pl.ds(share, extra), :].astype(f32) for ref in values]
        both = (part[0] + part[1]) + (part[2] + part[3])
        for group in range(4):
            span = pl.ds(group * 2 * extra + side * extra, extra)
            small[span, :] = both[:, group * share : (group + 1) * share]
    taps_ref[...] = small[pl.ds(0, TAPS), :]
    for number, ref in enumerate(vectors):
        ref[...] = small[pl.ds(TAPS + number, 1), :]
    for offset in range(OFFSETS):
        west_ref[pl.ds(offset, 1), :] = small[pl.ds(TAPS + 5 + lane_ref[offset], 1), :]
    rows = bias_ref.shape[0] // share
    first = TAPS + 5 + LANES
    bias_ref[...] = jnp.concatenate([small[pl.ds(first + row, 1), :] for row in range(rows)], axis=1).reshape(bias_ref.shape)


def spread_win(where, lane_of, values, share, after=()):
    width = values[0].shape[2]
    shapes = [array((share, 8 * width)), array((TAPS, share)), array((OFFSETS, share)), array((width,))]
    shapes += [array((1, share))] * 5
    scratch = [pltpu.VMEM((SMALL_ROWS, share), f32)]
    return call(spread_win_kernel, "spread_win", shapes, 1, scratch, smem=2, after=after)(where, lane_of, *values)


def pack_small_kernel(where_ref, gtaps_ref, gnorm_ref, gbout_ref, gscale_ref, gwest_ref, gbin_ref, here_ref, away_ref):
    slabs, _, share = here_ref.shape

    def fill(even_ref, odd_ref):
        for shard in range(2 * slabs):
            out = odd_ref if shard % 2 else even_ref
            cols = pl.ds(shard * share, share)
            line = 0
            for ref in (gtaps_ref, gnorm_ref, gbout_ref, gscale_ref, gwest_ref):
                out[shard // 2, pl.ds(line, ref.shape[0]), :] = ref[:, cols]
                line += ref.shape[0]
            lines = gbin_ref.shape[1] // gtaps_ref.shape[1]
            for extra in range(lines):
                span = pl.ds((shard * lines + extra) * share, share)
                out[shard // 2, pl.ds(line + extra, 1), :] = gbin_ref[:, span]
            rest = SMALL_ROWS - line - lines
            out[shard // 2, pl.ds(line + lines, rest), :] = jnp.zeros((rest, share), f32)

    @pl.when(where_ref[1] == 0)
    def _():
        fill(here_ref, away_ref)

    @pl.when(where_ref[1] == 1)
    def _():
        fill(away_ref, here_ref)


def pack_small(where, parts, slabs, share, after=()):
    shape = array((slabs, SMALL_ROWS, share))
    return call(pack_small_kernel, "pack_small", (shape, shape), 0.01, smem=1, after=after)(where, *parts)


AXES = ("dp", "fsdp")


class Routes:
    def __init__(self, groups, members):
        self.groups, self.members, self.slabs = groups, members, members // 2
        self.group = lax.axis_index("dp")
        member = lax.axis_index("fsdp")
        self.slab, self.core = member // 2, member % 2

    def send(self, value, target):
        pairs = [
            (group * self.members + 2 * slab + core, self.index(*target(group, slab, core)))
            for group in range(self.groups)
            for slab in range(self.slabs)
            for core in range(2)
        ]
        return lax.ppermute(value, AXES, pairs)

    def index(self, group, slab, core):
        return group * self.members + 2 * slab + core

    def to_core(self, value):
        return self.send(value, lambda group, slab, core: (group, slab, 1 - core))

    def to_slab(self, value, step):
        return self.send(value, lambda group, slab, core: (group, (slab + step) % self.slabs, core))

    def to_near(self, value, flip):
        return self.send(value, lambda group, slab, core: (group, slab ^ flip, core))

    def to_group(self, value, flip):
        return self.send(value, lambda group, slab, core: (group ^ flip, slab, core))


def shards(
    features,
    cotangent,
    image_sizes,
    warp_index,
    warp_weight,
    offsets,
    conv_kernel,
    conv_bias,
    norm_gain,
    norm_bias,
    w_in,
    bias_in,
    w_out,
    bias_out,
    layer_scale,
    w_estimate,
):
    share, units = w_in.shape
    channels = features.shape[-1]
    members = channels // share
    groups = lax.axis_size("dp")
    paired = groups == 4 and members == 8

    reach = WINDOW // 2
    lane_of = (offsets[:, 0] + reach) * CANVAS + offsets[:, 1] + reach
    place = jnp.pad(lane_of, (0, LANES - OFFSETS), constant_values=-1)[None]

    early = (features, cotangent, warp_index, warp_weight, place, lane_of)
    if paired:
        routes = Routes(groups, members)
        slabs = routes.slabs
        where = jnp.stack([routes.slab, routes.core, routes.group, jnp.int32(slabs)])
        vectors = (conv_bias, norm_gain, norm_bias, bias_out, layer_scale)
        packed = pack(where, w_in, conv_kernel, w_estimate, vectors, bias_in)
        win_parts = [routes.to_slab(packed, step) for step in range(1, slabs)]
        win_own = routes.to_core(w_in)
        small = stack([packed, *win_parts], after=early)
        quarter = cut(where, w_out, after=(packed,))
        wout_parts = [routes.to_slab(quarter, step) for step in range(1, slabs)]
        wout_own = routes.to_core(w_out)
        small, bin_all = unpack(where, small, routes.to_core(small), units, channels)
    else:
        where = jnp.zeros((4,), jnp.int32)
        small = jnp.concatenate(
            [
                conv_kernel,
                w_estimate,
                jnp.stack([conv_bias, norm_gain, norm_bias, bias_out, layer_scale]),
                bias_in.reshape(-1, share),
            ]
        )
        small = lax.all_gather(small, "fsdp")
        win_all = lax.all_gather(w_in, "fsdp", axis=0, tiled=True)
        wout_all = lax.all_gather(w_out, "fsdp", axis=0, tiled=True)
        bin_all = small[:, SMALL:].reshape(1, units).astype(f32)
        small = small[:, :SMALL].transpose(1, 0, 2).reshape(SMALL, channels).astype(f32)
    after = ()
    if paired:
        left, right = column(win_parts, share, after=(wout_parts[0],))
        left_in, right_in = routes.to_group(left, 1), routes.to_group(right, 2)
        after = (left,)
    x, up, begun = conv_begin(image_sizes, features, cotangent, small, after)
    if paired:
        to_x, to_y = onward(left, right, left_in, right_in, after=(begun,))
        win_halves = [to_x, to_y, routes.to_group(to_x, 1), routes.to_group(to_y, 2)]
        left, right = column(wout_parts, units // members // 4, after=(to_x,))
        left_in, right_in = routes.to_group(left, 1), routes.to_group(right, 2)
        after = (left,)
    normed, pair, xhat, rstd = conv_norm(where, x, begun, small, after)
    if paired:
        to_x, to_y = onward(left, right, left_in, right_in, after=(normed,))
        wout_halves = [to_x, to_y, routes.to_group(to_x, 1), routes.to_group(to_y, 2)]
        win_halves = gate(win_halves, (to_x,))
        win_theirs = [win_own] + [routes.to_core(value) for value in win_halves]
        win_all, active, slope = place_widen(where, [w_in, *win_halves], win_theirs, normed, bin_all)
        wout_halves = gate(wout_halves, (active,))
        wout_theirs = [wout_own] + [routes.to_core(value) for value in wout_halves]
        begun = place_narrow(0, where, [w_out, *wout_halves], active, small)
        wout_all, branch = place_narrow(1, where, wout_theirs, active, *begun)
    else:
        active, slope = widen(normed, win_all, bin_all)
        branch = narrow(active, wout_all, small)
    gated, d_mixed, d_branch, g_scale, g_bout = flow(
        image_sizes, x, branch, up, warp_index, warp_weight, place, small
    )
    if paired:
        wout_away = grad_narrow(where, active, d_branch, slabs)
        wout_in = routes.to_core(wout_away)
        d_hidden, g_bin = hidden_back(where, d_branch, wout_all, slope, after=(wout_away,))
        keep_out, left, right = grad_narrow_here(where, active, d_branch, wout_in, after=(d_hidden,))
        left_out, right_out = routes.to_group(left, 1), routes.to_group(right, 2)
        win_away = grad_widen_away(where, pair, d_hidden, after=(keep_out,))
        win_in = routes.to_core(win_away)
        mixed_out, g_west = finish(image_sizes, x, branch, up, gated, place, small, after=(win_away,))
        keep_in, left, right = grad_widen_here(where, pair, d_hidden, win_in, after=(g_west,))
        left_in, right_in = routes.to_group(left, 1), routes.to_group(right, 2)
        d_conv, g_norm = norm_back(d_hidden, win_all, xhat, rstd, small, after=(keep_in,))
        keep_out, left, right = halve(where, keep_out, left_out, right_out, after=(d_conv,))
        left_out, right_out = routes.to_group(left, 2), routes.to_group(right, 1)
        g_taps = grad_taps(x, d_conv, after=(keep_out,))
        parts = (g_taps, g_norm, g_bout, g_scale, g_west, g_bin)
        small_here, small_away = pack_small(where, parts, slabs, share)
        small_in = routes.to_core(small_away)
        keep_in, left, right = halve(where, keep_in, left_in, right_in, after=(small_away,))
        left_in, right_in = routes.to_group(left, 2), routes.to_group(right, 1)
        wout_parts = deal(where, keep_out, left_out, right_out, slabs, after=(keep_in,))
        wout_parts = wout_parts[:1] + tuple(routes.to_slab(v, n + 1) for n, v in enumerate(wout_parts[1:]))
        win_parts = deal_small(where, keep_in, left_in, right_in, small_here, small_in, after=wout_parts[:1])
        win_parts = win_parts[:1] + tuple(routes.to_slab(v, n + 1) for n, v in enumerate(win_parts[1:]))
        grad_features = conv_back(image_sizes, d_conv, small, d_mixed, after=win_parts[:1])
        g_wout = total(wout_parts, after=(grad_features,))
        wout_parts = [g_wout] + [routes.to_group(g_wout, flip) for flip in range(1, 4)]
        g_win = total(win_parts, after=(g_wout,))
        win_parts = [g_win] + [routes.to_group(g_win, flip) for flip in range(1, 4)]
        g_wout = spread_wout(where, wout_parts, after=(g_win,))
        g_win, g_taps, g_west, g_bin, *g_small = spread_win(where, lane_of, win_parts, share)
        g_small = [value.reshape(share) for value in g_small]
    else:
        g_wout = grad_narrow(where, active, d_branch, 8).reshape(units, channels)
        d_hidden, g_bin = hidden_back(where, d_branch, wout_all, slope)
        g_win = grad_widen_full(normed, d_hidden)
        d_conv, g_norm = norm_back(d_hidden, win_all, xhat, rstd, small)
        g_taps = grad_taps(x, d_conv)
        mixed_out, g_west = finish(image_sizes, x, branch, up, gated, place, small)
        grad_features = conv_back(image_sizes, d_conv, small, d_mixed)
        g_small = jnp.concatenate([g_taps, g_norm, g_bout, g_scale, g_west])
        g_small = g_small.reshape(-1, members, share).transpose(1, 0, 2)
        g_small = jnp.concatenate([g_small, g_bin.reshape(members, -1, share)], axis=1)

        def reduce(value):
            return lax.psum(lax.psum_scatter(value, "fsdp", scatter_dimension=0, tiled=True).astype(f32), "dp")

        g_wout, g_win, g_small = reduce(g_wout), reduce(g_win), reduce(g_small)[0]
        tail = TAPS + 5 + LANES
        g_taps, g_west, g_bin = g_small[:TAPS], jnp.take(g_small[TAPS + 5 : tail], lane_of, axis=0), g_small[tail:]
        g_small = g_small[TAPS : TAPS + 5]
    return (
        mixed_out,
        grad_features,
        g_taps,
        g_small[0],
        g_small[1],
        g_small[2],
        g_win,
        g_bin.reshape(-1),
        g_wout,
        g_small[3],
        g_small[4],
        g_west,
    )


def solution(mesh):
    in_specs = (
        P(("dp", "fsdp"), None, None, None, None),
        P(("dp", "fsdp"), None, None, None, None),
        P(("dp", "fsdp")),
        P(("dp", "fsdp"), None, None),
        P(("dp", "fsdp"), None, None),
        P(),
        P(None, "fsdp"),
        P("fsdp"),
        P("fsdp"),
        P("fsdp"),
        P("fsdp", None),
        P("fsdp"),
        P("fsdp", None),
        P("fsdp"),
        P("fsdp"),
        P(None, "fsdp"),
    )
    out_specs = (
        P(("dp", "fsdp"), None, None, None, None),
        P(("dp", "fsdp"), None, None, None, None),
        P(None, "fsdp"),
        P("fsdp"),
        P("fsdp"),
        P("fsdp"),
        P("fsdp", None),
        P("fsdp"),
        P("fsdp", None),
        P("fsdp"),
        P("fsdp"),
        P(None, "fsdp"),
    )
    return jax.shard_map(shards, mesh=mesh, in_specs=in_specs, out_specs=out_specs, check_vma=False)
```

```python
import functools

import jax
import jax.numpy as jnp
import numpy as np
from jax import lax
from jax.experimental import pallas as pl
from jax.experimental.pallas import tpu as pltpu
from jax.sharding import PartitionSpec as P

CANVAS = 10
KERNEL = 7
REACH = KERNEL // 2
TAPS = KERNEL * KERNEL
WINDOW = 9
OFFSETS = WINDOW * WINDOW
PIX = CANVAS * CANVAS
PADDED = 104
SPARE = 48
LANES = 128
EPSILON = 1e-06
f32 = jnp.float32
bf16 = jnp.bfloat16
WEST = TAPS
CBIAS, GAIN, SHIFT, BOUT, SCALE = range(TAPS + OFFSETS, TAPS + OFFSETS + 5)
SMALL = TAPS + OFFSETS + 5


def call(kernel, name, out_shape, micros, scratch=(), limit=4, smem=0, left=0, after=(), aliases=None):
    def body(*refs):
        kernel(*refs[len(after) :])

    def run(*args):
        specs = [pl.BlockSpec(memory_space=pl.ANY)] * len(after)
        specs += [pl.BlockSpec(memory_space=pltpu.SMEM)] * smem
        specs += [pl.BlockSpec(memory_space=pl.ANY)] * left
        specs += [pl.BlockSpec(memory_space=pltpu.VMEM)] * (len(args) - smem - left)
        return pl.pallas_call(
            body,
            name=name,
            in_specs=specs,
            out_specs=jax.tree.map(out_space, out_shape),
            out_shape=out_shape,
            input_output_aliases={len(after) + source: target for source, target in (aliases or {}).items()},
            scratch_shapes=list(scratch),
            compiler_params=pltpu.CompilerParams(vmem_limit_bytes=limit * 1024 * 1024),
            cost_estimate=pl.CostEstimate(flops=int(micros * 1.15e9), bytes_accessed=0, transcendentals=0),
        )(*after, *args[:smem], *[in_hbm(value) for value in args[smem : smem + left]], *args[smem + left :])

    return run


def out_space(shape):
    return pl.BlockSpec(memory_space=pltpu.VMEM if isinstance(shape, jax.ShapeDtypeStruct) else pltpu.HBM)


def in_hbm(value):
    return pltpu.with_memory_space_constraint(value, pltpu.HBM)


def gate(values, after):
    space = pl.BlockSpec(memory_space=pl.ANY)
    return pl.pallas_call(
        lambda *refs: None,
        name="gate",
        in_specs=[space] * (len(values) + len(after)),
        out_specs=[space] * len(values),
        out_shape=[array(value.shape, value.dtype) for value in values],
        input_output_aliases={number: number for number in range(len(values))},
        compiler_params=pltpu.CompilerParams(vmem_limit_bytes=1024 * 1024),
        cost_estimate=pl.CostEstimate(flops=0, bytes_accessed=0, transcendentals=0),
    )(*values, *after)


def array(shape, dtype=f32):
    return jax.ShapeDtypeStruct(shape, dtype)


def nt(left, right):
    return lax.dot_general(left, right, (((1,), (1,)), ((), ())), preferred_element_type=f32)


def tn(left, right):
    return lax.dot_general(left, right, (((0,), (0,)), ((), ())), preferred_element_type=f32)


def dot(left, right):
    return jnp.dot(left, right, preferred_element_type=f32)


def split(values):
    high = values.astype(bf16)
    return high, (values - high.astype(f32)).astype(bf16)


def lane_tile(tile):
    return pl.ds(tile * LANES, LANES)


def conv_rows(source, tile, kernel_ref, flip, finish):
    cols = pl.ds(pl.multiple_of(tile * LANES, LANES), LANES)
    for row in range(CANVAS):
        sums = [None] * CANVAS
        for ky in range(KERNEL):
            source_row = row + ky - REACH
            if not 0 <= source_row < CANVAS:
                continue
            cells = [source[tile, pl.ds((source_row * CANVAS + col) * 8, 8), :] for col in range(CANVAS)]
            for kx in range(KERNEL):
                tap = ky * KERNEL + kx
                tap = TAPS - 1 - tap if flip else tap
                weight = jnp.broadcast_to(kernel_ref[pl.ds(tap, 1), cols], (8, LANES))
                for col in range(CANVAS):
                    other = col + kx - REACH
                    if 0 <= other < CANVAS:
                        term = cells[other] * weight
                        sums[col] = term if sums[col] is None else sums[col] + term
        for col in range(CANVAS):
            finish(row * CANVAS + col, sums[col])


def side_of(sizes_ref, images):
    lines = lax.broadcasted_iota(jnp.int32, (2 * images, LANES), 0)
    side = jnp.zeros(lines.shape, jnp.int32)
    for image in range(images):
        side = jnp.where((lines == image) | (lines == images + image), sizes_ref[image], side)
    return side


def conv_tile(x_ref, tile, small_ref, conv_ref, target):
    cols = pl.ds(pl.multiple_of(tile * LANES, LANES), LANES)
    bias = jnp.broadcast_to(small_ref[pl.ds(CBIAS, 1), cols], (8, LANES))

    def finish(cell, total):
        conv_ref[target, pl.ds(cell * 8, 8), :] = total + bias

    conv_rows(x_ref, tile, small_ref, False, finish)


def conv_begin_kernel(
    sizes_ref, features_ref, upstream_ref, small_ref, x_ref, up_ref, conv_ref, features, upstream, sems,
):
    images = features_ref.shape[0]
    frames = 2 * images
    tiles, rows, _ = conv_ref.shape[0] * 2, *conv_ref.shape[1:]
    side = side_of(sizes_ref, images)
    copies = [
        pltpu.make_async_copy(source.at[image], target.at[image], sems.at[number, image])
        for number, (source, target) in enumerate(((features_ref, features), (upstream_ref, upstream)))
        for image in range(images)
    ]
    for copy in copies:
        copy.start()

    def lay(source, image, target):
        for which in range(2):
            for row in range(CANVAS):
                lines = pl.ds(row * CANVAS * frames + which * images + image, CANVAS, stride=frames)
                for tile in range(tiles):
                    target[tile, lines, :] = source[image, which, row, :, lane_tile(tile)].astype(f32)

    for image in range(images):
        copies[image].wait()
        lay(features, image, x_ref)

    @pl.loop(0, tiles)
    def _(tile):
        for cell in range(PIX):
            inside = side > max(cell // CANVAS, cell % CANVAS)
            lines = pl.ds(cell * 8, 8)
            x_ref[tile, lines, :] = jnp.where(inside, x_ref[tile, lines, :], 0.0)

    @pl.loop(0, tiles // 2)
    def _(tile):
        conv_tile(x_ref, tile, small_ref, conv_ref, tile)

    for tile in range(tiles):
        up_ref[tile, pl.ds(rows, SPARE), :] = jnp.zeros((SPARE, LANES), f32)
    for image in range(images):
        copies[images + image].wait()
        lay(upstream, image, up_ref)


def conv_begin(sizes, features, upstream, small, after=()):
    images, channels = features.shape[0], features.shape[-1]
    rows, tiles = PIX * 2 * images, channels // LANES
    shapes = (
        array((tiles, rows + SPARE, LANES)),
        array((tiles, rows + SPARE, LANES)),
        array((tiles // 2, rows, LANES)),
    )
    scratch = [pltpu.VMEM(features.shape, bf16), pltpu.VMEM(features.shape, bf16), pltpu.SemaphoreType.DMA((2, images))]
    return call(conv_begin_kernel, "conv_begin", shapes, 1, scratch, limit=8, smem=1, left=2, after=after)(
        sizes, features, upstream, small
    )


def conv_norm_kernel(where_ref, x_ref, begun_ref, small_ref, normed_ref, pair_ref, xhat_ref, rstd_ref, conv, order):
    tiles, rows = x_ref.shape[0], begun_ref.shape[1]
    channels = tiles * LANES

    @pl.loop(0, tiles // 2)
    def _(tile):
        conv_tile(x_ref, tile + tiles // 2, small_ref, conv, tile)

    share = channels // 8
    core = where_ref[1]
    for tile in range(tiles):
        source = lax.broadcasted_iota(jnp.int32, (channels, LANES), 0)
        target = lax.broadcasted_iota(jnp.int32, (1, LANES), 1) + tile * LANES
        shard = target // share
        wanted = jnp.where(shard < 4, 2 * shard + 1 - core, 2 * (shard - 4) + core) * share + target % share
        order[:, lane_tile(tile)] = (source == wanted).astype(bf16)
    size = 160

    @pl.loop(0, rows // size)
    def _(block):
        lines = pl.ds(pl.multiple_of(block * size, size), size)
        values = [begun_ref[tile, lines, :] for tile in range(tiles // 2)]
        values = jnp.concatenate(values + [conv[tile, lines, :] for tile in range(tiles // 2)], axis=1)
        mean = jnp.sum(values, axis=-1, keepdims=True) * (1.0 / channels)
        centred = values - mean
        variance = jnp.sum(centred * centred, axis=-1, keepdims=True) * (1.0 / channels)
        scale = lax.rsqrt(variance + EPSILON)
        xhat = centred * scale
        xhat_ref[lines, :] = xhat.astype(bf16)
        rstd_ref[lines, :] = scale
        normed = (xhat * small_ref[pl.ds(GAIN, 1), :] + small_ref[pl.ds(SHIFT, 1), :]).astype(bf16)
        normed_ref[lines, :] = normed
        pair_ref[lines, :] = dot(normed, order[...]).astype(bf16)


def conv_norm(where, x, begun, small, after=()):
    tiles, rows = x.shape[0], begun.shape[1]
    channels = tiles * LANES
    low = array((rows, channels), bf16)
    return call(
        conv_norm_kernel,
        "conv_norm",
        (low, low, low, array((rows, 1))),
        1,
        [pltpu.VMEM(begun.shape, f32), pltpu.VMEM((channels, channels), bf16)],
        limit=8,
        smem=1,
        after=after,
    )(where, x, begun, small)


def gelu_pair(hidden):
    cdf = 0.5 * lax.erf(hidden * 0.7071067811865476) + 0.5
    density = jnp.exp(hidden * hidden * -0.5) * 0.3989422804014327
    return hidden * cdf, cdf + hidden * density


def widen_part(group, normed_ref, weight_ref, bias_ref, active_ref, slope_ref, part):
    cols = pl.ds(part * 256, 256)
    quarter = weight_ref.shape[1] // 4
    start = jnp.bitwise_xor(group, part * 256 // quarter) * quarter + part * 256 % quarter
    hidden = dot(normed_ref[...], weight_ref[:, cols]) + bias_ref[:, pl.ds(pl.multiple_of(start, 256), 256)]
    active, slope = gelu_pair(hidden)
    active_ref[:, cols] = active.astype(bf16)
    slope_ref[:, cols] = slope.astype(bf16)


def widen_kernel(normed_ref, weight_ref, bias_ref, active_ref, slope_ref):
    for part in range(weight_ref.shape[1] // 256):
        widen_part(0, normed_ref, weight_ref, bias_ref, active_ref, slope_ref, part)


def widen(normed, weight, bias):
    rows, units = normed.shape[0], weight.shape[1]
    return call(widen_kernel, "widen", (array((rows, units), bf16),) * 2, 6.5, limit=24)(normed, weight, bias)


def crossed(pieces, flip):
    _, to_x, to_y, from_x, from_y = pieces
    left = (to_y.at[0], to_y.at[1], from_y.at[0], from_y.at[1])[flip]
    right = (to_x.at[0], from_x.at[0], to_x.at[1], from_x.at[1])[flip]
    return left, right


def place_widen_kernel(where_ref, *refs):
    pieces, (normed_ref, bias_ref, weight_ref, active_ref, slope_ref) = refs[:10], refs[10:]
    z, core, group, slabs = (where_ref[number] for number in range(4))
    share = pieces[0].shape[0]
    width = pieces[1].shape[3]
    for flip in range(4):
        for side in range(2):
            parity = core if side == 0 else 1 - core
            own_ref = pieces[5 * side]
            for step in range(4):
                shard = 2 * lax.rem(z - step + slabs, slabs) + parity
                lines = pl.ds(pl.multiple_of(shard * share, 16), share)
                if step == 0:
                    source = pl.ds(pl.multiple_of(jnp.bitwise_xor(group, flip) * 2 * width, LANES), 2 * width)
                    weight_ref[lines, pl.ds(flip * 2 * width, 2 * width)] = own_ref[:, source]
                    continue
                for turn, part in enumerate(crossed(pieces[5 * side : 5 * side + 5], flip)):
                    weight_ref[lines, pl.ds((2 * flip + turn) * width, width)] = part[step - 1]
    for part in range(weight_ref.shape[1] // 256):
        widen_part(group, normed_ref, weight_ref, bias_ref, active_ref, slope_ref, part)


def place_widen(where, mine, theirs, normed, bias, after=()):
    share, units = mine[0].shape
    rows, channels = normed.shape
    wide = array((rows, units), bf16)
    shapes = (array((channels, units), bf16), wide, wide)
    return call(place_widen_kernel, "place_widen", shapes, 8, smem=1, after=after)(where, *mine, *theirs, normed, bias)


def narrow_rows(active_ref, weight_ref, small_ref, branch_ref):
    size = 160
    for part in range(active_ref.shape[0] // size):
        lines = pl.ds(part * size, size)
        branch = dot(active_ref[lines, :], weight_ref[...]) + small_ref[pl.ds(BOUT, 1), :]
        for tile in range(branch_ref.shape[0]):
            branch_ref[tile, lines, :] = branch[:, tile * LANES : (tile + 1) * LANES]


def narrow(active, weight, small):
    rows, channels = active.shape[0], weight.shape[1]
    return call(narrow_rows, "narrow", array((channels // LANES, rows, LANES)), 4, limit=24)(active, weight, small)


def place_narrow_kernel(side, where_ref, *refs):
    pieces = refs[:5]
    if side == 0:
        active_ref, small_ref, weight_ref, branch_ref = refs[5:]
    else:
        active_ref, _, begun_ref, weight_ref, branch_ref = refs[5:]
    z, core, group, slabs = (where_ref[number] for number in range(4))
    parity = core if side == 0 else 1 - core
    tall = pieces[0].shape[0]
    _, _, lines, width = pieces[1].shape

    def base(slab):
        return pl.multiple_of(jnp.bitwise_xor(slab, group) * 2 * tall + parity * tall, 16)

    weight_ref[pl.ds(base(z), tall), :] = pieces[0][...]
    for step in range(1, 4):
        for flip in range(4):
            start = base(lax.rem(z - step + slabs, slabs)) + jnp.bitwise_xor(group, flip) * lines
            for turn, part in enumerate(crossed(pieces, flip)):
                weight_ref[pl.ds(pl.multiple_of(start, 16), lines), pl.ds(turn * width, width)] = part[step - 1]
    spans = [pl.ds(pl.multiple_of(part * 2 * tall + parity * tall, LANES), tall) for part in range(4)]
    weight = jnp.concatenate([weight_ref[span, :] for span in spans], axis=0)
    size = 160
    for part in range(active_ref.shape[0] // size):
        rows = pl.ds(part * size, size)
        branch = dot(jnp.concatenate([active_ref[rows, span] for span in spans], axis=1), weight)
        if side == 0:
            branch = branch + small_ref[pl.ds(BOUT, 1), :]
        for tile in range(branch_ref.shape[0]):
            value = branch[:, tile * LANES : (tile + 1) * LANES]
            branch_ref[tile, rows, :] = value if side == 0 else begun_ref[tile, rows, :] + value


def place_narrow(side, where, pieces, active, *more, after=()):
    tall, channels = pieces[0].shape
    rows, units = active.shape
    shapes = (array((units, channels), bf16), array((channels // LANES, rows, LANES)))
    return call(
        functools.partial(place_narrow_kernel, side),
        "place_narrow",
        shapes,
        3,
        smem=1,
        after=after,
        aliases={} if side == 0 else {7: 0},
    )(where, *pieces, active, *more)


def skew(values, inverse):
    rows = lax.broadcasted_iota(jnp.int32, values.shape, 0)
    centre = (WINDOW // 2) * (CANVAS + 1)
    amount = jnp.bitwise_and(rows - centre if inverse else centre - rows, LANES - 1)
    for bit in range(7):
        moved = pltpu.roll(values, 1 << bit, 1)
        values = jnp.where(jnp.bitwise_and(amount, 1 << bit) != 0, moved, values)
    return values


def movers(tiles, frames):
    def take(ref, frame):
        lines = pl.ds(frame, PADDED, stride=frames)
        return jnp.concatenate([ref[tile, lines, :] for tile in range(tiles)], axis=1)

    def put(ref, frame, values):
        lines = pl.ds(frame, PADDED, stride=frames)
        for tile in range(tiles):
            ref[tile, lines, :] = values[:, tile * LANES : (tile + 1) * LANES]

    return take, put


def mix(x_ref, branch_ref, small_ref, mixed):
    tiles, rows, _ = branch_ref.shape
    rest = mixed.shape[1] - rows
    for tile in range(tiles):
        scale = small_ref[pl.ds(SCALE, 1), lane_tile(tile)]
        mixed[tile, pl.ds(0, rows), :] = x_ref[tile, pl.ds(0, rows), :] + scale * branch_ref[tile]
        mixed[tile, pl.ds(rows, rest), :] = jnp.zeros((rest, LANES), f32)


def estimator(place_ref, small_ref, west_in):
    west_in[...] = jnp.zeros_like(west_in)
    west_in[pl.ds(0, OFFSETS), :] = small_ref[pl.ds(WEST, OFFSETS), :]
    lanes = lax.broadcasted_iota(jnp.int32, (LANES, LANES), 0)
    return dot((lanes == place_ref[...]).astype(bf16), west_in[...].astype(bf16)).astype(bf16)


def flow_kernel(
    sizes_ref, x_ref, branch_ref, up_ref, index_ref, weight_ref, place_ref, small_ref, window_ref,
    gated_ref, dmixed_ref, dbranch_ref, gscale_ref, gbout_ref, mixed, back, west_in, warp_in, sem,
):
    tiles, rows, _ = branch_ref.shape
    images = index_ref.shape[0]
    frames = 2 * images
    channels = tiles * LANES
    factor = channels ** (-0.5)
    every = range(images)
    mix(x_ref, branch_ref, small_ref, mixed)
    take, put = movers(tiles, frames)
    west = estimator(place_ref, small_ref, west_in)
    window = window_ref[0]
    reach = window_ref[1]
    cells = lax.broadcasted_iota(jnp.int32, (PIX, LANES), 1)
    warp_in[...] = jnp.zeros_like(warp_in)
    for image in every:
        warp = jnp.zeros((PIX, LANES), f32)
        for corner in range(4):
            place = index_ref[image, :, pl.ds(corner, 1)]
            amount = weight_ref[image, :, pl.ds(corner, 1)]
            warp = warp + jnp.where(cells == place, amount, 0.0)
        warp_in[image, pl.ds(0, PIX), :] = warp
    halves = [split(warp_in[image]) for image in every]
    wide_warps = [jnp.concatenate(pair, axis=1)[:PADDED] for pair in halves]
    tall_warps = [jnp.concatenate(pair, axis=0) for pair in halves]
    rest = jnp.zeros((LANES - PADDED, channels), f32)

    def twice(values):
        value = jnp.concatenate([values, rest], axis=0).astype(bf16)
        return jnp.concatenate([value, value], axis=0)

    inside = [(reach < sizes_ref[image].astype(f32)).astype(f32)[:, :1] for image in every]
    first = [take(mixed, image) * inside[image] for image in every]
    second = [take(mixed, images + image) * inside[image] for image in every]
    first_low = [value.astype(bf16) for value in first]
    warped = [dot(warp, twice(value)) for warp, value in zip(wide_warps, second)]
    warped = [jnp.concatenate([value, rest], axis=0).astype(bf16) for value in warped]
    scores = [nt(left, right) for left, right in zip(first_low, warped)]
    costs = [skew(value, False) * window * factor for value in scores]
    pairs = [gelu_pair(value) for value in costs]
    for image, (value, _) in enumerate(pairs):
        gated_ref[image] = value.astype(bf16)
    d_firsts = [take(up_ref, image) * inside[image] for image in every]
    d_heads = [value.astype(bf16) for value in d_firsts]
    d_costs = [slope * nt(d_head, west) * window * factor for (_, slope), d_head in zip(pairs, d_heads)]
    d_scores = [skew(value, True).astype(bf16) for value in d_costs]
    for image in every:
        put(back, image, d_firsts[image] + dot(d_scores[image], warped[image]))
    d_warped = [tn(value, low)[:PADDED] for value, low in zip(d_scores, first_low)]
    for image in every:
        d_second = take(up_ref, images + image) + tn(tall_warps[image], twice(d_warped[image]))[:PADDED]
        put(back, images + image, d_second * inside[image])
    save = pltpu.make_async_copy(back.at[:, pl.ds(0, rows)], dmixed_ref, sem)
    save.start()
    for tile in range(tiles):
        cols = lane_tile(tile)
        d_mixed = back[tile, pl.ds(0, rows), :]
        gscale_ref[:, cols] = jnp.sum(d_mixed * branch_ref[tile], axis=0, keepdims=True)
        d_branch = (d_mixed * small_ref[pl.ds(SCALE, 1), cols]).astype(bf16)
        dbranch_ref[:, cols] = d_branch
        gbout_ref[:, cols] = jnp.sum(d_branch.astype(f32), axis=0, keepdims=True)
    save.wait()


def finish_kernel(
    sizes_ref, lane_ref, x_ref, branch_ref, up_ref, gated_ref, place_ref, small_ref, window_ref,
    out_ref, gwest_ref, mixed, west_in, lanes,
):
    tiles, _, _ = x_ref.shape
    images = gated_ref.shape[0]
    frames = 2 * images
    take, put = movers(tiles, frames)
    mix(x_ref, branch_ref, small_ref, mixed)
    west = estimator(place_ref, small_ref, west_in)
    reach = window_ref[1]
    for image in range(images):
        inside = (reach < sizes_ref[image].astype(f32)).astype(f32)[:, :1]
        gated = gated_ref[image]
        part = tn(gated, (take(up_ref, image) * inside).astype(bf16))
        lanes[...] = part if image == 0 else lanes[...] + part
        put(mixed, image, (take(mixed, image) * inside + dot(gated, west)) * inside)
        put(mixed, images + image, take(mixed, images + image) * inside)
    for offset in range(OFFSETS):
        gwest_ref[pl.ds(offset, 1), :] = lanes[pl.ds(lane_ref[offset], 1), :]
    for image in range(images):
        for which in range(2):
            for row in range(CANVAS):
                lines = pl.ds(row * CANVAS * frames + which * images + image, CANVAS, stride=frames)
                for tile in range(tiles):
                    out_ref[image, which, row, :, lane_tile(tile)] = mixed[tile, lines, :].astype(bf16)


def finish(sizes, lane_of, x, branch, up, gated, place, small, after=()):
    tiles, rows, _ = branch.shape
    images, channels = gated.shape[0], tiles * LANES
    return call(
        finish_kernel,
        "finish",
        (array((images, 2, CANVAS, CANVAS, channels), bf16), array((OFFSETS, channels))),
        0.01,
        [pltpu.VMEM((tiles, rows + SPARE, LANES), f32)] + [pltpu.VMEM((LANES, channels), f32)] * 2,
        limit=10,
        smem=2,
        after=after,
    )(sizes, lane_of, x, branch, up, gated, place, small, jnp.asarray(tables()))


def tables():
    cells = np.arange(PADDED)[:, None]
    lane = np.arange(LANES)[None, :]
    reach = WINDOW // 2
    row = cells // CANVAS + lane // CANVAS - reach
    col = cells % CANVAS + lane % CANVAS - reach
    good = (lane % CANVAS < WINDOW) & (lane // CANVAS < WINDOW) & (cells < PIX)
    good &= (row >= 0) & (row < CANVAS) & (col >= 0) & (col < CANVAS)
    far = np.maximum(cells // CANVAS, cells % CANVAS) + 0 * lane
    return np.stack([good, far]).astype(np.float32)


def flow(sizes, x, branch, up, index, weight, place, small, after=()):
    tiles, rows, _ = branch.shape
    images, channels = index.shape[0], tiles * LANES
    padded = pltpu.VMEM((tiles, PADDED * 2 * images, LANES), f32)
    vector = array((1, channels))
    return call(
        flow_kernel,
        "flow",
        (
            array((images, PADDED, LANES), bf16),
            pltpu.HBM(branch.shape, f32),
            array((rows, channels), bf16),
            vector,
            vector,
        ),
        6.5,
        [padded, padded, pltpu.VMEM((LANES, channels), f32), pltpu.VMEM((images, LANES, LANES), f32), pltpu.SemaphoreType.DMA],
        limit=14,
        smem=1,
        after=after,
    )(sizes, x, branch, up, index, weight, place, small, jnp.asarray(tables()))


def grad_narrow_kernel(where_ref, active_ref, dbranch_ref, out_ref):
    count, tile, _ = out_ref.shape
    for part in range(count):
        block = 2 * jnp.bitwise_xor(part, where_ref[2]) + 1 - where_ref[1] if count < 8 else part
        cols = pl.ds(pl.multiple_of(block * tile, LANES), tile)
        out_ref[part] = tn(active_ref[:, cols], dbranch_ref[...]).astype(bf16)


def grad_narrow(where, active, dbranch, count, after=()):
    units, channels = active.shape[1], dbranch.shape[1]
    shape = array((count, units // 8, channels), bf16)
    return call(grad_narrow_kernel, "grad_narrow", shape, 0.3 * count, limit=2 * count, smem=1, after=after)(where, active, dbranch)


def send_halves(where_ref, blocks, keep_ref, left_ref, right_ref):
    x, y = lax.rem(where_ref[2], 2), where_ref[2] // 2
    for turn in range(2):
        keep_ref[0, turn] = blocks[2 * x + turn]
        keep_ref[1, turn] = blocks[4 + 2 * y + turn]
        left_ref[turn] = blocks[2 * (1 - x) + turn]
        right_ref[turn] = blocks[4 + 2 * (1 - y) + turn]


def halves_of(lines, width):
    half = array((2, lines, width), bf16)
    return (array((2, 2, lines, width), bf16), half, half), [pltpu.VMEM((8, lines, width), bf16)]


def grad_narrow_here_kernel(where_ref, active_ref, dbranch_ref, received_ref, keep_ref, left_ref, right_ref, blocks):
    count, tile, _ = received_ref.shape
    lines = tile // 8
    for part in range(count):
        block = 2 * jnp.bitwise_xor(part, where_ref[2]) + where_ref[1]
        cols = pl.ds(pl.multiple_of(block * tile, LANES), tile)
        total = tn(active_ref[:, cols], dbranch_ref[...]) + received_ref[part].astype(f32)
        for block in range(8):
            blocks[block, pl.ds(part * lines, lines), :] = total[block * lines : (block + 1) * lines].astype(bf16)
    send_halves(where_ref, blocks, keep_ref, left_ref, right_ref)


def grad_narrow_here(where, active, dbranch, received, after=()):
    count, tile, channels = received.shape
    shapes, scratch = halves_of(count * tile // 8, channels)
    return call(grad_narrow_here_kernel, "grad_narrow_here", shapes, 0.1, scratch, limit=6, smem=1, after=after)(
        where, active, dbranch, received
    )


def hidden_back_kernel(where_ref, dbranch_ref, weight_ref, slope_ref, dhidden_ref, gbin_ref):
    tile = slope_ref.shape[1] // 4
    for part in range(4):
        cols = pl.ds(part * tile, tile)
        d_active = nt(dbranch_ref[...], weight_ref[cols, :])
        d_hidden = (d_active * slope_ref[:, cols].astype(f32)).astype(bf16)
        dhidden_ref[:, cols] = d_hidden
        start = jnp.bitwise_xor(part, where_ref[2]) * tile
        gbin_ref[:, pl.ds(pl.multiple_of(start, LANES), tile)] = jnp.sum(d_hidden.astype(f32), axis=0, keepdims=True)


def hidden_back(where, dbranch, weight, slope, after=()):
    rows, units = slope.shape
    shapes = (array((rows, units), bf16), array((1, units)))
    return call(hidden_back_kernel, "hidden_back", shapes, 2, smem=1, after=after)(
        where, dbranch, weight, slope
    )


def grad_widen_full_kernel(normed_ref, dhidden_ref, out_ref):
    tile = 768
    for part in range(out_ref.shape[1] // tile):
        cols = pl.ds(part * tile, tile)
        out_ref[:, cols] = tn(normed_ref[...], dhidden_ref[:, cols]).astype(bf16)


def grad_widen_full(normed, dhidden):
    shape = array((normed.shape[1], dhidden.shape[1]), bf16)
    return call(grad_widen_full_kernel, "grad_widen_full", shape, 5, limit=24)(normed, dhidden)


def grad_widen_away_kernel(where_ref, pair_ref, dhidden_ref, out_ref):
    blocks, lines, width = out_ref.shape
    for part in range(blocks // 2):
        total = tn(pair_ref[:, pl.ds(0, lines)], dhidden_ref[:, pl.ds(2 * part * width, 2 * width)]).astype(bf16)
        block = 2 * jnp.bitwise_xor(part, where_ref[2])
        out_ref[block] = total[:, :width]
        out_ref[block + 1] = total[:, width:]


def grad_widen_away(where, pair, dhidden, after=()):
    shape = array((8, pair.shape[1] // 2, dhidden.shape[1] // 8), bf16)
    return call(grad_widen_away_kernel, "grad_widen_away", shape, 0.01, smem=1, after=after)(where, pair, dhidden)


def grad_widen_here_kernel(where_ref, pair_ref, dhidden_ref, received_ref, keep_ref, left_ref, right_ref, blocks):
    _, lines, width = blocks.shape
    for part in range(4):
        both = tn(pair_ref[:, pl.ds(lines, lines)], dhidden_ref[:, pl.ds(2 * part * width, 2 * width)])
        for turn in range(2):
            block = 2 * jnp.bitwise_xor(part, where_ref[2]) + turn
            value = both[:, turn * width : (turn + 1) * width] + received_ref[block].astype(f32)
            blocks[block] = value.astype(bf16)
    send_halves(where_ref, blocks, keep_ref, left_ref, right_ref)


def grad_widen_here(where, pair, dhidden, received, after=()):
    shapes, scratch = halves_of(*received.shape[1:])
    return call(grad_widen_here_kernel, "grad_widen_here", shapes, 0.01, scratch, limit=6, smem=1, after=after)(
        where, pair, dhidden, received
    )


def norm_back_kernel(dhidden_ref, weight_ref, xhat_ref, rstd_ref, small_ref, dconv_ref, sums_ref):
    rows, channels = xhat_ref.shape
    size = 160
    gain = small_ref[pl.ds(GAIN, 1), :]
    sums = [jnp.zeros((1, channels), f32)] * 3
    for part in range(rows // size):
        lines = pl.ds(part * size, size)
        d_normed = nt(dhidden_ref[lines, :], weight_ref[...])
        xhat = xhat_ref[lines, :].astype(f32)
        product = d_normed * xhat
        d_xhat = d_normed * gain
        mean = jnp.sum(d_xhat, axis=-1, keepdims=True) * (1.0 / channels)
        along = jnp.sum(product * gain, axis=-1, keepdims=True) * (1.0 / channels)
        d_conv = (d_xhat - mean - xhat * along) * rstd_ref[lines, :]
        for tile in range(dconv_ref.shape[0]):
            dconv_ref[tile, lines, :] = d_conv[:, tile * LANES : (tile + 1) * LANES]
        for number, value in enumerate((d_conv, product, d_normed)):
            sums[number] = sums[number] + jnp.sum(value, axis=0, keepdims=True)
    sums_ref[...] = jnp.concatenate(sums, axis=0)


def norm_back(dhidden, weight, xhat, rstd, small, after=()):
    rows, channels = xhat.shape
    return call(
        norm_back_kernel, "norm_back", (array((channels // LANES, rows, LANES)), array((3, channels))), 0.01, after=after
    )(dhidden, weight, xhat, rstd, small)


def grad_taps_kernel(x_ref, dconv_ref, out_ref):
    @pl.loop(0, x_ref.shape[0])
    def _(tile):
        cols = pl.ds(pl.multiple_of(tile * LANES, LANES), LANES)
        for ky in range(KERNEL):
            totals = [None] * KERNEL
            for row in range(CANVAS):
                source_row = row + ky - REACH
                if not 0 <= source_row < CANVAS:
                    continue
                cells = [x_ref[tile, pl.ds((source_row * CANVAS + col) * 8, 8), :] for col in range(CANVAS)]
                grads = [dconv_ref[tile, pl.ds((row * CANVAS + col) * 8, 8), :] for col in range(CANVAS)]
                for kx in range(KERNEL):
                    for col in range(CANVAS):
                        source = col + kx - REACH
                        if 0 <= source < CANVAS:
                            term = cells[source] * grads[col]
                            totals[kx] = term if totals[kx] is None else totals[kx] + term
            for kx in range(KERNEL):
                out_ref[pl.ds(ky * KERNEL + kx, 1), cols] = jnp.sum(totals[kx], axis=0, keepdims=True)


def grad_taps(x, dconv, after=()):
    return call(grad_taps_kernel, "grad_taps", array((TAPS, x.shape[0] * LANES)), 0.01, after=after)(x, dconv)


def conv_back_kernel(sizes_ref, dconv_ref, small_ref, dmixed_ref, out_ref, total):
    tiles = dconv_ref.shape[0]
    images = out_ref.shape[0]
    frames = 2 * images
    side = side_of(sizes_ref, images)

    @pl.loop(0, tiles)
    def _(tile):
        def finish(cell, value):
            lines = pl.ds(cell * 8, 8)
            inside = side > max(cell // CANVAS, cell % CANVAS)
            total[tile, lines, :] = jnp.where(inside, value + dmixed_ref[tile, lines, :], 0.0)

        conv_rows(dconv_ref, tile, small_ref, True, finish)

    for image in range(images):
        for which in range(2):
            for row in range(CANVAS):
                lines = pl.ds(row * CANVAS * frames + which * images + image, CANVAS, stride=frames)
                for tile in range(tiles):
                    out_ref[image, which, row, :, lane_tile(tile)] = total[tile, lines, :]


def conv_back(sizes, dconv, small, dmixed, after=()):
    tiles, rows, _ = dconv.shape
    images = sizes.shape[0]
    return call(
        conv_back_kernel,
        "conv_back",
        array((images, 2, CANVAS, CANVAS, tiles * LANES)),
        0.1,
        [pltpu.VMEM((tiles, rows + SPARE, LANES), f32)],
        limit=6,
        smem=1,
        after=after,
    )(sizes, dconv, small, dmixed)


def start_all(copies, sems):
    running = [pltpu.make_async_copy(source, target, sems.at[number]) for number, (source, target) in enumerate(copies)]
    for copy in running:
        copy.start()
    return running

GROUPS = 6
LINES = 24
BIAS = SMALL


def pack_kernel(where_ref, weight_ref, taps_ref, west_ref, *refs):
    vectors, (bias_ref, out_ref, small, taps, west, *held, bias, sems) = refs[:5], refs[5:]
    share = weight_ref.shape[0]
    wide = out_ref.shape[1]
    cols = pl.ds(pl.multiple_of(where_ref[2] * wide, LANES), wide)
    copies = [(taps_ref, taps), (west_ref, west), (bias_ref, bias)]
    copies += list(zip(vectors, held))
    copies += [(weight_ref.at[:, cols], out_ref.at[pl.ds(0, share)])]
    running = start_all(copies, sems)
    small[...] = jnp.zeros_like(small)
    lane = pl.ds(0, share)
    for copy in running[:-1]:
        copy.wait()
    small[pl.ds(0, TAPS), lane] = taps[...].astype(f32)
    small[pl.ds(WEST, OFFSETS), lane] = west[...].astype(f32)
    for number, vector in enumerate(held):
        small[pl.ds(CBIAS + number, 1), lane] = vector[...].astype(f32).reshape(1, share)
    for part in range(bias.shape[0] // LANES):
        small[pl.ds(BIAS + part, 1), :] = bias[lane_tile(part)].astype(f32).reshape(1, LANES)
    for group in range(GROUPS):
        out_ref[pl.ds(share, LINES), lane_tile(group)] = small[pl.ds(group * LINES, LINES), :].astype(bf16)
    running[-1].wait()


def pack(where, weight, taps, west, vectors, bias, after=()):
    share, units = weight.shape
    args = (weight, taps, west, *vectors, bias)
    return call(
        pack_kernel,
        "pack",
        array((share + LINES, units // 4), bf16),
        2,
        [
            pltpu.VMEM((GROUPS * LINES, LANES), f32),
            pltpu.VMEM(taps.shape, bf16),
            pltpu.VMEM(west.shape, bf16),
            *[pltpu.VMEM((share,), bf16)] * len(vectors),
            pltpu.VMEM(bias.shape, bf16),
            pltpu.SemaphoreType.DMA((len(args),)),
        ],
        smem=1,
        left=len(args),
        after=after,
    )(where, *args)


def stack_kernel(*refs):
    first = refs[0].shape[0] - LINES
    for number, ref in enumerate(refs[:-1]):
        refs[-1][number] = ref[pl.ds(first, LINES), :]


def stack(parts, after=()):
    shape = array((len(parts), LINES, parts[0].shape[1]), bf16)
    return call(stack_kernel, "stack", shape, 0.05, after=after)(*parts)


def unpack_kernel(where_ref, mine_ref, theirs_ref, small_ref, bias_ref):
    z, core, slabs = where_ref[0], where_ref[1], where_ref[3]
    channels = small_ref.shape[1]
    share = channels // 8
    everything = None
    for number in range(8):
        ref = mine_ref if number < 4 else theirs_ref
        shard = 2 * lax.rem(z - number % 4 + slabs, slabs) + (core if number < 4 else 1 - core)
        rows = jnp.concatenate([ref[number % 4, :, lane_tile(group)].astype(f32) for group in range(GROUPS)], axis=0)
        source = lax.broadcasted_iota(jnp.int32, (LANES, channels), 0)
        target = lax.broadcasted_iota(jnp.int32, (LANES, channels), 1)
        spread = ((target - shard * share == source) & (source < share)).astype(bf16)
        value = dot(rows.astype(bf16), spread)
        everything = value if everything is None else everything + value
        width = bias_ref.shape[1] // 8
        for part in range(width // LANES):
            cols = pl.ds(pl.multiple_of(shard * width + part * LANES, LANES), LANES)
            bias_ref[:, cols] = rows[BIAS + part : BIAS + part + 1, :]
    small_ref[...] = everything[: small_ref.shape[0]]


def unpack(where, mine, theirs, units, channels):
    return call(unpack_kernel, "unpack", (array((SMALL, channels)), array((1, units))), 1.2, smem=1)(where, mine, theirs)


def column_kernel(*refs):
    parts, outs = refs[:-2], refs[-2:]
    rows, width = outs[0].shape[1:]
    for turn, out in enumerate(outs):
        for number, part in enumerate(parts):
            out[number] = part[pl.ds(0, rows), pl.ds(turn * width, width)]


def column(parts, rows, after=()):
    half = array((len(parts), rows, parts[0].shape[1] // 2), bf16)
    return call(column_kernel, "column", (half, half), 0.05, after=after)(*parts)


def cut_kernel(where_ref, weight_ref, out_ref, sem):
    tall = out_ref.shape[0]
    lines = pl.ds(pl.multiple_of(where_ref[2] * tall, 16), tall)
    copy = pltpu.make_async_copy(weight_ref.at[lines], out_ref, sem)
    copy.start()
    copy.wait()


def cut(where, weight, after=()):
    tall, channels = weight.shape
    shape = array((tall // 4, channels), bf16)
    return call(cut_kernel, "cut", shape, 1, [pltpu.SemaphoreType.DMA], smem=1, left=1, after=after)(where, weight)


def onward_kernel(left_ref, right_ref, left_in_ref, right_in_ref, to_x_ref, to_y_ref):
    to_y_ref[0] = left_ref[...]
    to_y_ref[1] = left_in_ref[...]
    to_x_ref[0] = right_ref[...]
    to_x_ref[1] = right_in_ref[...]


def onward(left, right, left_in, right_in, after=()):
    shape = array((2, *left.shape), bf16)
    return call(onward_kernel, "onward", (shape, shape), 1, after=after)(left, right, left_in, right_in)


def halve_kernel(where_ref, keep_ref, left_in_ref, right_in_ref, keep_out_ref, left_ref, right_ref):
    x, y = lax.rem(where_ref[2], 2), where_ref[2] // 2

    def total(side, which):
        received = left_in_ref if side == 0 else right_in_ref
        return keep_ref[side, which].astype(f32) + received[which].astype(f32)

    keep_out_ref[0] = total(0, y).astype(bf16)
    keep_out_ref[1] = total(1, x).astype(bf16)
    left_ref[...] = total(0, 1 - y).astype(bf16)
    right_ref[...] = total(1, 1 - x).astype(bf16)


def halve(where, keep, left_in, right_in, after=()):
    _, _, lines, width = keep.shape
    half = array((lines, width), bf16)
    shapes = (array((2, lines, width), bf16), half, half)
    return call(halve_kernel, "halve", shapes, 0.01, smem=1, after=after)(where, keep, left_in, right_in)


def deal_total(where_ref, keep_ref, left_in_ref, right_in_ref, total):
    total[0] = (keep_ref[0].astype(f32) + left_in_ref[...].astype(f32)).astype(bf16)
    total[1] = (keep_ref[1].astype(f32) + right_in_ref[...].astype(f32)).astype(bf16)


def deal_kernel(where_ref, keep_ref, left_in_ref, right_in_ref, *refs):
    outs, total = refs[:-1], refs[-1]
    share = outs[0].shape[1]
    deal_total(where_ref, keep_ref, left_in_ref, right_in_ref, total)
    for step, out in enumerate(outs):
        slab = lax.rem(where_ref[0] + step, len(outs))
        for side in range(2):
            out[side] = total[side, pl.ds(pl.multiple_of(slab * share, 16), share), :]


def deal(where, keep, left_in, right_in, slabs, after=()):
    _, lines, width = keep.shape
    shapes = (array((2, lines // slabs, width), bf16),) * slabs
    scratch = [pltpu.VMEM(keep.shape, bf16)]
    return call(deal_kernel, "deal", shapes, 0.01, scratch, smem=1, after=after)(where, keep, left_in, right_in)


SMALL_ROWS = 144


def deal_small_kernel(where_ref, keep_ref, left_in_ref, right_in_ref, here_ref, received_ref, *refs):
    outs, total = refs[:-1], refs[-1]
    deal_total(where_ref, keep_ref, left_in_ref, right_in_ref, total)
    share = total.shape[1] // len(outs)
    extra = outs[0].shape[1] - share
    for step, out in enumerate(outs):
        slab = lax.rem(where_ref[0] + step, len(outs))
        small = here_ref[slab] + received_ref[slab]
        lines = SMALL_ROWS // 4
        small = jnp.concatenate([small[part * lines : (part + 1) * lines] for part in range(4)], axis=1)
        for side in range(2):
            out[side, pl.ds(0, share), :] = total[side, pl.ds(pl.multiple_of(slab * share, 16), share), :]
            out[side, pl.ds(share, extra), :] = small[side * extra : (side + 1) * extra].astype(bf16)


def deal_small(where, keep, left_in, right_in, here, received, after=()):
    slabs = here.shape[0]
    _, lines, width = keep.shape
    extra = SMALL_ROWS * here.shape[2] // width // 2
    shapes = (array((2, lines // slabs + extra, width), bf16),) * slabs
    scratch = [pltpu.VMEM(keep.shape, bf16)]
    return call(deal_small_kernel, "deal_small", shapes, 0.01, scratch, smem=1, after=after)(
        where, keep, left_in, right_in, here, received
    )


def total_kernel(*refs):
    total = refs[0][...].astype(f32)
    for ref in refs[1:-1]:
        total = total + ref[...].astype(f32)
    refs[-1][...] = total.astype(refs[-1].dtype)


def total(values, after=()):
    return call(total_kernel, "total", array(values[0].shape, values[0].dtype), 1, after=after)(*values)


def blocks_of(where_ref, flip):
    group = jnp.bitwise_xor(where_ref[2], flip)
    x, y = lax.rem(group, 2), group // 2
    return 2 * x + y, 4 + 2 * y + x


def spread_wout_kernel(where_ref, *refs):
    *values, out_ref = refs
    lines = values[0].shape[1]
    for flip, ref in enumerate(values):
        for side, block in enumerate(blocks_of(where_ref, flip)):
            out_ref[pl.ds(pl.multiple_of(block * lines, 16), lines), :] = ref[side].astype(f32)


def spread_wout(where, values, after=()):
    _, lines, channels = values[0].shape
    return call(spread_wout_kernel, "spread_wout", array((8 * lines, channels)), 1, smem=1, after=after)(where, *values)


def spread_win_kernel(where_ref, *refs):
    values, (out_ref, taps_ref, west_ref, bias_ref, *vectors, small) = refs[:4], refs[4:]
    share = out_ref.shape[0]
    _, lines, width = values[0].shape
    extra = lines - share
    for flip, ref in enumerate(values):
        for side, block in enumerate(blocks_of(where_ref, flip)):
            out_ref[:, pl.ds(pl.multiple_of(block * width, LANES), width)] = ref[side, pl.ds(0, share), :].astype(f32)
    for side in range(2):
        part = [ref[side, pl.ds(share, extra), :].astype(f32) for ref in values]
        both = (part[0] + part[1]) + (part[2] + part[3])
        for group in range(4):
            span = pl.ds(group * 2 * extra + side * extra, extra)
            small[span, :] = both[:, group * share : (group + 1) * share]
    taps_ref[...] = small[pl.ds(0, TAPS), :]
    for number, ref in enumerate(vectors):
        ref[...] = small[pl.ds(TAPS + number, 1), :]
    west_ref[...] = small[pl.ds(TAPS + 5, OFFSETS), :]
    rows = bias_ref.shape[0] // share
    first = TAPS + 5 + OFFSETS
    bias_ref[...] = jnp.concatenate([small[pl.ds(first + row, 1), :] for row in range(rows)], axis=1).reshape(bias_ref.shape)


def spread_win(where, values, share, after=()):
    width = values[0].shape[2]
    shapes = [array((share, 8 * width)), array((TAPS, share)), array((OFFSETS, share)), array((width,))]
    shapes += [array((1, share))] * 5
    scratch = [pltpu.VMEM((SMALL_ROWS, share), f32)]
    return call(spread_win_kernel, "spread_win", shapes, 1, scratch, smem=1, after=after)(where, *values)


def pack_small_kernel(where_ref, gtaps_ref, gnorm_ref, gbout_ref, gscale_ref, gwest_ref, gbin_ref, here_ref, away_ref):
    slabs, _, share = here_ref.shape

    def fill(even_ref, odd_ref):
        for shard in range(2 * slabs):
            out = odd_ref if shard % 2 else even_ref
            cols = pl.ds(shard * share, share)
            line = 0
            for ref in (gtaps_ref, gnorm_ref, gbout_ref, gscale_ref, gwest_ref):
                out[shard // 2, pl.ds(line, ref.shape[0]), :] = ref[:, cols]
                line += ref.shape[0]
            lines = gbin_ref.shape[1] // gtaps_ref.shape[1]
            for extra in range(lines):
                span = pl.ds((shard * lines + extra) * share, share)
                out[shard // 2, pl.ds(line + extra, 1), :] = gbin_ref[:, span]
            rest = SMALL_ROWS - line - lines
            out[shard // 2, pl.ds(line + lines, rest), :] = jnp.zeros((rest, share), f32)

    @pl.when(where_ref[1] == 0)
    def _():
        fill(here_ref, away_ref)

    @pl.when(where_ref[1] == 1)
    def _():
        fill(away_ref, here_ref)


def pack_small(where, parts, slabs, share, after=()):
    shape = array((slabs, SMALL_ROWS, share))
    return call(pack_small_kernel, "pack_small", (shape, shape), 0.01, smem=1, after=after)(where, *parts)


AXES = ("dp", "fsdp")


class Routes:
    def __init__(self, groups, members):
        self.groups, self.members, self.slabs = groups, members, members // 2
        self.group = lax.axis_index("dp")
        member = lax.axis_index("fsdp")
        self.slab, self.core = member // 2, member % 2

    def send(self, value, target):
        pairs = [
            (group * self.members + 2 * slab + core, self.index(*target(group, slab, core)))
            for group in range(self.groups)
            for slab in range(self.slabs)
            for core in range(2)
        ]
        return lax.ppermute(value, AXES, pairs)

    def index(self, group, slab, core):
        return group * self.members + 2 * slab + core

    def to_core(self, value):
        return self.send(value, lambda group, slab, core: (group, slab, 1 - core))

    def to_slab(self, value, step):
        return self.send(value, lambda group, slab, core: (group, (slab + step) % self.slabs, core))

    def to_near(self, value, flip):
        return self.send(value, lambda group, slab, core: (group, slab ^ flip, core))

    def to_group(self, value, flip):
        return self.send(value, lambda group, slab, core: (group ^ flip, slab, core))


def shards(
    features,
    cotangent,
    image_sizes,
    warp_index,
    warp_weight,
    offsets,
    conv_kernel,
    conv_bias,
    norm_gain,
    norm_bias,
    w_in,
    bias_in,
    w_out,
    bias_out,
    layer_scale,
    w_estimate,
):
    share, units = w_in.shape
    channels = features.shape[-1]
    members = channels // share
    groups = lax.axis_size("dp")
    paired = groups == 4 and members == 8

    reach = WINDOW // 2
    lane_of = (offsets[:, 0] + reach) * CANVAS + offsets[:, 1] + reach
    place = jnp.pad(lane_of, (0, LANES - OFFSETS), constant_values=-1)[None]

    early = (features, cotangent, warp_index, warp_weight, place, lane_of)
    if paired:
        routes = Routes(groups, members)
        slabs = routes.slabs
        where = jnp.stack([routes.slab, routes.core, routes.group, jnp.int32(slabs)])
        vectors = (conv_bias, norm_gain, norm_bias, bias_out, layer_scale)
        packed = pack(where, w_in, conv_kernel, w_estimate, vectors, bias_in)
        win_parts = [routes.to_slab(packed, step) for step in range(1, slabs)]
        win_own = routes.to_core(w_in)
        small = stack([packed, *win_parts], after=early)
        quarter = cut(where, w_out, after=(packed,))
        wout_parts = [routes.to_slab(quarter, step) for step in range(1, slabs)]
        wout_own = routes.to_core(w_out)
        small, bin_all = unpack(where, small, routes.to_core(small), units, channels)
    else:
        where = jnp.zeros((4,), jnp.int32)
        small = jnp.concatenate(
            [
                conv_kernel,
                w_estimate,
                jnp.stack([conv_bias, norm_gain, norm_bias, bias_out, layer_scale]),
                bias_in.reshape(-1, share),
            ]
        )
        small = lax.all_gather(small, "fsdp")
        win_all = lax.all_gather(w_in, "fsdp", axis=0, tiled=True)
        wout_all = lax.all_gather(w_out, "fsdp", axis=0, tiled=True)
        bin_all = small[:, SMALL:].reshape(1, units).astype(f32)
        small = small[:, :SMALL].transpose(1, 0, 2).reshape(SMALL, channels).astype(f32)
    after = ()
    if paired:
        left, right = column(win_parts, share, after=(wout_parts[0],))
        left_in, right_in = routes.to_group(left, 1), routes.to_group(right, 2)
        after = (left,)
    x, up, begun = conv_begin(image_sizes, features, cotangent, small, after)
    if paired:
        to_x, to_y = onward(left, right, left_in, right_in, after=(begun,))
        win_halves = [to_x, to_y, routes.to_group(to_x, 1), routes.to_group(to_y, 2)]
        left, right = column(wout_parts, units // members // 4, after=(to_x,))
        left_in, right_in = routes.to_group(left, 1), routes.to_group(right, 2)
        after = (left,)
    normed, pair, xhat, rstd = conv_norm(where, x, begun, small, after)
    if paired:
        to_x, to_y = onward(left, right, left_in, right_in, after=(normed,))
        wout_halves = [to_x, to_y, routes.to_group(to_x, 1), routes.to_group(to_y, 2)]
        win_halves = gate(win_halves, (to_x,))
        win_theirs = [win_own] + [routes.to_core(value) for value in win_halves]
        win_all, active, slope = place_widen(where, [w_in, *win_halves], win_theirs, normed, bin_all)
        wout_halves = gate(wout_halves, (active,))
        wout_theirs = [wout_own] + [routes.to_core(value) for value in wout_halves]
        begun = place_narrow(0, where, [w_out, *wout_halves], active, small)
        wout_all, branch = place_narrow(1, where, wout_theirs, active, *begun)
    else:
        active, slope = widen(normed, win_all, bin_all)
        branch = narrow(active, wout_all, small)
    gated, d_mixed, d_branch, g_scale, g_bout = flow(
        image_sizes, x, branch, up, warp_index, warp_weight, place, small
    )
    if paired:
        wout_away = grad_narrow(where, active, d_branch, slabs)
        wout_in = routes.to_core(wout_away)
        d_hidden, g_bin = hidden_back(where, d_branch, wout_all, slope, after=(wout_away,))
        keep_out, left, right = grad_narrow_here(where, active, d_branch, wout_in, after=(d_hidden,))
        left_out, right_out = routes.to_group(left, 1), routes.to_group(right, 2)
        win_away = grad_widen_away(where, pair, d_hidden, after=(keep_out,))
        win_in = routes.to_core(win_away)
        mixed_out, g_west = finish(image_sizes, lane_of, x, branch, up, gated, place, small, after=(win_away,))
        keep_in, left, right = grad_widen_here(where, pair, d_hidden, win_in, after=(g_west,))
        left_in, right_in = routes.to_group(left, 1), routes.to_group(right, 2)
        d_conv, g_norm = norm_back(d_hidden, win_all, xhat, rstd, small, after=(keep_in,))
        keep_out, left, right = halve(where, keep_out, left_out, right_out, after=(d_conv,))
        left_out, right_out = routes.to_group(left, 2), routes.to_group(right, 1)
        g_taps = grad_taps(x, d_conv, after=(keep_out,))
        parts = (g_taps, g_norm, g_bout, g_scale, g_west, g_bin)
        small_here, small_away = pack_small(where, parts, slabs, share)
        small_in = routes.to_core(small_away)
        keep_in, left, right = halve(where, keep_in, left_in, right_in, after=(small_away,))
        left_in, right_in = routes.to_group(left, 2), routes.to_group(right, 1)
        wout_parts = deal(where, keep_out, left_out, right_out, slabs, after=(keep_in,))
        wout_parts = wout_parts[:1] + tuple(routes.to_slab(v, n + 1) for n, v in enumerate(wout_parts[1:]))
        win_parts = deal_small(where, keep_in, left_in, right_in, small_here, small_in, after=wout_parts[:1])
        win_parts = win_parts[:1] + tuple(routes.to_slab(v, n + 1) for n, v in enumerate(win_parts[1:]))
        grad_features = conv_back(image_sizes, d_conv, small, d_mixed, after=win_parts[:1])
        g_wout = total(wout_parts, after=(grad_features,))
        wout_parts = [g_wout] + [routes.to_group(g_wout, flip) for flip in range(1, 4)]
        g_win = total(win_parts, after=(g_wout,))
        win_parts = [g_win] + [routes.to_group(g_win, flip) for flip in range(1, 4)]
        g_wout = spread_wout(where, wout_parts, after=(g_win,))
        g_win, g_taps, g_west, g_bin, *g_small = spread_win(where, win_parts, share)
        g_small = [value.reshape(share) for value in g_small]
    else:
        g_wout = grad_narrow(where, active, d_branch, 8).reshape(units, channels)
        d_hidden, g_bin = hidden_back(where, d_branch, wout_all, slope)
        g_win = grad_widen_full(normed, d_hidden)
        d_conv, g_norm = norm_back(d_hidden, win_all, xhat, rstd, small)
        g_taps = grad_taps(x, d_conv)
        mixed_out, g_west = finish(image_sizes, lane_of, x, branch, up, gated, place, small)
        grad_features = conv_back(image_sizes, d_conv, small, d_mixed)
        g_small = jnp.concatenate([g_taps, g_norm, g_bout, g_scale, g_west])
        g_small = g_small.reshape(-1, members, share).transpose(1, 0, 2)
        g_small = jnp.concatenate([g_small, g_bin.reshape(members, -1, share)], axis=1)

        def reduce(value):
            return lax.psum(lax.psum_scatter(value, "fsdp", scatter_dimension=0, tiled=True).astype(f32), "dp")

        g_wout, g_win, g_small = reduce(g_wout), reduce(g_win), reduce(g_small)[0]
        tail = TAPS + 5 + OFFSETS
        g_taps, g_west, g_bin = g_small[:TAPS], g_small[TAPS + 5 : tail], g_small[tail:]
        g_small = g_small[TAPS : TAPS + 5]
    return (
        mixed_out,
        grad_features,
        g_taps,
        g_small[0],
        g_small[1],
        g_small[2],
        g_win,
        g_bin.reshape(-1),
        g_wout,
        g_small[3],
        g_small[4],
        g_west,
    )


def solution(mesh):
    in_specs = (
        P(("dp", "fsdp"), None, None, None, None),
        P(("dp", "fsdp"), None, None, None, None),
        P(("dp", "fsdp")),
        P(("dp", "fsdp"), None, None),
        P(("dp", "fsdp"), None, None),
        P(),
        P(None, "fsdp"),
        P("fsdp"),
        P("fsdp"),
        P("fsdp"),
        P("fsdp", None),
        P("fsdp"),
        P("fsdp", None),
        P("fsdp"),
        P("fsdp"),
        P(None, "fsdp"),
    )
    out_specs = (
        P(("dp", "fsdp"), None, None, None, None),
        P(("dp", "fsdp"), None, None, None, None),
        P(None, "fsdp"),
        P("fsdp"),
        P("fsdp"),
        P("fsdp"),
        P("fsdp", None),
        P("fsdp"),
        P("fsdp", None),
        P("fsdp"),
        P("fsdp"),
        P(None, "fsdp"),
    )
    return jax.shard_map(shards, mesh=mesh, in_specs=in_specs, out_specs=out_specs, check_vma=False)
```

```python
import functools

import jax
import jax.numpy as jnp
import numpy as np
from jax import lax
from jax.experimental import pallas as pl
from jax.experimental.pallas import tpu as pltpu
from jax.sharding import PartitionSpec as P

CANVAS = 10
KERNEL = 7
REACH = KERNEL // 2
TAPS = KERNEL * KERNEL
WINDOW = 9
OFFSETS = WINDOW * WINDOW
PIX = CANVAS * CANVAS
PADDED = 104
SPARE = 48
LANES = 128
EPSILON = 1e-06
f32 = jnp.float32
bf16 = jnp.bfloat16
WEST = TAPS
CBIAS, GAIN, SHIFT, BOUT, SCALE = range(TAPS + OFFSETS, TAPS + OFFSETS + 5)
SMALL = TAPS + OFFSETS + 5


def call(kernel, name, out_shape, micros, scratch=(), limit=4, smem=0, left=0, after=(), aliases=None):
    def body(*refs):
        kernel(*refs[len(after) :])

    def run(*args):
        specs = [pl.BlockSpec(memory_space=pl.ANY)] * len(after)
        specs += [pl.BlockSpec(memory_space=pltpu.SMEM)] * smem
        specs += [pl.BlockSpec(memory_space=pl.ANY)] * left
        specs += [pl.BlockSpec(memory_space=pltpu.VMEM)] * (len(args) - smem - left)
        return pl.pallas_call(
            body,
            name=name,
            in_specs=specs,
            out_specs=jax.tree.map(out_space, out_shape),
            out_shape=out_shape,
            input_output_aliases={len(after) + source: target for source, target in (aliases or {}).items()},
            scratch_shapes=list(scratch),
            compiler_params=pltpu.CompilerParams(vmem_limit_bytes=limit * 1024 * 1024),
            cost_estimate=pl.CostEstimate(flops=int(micros * 1.15e9), bytes_accessed=0, transcendentals=0),
        )(*after, *args[:smem], *[in_hbm(value) for value in args[smem : smem + left]], *args[smem + left :])

    return run


def out_space(shape):
    return pl.BlockSpec(memory_space=pltpu.VMEM if isinstance(shape, jax.ShapeDtypeStruct) else pltpu.HBM)


def in_hbm(value):
    return pltpu.with_memory_space_constraint(value, pltpu.HBM)


def gate(values, after):
    space = pl.BlockSpec(memory_space=pl.ANY)
    return pl.pallas_call(
        lambda *refs: None,
        name="gate",
        in_specs=[space] * (len(values) + len(after)),
        out_specs=[space] * len(values),
        out_shape=[array(value.shape, value.dtype) for value in values],
        input_output_aliases={number: number for number in range(len(values))},
        compiler_params=pltpu.CompilerParams(vmem_limit_bytes=1024 * 1024),
        cost_estimate=pl.CostEstimate(flops=0, bytes_accessed=0, transcendentals=0),
    )(*values, *after)


def array(shape, dtype=f32):
    return jax.ShapeDtypeStruct(shape, dtype)


def nt(left, right):
    return lax.dot_general(left, right, (((1,), (1,)), ((), ())), preferred_element_type=f32)


def tn(left, right):
    return lax.dot_general(left, right, (((0,), (0,)), ((), ())), preferred_element_type=f32)


def dot(left, right):
    return jnp.dot(left, right, preferred_element_type=f32)


def split(values):
    high = values.astype(bf16)
    return high, (values - high.astype(f32)).astype(bf16)


def lane_tile(tile):
    return pl.ds(tile * LANES, LANES)


def conv_rows(source, tile, kernel_ref, flip, finish):
    cols = pl.ds(pl.multiple_of(tile * LANES, LANES), LANES)
    for row in range(CANVAS):
        sums = [None] * CANVAS
        for ky in range(KERNEL):
            source_row = row + ky - REACH
            if not 0 <= source_row < CANVAS:
                continue
            cells = [source[tile, pl.ds((source_row * CANVAS + col) * 8, 8), :] for col in range(CANVAS)]
            for kx in range(KERNEL):
                tap = ky * KERNEL + kx
                tap = TAPS - 1 - tap if flip else tap
                weight = jnp.broadcast_to(kernel_ref[pl.ds(tap, 1), cols], (8, LANES))
                for col in range(CANVAS):
                    other = col + kx - REACH
                    if 0 <= other < CANVAS:
                        term = cells[other] * weight
                        sums[col] = term if sums[col] is None else sums[col] + term
        for col in range(CANVAS):
            finish(row * CANVAS + col, sums[col])


def side_of(sizes_ref, images):
    lines = lax.broadcasted_iota(jnp.int32, (2 * images, LANES), 0)
    side = jnp.zeros(lines.shape, jnp.int32)
    for image in range(images):
        side = jnp.where((lines == image) | (lines == images + image), sizes_ref[image], side)
    return side


def conv_tile(x_ref, tile, small_ref, conv_ref, target):
    cols = pl.ds(pl.multiple_of(tile * LANES, LANES), LANES)
    bias = jnp.broadcast_to(small_ref[pl.ds(CBIAS, 1), cols], (8, LANES))

    def finish(cell, total):
        conv_ref[target, pl.ds(cell * 8, 8), :] = total + bias

    conv_rows(x_ref, tile, small_ref, False, finish)


def conv_begin_kernel(
    sizes_ref, features_ref, upstream_ref, small_ref, x_ref, up_ref, conv_ref, features, upstream, sems,
):
    images = features_ref.shape[0]
    frames = 2 * images
    tiles, rows, _ = conv_ref.shape[0] * 2, *conv_ref.shape[1:]
    side = side_of(sizes_ref, images)
    copies = [
        pltpu.make_async_copy(source.at[image], target.at[image], sems.at[number, image])
        for number, (source, target) in enumerate(((features_ref, features), (upstream_ref, upstream)))
        for image in range(images)
    ]
    for copy in copies:
        copy.start()

    def lay(source, image, target):
        for which in range(2):
            for row in range(CANVAS):
                lines = pl.ds(row * CANVAS * frames + which * images + image, CANVAS, stride=frames)
                for tile in range(tiles):
                    target[tile, lines, :] = source[image, which, row, :, lane_tile(tile)].astype(f32)

    for image in range(images):
        copies[image].wait()
        lay(features, image, x_ref)

    @pl.loop(0, tiles)
    def _(tile):
        for cell in range(PIX):
            inside = side > max(cell // CANVAS, cell % CANVAS)
            lines = pl.ds(cell * 8, 8)
            x_ref[tile, lines, :] = jnp.where(inside, x_ref[tile, lines, :], 0.0)

    @pl.loop(0, tiles // 2)
    def _(tile):
        conv_tile(x_ref, tile, small_ref, conv_ref, tile)

    for tile in range(tiles):
        up_ref[tile, pl.ds(rows, SPARE), :] = jnp.zeros((SPARE, LANES), f32)
    for image in range(images):
        copies[images + image].wait()
        lay(upstream, image, up_ref)


def conv_begin(sizes, features, upstream, small, after=()):
    images, channels = features.shape[0], features.shape[-1]
    rows, tiles = PIX * 2 * images, channels // LANES
    shapes = (
        array((tiles, rows + SPARE, LANES)),
        array((tiles, rows + SPARE, LANES)),
        array((tiles // 2, rows, LANES)),
    )
    scratch = [pltpu.VMEM(features.shape, bf16), pltpu.VMEM(features.shape, bf16), pltpu.SemaphoreType.DMA((2, images))]
    return call(conv_begin_kernel, "conv_begin", shapes, 1, scratch, limit=8, smem=1, left=2, after=after)(
        sizes, features, upstream, small
    )


def conv_norm_kernel(where_ref, x_ref, begun_ref, small_ref, normed_ref, pair_ref, xhat_ref, rstd_ref, conv, order):
    tiles, rows = x_ref.shape[0], begun_ref.shape[1]
    channels = tiles * LANES

    @pl.loop(0, tiles // 2)
    def _(tile):
        conv_tile(x_ref, tile + tiles // 2, small_ref, conv, tile)

    share = channels // 8
    core = where_ref[1]
    for tile in range(tiles):
        source = lax.broadcasted_iota(jnp.int32, (channels, LANES), 0)
        target = lax.broadcasted_iota(jnp.int32, (1, LANES), 1) + tile * LANES
        shard = target // share
        wanted = jnp.where(shard < 4, 2 * shard + 1 - core, 2 * (shard - 4) + core) * share + target % share
        order[:, lane_tile(tile)] = (source == wanted).astype(bf16)
    size = 160

    @pl.loop(0, rows // size)
    def _(block):
        lines = pl.ds(pl.multiple_of(block * size, size), size)
        values = [begun_ref[tile, lines, :] for tile in range(tiles // 2)]
        values = jnp.concatenate(values + [conv[tile, lines, :] for tile in range(tiles // 2)], axis=1)
        mean = jnp.sum(values, axis=-1, keepdims=True) * (1.0 / channels)
        centred = values - mean
        variance = jnp.sum(centred * centred, axis=-1, keepdims=True) * (1.0 / channels)
        scale = lax.rsqrt(variance + EPSILON)
        xhat = centred * scale
        xhat_ref[lines, :] = xhat.astype(bf16)
        rstd_ref[lines, :] = scale
        normed = (xhat * small_ref[pl.ds(GAIN, 1), :] + small_ref[pl.ds(SHIFT, 1), :]).astype(bf16)
        normed_ref[lines, :] = normed
        pair_ref[lines, :] = dot(normed, order[...]).astype(bf16)


def conv_norm(where, x, begun, small, after=()):
    tiles, rows = x.shape[0], begun.shape[1]
    channels = tiles * LANES
    low = array((rows, channels), bf16)
    return call(
        conv_norm_kernel,
        "conv_norm",
        (low, low, low, array((rows, 1))),
        1,
        [pltpu.VMEM(begun.shape, f32), pltpu.VMEM((channels, channels), bf16)],
        limit=8,
        smem=1,
        after=after,
    )(where, x, begun, small)


def gelu_pair(hidden):
    cdf = 0.5 * lax.erf(hidden * 0.7071067811865476) + 0.5
    density = jnp.exp(hidden * hidden * -0.5) * 0.3989422804014327
    return hidden * cdf, cdf + hidden * density


def widen_part(group, normed_ref, weight_ref, bias_ref, active_ref, slope_ref, part):
    cols = pl.ds(part * 256, 256)
    quarter = weight_ref.shape[1] // 4
    start = jnp.bitwise_xor(group, part * 256 // quarter) * quarter + part * 256 % quarter
    hidden = dot(normed_ref[...], weight_ref[:, cols]) + bias_ref[:, pl.ds(pl.multiple_of(start, 256), 256)]
    active, slope = gelu_pair(hidden)
    active_ref[:, cols] = active.astype(bf16)
    slope_ref[:, cols] = slope.astype(bf16)


def widen_kernel(normed_ref, weight_ref, bias_ref, active_ref, slope_ref):
    for part in range(weight_ref.shape[1] // 256):
        widen_part(0, normed_ref, weight_ref, bias_ref, active_ref, slope_ref, part)


def widen(normed, weight, bias):
    rows, units = normed.shape[0], weight.shape[1]
    return call(widen_kernel, "widen", (array((rows, units), bf16),) * 2, 6.5, limit=24)(normed, weight, bias)


def crossed(pieces, flip):
    _, to_x, to_y, from_x, from_y = pieces
    left = (to_y.at[0], to_y.at[1], from_y.at[0], from_y.at[1])[flip]
    right = (to_x.at[0], from_x.at[0], to_x.at[1], from_x.at[1])[flip]
    return left, right


def place_widen_kernel(where_ref, *refs):
    pieces, (normed_ref, bias_ref, weight_ref, active_ref, slope_ref) = refs[:10], refs[10:]
    z, core, group, slabs = (where_ref[number] for number in range(4))
    share = pieces[0].shape[0]
    width = pieces[1].shape[3]
    for flip in range(4):
        for side in range(2):
            parity = core if side == 0 else 1 - core
            own_ref = pieces[5 * side]
            for step in range(4):
                shard = 2 * lax.rem(z - step + slabs, slabs) + parity
                lines = pl.ds(pl.multiple_of(shard * share, 16), share)
                if step == 0:
                    source = pl.ds(pl.multiple_of(jnp.bitwise_xor(group, flip) * 2 * width, LANES), 2 * width)
                    weight_ref[lines, pl.ds(flip * 2 * width, 2 * width)] = own_ref[:, source]
                    continue
                for turn, part in enumerate(crossed(pieces[5 * side : 5 * side + 5], flip)):
                    weight_ref[lines, pl.ds((2 * flip + turn) * width, width)] = part[step - 1]
    for part in range(weight_ref.shape[1] // 256):
        widen_part(group, normed_ref, weight_ref, bias_ref, active_ref, slope_ref, part)


def place_widen(where, mine, theirs, normed, bias, after=()):
    share, units = mine[0].shape
    rows, channels = normed.shape
    wide = array((rows, units), bf16)
    shapes = (array((channels, units), bf16), wide, wide)
    return call(place_widen_kernel, "place_widen", shapes, 8, smem=1, after=after)(where, *mine, *theirs, normed, bias)


def narrow_rows(active_ref, weight_ref, small_ref, branch_ref):
    size = 160
    for part in range(active_ref.shape[0] // size):
        lines = pl.ds(part * size, size)
        branch = dot(active_ref[lines, :], weight_ref[...]) + small_ref[pl.ds(BOUT, 1), :]
        for tile in range(branch_ref.shape[0]):
            branch_ref[tile, lines, :] = branch[:, tile * LANES : (tile + 1) * LANES]


def narrow(active, weight, small):
    rows, channels = active.shape[0], weight.shape[1]
    return call(narrow_rows, "narrow", array((channels // LANES, rows, LANES)), 4, limit=24)(active, weight, small)


def place_narrow_kernel(side, where_ref, *refs):
    pieces = refs[:5]
    if side == 0:
        active_ref, small_ref, weight_ref, branch_ref = refs[5:]
    else:
        active_ref, _, begun_ref, weight_ref, branch_ref = refs[5:]
    z, core, group, slabs = (where_ref[number] for number in range(4))
    parity = core if side == 0 else 1 - core
    tall = pieces[0].shape[0]
    _, _, lines, width = pieces[1].shape

    def base(slab):
        return pl.multiple_of(jnp.bitwise_xor(slab, group) * 2 * tall + parity * tall, 16)

    weight_ref[pl.ds(base(z), tall), :] = pieces[0][...]
    for step in range(1, 4):
        for flip in range(4):
            start = base(lax.rem(z - step + slabs, slabs)) + jnp.bitwise_xor(group, flip) * lines
            for turn, part in enumerate(crossed(pieces, flip)):
                weight_ref[pl.ds(pl.multiple_of(start, 16), lines), pl.ds(turn * width, width)] = part[step - 1]
    spans = [pl.ds(pl.multiple_of(part * 2 * tall + parity * tall, LANES), tall) for part in range(4)]
    weight = jnp.concatenate([weight_ref[span, :] for span in spans], axis=0)
    size = 160
    for part in range(active_ref.shape[0] // size):
        rows = pl.ds(part * size, size)
        branch = dot(jnp.concatenate([active_ref[rows, span] for span in spans], axis=1), weight)
        if side == 0:
            branch = branch + small_ref[pl.ds(BOUT, 1), :]
        for tile in range(branch_ref.shape[0]):
            value = branch[:, tile * LANES : (tile + 1) * LANES]
            branch_ref[tile, rows, :] = value if side == 0 else begun_ref[tile, rows, :] + value


def place_narrow(side, where, pieces, active, *more, after=()):
    tall, channels = pieces[0].shape
    rows, units = active.shape
    shapes = (array((units, channels), bf16), array((channels // LANES, rows, LANES)))
    return call(
        functools.partial(place_narrow_kernel, side),
        "place_narrow",
        shapes,
        3,
        smem=1,
        after=after,
        aliases={} if side == 0 else {7: 0},
    )(where, *pieces, active, *more)


def skew(values, inverse):
    rows = lax.broadcasted_iota(jnp.int32, values.shape, 0)
    centre = (WINDOW // 2) * (CANVAS + 1)
    amount = jnp.bitwise_and(rows - centre if inverse else centre - rows, LANES - 1)
    for bit in range(7):
        moved = pltpu.roll(values, 1 << bit, 1)
        values = jnp.where(jnp.bitwise_and(amount, 1 << bit) != 0, moved, values)
    return values


def movers(tiles, frames):
    def take(ref, frame):
        lines = pl.ds(frame, PADDED, stride=frames)
        return jnp.concatenate([ref[tile, lines, :] for tile in range(tiles)], axis=1)

    def put(ref, frame, values):
        lines = pl.ds(frame, PADDED, stride=frames)
        for tile in range(tiles):
            ref[tile, lines, :] = values[:, tile * LANES : (tile + 1) * LANES]

    return take, put


def mix(x_ref, branch_ref, small_ref, mixed):
    tiles, rows, _ = branch_ref.shape
    rest = mixed.shape[1] - rows
    for tile in range(tiles):
        scale = small_ref[pl.ds(SCALE, 1), lane_tile(tile)]
        mixed[tile, pl.ds(0, rows), :] = x_ref[tile, pl.ds(0, rows), :] + scale * branch_ref[tile]
        mixed[tile, pl.ds(rows, rest), :] = jnp.zeros((rest, LANES), f32)


def estimator(place_ref, small_ref, west_in):
    west_in[...] = jnp.zeros_like(west_in)
    west_in[pl.ds(0, OFFSETS), :] = small_ref[pl.ds(WEST, OFFSETS), :]
    lanes = lax.broadcasted_iota(jnp.int32, (LANES, LANES), 0)
    return dot((lanes == place_ref[...]).astype(bf16), west_in[...].astype(bf16)).astype(bf16)


def flow_kernel(
    sizes_ref, x_ref, branch_ref, up_ref, index_ref, weight_ref, place_ref, small_ref, window_ref,
    gated_ref, dmixed_ref, dbranch_ref, gscale_ref, gbout_ref, mixed, back, west_in, warp_in, sem,
):
    tiles, rows, _ = branch_ref.shape
    images = index_ref.shape[0]
    frames = 2 * images
    channels = tiles * LANES
    factor = channels ** (-0.5)
    every = range(images)
    mix(x_ref, branch_ref, small_ref, mixed)
    take, put = movers(tiles, frames)
    west = estimator(place_ref, small_ref, west_in)
    window = window_ref[0]
    reach = window_ref[1]
    cells = lax.broadcasted_iota(jnp.int32, (PIX, LANES), 1)
    warp_in[...] = jnp.zeros_like(warp_in)
    for image in every:
        warp = jnp.zeros((PIX, LANES), f32)
        for corner in range(4):
            place = index_ref[image, :, pl.ds(corner, 1)]
            amount = weight_ref[image, :, pl.ds(corner, 1)]
            warp = warp + jnp.where(cells == place, amount, 0.0)
        warp_in[image, pl.ds(0, PIX), :] = warp
    halves = [split(warp_in[image]) for image in every]
    wide_warps = [jnp.concatenate(pair, axis=1)[:PADDED] for pair in halves]
    tall_warps = [jnp.concatenate(pair, axis=0) for pair in halves]
    rest = jnp.zeros((LANES - PADDED, channels), f32)

    def twice(values):
        value = jnp.concatenate([values, rest], axis=0).astype(bf16)
        return jnp.concatenate([value, value], axis=0)

    inside = [(reach < sizes_ref[image].astype(f32)).astype(f32)[:, :1] for image in every]
    first = [take(mixed, image) * inside[image] for image in every]
    second = [take(mixed, images + image) * inside[image] for image in every]
    first_low = [value.astype(bf16) for value in first]
    warped = [dot(warp, twice(value)) for warp, value in zip(wide_warps, second)]
    warped = [jnp.concatenate([value, rest], axis=0).astype(bf16) for value in warped]
    scores = [nt(left, right) for left, right in zip(first_low, warped)]
    costs = [skew(value, False) * window * factor for value in scores]
    pairs = [gelu_pair(value) for value in costs]
    for image, (value, _) in enumerate(pairs):
        gated_ref[image] = value.astype(bf16)
    d_firsts = [take(up_ref, image) * inside[image] for image in every]
    d_heads = [value.astype(bf16) for value in d_firsts]
    d_costs = [slope * nt(d_head, west) * window * factor for (_, slope), d_head in zip(pairs, d_heads)]
    d_scores = [skew(value, True).astype(bf16) for value in d_costs]
    for image in every:
        put(back, image, d_firsts[image] + dot(d_scores[image], warped[image]))
    d_warped = [tn(value, low)[:PADDED] for value, low in zip(d_scores, first_low)]
    for image in every:
        d_second = take(up_ref, images + image) + tn(tall_warps[image], twice(d_warped[image]))[:PADDED]
        put(back, images + image, d_second * inside[image])
    save = pltpu.make_async_copy(back.at[:, pl.ds(0, rows)], dmixed_ref, sem)
    save.start()
    for tile in range(tiles):
        cols = lane_tile(tile)
        d_mixed = back[tile, pl.ds(0, rows), :]
        gscale_ref[:, cols] = jnp.sum(d_mixed * branch_ref[tile], axis=0, keepdims=True)
        d_branch = (d_mixed * small_ref[pl.ds(SCALE, 1), cols]).astype(bf16)
        dbranch_ref[:, cols] = d_branch
        gbout_ref[:, cols] = jnp.sum(d_branch.astype(f32), axis=0, keepdims=True)
    save.wait()


def finish_kernel(
    sizes_ref, lane_ref, x_ref, branch_ref, up_ref, gated_ref, place_ref, small_ref, window_ref,
    out_ref, gwest_ref, mixed, west_in, lanes,
):
    tiles, _, _ = x_ref.shape
    images = gated_ref.shape[0]
    frames = 2 * images
    take, put = movers(tiles, frames)
    mix(x_ref, branch_ref, small_ref, mixed)
    west = estimator(place_ref, small_ref, west_in)
    reach = window_ref[1]
    for image in range(images):
        inside = (reach < sizes_ref[image].astype(f32)).astype(f32)[:, :1]
        gated = gated_ref[image]
        part = tn(gated, (take(up_ref, image) * inside).astype(bf16))
        lanes[...] = part if image == 0 else lanes[...] + part
        put(mixed, image, (take(mixed, image) * inside + dot(gated, west)) * inside)
        put(mixed, images + image, take(mixed, images + image) * inside)
    for offset in range(OFFSETS):
        gwest_ref[pl.ds(offset, 1), :] = lanes[pl.ds(lane_ref[offset], 1), :]
    for image in range(images):
        for which in range(2):
            for row in range(CANVAS):
                lines = pl.ds(row * CANVAS * frames + which * images + image, CANVAS, stride=frames)
                for tile in range(tiles):
                    out_ref[image, which, row, :, lane_tile(tile)] = mixed[tile, lines, :].astype(bf16)


def finish(sizes, lane_of, x, branch, up, gated, place, small, after=()):
    tiles, rows, _ = branch.shape
    images, channels = gated.shape[0], tiles * LANES
    return call(
        finish_kernel,
        "finish",
        (array((images, 2, CANVAS, CANVAS, channels), bf16), array((OFFSETS, channels))),
        0.01,
        [pltpu.VMEM((tiles, rows + SPARE, LANES), f32)] + [pltpu.VMEM((LANES, channels), f32)] * 2,
        limit=10,
        smem=2,
        after=after,
    )(sizes, lane_of, x, branch, up, gated, place, small, jnp.asarray(tables()))


def tables():
    cells = np.arange(PADDED)[:, None]
    lane = np.arange(LANES)[None, :]
    reach = WINDOW // 2
    row = cells // CANVAS + lane // CANVAS - reach
    col = cells % CANVAS + lane % CANVAS - reach
    good = (lane % CANVAS < WINDOW) & (lane // CANVAS < WINDOW) & (cells < PIX)
    good &= (row >= 0) & (row < CANVAS) & (col >= 0) & (col < CANVAS)
    far = np.maximum(cells // CANVAS, cells % CANVAS) + 0 * lane
    return np.stack([good, far]).astype(np.float32)


def flow(sizes, x, branch, up, index, weight, place, small, after=()):
    tiles, rows, _ = branch.shape
    images, channels = index.shape[0], tiles * LANES
    padded = pltpu.VMEM((tiles, PADDED * 2 * images, LANES), f32)
    vector = array((1, channels))
    return call(
        flow_kernel,
        "flow",
        (
            array((images, PADDED, LANES), bf16),
            pltpu.HBM(branch.shape, f32),
            array((rows, channels), bf16),
            vector,
            vector,
        ),
        6.5,
        [padded, padded, pltpu.VMEM((LANES, channels), f32), pltpu.VMEM((images, LANES, LANES), f32), pltpu.SemaphoreType.DMA],
        limit=14,
        smem=1,
        after=after,
    )(sizes, x, branch, up, index, weight, place, small, jnp.asarray(tables()))


def grad_narrow_kernel(where_ref, active_ref, dbranch_ref, out_ref):
    count, tile, _ = out_ref.shape
    for first in range(0, count, 2):
        spans = []
        for part in (first, first + 1):
            block = 2 * jnp.bitwise_xor(part, where_ref[2]) + 1 - where_ref[1] if count < 8 else part
            spans.append(pl.ds(pl.multiple_of(block * tile, LANES), tile))
        both = tn(jnp.concatenate([active_ref[:, span] for span in spans], axis=1), dbranch_ref[...]).astype(bf16)
        out_ref[first] = both[:tile]
        out_ref[first + 1] = both[tile:]


def grad_narrow(where, active, dbranch, count, after=()):
    units, channels = active.shape[1], dbranch.shape[1]
    shape = array((count, units // 8, channels), bf16)
    return call(grad_narrow_kernel, "grad_narrow", shape, 0.3 * count, limit=2 * count, smem=1, after=after)(where, active, dbranch)


def send_halves(where_ref, blocks, keep_ref, left_ref, right_ref):
    x, y = lax.rem(where_ref[2], 2), where_ref[2] // 2
    for turn in range(2):
        keep_ref[0, turn] = blocks[2 * x + turn]
        keep_ref[1, turn] = blocks[4 + 2 * y + turn]
        left_ref[turn] = blocks[2 * (1 - x) + turn]
        right_ref[turn] = blocks[4 + 2 * (1 - y) + turn]


def halves_of(lines, width):
    half = array((2, lines, width), bf16)
    return (array((2, 2, lines, width), bf16), half, half), [pltpu.VMEM((8, lines, width), bf16)]


def grad_narrow_here_kernel(where_ref, active_ref, dbranch_ref, received_ref, keep_ref, left_ref, right_ref, blocks):
    count, tile, _ = received_ref.shape
    lines = tile // 8
    for first in range(0, count, 2):
        spans = []
        for part in (first, first + 1):
            block = 2 * jnp.bitwise_xor(part, where_ref[2]) + where_ref[1]
            spans.append(pl.ds(pl.multiple_of(block * tile, LANES), tile))
        both = tn(jnp.concatenate([active_ref[:, span] for span in spans], axis=1), dbranch_ref[...])
        for turn in range(2):
            part = first + turn
            total = both[turn * tile : (turn + 1) * tile] + received_ref[part].astype(f32)
            for block in range(8):
                blocks[block, pl.ds(part * lines, lines), :] = total[block * lines : (block + 1) * lines].astype(bf16)
    send_halves(where_ref, blocks, keep_ref, left_ref, right_ref)


def grad_narrow_here(where, active, dbranch, received, after=()):
    count, tile, channels = received.shape
    shapes, scratch = halves_of(count * tile // 8, channels)
    return call(grad_narrow_here_kernel, "grad_narrow_here", shapes, 0.1, scratch, limit=10, smem=1, after=after)(
        where, active, dbranch, received
    )


def hidden_back_kernel(where_ref, dbranch_ref, weight_ref, slope_ref, dhidden_ref, gbin_ref):
    tile = slope_ref.shape[1] // 4
    for part in range(4):
        cols = pl.ds(part * tile, tile)
        d_active = nt(dbranch_ref[...], weight_ref[cols, :])
        d_hidden = (d_active * slope_ref[:, cols].astype(f32)).astype(bf16)
        dhidden_ref[:, cols] = d_hidden
        start = jnp.bitwise_xor(part, where_ref[2]) * tile
        gbin_ref[:, pl.ds(pl.multiple_of(start, LANES), tile)] = jnp.sum(d_hidden.astype(f32), axis=0, keepdims=True)


def hidden_back(where, dbranch, weight, slope, after=()):
    rows, units = slope.shape
    shapes = (array((rows, units), bf16), array((1, units)))
    return call(hidden_back_kernel, "hidden_back", shapes, 2, smem=1, after=after)(
        where, dbranch, weight, slope
    )


def grad_widen_full_kernel(normed_ref, dhidden_ref, out_ref):
    tile = 768
    for part in range(out_ref.shape[1] // tile):
        cols = pl.ds(part * tile, tile)
        out_ref[:, cols] = tn(normed_ref[...], dhidden_ref[:, cols]).astype(bf16)


def grad_widen_full(normed, dhidden):
    shape = array((normed.shape[1], dhidden.shape[1]), bf16)
    return call(grad_widen_full_kernel, "grad_widen_full", shape, 5, limit=24)(normed, dhidden)


def grad_widen_away_kernel(where_ref, pair_ref, dhidden_ref, out_ref):
    blocks, lines, width = out_ref.shape
    for part in range(blocks // 2):
        total = tn(pair_ref[:, pl.ds(0, lines)], dhidden_ref[:, pl.ds(2 * part * width, 2 * width)]).astype(bf16)
        block = 2 * jnp.bitwise_xor(part, where_ref[2])
        out_ref[block] = total[:, :width]
        out_ref[block + 1] = total[:, width:]


def grad_widen_away(where, pair, dhidden, after=()):
    shape = array((8, pair.shape[1] // 2, dhidden.shape[1] // 8), bf16)
    return call(grad_widen_away_kernel, "grad_widen_away", shape, 0.01, smem=1, after=after)(where, pair, dhidden)


def grad_widen_here_kernel(where_ref, pair_ref, dhidden_ref, received_ref, keep_ref, left_ref, right_ref, blocks):
    _, lines, width = blocks.shape
    for part in range(4):
        both = tn(pair_ref[:, pl.ds(lines, lines)], dhidden_ref[:, pl.ds(2 * part * width, 2 * width)])
        for turn in range(2):
            block = 2 * jnp.bitwise_xor(part, where_ref[2]) + turn
            value = both[:, turn * width : (turn + 1) * width] + received_ref[block].astype(f32)
            blocks[block] = value.astype(bf16)
    send_halves(where_ref, blocks, keep_ref, left_ref, right_ref)


def grad_widen_here(where, pair, dhidden, received, after=()):
    shapes, scratch = halves_of(*received.shape[1:])
    return call(grad_widen_here_kernel, "grad_widen_here", shapes, 0.01, scratch, limit=6, smem=1, after=after)(
        where, pair, dhidden, received
    )


def norm_back_kernel(dhidden_ref, weight_ref, xhat_ref, rstd_ref, small_ref, dconv_ref, sums_ref):
    rows, channels = xhat_ref.shape
    size = 160
    gain = small_ref[pl.ds(GAIN, 1), :]
    sums = [jnp.zeros((1, channels), f32)] * 3
    for part in range(rows // size):
        lines = pl.ds(part * size, size)
        d_normed = nt(dhidden_ref[lines, :], weight_ref[...])
        xhat = xhat_ref[lines, :].astype(f32)
        product = d_normed * xhat
        d_xhat = d_normed * gain
        mean = jnp.sum(d_xhat, axis=-1, keepdims=True) * (1.0 / channels)
        along = jnp.sum(product * gain, axis=-1, keepdims=True) * (1.0 / channels)
        d_conv = (d_xhat - mean - xhat * along) * rstd_ref[lines, :]
        for tile in range(dconv_ref.shape[0]):
            dconv_ref[tile, lines, :] = d_conv[:, tile * LANES : (tile + 1) * LANES]
        for number, value in enumerate((d_conv, product, d_normed)):
            sums[number] = sums[number] + jnp.sum(value, axis=0, keepdims=True)
    sums_ref[...] = jnp.concatenate(sums, axis=0)


def norm_back(dhidden, weight, xhat, rstd, small, after=()):
    rows, channels = xhat.shape
    return call(
        norm_back_kernel, "norm_back", (array((channels // LANES, rows, LANES)), array((3, channels))), 0.01, after=after
    )(dhidden, weight, xhat, rstd, small)


def grad_taps_kernel(x_ref, dconv_ref, out_ref):
    @pl.loop(0, x_ref.shape[0])
    def _(tile):
        cols = pl.ds(pl.multiple_of(tile * LANES, LANES), LANES)
        for ky in range(KERNEL):
            totals = [None] * KERNEL
            for row in range(CANVAS):
                source_row = row + ky - REACH
                if not 0 <= source_row < CANVAS:
                    continue
                cells = [x_ref[tile, pl.ds((source_row * CANVAS + col) * 8, 8), :] for col in range(CANVAS)]
                grads = [dconv_ref[tile, pl.ds((row * CANVAS + col) * 8, 8), :] for col in range(CANVAS)]
                for kx in range(KERNEL):
                    for col in range(CANVAS):
                        source = col + kx - REACH
                        if 0 <= source < CANVAS:
                            term = cells[source] * grads[col]
                            totals[kx] = term if totals[kx] is None else totals[kx] + term
            for kx in range(KERNEL):
                out_ref[pl.ds(ky * KERNEL + kx, 1), cols] = jnp.sum(totals[kx], axis=0, keepdims=True)


def grad_taps(x, dconv, after=()):
    return call(grad_taps_kernel, "grad_taps", array((TAPS, x.shape[0] * LANES)), 0.01, after=after)(x, dconv)


def conv_back_kernel(sizes_ref, dconv_ref, small_ref, dmixed_ref, out_ref, total):
    tiles = dconv_ref.shape[0]
    images = out_ref.shape[0]
    frames = 2 * images
    side = side_of(sizes_ref, images)

    @pl.loop(0, tiles)
    def _(tile):
        def finish(cell, value):
            lines = pl.ds(cell * 8, 8)
            inside = side > max(cell // CANVAS, cell % CANVAS)
            total[tile, lines, :] = jnp.where(inside, value + dmixed_ref[tile, lines, :], 0.0)

        conv_rows(dconv_ref, tile, small_ref, True, finish)

    for image in range(images):
        for which in range(2):
            for row in range(CANVAS):
                lines = pl.ds(row * CANVAS * frames + which * images + image, CANVAS, stride=frames)
                for tile in range(tiles):
                    out_ref[image, which, row, :, lane_tile(tile)] = total[tile, lines, :]


def conv_back(sizes, dconv, small, dmixed, after=()):
    tiles, rows, _ = dconv.shape
    images = sizes.shape[0]
    return call(
        conv_back_kernel,
        "conv_back",
        array((images, 2, CANVAS, CANVAS, tiles * LANES)),
        0.1,
        [pltpu.VMEM((tiles, rows + SPARE, LANES), f32)],
        limit=6,
        smem=1,
        after=after,
    )(sizes, dconv, small, dmixed)


def start_all(copies, sems):
    running = [pltpu.make_async_copy(source, target, sems.at[number]) for number, (source, target) in enumerate(copies)]
    for copy in running:
        copy.start()
    return running

GROUPS = 8
LINES = 18
BIAS = SMALL


def pack_kernel(where_ref, weight_ref, taps_ref, west_ref, *refs):
    vectors, (bias_ref, out_ref, small, taps, west, *held, bias, sems) = refs[:5], refs[5:]
    share = weight_ref.shape[0]
    wide = out_ref.shape[1]
    cols = pl.ds(pl.multiple_of(where_ref[2] * wide, LANES), wide)
    copies = [(taps_ref, taps), (west_ref, west), (bias_ref, bias)]
    copies += list(zip(vectors, held))
    copies += [(weight_ref.at[:, cols], out_ref.at[pl.ds(0, share)])]
    running = start_all(copies, sems)
    small[...] = jnp.zeros_like(small)
    lane = pl.ds(0, share)
    for copy in running[:-1]:
        copy.wait()
    small[pl.ds(0, TAPS), lane] = taps[...].astype(f32)
    small[pl.ds(WEST, OFFSETS), lane] = west[...].astype(f32)
    for number, vector in enumerate(held):
        small[pl.ds(CBIAS + number, 1), lane] = vector[...].astype(f32).reshape(1, share)
    rows = bias[...].astype(f32).reshape(1, bias.shape[0])
    for part in range(bias.shape[0] // share):
        small[pl.ds(BIAS + part, 1), lane] = rows[:, part * share : (part + 1) * share]
    lined = [small[pl.ds(group * LINES, LINES), :][:, :share] for group in range(GROUPS)]
    out_ref[pl.ds(share, LINES), :] = jnp.concatenate(lined, axis=1).astype(bf16)
    running[-1].wait()


def pack(where, weight, taps, west, vectors, bias, after=()):
    share, units = weight.shape
    args = (weight, taps, west, *vectors, bias)
    return call(
        pack_kernel,
        "pack",
        array((share + LINES, units // 4), bf16),
        2,
        [
            pltpu.VMEM((GROUPS * LINES, LANES), f32),
            pltpu.VMEM(taps.shape, bf16),
            pltpu.VMEM(west.shape, bf16),
            *[pltpu.VMEM((share,), bf16)] * len(vectors),
            pltpu.VMEM(bias.shape, bf16),
            pltpu.SemaphoreType.DMA((len(args),)),
        ],
        smem=1,
        left=len(args),
        after=after,
    )(where, *args)


def stack_kernel(*refs):
    first = refs[0].shape[0] - LINES
    for number, ref in enumerate(refs[:-1]):
        refs[-1][number] = ref[pl.ds(first, LINES), :]


def stack(parts, after=()):
    shape = array((len(parts), LINES, parts[0].shape[1]), bf16)
    return call(stack_kernel, "stack", shape, 0.05, after=after)(*parts)


def unpack_kernel(where_ref, mine_ref, theirs_ref, small_ref, bias_ref, table):
    z, core, slabs = where_ref[0], where_ref[1], where_ref[3]
    channels = small_ref.shape[1]
    share = channels // 8
    table[...] = jnp.zeros_like(table)
    everything = None
    for number in range(8):
        ref = mine_ref if number < 4 else theirs_ref
        shard = 2 * lax.rem(z - number % 4 + slabs, slabs) + (core if number < 4 else 1 - core)
        lined = ref[number % 4].astype(f32)
        for group in range(GROUPS):
            part = lined[:, group * share : (group + 1) * share]
            table[number, pl.ds(group * LINES, LINES), pl.ds(0, share)] = part
        source = lax.broadcasted_iota(jnp.int32, (LANES, channels), 0)
        target = lax.broadcasted_iota(jnp.int32, (LANES, channels), 1)
        spread = ((target - shard * share == source) & (source < share)).astype(bf16)
        value = dot(table[number].astype(bf16), spread)
        everything = value if everything is None else everything + value
        width = bias_ref.shape[1] // 8
        rows = [table[number, pl.ds(BIAS + part, 1), :][:, :share] for part in range(width // share)]
        bias_ref[:, pl.ds(pl.multiple_of(shard * width, LANES), width)] = jnp.concatenate(rows, axis=1)
    small_ref[...] = everything[: small_ref.shape[0]]


def unpack(where, mine, theirs, units, channels):
    shapes = (array((SMALL, channels)), array((1, units)))
    scratch = [pltpu.VMEM((8, GROUPS * LINES, LANES), f32)]
    return call(unpack_kernel, "unpack", shapes, 1.2, scratch, smem=1)(where, mine, theirs)


def column_kernel(*refs):
    parts, outs = refs[:-2], refs[-2:]
    rows, width = outs[0].shape[1:]
    for turn, out in enumerate(outs):
        for number, part in enumerate(parts):
            out[number] = part[pl.ds(0, rows), pl.ds(turn * width, width)]


def column(parts, rows, after=()):
    half = array((len(parts), rows, parts[0].shape[1] // 2), bf16)
    return call(column_kernel, "column", (half, half), 0.05, after=after)(*parts)


def cut_kernel(where_ref, weight_ref, out_ref, sem):
    tall = out_ref.shape[0]
    lines = pl.ds(pl.multiple_of(where_ref[2] * tall, 16), tall)
    copy = pltpu.make_async_copy(weight_ref.at[lines], out_ref, sem)
    copy.start()
    copy.wait()


def cut(where, weight, after=()):
    tall, channels = weight.shape
    shape = array((tall // 4, channels), bf16)
    return call(cut_kernel, "cut", shape, 1, [pltpu.SemaphoreType.DMA], smem=1, left=1, after=after)(where, weight)


def onward_kernel(left_ref, right_ref, left_in_ref, right_in_ref, to_x_ref, to_y_ref):
    to_y_ref[0] = left_ref[...]
    to_y_ref[1] = left_in_ref[...]
    to_x_ref[0] = right_ref[...]
    to_x_ref[1] = right_in_ref[...]


def onward(left, right, left_in, right_in, after=()):
    shape = array((2, *left.shape), bf16)
    return call(onward_kernel, "onward", (shape, shape), 1, after=after)(left, right, left_in, right_in)


def halve_kernel(where_ref, keep_ref, left_in_ref, right_in_ref, keep_out_ref, left_ref, right_ref):
    x, y = lax.rem(where_ref[2], 2), where_ref[2] // 2

    def total(side, which):
        received = left_in_ref if side == 0 else right_in_ref
        return keep_ref[side, which].astype(f32) + received[which].astype(f32)

    keep_out_ref[0] = total(0, y).astype(bf16)
    keep_out_ref[1] = total(1, x).astype(bf16)
    left_ref[...] = total(0, 1 - y).astype(bf16)
    right_ref[...] = total(1, 1 - x).astype(bf16)


def halve(where, keep, left_in, right_in, after=()):
    _, _, lines, width = keep.shape
    half = array((lines, width), bf16)
    shapes = (array((2, lines, width), bf16), half, half)
    return call(halve_kernel, "halve", shapes, 0.01, smem=1, after=after)(where, keep, left_in, right_in)


def deal_total(where_ref, keep_ref, left_in_ref, right_in_ref, total):
    total[0] = (keep_ref[0].astype(f32) + left_in_ref[...].astype(f32)).astype(bf16)
    total[1] = (keep_ref[1].astype(f32) + right_in_ref[...].astype(f32)).astype(bf16)


def deal_kernel(where_ref, keep_ref, left_in_ref, right_in_ref, *refs):
    outs, total = refs[:-1], refs[-1]
    share = outs[0].shape[1]
    deal_total(where_ref, keep_ref, left_in_ref, right_in_ref, total)
    for step, out in enumerate(outs):
        slab = lax.rem(where_ref[0] + step, len(outs))
        for side in range(2):
            out[side] = total[side, pl.ds(pl.multiple_of(slab * share, 16), share), :]


def deal(where, keep, left_in, right_in, slabs, after=()):
    _, lines, width = keep.shape
    shapes = (array((2, lines // slabs, width), bf16),) * slabs
    scratch = [pltpu.VMEM(keep.shape, bf16)]
    return call(deal_kernel, "deal", shapes, 0.01, scratch, smem=1, after=after)(where, keep, left_in, right_in)


SMALL_ROWS = 144


def deal_small_kernel(where_ref, keep_ref, left_in_ref, right_in_ref, here_ref, received_ref, *refs):
    outs, total = refs[:-1], refs[-1]
    deal_total(where_ref, keep_ref, left_in_ref, right_in_ref, total)
    share = total.shape[1] // len(outs)
    extra = outs[0].shape[1] - share
    for step, out in enumerate(outs):
        slab = lax.rem(where_ref[0] + step, len(outs))
        small = here_ref[slab] + received_ref[slab]
        lines = SMALL_ROWS // 4
        small = jnp.concatenate([small[part * lines : (part + 1) * lines] for part in range(4)], axis=1)
        for side in range(2):
            out[side, pl.ds(0, share), :] = total[side, pl.ds(pl.multiple_of(slab * share, 16), share), :]
            out[side, pl.ds(share, extra), :] = small[side * extra : (side + 1) * extra].astype(bf16)


def deal_small(where, keep, left_in, right_in, here, received, after=()):
    slabs = here.shape[0]
    _, lines, width = keep.shape
    extra = SMALL_ROWS * here.shape[2] // width // 2
    shapes = (array((2, lines // slabs + extra, width), bf16),) * slabs
    scratch = [pltpu.VMEM(keep.shape, bf16)]
    return call(deal_small_kernel, "deal_small", shapes, 0.01, scratch, smem=1, after=after)(
        where, keep, left_in, right_in, here, received
    )


def total_kernel(*refs):
    total = refs[0][...].astype(f32)
    for ref in refs[1:-1]:
        total = total + ref[...].astype(f32)
    refs[-1][...] = total.astype(refs[-1].dtype)


def total(values, after=()):
    return call(total_kernel, "total", array(values[0].shape, values[0].dtype), 1, after=after)(*values)


def blocks_of(where_ref, flip):
    group = jnp.bitwise_xor(where_ref[2], flip)
    x, y = lax.rem(group, 2), group // 2
    return 2 * x + y, 4 + 2 * y + x


def spread_wout_kernel(where_ref, *refs):
    *values, out_ref = refs
    lines = values[0].shape[1]
    for flip, ref in enumerate(values):
        for side, block in enumerate(blocks_of(where_ref, flip)):
            out_ref[pl.ds(pl.multiple_of(block * lines, 16), lines), :] = ref[side].astype(f32)


def spread_wout(where, values, after=()):
    _, lines, channels = values[0].shape
    return call(spread_wout_kernel, "spread_wout", array((8 * lines, channels)), 1, smem=1, after=after)(where, *values)


def spread_win_kernel(where_ref, *refs):
    values, (out_ref, taps_ref, west_ref, bias_ref, *vectors, small) = refs[:4], refs[4:]
    share = out_ref.shape[0]
    _, lines, width = values[0].shape
    extra = lines - share
    for flip, ref in enumerate(values):
        for side, block in enumerate(blocks_of(where_ref, flip)):
            out_ref[:, pl.ds(pl.multiple_of(block * width, LANES), width)] = ref[side, pl.ds(0, share), :].astype(f32)
    for side in range(2):
        part = [ref[side, pl.ds(share, extra), :].astype(f32) for ref in values]
        both = (part[0] + part[1]) + (part[2] + part[3])
        for group in range(4):
            span = pl.ds(group * 2 * extra + side * extra, extra)
            small[span, :] = both[:, group * share : (group + 1) * share]
    taps_ref[...] = small[pl.ds(0, TAPS), :]
    for number, ref in enumerate(vectors):
        ref[...] = small[pl.ds(TAPS + number, 1), :]
    west_ref[...] = small[pl.ds(TAPS + 5, OFFSETS), :]
    rows = bias_ref.shape[0] // share
    first = TAPS + 5 + OFFSETS
    bias_ref[...] = jnp.concatenate([small[pl.ds(first + row, 1), :] for row in range(rows)], axis=1).reshape(bias_ref.shape)


def spread_win(where, values, share, after=()):
    width = values[0].shape[2]
    shapes = [array((share, 8 * width)), array((TAPS, share)), array((OFFSETS, share)), array((width,))]
    shapes += [array((1, share))] * 5
    scratch = [pltpu.VMEM((SMALL_ROWS, share), f32)]
    return call(spread_win_kernel, "spread_win", shapes, 1, scratch, smem=1, after=after)(where, *values)


def pack_small_kernel(where_ref, gtaps_ref, gnorm_ref, gbout_ref, gscale_ref, gwest_ref, gbin_ref, here_ref, away_ref):
    slabs, _, share = here_ref.shape

    def fill(even_ref, odd_ref):
        for shard in range(2 * slabs):
            out = odd_ref if shard % 2 else even_ref
            cols = pl.ds(shard * share, share)
            line = 0
            for ref in (gtaps_ref, gnorm_ref, gbout_ref, gscale_ref, gwest_ref):
                out[shard // 2, pl.ds(line, ref.shape[0]), :] = ref[:, cols]
                line += ref.shape[0]
            lines = gbin_ref.shape[1] // gtaps_ref.shape[1]
            for extra in range(lines):
                span = pl.ds((shard * lines + extra) * share, share)
                out[shard // 2, pl.ds(line + extra, 1), :] = gbin_ref[:, span]
            rest = SMALL_ROWS - line - lines
            out[shard // 2, pl.ds(line + lines, rest), :] = jnp.zeros((rest, share), f32)

    @pl.when(where_ref[1] == 0)
    def _():
        fill(here_ref, away_ref)

    @pl.when(where_ref[1] == 1)
    def _():
        fill(away_ref, here_ref)


def pack_small(where, parts, slabs, share, after=()):
    shape = array((slabs, SMALL_ROWS, share))
    return call(pack_small_kernel, "pack_small", (shape, shape), 0.01, smem=1, after=after)(where, *parts)


AXES = ("dp", "fsdp")


class Routes:
    def __init__(self, groups, members):
        self.groups, self.members, self.slabs = groups, members, members // 2
        self.group = lax.axis_index("dp")
        member = lax.axis_index("fsdp")
        self.slab, self.core = member // 2, member % 2

    def send(self, value, target):
        pairs = [
            (group * self.members + 2 * slab + core, self.index(*target(group, slab, core)))
            for group in range(self.groups)
            for slab in range(self.slabs)
            for core in range(2)
        ]
        return lax.ppermute(value, AXES, pairs)

    def index(self, group, slab, core):
        return group * self.members + 2 * slab + core

    def to_core(self, value):
        return self.send(value, lambda group, slab, core: (group, slab, 1 - core))

    def to_slab(self, value, step):
        return self.send(value, lambda group, slab, core: (group, (slab + step) % self.slabs, core))

    def to_near(self, value, flip):
        return self.send(value, lambda group, slab, core: (group, slab ^ flip, core))

    def to_group(self, value, flip):
        return self.send(value, lambda group, slab, core: (group ^ flip, slab, core))


def shards(
    features,
    cotangent,
    image_sizes,
    warp_index,
    warp_weight,
    offsets,
    conv_kernel,
    conv_bias,
    norm_gain,
    norm_bias,
    w_in,
    bias_in,
    w_out,
    bias_out,
    layer_scale,
    w_estimate,
):
    share, units = w_in.shape
    channels = features.shape[-1]
    members = channels // share
    groups = lax.axis_size("dp")
    paired = groups == 4 and members == 8

    reach = WINDOW // 2
    lane_of = (offsets[:, 0] + reach) * CANVAS + offsets[:, 1] + reach
    place = jnp.pad(lane_of, (0, LANES - OFFSETS), constant_values=-1)[None]

    early = (features, cotangent, warp_index, warp_weight, place, lane_of)
    if paired:
        routes = Routes(groups, members)
        slabs = routes.slabs
        where = jnp.stack([routes.slab, routes.core, routes.group, jnp.int32(slabs)])
        vectors = (conv_bias, norm_gain, norm_bias, bias_out, layer_scale)
        packed = pack(where, w_in, conv_kernel, w_estimate, vectors, bias_in)
        win_parts = [routes.to_slab(packed, step) for step in range(1, slabs)]
        win_own = routes.to_core(w_in)
        small = stack([packed, *win_parts], after=early)
        quarter = cut(where, w_out, after=(packed,))
        wout_parts = [routes.to_slab(quarter, step) for step in range(1, slabs)]
        wout_own = routes.to_core(w_out)
        small, bin_all = unpack(where, small, routes.to_core(small), units, channels)
    else:
        where = jnp.zeros((4,), jnp.int32)
        small = jnp.concatenate(
            [
                conv_kernel,
                w_estimate,
                jnp.stack([conv_bias, norm_gain, norm_bias, bias_out, layer_scale]),
                bias_in.reshape(-1, share),
            ]
        )
        small = lax.all_gather(small, "fsdp")
        win_all = lax.all_gather(w_in, "fsdp", axis=0, tiled=True)
        wout_all = lax.all_gather(w_out, "fsdp", axis=0, tiled=True)
        bin_all = small[:, SMALL:].reshape(1, units).astype(f32)
        small = small[:, :SMALL].transpose(1, 0, 2).reshape(SMALL, channels).astype(f32)
    after = ()
    if paired:
        left, right = column(win_parts, share, after=(wout_parts[0],))
        left_in, right_in = routes.to_group(left, 1), routes.to_group(right, 2)
        after = (left,)
    x, up, begun = conv_begin(image_sizes, features, cotangent, small, after)
    if paired:
        to_x, to_y = onward(left, right, left_in, right_in, after=(begun,))
        win_halves = [to_x, to_y, routes.to_group(to_x, 1), routes.to_group(to_y, 2)]
        left, right = column(wout_parts, units // members // 4, after=(to_x,))
        left_in, right_in = routes.to_group(left, 1), routes.to_group(right, 2)
        after = (left,)
    normed, pair, xhat, rstd = conv_norm(where, x, begun, small, after)
    if paired:
        to_x, to_y = onward(left, right, left_in, right_in, after=(normed,))
        wout_halves = [to_x, to_y, routes.to_group(to_x, 1), routes.to_group(to_y, 2)]
        win_halves = gate(win_halves, (to_x,))
        win_theirs = [win_own] + [routes.to_core(value) for value in win_halves]
        win_all, active, slope = place_widen(where, [w_in, *win_halves], win_theirs, normed, bin_all)
        wout_halves = gate(wout_halves, (active,))
        wout_theirs = [wout_own] + [routes.to_core(value) for value in wout_halves]
        begun = place_narrow(0, where, [w_out, *wout_halves], active, small)
        wout_all, branch = place_narrow(1, where, wout_theirs, active, *begun)
    else:
        active, slope = widen(normed, win_all, bin_all)
        branch = narrow(active, wout_all, small)
    gated, d_mixed, d_branch, g_scale, g_bout = flow(
        image_sizes, x, branch, up, warp_index, warp_weight, place, small
    )
    if paired:
        wout_away = grad_narrow(where, active, d_branch, slabs)
        wout_in = routes.to_core(wout_away)
        d_hidden, g_bin = hidden_back(where, d_branch, wout_all, slope, after=(wout_away,))
        keep_out, left, right = grad_narrow_here(where, active, d_branch, wout_in, after=(d_hidden,))
        left_out, right_out = routes.to_group(left, 1), routes.to_group(right, 2)
        win_away = grad_widen_away(where, pair, d_hidden, after=(keep_out,))
        win_in = routes.to_core(win_away)
        mixed_out, g_west = finish(image_sizes, lane_of, x, branch, up, gated, place, small, after=(win_away,))
        keep_in, left, right = grad_widen_here(where, pair, d_hidden, win_in, after=(g_west,))
        left_in, right_in = routes.to_group(left, 1), routes.to_group(right, 2)
        d_conv, g_norm = norm_back(d_hidden, win_all, xhat, rstd, small, after=(keep_in,))
        keep_out, left, right = halve(where, keep_out, left_out, right_out, after=(d_conv,))
        left_out, right_out = routes.to_group(left, 2), routes.to_group(right, 1)
        g_taps = grad_taps(x, d_conv, after=(keep_out,))
        parts = (g_taps, g_norm, g_bout, g_scale, g_west, g_bin)
        small_here, small_away = pack_small(where, parts, slabs, share)
        small_in = routes.to_core(small_away)
        keep_in, left, right = halve(where, keep_in, left_in, right_in, after=(small_away,))
        left_in, right_in = routes.to_group(left, 2), routes.to_group(right, 1)
        wout_parts = deal(where, keep_out, left_out, right_out, slabs, after=(keep_in,))
        wout_parts = wout_parts[:1] + tuple(routes.to_slab(v, n + 1) for n, v in enumerate(wout_parts[1:]))
        win_parts = deal_small(where, keep_in, left_in, right_in, small_here, small_in, after=wout_parts[:1])
        win_parts = win_parts[:1] + tuple(routes.to_slab(v, n + 1) for n, v in enumerate(win_parts[1:]))
        grad_features = conv_back(image_sizes, d_conv, small, d_mixed, after=win_parts[:1])
        g_wout = total(wout_parts, after=(grad_features,))
        wout_parts = [g_wout] + [routes.to_group(g_wout, flip) for flip in range(1, 4)]
        g_win = total(win_parts, after=(g_wout,))
        win_parts = [g_win] + [routes.to_group(g_win, flip) for flip in range(1, 4)]
        g_wout = spread_wout(where, wout_parts, after=(g_win,))
        g_win, g_taps, g_west, g_bin, *g_small = spread_win(where, win_parts, share)
        g_small = [value.reshape(share) for value in g_small]
    else:
        g_wout = grad_narrow(where, active, d_branch, 8).reshape(units, channels)
        d_hidden, g_bin = hidden_back(where, d_branch, wout_all, slope)
        g_win = grad_widen_full(normed, d_hidden)
        d_conv, g_norm = norm_back(d_hidden, win_all, xhat, rstd, small)
        g_taps = grad_taps(x, d_conv)
        mixed_out, g_west = finish(image_sizes, lane_of, x, branch, up, gated, place, small)
        grad_features = conv_back(image_sizes, d_conv, small, d_mixed)
        g_small = jnp.concatenate([g_taps, g_norm, g_bout, g_scale, g_west])
        g_small = g_small.reshape(-1, members, share).transpose(1, 0, 2)
        g_small = jnp.concatenate([g_small, g_bin.reshape(members, -1, share)], axis=1)

        def reduce(value):
            return lax.psum(lax.psum_scatter(value, "fsdp", scatter_dimension=0, tiled=True).astype(f32), "dp")

        g_wout, g_win, g_small = reduce(g_wout), reduce(g_win), reduce(g_small)[0]
        tail = TAPS + 5 + OFFSETS
        g_taps, g_west, g_bin = g_small[:TAPS], g_small[TAPS + 5 : tail], g_small[tail:]
        g_small = g_small[TAPS : TAPS + 5]
    return (
        mixed_out,
        grad_features,
        g_taps,
        g_small[0],
        g_small[1],
        g_small[2],
        g_win,
        g_bin.reshape(-1),
        g_wout,
        g_small[3],
        g_small[4],
        g_west,
    )


def solution(mesh):
    in_specs = (
        P(("dp", "fsdp"), None, None, None, None),
        P(("dp", "fsdp"), None, None, None, None),
        P(("dp", "fsdp")),
        P(("dp", "fsdp"), None, None),
        P(("dp", "fsdp"), None, None),
        P(),
        P(None, "fsdp"),
        P("fsdp"),
        P("fsdp"),
        P("fsdp"),
        P("fsdp", None),
        P("fsdp"),
        P("fsdp", None),
        P("fsdp"),
        P("fsdp"),
        P(None, "fsdp"),
    )
    out_specs = (
        P(("dp", "fsdp"), None, None, None, None),
        P(("dp", "fsdp"), None, None, None, None),
        P(None, "fsdp"),
        P("fsdp"),
        P("fsdp"),
        P("fsdp"),
        P("fsdp", None),
        P("fsdp"),
        P("fsdp", None),
        P("fsdp"),
        P("fsdp"),
        P(None, "fsdp"),
    )
    return jax.shard_map(shards, mesh=mesh, in_specs=in_specs, out_specs=out_specs, check_vma=False)
```

```python
import functools

import jax
import jax.numpy as jnp
import numpy as np
from jax import lax
from jax.experimental import pallas as pl
from jax.experimental.pallas import tpu as pltpu
from jax.sharding import PartitionSpec as P

CANVAS = 10
KERNEL = 7
REACH = KERNEL // 2
TAPS = KERNEL * KERNEL
WINDOW = 9
OFFSETS = WINDOW * WINDOW
PIX = CANVAS * CANVAS
PADDED = 104
SPARE = 48
LANES = 128
EPSILON = 1e-06
f32 = jnp.float32
bf16 = jnp.bfloat16
WEST = TAPS
CBIAS, GAIN, SHIFT, BOUT, SCALE = range(TAPS + OFFSETS, TAPS + OFFSETS + 5)
SMALL = TAPS + OFFSETS + 5


def call(kernel, name, out_shape, micros, scratch=(), limit=4, smem=0, left=0, after=(), aliases=None):
    def body(*refs):
        kernel(*refs[len(after) :])

    def run(*args):
        specs = [pl.BlockSpec(memory_space=pl.ANY)] * len(after)
        specs += [pl.BlockSpec(memory_space=pltpu.SMEM)] * smem
        specs += [pl.BlockSpec(memory_space=pl.ANY)] * left
        specs += [pl.BlockSpec(memory_space=pltpu.VMEM)] * (len(args) - smem - left)
        return pl.pallas_call(
            body,
            name=name,
            in_specs=specs,
            out_specs=jax.tree.map(out_space, out_shape),
            out_shape=out_shape,
            input_output_aliases={len(after) + source: target for source, target in (aliases or {}).items()},
            scratch_shapes=list(scratch),
            compiler_params=pltpu.CompilerParams(vmem_limit_bytes=limit * 1024 * 1024),
            cost_estimate=pl.CostEstimate(flops=int(micros * 1.15e9), bytes_accessed=0, transcendentals=0),
        )(*after, *args[:smem], *[in_hbm(value) for value in args[smem : smem + left]], *args[smem + left :])

    return run


def out_space(shape):
    return pl.BlockSpec(memory_space=pltpu.VMEM if isinstance(shape, jax.ShapeDtypeStruct) else pltpu.HBM)


def in_hbm(value):
    return pltpu.with_memory_space_constraint(value, pltpu.HBM)


def gate(values, after):
    space = pl.BlockSpec(memory_space=pl.ANY)
    return pl.pallas_call(
        lambda *refs: None,
        name="gate",
        in_specs=[space] * (len(values) + len(after)),
        out_specs=[space] * len(values),
        out_shape=[array(value.shape, value.dtype) for value in values],
        input_output_aliases={number: number for number in range(len(values))},
        compiler_params=pltpu.CompilerParams(vmem_limit_bytes=1024 * 1024),
        cost_estimate=pl.CostEstimate(flops=0, bytes_accessed=0, transcendentals=0),
    )(*values, *after)


def array(shape, dtype=f32):
    return jax.ShapeDtypeStruct(shape, dtype)


def nt(left, right):
    return lax.dot_general(left, right, (((1,), (1,)), ((), ())), preferred_element_type=f32)


def tn(left, right):
    return lax.dot_general(left, right, (((0,), (0,)), ((), ())), preferred_element_type=f32)


def dot(left, right):
    return jnp.dot(left, right, preferred_element_type=f32)


def split(values):
    high = values.astype(bf16)
    return high, (values - high.astype(f32)).astype(bf16)


def lane_tile(tile):
    return pl.ds(tile * LANES, LANES)


def conv_rows(source, tile, kernel_ref, flip, finish):
    cols = pl.ds(pl.multiple_of(tile * LANES, LANES), LANES)
    for row in range(CANVAS):
        sums = [None] * CANVAS
        for ky in range(KERNEL):
            source_row = row + ky - REACH
            if not 0 <= source_row < CANVAS:
                continue
            cells = [source[tile, pl.ds((source_row * CANVAS + col) * 8, 8), :] for col in range(CANVAS)]
            for kx in range(KERNEL):
                tap = ky * KERNEL + kx
                tap = TAPS - 1 - tap if flip else tap
                weight = jnp.broadcast_to(kernel_ref[pl.ds(tap, 1), cols], (8, LANES))
                for col in range(CANVAS):
                    other = col + kx - REACH
                    if 0 <= other < CANVAS:
                        term = cells[other] * weight
                        sums[col] = term if sums[col] is None else sums[col] + term
        for col in range(CANVAS):
            finish(row * CANVAS + col, sums[col])


def side_of(sizes_ref, images):
    lines = lax.broadcasted_iota(jnp.int32, (2 * images, LANES), 0)
    side = jnp.zeros(lines.shape, jnp.int32)
    for image in range(images):
        side = jnp.where((lines == image) | (lines == images + image), sizes_ref[image], side)
    return side


def conv_tile(x_ref, tile, small_ref, conv_ref, target):
    cols = pl.ds(pl.multiple_of(tile * LANES, LANES), LANES)
    bias = jnp.broadcast_to(small_ref[pl.ds(CBIAS, 1), cols], (8, LANES))

    def finish(cell, total):
        conv_ref[target, pl.ds(cell * 8, 8), :] = total + bias

    conv_rows(x_ref, tile, small_ref, False, finish)


def conv_begin_kernel(
    sizes_ref, features_ref, upstream_ref, small_ref, x_ref, up_ref, conv_ref, features, upstream, sems,
):
    images = features_ref.shape[0]
    frames = 2 * images
    tiles, rows, _ = conv_ref.shape[0] * 2, *conv_ref.shape[1:]
    side = side_of(sizes_ref, images)
    copies = [
        pltpu.make_async_copy(source.at[image], target.at[image], sems.at[number, image])
        for number, (source, target) in enumerate(((features_ref, features), (upstream_ref, upstream)))
        for image in range(images)
    ]
    for copy in copies:
        copy.start()

    def lay(source, image, target):
        for which in range(2):
            for row in range(CANVAS):
                lines = pl.ds(row * CANVAS * frames + which * images + image, CANVAS, stride=frames)
                for tile in range(tiles):
                    target[tile, lines, :] = source[image, which, row, :, lane_tile(tile)].astype(f32)

    for image in range(images):
        copies[image].wait()
        lay(features, image, x_ref)

    @pl.loop(0, tiles)
    def _(tile):
        for cell in range(PIX):
            inside = side > max(cell // CANVAS, cell % CANVAS)
            lines = pl.ds(cell * 8, 8)
            x_ref[tile, lines, :] = jnp.where(inside, x_ref[tile, lines, :], 0.0)

    @pl.loop(0, tiles // 2)
    def _(tile):
        conv_tile(x_ref, tile, small_ref, conv_ref, tile)

    for tile in range(tiles):
        up_ref[tile, pl.ds(rows, SPARE), :] = jnp.zeros((SPARE, LANES), f32)
    for image in range(images):
        copies[images + image].wait()
        lay(upstream, image, up_ref)


def conv_begin(sizes, features, upstream, small, after=()):
    images, channels = features.shape[0], features.shape[-1]
    rows, tiles = PIX * 2 * images, channels // LANES
    shapes = (
        array((tiles, rows + SPARE, LANES)),
        array((tiles, rows + SPARE, LANES)),
        array((tiles // 2, rows, LANES)),
    )
    scratch = [pltpu.VMEM(features.shape, bf16), pltpu.VMEM(features.shape, bf16), pltpu.SemaphoreType.DMA((2, images))]
    return call(conv_begin_kernel, "conv_begin", shapes, 1, scratch, limit=8, smem=1, left=2, after=after)(
        sizes, features, upstream, small
    )


def conv_norm_kernel(where_ref, x_ref, begun_ref, small_ref, normed_ref, pair_ref, xhat_ref, rstd_ref, conv, order):
    tiles, rows = x_ref.shape[0], begun_ref.shape[1]
    channels = tiles * LANES

    @pl.loop(0, tiles // 2)
    def _(tile):
        conv_tile(x_ref, tile + tiles // 2, small_ref, conv, tile)

    share = channels // 8
    core = where_ref[1]
    for tile in range(tiles):
        source = lax.broadcasted_iota(jnp.int32, (channels, LANES), 0)
        target = lax.broadcasted_iota(jnp.int32, (1, LANES), 1) + tile * LANES
        shard = target // share
        wanted = jnp.where(shard < 4, 2 * shard + 1 - core, 2 * (shard - 4) + core) * share + target % share
        order[:, lane_tile(tile)] = (source == wanted).astype(bf16)
    size = 160

    @pl.loop(0, rows // size)
    def _(block):
        lines = pl.ds(pl.multiple_of(block * size, size), size)
        values = [begun_ref[tile, lines, :] for tile in range(tiles // 2)]
        values = jnp.concatenate(values + [conv[tile, lines, :] for tile in range(tiles // 2)], axis=1)
        mean = jnp.sum(values, axis=-1, keepdims=True) * (1.0 / channels)
        centred = values - mean
        variance = jnp.sum(centred * centred, axis=-1, keepdims=True) * (1.0 / channels)
        scale = lax.rsqrt(variance + EPSILON)
        xhat = centred * scale
        xhat_ref[lines, :] = xhat.astype(bf16)
        rstd_ref[lines, :] = scale
        normed = (xhat * small_ref[pl.ds(GAIN, 1), :] + small_ref[pl.ds(SHIFT, 1), :]).astype(bf16)
        normed_ref[lines, :] = normed
        pair_ref[lines, :] = dot(normed, order[...]).astype(bf16)


def conv_norm(where, x, begun, small, after=()):
    tiles, rows = x.shape[0], begun.shape[1]
    channels = tiles * LANES
    low = array((rows, channels), bf16)
    return call(
        conv_norm_kernel,
        "conv_norm",
        (low, low, low, array((rows, 1))),
        1,
        [pltpu.VMEM(begun.shape, f32), pltpu.VMEM((channels, channels), bf16)],
        limit=8,
        smem=1,
        after=after,
    )(where, x, begun, small)


def gelu_pair(hidden):
    cdf = 0.5 * lax.erf(hidden * 0.7071067811865476) + 0.5
    density = jnp.exp(hidden * hidden * -0.5) * 0.3989422804014327
    return hidden * cdf, cdf + hidden * density


def widen_part(group, normed_ref, weight_ref, bias_ref, active_ref, slope_ref, part):
    cols = pl.ds(part * 256, 256)
    quarter = weight_ref.shape[1] // 4
    start = jnp.bitwise_xor(group, part * 256 // quarter) * quarter + part * 256 % quarter
    hidden = dot(normed_ref[...], weight_ref[:, cols]) + bias_ref[:, pl.ds(pl.multiple_of(start, 256), 256)]
    active, slope = gelu_pair(hidden)
    active_ref[:, cols] = active.astype(bf16)
    slope_ref[:, cols] = slope.astype(bf16)


def widen_kernel(normed_ref, weight_ref, bias_ref, active_ref, slope_ref):
    for part in range(weight_ref.shape[1] // 256):
        widen_part(0, normed_ref, weight_ref, bias_ref, active_ref, slope_ref, part)


def widen(normed, weight, bias):
    rows, units = normed.shape[0], weight.shape[1]
    return call(widen_kernel, "widen", (array((rows, units), bf16),) * 2, 6.5, limit=24)(normed, weight, bias)


def crossed(pieces, flip):
    _, to_x, to_y, from_x, from_y = pieces
    left = (to_y.at[0], to_y.at[1], from_y.at[0], from_y.at[1])[flip]
    right = (to_x.at[0], from_x.at[0], to_x.at[1], from_x.at[1])[flip]
    return left, right


def place_widen_kernel(where_ref, *refs):
    pieces, (normed_ref, bias_ref, weight_ref, active_ref, slope_ref) = refs[:10], refs[10:]
    z, core, group, slabs = (where_ref[number] for number in range(4))
    share = pieces[0].shape[0]
    width = pieces[1].shape[3]
    for flip in range(4):
        for side in range(2):
            parity = core if side == 0 else 1 - core
            own_ref = pieces[5 * side]
            for step in range(4):
                shard = 2 * lax.rem(z - step + slabs, slabs) + parity
                lines = pl.ds(pl.multiple_of(shard * share, 16), share)
                if step == 0:
                    source = pl.ds(pl.multiple_of(jnp.bitwise_xor(group, flip) * 2 * width, LANES), 2 * width)
                    weight_ref[lines, pl.ds(flip * 2 * width, 2 * width)] = own_ref[:, source]
                    continue
                for turn, part in enumerate(crossed(pieces[5 * side : 5 * side + 5], flip)):
                    weight_ref[lines, pl.ds((2 * flip + turn) * width, width)] = part[step - 1]
    for part in range(weight_ref.shape[1] // 256):
        widen_part(group, normed_ref, weight_ref, bias_ref, active_ref, slope_ref, part)


def place_widen(where, mine, theirs, normed, bias, after=()):
    share, units = mine[0].shape
    rows, channels = normed.shape
    wide = array((rows, units), bf16)
    shapes = (array((channels, units), bf16), wide, wide)
    return call(place_widen_kernel, "place_widen", shapes, 8, smem=1, after=after)(where, *mine, *theirs, normed, bias)


def narrow_rows(active_ref, weight_ref, small_ref, branch_ref):
    size = 160
    for part in range(active_ref.shape[0] // size):
        lines = pl.ds(part * size, size)
        branch = dot(active_ref[lines, :], weight_ref[...]) + small_ref[pl.ds(BOUT, 1), :]
        for tile in range(branch_ref.shape[0]):
            branch_ref[tile, lines, :] = branch[:, tile * LANES : (tile + 1) * LANES]


def narrow(active, weight, small):
    rows, channels = active.shape[0], weight.shape[1]
    return call(narrow_rows, "narrow", array((channels // LANES, rows, LANES)), 4, limit=24)(active, weight, small)


def place_narrow_kernel(side, where_ref, *refs):
    pieces = refs[:5]
    if side == 0:
        active_ref, small_ref, weight_ref, branch_ref = refs[5:]
    else:
        active_ref, _, begun_ref, weight_ref, branch_ref = refs[5:]
    z, core, group, slabs = (where_ref[number] for number in range(4))
    parity = core if side == 0 else 1 - core
    tall = pieces[0].shape[0]
    _, _, lines, width = pieces[1].shape

    def base(slab):
        return pl.multiple_of(jnp.bitwise_xor(slab, group) * 2 * tall + parity * tall, 16)

    weight_ref[pl.ds(base(z), tall), :] = pieces[0][...]
    for step in range(1, 4):
        for flip in range(4):
            start = base(lax.rem(z - step + slabs, slabs)) + jnp.bitwise_xor(group, flip) * lines
            for turn, part in enumerate(crossed(pieces, flip)):
                weight_ref[pl.ds(pl.multiple_of(start, 16), lines), pl.ds(turn * width, width)] = part[step - 1]
    spans = [pl.ds(pl.multiple_of(part * 2 * tall + parity * tall, LANES), tall) for part in range(4)]
    weight = jnp.concatenate([weight_ref[span, :] for span in spans], axis=0)
    size = 160
    for part in range(active_ref.shape[0] // size):
        rows = pl.ds(part * size, size)
        branch = dot(jnp.concatenate([active_ref[rows, span] for span in spans], axis=1), weight)
        if side == 0:
            branch = branch + small_ref[pl.ds(BOUT, 1), :]
        for tile in range(branch_ref.shape[0]):
            value = branch[:, tile * LANES : (tile + 1) * LANES]
            branch_ref[tile, rows, :] = value if side == 0 else begun_ref[tile, rows, :] + value


def place_narrow(side, where, pieces, active, *more, after=()):
    tall, channels = pieces[0].shape
    rows, units = active.shape
    shapes = (array((units, channels), bf16), array((channels // LANES, rows, LANES)))
    return call(
        functools.partial(place_narrow_kernel, side),
        "place_narrow",
        shapes,
        3,
        smem=1,
        after=after,
        aliases={} if side == 0 else {7: 0},
    )(where, *pieces, active, *more)


def skew(values, inverse):
    rows = lax.broadcasted_iota(jnp.int32, values.shape, 0)
    centre = (WINDOW // 2) * (CANVAS + 1)
    amount = jnp.bitwise_and(rows - centre if inverse else centre - rows, LANES - 1)
    for bit in range(7):
        moved = pltpu.roll(values, 1 << bit, 1)
        values = jnp.where(jnp.bitwise_and(amount, 1 << bit) != 0, moved, values)
    return values


def movers(tiles, frames):
    def take(ref, frame):
        lines = pl.ds(frame, PADDED, stride=frames)
        return jnp.concatenate([ref[tile, lines, :] for tile in range(tiles)], axis=1)

    def put(ref, frame, values):
        lines = pl.ds(frame, PADDED, stride=frames)
        for tile in range(tiles):
            ref[tile, lines, :] = values[:, tile * LANES : (tile + 1) * LANES]

    return take, put


def mix(x_ref, branch_ref, small_ref, mixed):
    tiles, rows, _ = branch_ref.shape
    rest = mixed.shape[1] - rows
    for tile in range(tiles):
        scale = small_ref[pl.ds(SCALE, 1), lane_tile(tile)]
        mixed[tile, pl.ds(0, rows), :] = x_ref[tile, pl.ds(0, rows), :] + scale * branch_ref[tile]
        mixed[tile, pl.ds(rows, rest), :] = jnp.zeros((rest, LANES), f32)


def estimator(place_ref, small_ref, west_in):
    west_in[...] = jnp.zeros_like(west_in)
    west_in[pl.ds(0, OFFSETS), :] = small_ref[pl.ds(WEST, OFFSETS), :]
    lanes = lax.broadcasted_iota(jnp.int32, (LANES, LANES), 0)
    return dot((lanes == place_ref[...]).astype(bf16), west_in[...].astype(bf16)).astype(bf16)


def flow_kernel(
    sizes_ref, x_ref, branch_ref, up_ref, index_ref, weight_ref, place_ref, small_ref, window_ref,
    gated_ref, dmixed_ref, dbranch_ref, gscale_ref, gbout_ref, mixed, back, west_in, warp_in, sem,
):
    tiles, rows, _ = branch_ref.shape
    images = index_ref.shape[0]
    frames = 2 * images
    channels = tiles * LANES
    factor = channels ** (-0.5)
    every = range(images)
    mix(x_ref, branch_ref, small_ref, mixed)
    take, put = movers(tiles, frames)
    west = estimator(place_ref, small_ref, west_in)
    window = window_ref[0]
    reach = window_ref[1]
    cells = lax.broadcasted_iota(jnp.int32, (PIX, LANES), 1)
    warp_in[...] = jnp.zeros_like(warp_in)
    for image in every:
        warp = jnp.zeros((PIX, LANES), f32)
        for corner in range(4):
            place = index_ref[image, :, pl.ds(corner, 1)]
            amount = weight_ref[image, :, pl.ds(corner, 1)]
            warp = warp + jnp.where(cells == place, amount, 0.0)
        warp_in[image, pl.ds(0, PIX), :] = warp
    halves = [split(warp_in[image]) for image in every]
    wide_warps = [jnp.concatenate(pair, axis=1)[:PADDED] for pair in halves]
    tall_warps = [jnp.concatenate(pair, axis=0) for pair in halves]
    rest = jnp.zeros((LANES - PADDED, channels), f32)

    def twice(values):
        value = jnp.concatenate([values, rest], axis=0).astype(bf16)
        return jnp.concatenate([value, value], axis=0)

    inside = [(reach < sizes_ref[image].astype(f32)).astype(f32)[:, :1] for image in every]
    first = [take(mixed, image) * inside[image] for image in every]
    second = [take(mixed, images + image) * inside[image] for image in every]
    first_low = [value.astype(bf16) for value in first]
    warped = [dot(warp, twice(value)) for warp, value in zip(wide_warps, second)]
    warped = [jnp.concatenate([value, rest], axis=0).astype(bf16) for value in warped]
    scores = [nt(left, right) for left, right in zip(first_low, warped)]
    costs = [skew(value, False) * window * factor for value in scores]
    pairs = [gelu_pair(value) for value in costs]
    for image, (value, _) in enumerate(pairs):
        gated_ref[image] = value.astype(bf16)
    d_firsts = [take(up_ref, image) * inside[image] for image in every]
    d_heads = [value.astype(bf16) for value in d_firsts]
    d_costs = [slope * nt(d_head, west) * window * factor for (_, slope), d_head in zip(pairs, d_heads)]
    d_scores = [skew(value, True).astype(bf16) for value in d_costs]
    for image in every:
        put(back, image, d_firsts[image] + dot(d_scores[image], warped[image]))
    d_warped = [tn(value, low)[:PADDED] for value, low in zip(d_scores, first_low)]
    for image in every:
        d_second = take(up_ref, images + image) + tn(tall_warps[image], twice(d_warped[image]))[:PADDED]
        put(back, images + image, d_second * inside[image])
    save = pltpu.make_async_copy(back.at[:, pl.ds(0, rows)], dmixed_ref, sem)
    save.start()
    for tile in range(tiles):
        cols = lane_tile(tile)
        d_mixed = back[tile, pl.ds(0, rows), :]
        gscale_ref[:, cols] = jnp.sum(d_mixed * branch_ref[tile], axis=0, keepdims=True)
        d_branch = (d_mixed * small_ref[pl.ds(SCALE, 1), cols]).astype(bf16)
        dbranch_ref[:, cols] = d_branch
        gbout_ref[:, cols] = jnp.sum(d_branch.astype(f32), axis=0, keepdims=True)
    save.wait()


def finish_kernel(
    sizes_ref, lane_ref, x_ref, branch_ref, up_ref, gated_ref, place_ref, small_ref, window_ref,
    out_ref, gwest_ref, mixed, west_in, lanes,
):
    tiles, _, _ = x_ref.shape
    images = gated_ref.shape[0]
    frames = 2 * images
    take, put = movers(tiles, frames)
    mix(x_ref, branch_ref, small_ref, mixed)
    west = estimator(place_ref, small_ref, west_in)
    reach = window_ref[1]
    for image in range(images):
        inside = (reach < sizes_ref[image].astype(f32)).astype(f32)[:, :1]
        gated = gated_ref[image]
        part = tn(gated, (take(up_ref, image) * inside).astype(bf16))
        lanes[...] = part if image == 0 else lanes[...] + part
        put(mixed, image, (take(mixed, image) * inside + dot(gated, west)) * inside)
        put(mixed, images + image, take(mixed, images + image) * inside)
    for offset in range(OFFSETS):
        gwest_ref[pl.ds(offset, 1), :] = lanes[pl.ds(lane_ref[offset], 1), :]
    for image in range(images):
        for which in range(2):
            for row in range(CANVAS):
                lines = pl.ds(row * CANVAS * frames + which * images + image, CANVAS, stride=frames)
                for tile in range(tiles):
                    out_ref[image, which, row, :, lane_tile(tile)] = mixed[tile, lines, :].astype(bf16)


def finish(sizes, lane_of, x, branch, up, gated, place, small, after=()):
    tiles, rows, _ = branch.shape
    images, channels = gated.shape[0], tiles * LANES
    return call(
        finish_kernel,
        "finish",
        (array((images, 2, CANVAS, CANVAS, channels), bf16), array((OFFSETS, channels))),
        0.01,
        [pltpu.VMEM((tiles, rows + SPARE, LANES), f32)] + [pltpu.VMEM((LANES, channels), f32)] * 2,
        limit=10,
        smem=2,
        after=after,
    )(sizes, lane_of, x, branch, up, gated, place, small, jnp.asarray(tables()))


def tables():
    cells = np.arange(PADDED)[:, None]
    lane = np.arange(LANES)[None, :]
    reach = WINDOW // 2
    row = cells // CANVAS + lane // CANVAS - reach
    col = cells % CANVAS + lane % CANVAS - reach
    good = (lane % CANVAS < WINDOW) & (lane // CANVAS < WINDOW) & (cells < PIX)
    good &= (row >= 0) & (row < CANVAS) & (col >= 0) & (col < CANVAS)
    far = np.maximum(cells // CANVAS, cells % CANVAS) + 0 * lane
    return np.stack([good, far]).astype(np.float32)


def flow(sizes, x, branch, up, index, weight, place, small, after=()):
    tiles, rows, _ = branch.shape
    images, channels = index.shape[0], tiles * LANES
    padded = pltpu.VMEM((tiles, PADDED * 2 * images, LANES), f32)
    vector = array((1, channels))
    return call(
        flow_kernel,
        "flow",
        (
            array((images, PADDED, LANES), bf16),
            pltpu.HBM(branch.shape, f32),
            array((rows, channels), bf16),
            vector,
            vector,
        ),
        6.5,
        [padded, padded, pltpu.VMEM((LANES, channels), f32), pltpu.VMEM((images, LANES, LANES), f32), pltpu.SemaphoreType.DMA],
        limit=14,
        smem=1,
        after=after,
    )(sizes, x, branch, up, index, weight, place, small, jnp.asarray(tables()))


def grad_narrow_kernel(where_ref, active_ref, dbranch_ref, out_ref):
    count, tile, _ = out_ref.shape
    for part in range(count):
        block = 2 * jnp.bitwise_xor(part, where_ref[2]) + 1 - where_ref[1] if count < 8 else part
        cols = pl.ds(pl.multiple_of(block * tile, LANES), tile)
        out_ref[part] = tn(active_ref[:, cols], dbranch_ref[...]).astype(bf16)


def grad_narrow(where, active, dbranch, count, after=()):
    units, channels = active.shape[1], dbranch.shape[1]
    shape = array((count, units // 8, channels), bf16)
    return call(grad_narrow_kernel, "grad_narrow", shape, 0.3 * count, limit=2 * count, smem=1, after=after)(where, active, dbranch)


def send_halves(where_ref, blocks, keep_ref, left_ref, right_ref):
    x, y = lax.rem(where_ref[2], 2), where_ref[2] // 2
    for turn in range(2):
        keep_ref[0, turn] = blocks[2 * x + turn]
        keep_ref[1, turn] = blocks[4 + 2 * y + turn]
        left_ref[turn] = blocks[2 * (1 - x) + turn]
        right_ref[turn] = blocks[4 + 2 * (1 - y) + turn]


def halves_of(lines, width):
    half = array((2, lines, width), bf16)
    return (array((2, 2, lines, width), bf16), half, half), [pltpu.VMEM((8, lines, width), bf16)]


def grad_narrow_here_kernel(where_ref, active_ref, dbranch_ref, received_ref, keep_ref, left_ref, right_ref, blocks):
    count, tile, _ = received_ref.shape
    lines = tile // 8
    for part in range(count):
        block = 2 * jnp.bitwise_xor(part, where_ref[2]) + where_ref[1]
        cols = pl.ds(pl.multiple_of(block * tile, LANES), tile)
        total = tn(active_ref[:, cols], dbranch_ref[...]) + received_ref[part].astype(f32)
        for block in range(8):
            blocks[block, pl.ds(part * lines, lines), :] = total[block * lines : (block + 1) * lines].astype(bf16)
    send_halves(where_ref, blocks, keep_ref, left_ref, right_ref)


def grad_narrow_here(where, active, dbranch, received, after=()):
    count, tile, channels = received.shape
    shapes, scratch = halves_of(count * tile // 8, channels)
    return call(grad_narrow_here_kernel, "grad_narrow_here", shapes, 0.1, scratch, limit=6, smem=1, after=after)(
        where, active, dbranch, received
    )


def hidden_back_kernel(where_ref, dbranch_ref, weight_ref, slope_ref, dhidden_ref, gbin_ref):
    tile = slope_ref.shape[1] // 4
    for part in range(4):
        cols = pl.ds(part * tile, tile)
        d_active = nt(dbranch_ref[...], weight_ref[cols, :])
        d_hidden = (d_active * slope_ref[:, cols].astype(f32)).astype(bf16)
        dhidden_ref[:, cols] = d_hidden
        start = jnp.bitwise_xor(part, where_ref[2]) * tile
        gbin_ref[:, pl.ds(pl.multiple_of(start, LANES), tile)] = jnp.sum(d_hidden.astype(f32), axis=0, keepdims=True)


def hidden_back(where, dbranch, weight, slope, after=()):
    rows, units = slope.shape
    shapes = (array((rows, units), bf16), array((1, units)))
    return call(hidden_back_kernel, "hidden_back", shapes, 2, smem=1, after=after)(
        where, dbranch, weight, slope
    )


def grad_widen_full_kernel(normed_ref, dhidden_ref, out_ref):
    tile = 768
    for part in range(out_ref.shape[1] // tile):
        cols = pl.ds(part * tile, tile)
        out_ref[:, cols] = tn(normed_ref[...], dhidden_ref[:, cols]).astype(bf16)


def grad_widen_full(normed, dhidden):
    shape = array((normed.shape[1], dhidden.shape[1]), bf16)
    return call(grad_widen_full_kernel, "grad_widen_full", shape, 5, limit=24)(normed, dhidden)


def grad_widen_away_kernel(where_ref, pair_ref, dhidden_ref, out_ref):
    blocks, lines, width = out_ref.shape
    for part in range(blocks // 2):
        total = tn(pair_ref[:, pl.ds(0, lines)], dhidden_ref[:, pl.ds(2 * part * width, 2 * width)]).astype(bf16)
        block = 2 * jnp.bitwise_xor(part, where_ref[2])
        out_ref[block] = total[:, :width]
        out_ref[block + 1] = total[:, width:]


def grad_widen_away(where, pair, dhidden, after=()):
    shape = array((8, pair.shape[1] // 2, dhidden.shape[1] // 8), bf16)
    return call(grad_widen_away_kernel, "grad_widen_away", shape, 0.01, smem=1, after=after)(where, pair, dhidden)


def grad_widen_here_kernel(where_ref, pair_ref, dhidden_ref, received_ref, keep_ref, left_ref, right_ref, blocks):
    _, lines, width = blocks.shape
    for part in range(4):
        both = tn(pair_ref[:, pl.ds(lines, lines)], dhidden_ref[:, pl.ds(2 * part * width, 2 * width)])
        for turn in range(2):
            block = 2 * jnp.bitwise_xor(part, where_ref[2]) + turn
            value = both[:, turn * width : (turn + 1) * width] + received_ref[block].astype(f32)
            blocks[block] = value.astype(bf16)
    send_halves(where_ref, blocks, keep_ref, left_ref, right_ref)


def grad_widen_here(where, pair, dhidden, received, after=()):
    shapes, scratch = halves_of(*received.shape[1:])
    return call(grad_widen_here_kernel, "grad_widen_here", shapes, 0.01, scratch, limit=6, smem=1, after=after)(
        where, pair, dhidden, received
    )


def norm_back_kernel(dhidden_ref, weight_ref, xhat_ref, rstd_ref, small_ref, dconv_ref, sums_ref):
    rows, channels = xhat_ref.shape
    size = 160
    gain = small_ref[pl.ds(GAIN, 1), :]
    sums = [jnp.zeros((1, channels), f32)] * 3
    for part in range(rows // size):
        lines = pl.ds(part * size, size)
        d_normed = nt(dhidden_ref[lines, :], weight_ref[...])
        xhat = xhat_ref[lines, :].astype(f32)
        product = d_normed * xhat
        d_xhat = d_normed * gain
        mean = jnp.sum(d_xhat, axis=-1, keepdims=True) * (1.0 / channels)
        along = jnp.sum(product * gain, axis=-1, keepdims=True) * (1.0 / channels)
        d_conv = (d_xhat - mean - xhat * along) * rstd_ref[lines, :]
        for tile in range(dconv_ref.shape[0]):
            dconv_ref[tile, lines, :] = d_conv[:, tile * LANES : (tile + 1) * LANES]
        for number, value in enumerate((d_conv, product, d_normed)):
            sums[number] = sums[number] + jnp.sum(value, axis=0, keepdims=True)
    sums_ref[...] = jnp.concatenate(sums, axis=0)


def norm_back(dhidden, weight, xhat, rstd, small, after=()):
    rows, channels = xhat.shape
    return call(
        norm_back_kernel, "norm_back", (array((channels // LANES, rows, LANES)), array((3, channels))), 0.01, after=after
    )(dhidden, weight, xhat, rstd, small)


def grad_taps_kernel(x_ref, dconv_ref, out_ref):
    @pl.loop(0, x_ref.shape[0])
    def _(tile):
        cols = pl.ds(pl.multiple_of(tile * LANES, LANES), LANES)
        for ky in range(KERNEL):
            totals = [None] * KERNEL
            for row in range(CANVAS):
                source_row = row + ky - REACH
                if not 0 <= source_row < CANVAS:
                    continue
                cells = [x_ref[tile, pl.ds((source_row * CANVAS + col) * 8, 8), :] for col in range(CANVAS)]
                grads = [dconv_ref[tile, pl.ds((row * CANVAS + col) * 8, 8), :] for col in range(CANVAS)]
                for kx in range(KERNEL):
                    for col in range(CANVAS):
                        source = col + kx - REACH
                        if 0 <= source < CANVAS:
                            term = cells[source] * grads[col]
                            totals[kx] = term if totals[kx] is None else totals[kx] + term
            for kx in range(KERNEL):
                out_ref[pl.ds(ky * KERNEL + kx, 1), cols] = jnp.sum(totals[kx], axis=0, keepdims=True)


def grad_taps(x, dconv, after=()):
    return call(grad_taps_kernel, "grad_taps", array((TAPS, x.shape[0] * LANES)), 0.01, after=after)(x, dconv)


def conv_back_kernel(sizes_ref, dconv_ref, small_ref, dmixed_ref, out_ref, total):
    tiles = dconv_ref.shape[0]
    images = out_ref.shape[0]
    frames = 2 * images
    side = side_of(sizes_ref, images)

    @pl.loop(0, tiles)
    def _(tile):
        def finish(cell, value):
            lines = pl.ds(cell * 8, 8)
            inside = side > max(cell // CANVAS, cell % CANVAS)
            total[tile, lines, :] = jnp.where(inside, value + dmixed_ref[tile, lines, :], 0.0)

        conv_rows(dconv_ref, tile, small_ref, True, finish)

    for image in range(images):
        for which in range(2):
            for row in range(CANVAS):
                lines = pl.ds(row * CANVAS * frames + which * images + image, CANVAS, stride=frames)
                for tile in range(tiles):
                    out_ref[image, which, row, :, lane_tile(tile)] = total[tile, lines, :]


def conv_back(sizes, dconv, small, dmixed, after=()):
    tiles, rows, _ = dconv.shape
    images = sizes.shape[0]
    return call(
        conv_back_kernel,
        "conv_back",
        array((images, 2, CANVAS, CANVAS, tiles * LANES)),
        0.1,
        [pltpu.VMEM((tiles, rows + SPARE, LANES), f32)],
        limit=6,
        smem=1,
        after=after,
    )(sizes, dconv, small, dmixed)


def start_all(copies, sems):
    running = [pltpu.make_async_copy(source, target, sems.at[number]) for number, (source, target) in enumerate(copies)]
    for copy in running:
        copy.start()
    return running

GROUPS = 6
LINES = 24
BIAS = SMALL


def pack_kernel(where_ref, weight_ref, taps_ref, west_ref, *refs):
    vectors, (bias_ref, out_ref, small, taps, west, *held, bias, sems) = refs[:5], refs[5:]
    share = weight_ref.shape[0]
    wide = out_ref.shape[1]
    cols = pl.ds(pl.multiple_of(where_ref[2] * wide, LANES), wide)
    copies = [(taps_ref, taps), (west_ref, west), (bias_ref, bias)]
    copies += list(zip(vectors, held))
    copies += [(weight_ref.at[:, cols], out_ref.at[pl.ds(0, share)])]
    running = start_all(copies, sems)
    small[...] = jnp.zeros_like(small)
    lane = pl.ds(0, share)
    for copy in running[:-1]:
        copy.wait()
    small[pl.ds(0, TAPS), lane] = taps[...].astype(f32)
    small[pl.ds(WEST, OFFSETS), lane] = west[...].astype(f32)
    for number, vector in enumerate(held):
        small[pl.ds(CBIAS + number, 1), lane] = vector[...].astype(f32).reshape(1, share)
    for part in range(bias.shape[0] // LANES):
        small[pl.ds(BIAS + part, 1), :] = bias[lane_tile(part)].astype(f32).reshape(1, LANES)
    for group in range(GROUPS):
        out_ref[pl.ds(share, LINES), lane_tile(group)] = small[pl.ds(group * LINES, LINES), :].astype(bf16)
    running[-1].wait()


def pack(where, weight, taps, west, vectors, bias, after=()):
    share, units = weight.shape
    args = (weight, taps, west, *vectors, bias)
    return call(
        pack_kernel,
        "pack",
        array((share + LINES, units // 4), bf16),
        2,
        [
            pltpu.VMEM((GROUPS * LINES, LANES), f32),
            pltpu.VMEM(taps.shape, bf16),
            pltpu.VMEM(west.shape, bf16),
            *[pltpu.VMEM((share,), bf16)] * len(vectors),
            pltpu.VMEM(bias.shape, bf16),
            pltpu.SemaphoreType.DMA((len(args),)),
        ],
        smem=1,
        left=len(args),
        after=after,
    )(where, *args)


def stack_kernel(*refs):
    first = refs[0].shape[0] - LINES
    for number, ref in enumerate(refs[:-1]):
        refs[-1][number] = ref[pl.ds(first, LINES), :]


def stack(parts, after=()):
    shape = array((len(parts), LINES, parts[0].shape[1]), bf16)
    return call(stack_kernel, "stack", shape, 0.05, after=after)(*parts)


def unpack_kernel(where_ref, mine_ref, theirs_ref, small_ref, bias_ref):
    z, core, slabs = where_ref[0], where_ref[1], where_ref[3]
    channels = small_ref.shape[1]
    share = channels // 8
    everything = None
    for number in range(8):
        ref = mine_ref if number < 4 else theirs_ref
        shard = 2 * lax.rem(z - number % 4 + slabs, slabs) + (core if number < 4 else 1 - core)
        rows = jnp.concatenate([ref[number % 4, :, lane_tile(group)].astype(f32) for group in range(GROUPS)], axis=0)
        source = lax.broadcasted_iota(jnp.int32, (LANES, channels), 0)
        target = lax.broadcasted_iota(jnp.int32, (LANES, channels), 1)
        spread = ((target - shard * share == source) & (source < share)).astype(bf16)
        value = dot(rows.astype(bf16), spread)
        everything = value if everything is None else everything + value
        width = bias_ref.shape[1] // 8
        for part in range(width // LANES):
            cols = pl.ds(pl.multiple_of(shard * width + part * LANES, LANES), LANES)
            bias_ref[:, cols] = rows[BIAS + part : BIAS + part + 1, :]
    small_ref[...] = everything[: small_ref.shape[0]]


def unpack(where, mine, theirs, units, channels):
    return call(unpack_kernel, "unpack", (array((SMALL, channels)), array((1, units))), 1.2, smem=1)(where, mine, theirs)


def column_kernel(*refs):
    parts, outs = refs[:-2], refs[-2:]
    rows, width = outs[0].shape[1:]
    for turn, out in enumerate(outs):
        for number, part in enumerate(parts):
            out[number] = part[pl.ds(0, rows), pl.ds(turn * width, width)]


def column(parts, rows, after=()):
    half = array((len(parts), rows, parts[0].shape[1] // 2), bf16)
    return call(column_kernel, "column", (half, half), 0.05, after=after)(*parts)


def cut_kernel(where_ref, weight_ref, out_ref, sem):
    tall = out_ref.shape[0]
    lines = pl.ds(pl.multiple_of(where_ref[2] * tall, 16), tall)
    copy = pltpu.make_async_copy(weight_ref.at[lines], out_ref, sem)
    copy.start()
    copy.wait()


def cut(where, weight, after=()):
    tall, channels = weight.shape
    shape = array((tall // 4, channels), bf16)
    return call(cut_kernel, "cut", shape, 1, [pltpu.SemaphoreType.DMA], smem=1, left=1, after=after)(where, weight)


def onward_kernel(left_ref, right_ref, left_in_ref, right_in_ref, to_x_ref, to_y_ref):
    to_y_ref[0] = left_ref[...]
    to_y_ref[1] = left_in_ref[...]
    to_x_ref[0] = right_ref[...]
    to_x_ref[1] = right_in_ref[...]


def onward(left, right, left_in, right_in, after=()):
    shape = array((2, *left.shape), bf16)
    return call(onward_kernel, "onward", (shape, shape), 1, after=after)(left, right, left_in, right_in)


def halve_kernel(where_ref, keep_ref, left_in_ref, right_in_ref, keep_out_ref, left_ref, right_ref):
    x, y = lax.rem(where_ref[2], 2), where_ref[2] // 2

    def total(side, which):
        received = left_in_ref if side == 0 else right_in_ref
        return keep_ref[side, which].astype(f32) + received[which].astype(f32)

    keep_out_ref[0] = total(0, y).astype(bf16)
    keep_out_ref[1] = total(1, x).astype(bf16)
    left_ref[...] = total(0, 1 - y).astype(bf16)
    right_ref[...] = total(1, 1 - x).astype(bf16)


def halve(where, keep, left_in, right_in, after=()):
    _, _, lines, width = keep.shape
    half = array((lines, width), bf16)
    shapes = (array((2, lines, width), bf16), half, half)
    return call(halve_kernel, "halve", shapes, 0.01, smem=1, after=after)(where, keep, left_in, right_in)


def deal_total(where_ref, keep_ref, left_in_ref, right_in_ref, total):
    total[0] = (keep_ref[0].astype(f32) + left_in_ref[...].astype(f32)).astype(bf16)
    total[1] = (keep_ref[1].astype(f32) + right_in_ref[...].astype(f32)).astype(bf16)


def deal_kernel(where_ref, keep_ref, left_in_ref, right_in_ref, *refs):
    outs, total = refs[:-1], refs[-1]
    share = outs[0].shape[1]
    deal_total(where_ref, keep_ref, left_in_ref, right_in_ref, total)
    for step, out in enumerate(outs):
        slab = lax.rem(where_ref[0] + step, len(outs))
        for side in range(2):
            out[side] = total[side, pl.ds(pl.multiple_of(slab * share, 16), share), :]


def deal(where, keep, left_in, right_in, slabs, after=()):
    _, lines, width = keep.shape
    shapes = (array((2, lines // slabs, width), bf16),) * slabs
    scratch = [pltpu.VMEM(keep.shape, bf16)]
    return call(deal_kernel, "deal", shapes, 0.01, scratch, smem=1, after=after)(where, keep, left_in, right_in)


SMALL_ROWS = 144


def deal_small_kernel(where_ref, keep_ref, left_in_ref, right_in_ref, here_ref, received_ref, *refs):
    outs, total = refs[:-1], refs[-1]
    deal_total(where_ref, keep_ref, left_in_ref, right_in_ref, total)
    share = total.shape[1] // len(outs)
    extra = outs[0].shape[1] - share
    for step, out in enumerate(outs):
        slab = lax.rem(where_ref[0] + step, len(outs))
        small = here_ref[slab] + received_ref[slab]
        lines = SMALL_ROWS // 4
        small = jnp.concatenate([small[part * lines : (part + 1) * lines] for part in range(4)], axis=1)
        for side in range(2):
            out[side, pl.ds(0, share), :] = total[side, pl.ds(pl.multiple_of(slab * share, 16), share), :]
            out[side, pl.ds(share, extra), :] = small[side * extra : (side + 1) * extra].astype(bf16)


def deal_small(where, keep, left_in, right_in, here, received, after=()):
    slabs = here.shape[0]
    _, lines, width = keep.shape
    extra = SMALL_ROWS * here.shape[2] // width // 2
    shapes = (array((2, lines // slabs + extra, width), bf16),) * slabs
    scratch = [pltpu.VMEM(keep.shape, bf16)]
    return call(deal_small_kernel, "deal_small", shapes, 0.01, scratch, smem=1, after=after)(
        where, keep, left_in, right_in, here, received
    )


def total_kernel(*refs):
    total = refs[0][...].astype(f32)
    for ref in refs[1:-1]:
        total = total + ref[...].astype(f32)
    refs[-1][...] = total.astype(refs[-1].dtype)


def total(values, after=()):
    return call(total_kernel, "total", array(values[0].shape, values[0].dtype), 1, after=after)(*values)


def blocks_of(where_ref, flip):
    group = jnp.bitwise_xor(where_ref[2], flip)
    x, y = lax.rem(group, 2), group // 2
    return 2 * x + y, 4 + 2 * y + x


def spread_wout_kernel(where_ref, *refs):
    *values, out_ref = refs
    lines = values[0].shape[1]
    for flip, ref in enumerate(values):
        for side, block in enumerate(blocks_of(where_ref, flip)):
            out_ref[pl.ds(pl.multiple_of(block * lines, 16), lines), :] = ref[side].astype(f32)


def spread_wout(where, values, after=()):
    _, lines, channels = values[0].shape
    return call(spread_wout_kernel, "spread_wout", array((8 * lines, channels)), 1, smem=1, after=after)(where, *values)


def spread_win_kernel(where_ref, *refs):
    values, (out_ref, taps_ref, west_ref, bias_ref, *vectors, small) = refs[:4], refs[4:]
    share = out_ref.shape[0]
    _, lines, width = values[0].shape
    extra = lines - share
    for flip, ref in enumerate(values):
        for side, block in enumerate(blocks_of(where_ref, flip)):
            out_ref[:, pl.ds(pl.multiple_of(block * width, LANES), width)] = ref[side, pl.ds(0, share), :].astype(f32)
    for side in range(2):
        part = [ref[side, pl.ds(share, extra), :].astype(f32) for ref in values]
        both = (part[0] + part[1]) + (part[2] + part[3])
        for group in range(4):
            span = pl.ds(group * 2 * extra + side * extra, extra)
            small[span, :] = both[:, group * share : (group + 1) * share]
    taps_ref[...] = small[pl.ds(0, TAPS), :]
    for number, ref in enumerate(vectors):
        ref[...] = small[pl.ds(TAPS + number, 1), :]
    west_ref[...] = small[pl.ds(TAPS + 5, OFFSETS), :]
    rows = bias_ref.shape[0] // share
    first = TAPS + 5 + OFFSETS
    bias_ref[...] = jnp.concatenate([small[pl.ds(first + row, 1), :] for row in range(rows)], axis=1).reshape(bias_ref.shape)


def spread_win(where, values, share, after=()):
    width = values[0].shape[2]
    shapes = [array((share, 8 * width)), array((TAPS, share)), array((OFFSETS, share)), array((width,))]
    shapes += [array((1, share))] * 5
    scratch = [pltpu.VMEM((SMALL_ROWS, share), f32)]
    return call(spread_win_kernel, "spread_win", shapes, 1, scratch, smem=1, after=after)(where, *values)


def pack_small_kernel(where_ref, gtaps_ref, gnorm_ref, gbout_ref, gscale_ref, gwest_ref, gbin_ref, here_ref, away_ref):
    slabs, _, share = here_ref.shape

    def fill(even_ref, odd_ref):
        for shard in range(2 * slabs):
            out = odd_ref if shard % 2 else even_ref
            cols = pl.ds(shard * share, share)
            line = 0
            for ref in (gtaps_ref, gnorm_ref, gbout_ref, gscale_ref, gwest_ref):
                out[shard // 2, pl.ds(line, ref.shape[0]), :] = ref[:, cols]
                line += ref.shape[0]
            lines = gbin_ref.shape[1] // gtaps_ref.shape[1]
            for extra in range(lines):
                span = pl.ds((shard * lines + extra) * share, share)
                out[shard // 2, pl.ds(line + extra, 1), :] = gbin_ref[:, span]
            rest = SMALL_ROWS - line - lines
            out[shard // 2, pl.ds(line + lines, rest), :] = jnp.zeros((rest, share), f32)

    @pl.when(where_ref[1] == 0)
    def _():
        fill(here_ref, away_ref)

    @pl.when(where_ref[1] == 1)
    def _():
        fill(away_ref, here_ref)


def pack_small(where, parts, slabs, share, after=()):
    shape = array((slabs, SMALL_ROWS, share))
    return call(pack_small_kernel, "pack_small", (shape, shape), 0.01, smem=1, after=after)(where, *parts)


AXES = ("dp", "fsdp")


class Routes:
    def __init__(self, groups, members):
        self.groups, self.members, self.slabs = groups, members, members // 2
        self.group = lax.axis_index("dp")
        member = lax.axis_index("fsdp")
        self.slab, self.core = member // 2, member % 2

    def send(self, value, target):
        pairs = [
            (group * self.members + 2 * slab + core, self.index(*target(group, slab, core)))
            for group in range(self.groups)
            for slab in range(self.slabs)
            for core in range(2)
        ]
        return lax.ppermute(value, AXES, pairs)

    def index(self, group, slab, core):
        return group * self.members + 2 * slab + core

    def to_core(self, value):
        return self.send(value, lambda group, slab, core: (group, slab, 1 - core))

    def to_slab(self, value, step):
        return self.send(value, lambda group, slab, core: (group, (slab + step) % self.slabs, core))

    def to_near(self, value, flip):
        return self.send(value, lambda group, slab, core: (group, slab ^ flip, core))

    def to_group(self, value, flip):
        return self.send(value, lambda group, slab, core: (group ^ flip, slab, core))


def shards(
    features,
    cotangent,
    image_sizes,
    warp_index,
    warp_weight,
    offsets,
    conv_kernel,
    conv_bias,
    norm_gain,
    norm_bias,
    w_in,
    bias_in,
    w_out,
    bias_out,
    layer_scale,
    w_estimate,
):
    share, units = w_in.shape
    channels = features.shape[-1]
    members = channels // share
    groups = lax.axis_size("dp")
    paired = groups == 4 and members == 8

    reach = WINDOW // 2
    lane_of = (offsets[:, 0] + reach) * CANVAS + offsets[:, 1] + reach
    place = jnp.pad(lane_of, (0, LANES - OFFSETS), constant_values=-1)[None]

    early = (features, cotangent, warp_index, warp_weight, place, lane_of)
    if paired:
        routes = Routes(groups, members)
        slabs = routes.slabs
        where = jnp.stack([routes.slab, routes.core, routes.group, jnp.int32(slabs)])
        vectors = (conv_bias, norm_gain, norm_bias, bias_out, layer_scale)
        packed = pack(where, w_in, conv_kernel, w_estimate, vectors, bias_in)
        win_parts = [routes.to_slab(packed, step) for step in range(1, slabs)]
        win_own = routes.to_core(w_in)
        small = stack([packed, *win_parts], after=early)
        quarter = cut(where, w_out, after=(packed,))
        wout_parts = [routes.to_slab(quarter, step) for step in range(1, slabs)]
        wout_own = routes.to_core(w_out)
        small, bin_all = unpack(where, small, routes.to_core(small), units, channels)
    else:
        where = jnp.zeros((4,), jnp.int32)
        small = jnp.concatenate(
            [
                conv_kernel,
                w_estimate,
                jnp.stack([conv_bias, norm_gain, norm_bias, bias_out, layer_scale]),
                bias_in.reshape(-1, share),
            ]
        )
        small = lax.all_gather(small, "fsdp")
        win_all = lax.all_gather(w_in, "fsdp", axis=0, tiled=True)
        wout_all = lax.all_gather(w_out, "fsdp", axis=0, tiled=True)
        bin_all = small[:, SMALL:].reshape(1, units).astype(f32)
        small = small[:, :SMALL].transpose(1, 0, 2).reshape(SMALL, channels).astype(f32)
    after = ()
    if paired:
        left, right = column(win_parts, share, after=(wout_parts[0],))
        left_in, right_in = routes.to_group(left, 1), routes.to_group(right, 2)
        after = (left,)
    x, up, begun = conv_begin(image_sizes, features, cotangent, small, after)
    if paired:
        to_x, to_y = onward(left, right, left_in, right_in, after=(begun,))
        win_halves = [to_x, to_y, routes.to_group(to_x, 1), routes.to_group(to_y, 2)]
        left, right = column(wout_parts, units // members // 4, after=(to_x,))
        left_in, right_in = routes.to_group(left, 1), routes.to_group(right, 2)
        after = (left,)
    normed, pair, xhat, rstd = conv_norm(where, x, begun, small, after)
    if paired:
        to_x, to_y = onward(left, right, left_in, right_in, after=(normed,))
        wout_halves = [to_x, to_y, routes.to_group(to_x, 1), routes.to_group(to_y, 2)]
        win_halves = gate(win_halves, (to_x,))
        win_theirs = [win_own] + [routes.to_core(value) for value in win_halves]
        win_all, active, slope = place_widen(where, [w_in, *win_halves], win_theirs, normed, bin_all)
        wout_halves = gate(wout_halves, (active,))
        wout_theirs = [wout_own] + [routes.to_core(value) for value in wout_halves]
        begun = place_narrow(0, where, [w_out, *wout_halves], active, small)
        wout_all, branch = place_narrow(1, where, wout_theirs, active, *begun)
    else:
        active, slope = widen(normed, win_all, bin_all)
        branch = narrow(active, wout_all, small)
    gated, d_mixed, d_branch, g_scale, g_bout = flow(
        image_sizes, x, branch, up, warp_index, warp_weight, place, small
    )
    if paired:
        wout_away = grad_narrow(where, active, d_branch, slabs)
        wout_in = routes.to_core(wout_away)
        d_hidden, g_bin = hidden_back(where, d_branch, wout_all, slope, after=(wout_away,))
        win_away = grad_widen_away(where, pair, d_hidden)
        win_in = routes.to_core(win_away)
        keep_out, left, right = grad_narrow_here(where, active, d_branch, wout_in, after=(win_away,))
        left_out, right_out = routes.to_group(left, 1), routes.to_group(right, 2)
        keep_in, left, right = grad_widen_here(where, pair, d_hidden, win_in, after=(keep_out,))
        left_in, right_in = routes.to_group(left, 1), routes.to_group(right, 2)
        d_conv, g_norm = norm_back(d_hidden, win_all, xhat, rstd, small, after=(keep_in,))
        mixed_out, g_west = finish(image_sizes, lane_of, x, branch, up, gated, place, small, after=(d_conv,))
        keep_out, left, right = halve(where, keep_out, left_out, right_out, after=(g_west,))
        left_out, right_out = routes.to_group(left, 2), routes.to_group(right, 1)
        g_taps = grad_taps(x, d_conv, after=(keep_out,))
        parts = (g_taps, g_norm, g_bout, g_scale, g_west, g_bin)
        small_here, small_away = pack_small(where, parts, slabs, share)
        small_in = routes.to_core(small_away)
        keep_in, left, right = halve(where, keep_in, left_in, right_in, after=(small_away,))
        left_in, right_in = routes.to_group(left, 2), routes.to_group(right, 1)
        wout_parts = deal(where, keep_out, left_out, right_out, slabs, after=(keep_in,))
        wout_parts = wout_parts[:1] + tuple(routes.to_slab(v, n + 1) for n, v in enumerate(wout_parts[1:]))
        win_parts = deal_small(where, keep_in, left_in, right_in, small_here, small_in, after=wout_parts[:1])
        win_parts = win_parts[:1] + tuple(routes.to_slab(v, n + 1) for n, v in enumerate(win_parts[1:]))
        grad_features = conv_back(image_sizes, d_conv, small, d_mixed, after=win_parts[:1])
        g_wout = total(wout_parts, after=(grad_features,))
        wout_parts = [g_wout] + [routes.to_group(g_wout, flip) for flip in range(1, 4)]
        g_win = total(win_parts, after=(g_wout,))
        win_parts = [g_win] + [routes.to_group(g_win, flip) for flip in range(1, 4)]
        g_wout = spread_wout(where, wout_parts, after=(g_win,))
        g_win, g_taps, g_west, g_bin, *g_small = spread_win(where, win_parts, share)
        g_small = [value.reshape(share) for value in g_small]
    else:
        g_wout = grad_narrow(where, active, d_branch, 8).reshape(units, channels)
        d_hidden, g_bin = hidden_back(where, d_branch, wout_all, slope)
        g_win = grad_widen_full(normed, d_hidden)
        d_conv, g_norm = norm_back(d_hidden, win_all, xhat, rstd, small)
        g_taps = grad_taps(x, d_conv)
        mixed_out, g_west = finish(image_sizes, lane_of, x, branch, up, gated, place, small)
        grad_features = conv_back(image_sizes, d_conv, small, d_mixed)
        g_small = jnp.concatenate([g_taps, g_norm, g_bout, g_scale, g_west])
        g_small = g_small.reshape(-1, members, share).transpose(1, 0, 2)
        g_small = jnp.concatenate([g_small, g_bin.reshape(members, -1, share)], axis=1)

        def reduce(value):
            return lax.psum(lax.psum_scatter(value, "fsdp", scatter_dimension=0, tiled=True).astype(f32), "dp")

        g_wout, g_win, g_small = reduce(g_wout), reduce(g_win), reduce(g_small)[0]
        tail = TAPS + 5 + OFFSETS
        g_taps, g_west, g_bin = g_small[:TAPS], g_small[TAPS + 5 : tail], g_small[tail:]
        g_small = g_small[TAPS : TAPS + 5]
    return (
        mixed_out,
        grad_features,
        g_taps,
        g_small[0],
        g_small[1],
        g_small[2],
        g_win,
        g_bin.reshape(-1),
        g_wout,
        g_small[3],
        g_small[4],
        g_west,
    )


def solution(mesh):
    in_specs = (
        P(("dp", "fsdp"), None, None, None, None),
        P(("dp", "fsdp"), None, None, None, None),
        P(("dp", "fsdp")),
        P(("dp", "fsdp"), None, None),
        P(("dp", "fsdp"), None, None),
        P(),
        P(None, "fsdp"),
        P("fsdp"),
        P("fsdp"),
        P("fsdp"),
        P("fsdp", None),
        P("fsdp"),
        P("fsdp", None),
        P("fsdp"),
        P("fsdp"),
        P(None, "fsdp"),
    )
    out_specs = (
        P(("dp", "fsdp"), None, None, None, None),
        P(("dp", "fsdp"), None, None, None, None),
        P(None, "fsdp"),
        P("fsdp"),
        P("fsdp"),
        P("fsdp"),
        P("fsdp", None),
        P("fsdp"),
        P("fsdp", None),
        P("fsdp"),
        P("fsdp"),
        P(None, "fsdp"),
    )
    return jax.shard_map(shards, mesh=mesh, in_specs=in_specs, out_specs=out_specs, check_vma=False)
```
